32 devices in a mesh: dp: 16 (over z, y, x), tensor: 2 (over core).
Axes of the slice: x: 2, y: 2, z: 4, core: 2. Of those that a mesh axis runs over, the one named last changes fastest.
Arguments:
- tokens: bfloat16 [36864, 768], P(('dp', 'tensor')), may hold values from -6 to 6
- segment: int32 [36864], P('dp'), may hold values from -1 to 17, as said below
- norm_attn_gain: bfloat16 [768], P('dp'), may hold values from 0.099609375 to 1.8984375
- qkv_weight: bfloat16 [768, 3, 768], P('dp', None, 'tensor'), may hold values from -0.21875 to 0.21875
- attn_out_weight: bfloat16 [768, 768], P('tensor', 'dp'), may hold values from -0.625 to 0.625
- norm_mlp_gain: bfloat16 [768], P('dp'), may hold values from 0.099609375 to 1.8984375
- in_weight: bfloat16 [768, 2, 1152], P('dp', None, 'tensor'), may hold values from -0.21875 to 0.21875
- out_weight: bfloat16 [1152, 768], P('tensor', 'dp'), may hold values from -0.25 to 0.25
- cotangent: bfloat16 [36864, 768], P(('dp', 'tensor')), may hold values from -6 to 6
Outputs:
- layer_out: bfloat16 [36864, 768], P(('dp', 'tensor'))
- grad_tokens: float32 [36864, 768], P(('dp', 'tensor'))
- grad_norm_attn_gain: float32 [768], P('dp')
- grad_qkv_weight: float32 [768, 3, 768], P('dp', None, 'tensor')
- grad_attn_out_weight: float32 [768, 768], P('tensor', 'dp')
- grad_norm_mlp_gain: float32 [768], P('dp')
- grad_in_weight: float32 [768, 2, 1152], P('dp', None, 'tensor')
- grad_out_weight: float32 [1152, 768], P('tensor', 'dp')
The draws below stay inside these ranges and needn't reach their ends.
Inputs may be any that keep to these rules, and one draw needn't show every extreme that they name: Within each group of 2304 slots, a sequence occupies whole consecutive padding blocks starting at the block named by its segment value; its live slots come first and fewer than 128 padding slots end its last block; whole padding blocks may end a group, at most a quarter of them. In every group one sequence holds the last slot of the first half of the group and the first slot of the second half.
All inputs are finite; a program needn't handle non-finite values.
Results may differ from the reference program's by a relative error of at most 0.018.
Values may be sent and summed in bfloat16 or wider, within the bound.
No kernel may reach another device: no remote copies, remote signals or barrier semaphores. Data moves between devices by JAX's collectives and lax.ppermute only.
A program may use at most 192 MiB of HBM per device.

```python
import jax
import jax.numpy as jnp
from jax import lax

D = 768
HEADS = 12
HEAD_DIM = 64
FF = 1152
WINDOW_HALF = 64
PAD_BLOCK = 128
QBLOCK = 1152
GROUP = 2304
TOKENS = 36864
N_DP = 16


def draw_segment(key, part):
    key = jax.random.fold_in(key, 7)
    key_starts, key_empty, key_pad = jax.random.split(key, 3)
    block_count = GROUP // PAD_BLOCK
    group_count = TOKENS // GROUP
    blocks = jnp.arange(block_count, dtype=jnp.int32)
    groups = jnp.arange(group_count, dtype=jnp.int32)
    first_group = (groups == 0)[:, None]
    starts = jax.random.randint(key_starts, (group_count, block_count), 0, 3) == 0
    forced = first_group & (blocks == block_count - 1)[None, :]
    starts = (starts | (blocks == 0)[None, :] | forced) & (blocks != block_count // 2)[None, :]
    empty = jax.random.randint(key_empty, (group_count, 1), 0, block_count // 4 + 1)
    empty = jnp.where(first_group, 0, empty)
    live_block = blocks[None, :] < block_count - empty
    first_block = lax.cummax(jnp.where(starts, blocks[None, :], 0), axis=1)
    follower = jnp.concatenate([starts[:, 1:] | ~live_block[:, 1:], jnp.ones((group_count, 1), jnp.bool_)], axis=1)
    closing = live_block & follower
    padding = jax.random.randint(key_pad, (group_count, block_count, 1), 0, PAD_BLOCK)
    padding = jnp.where(first_group[:, :, None] & (blocks == block_count - 1)[None, :, None], jnp.maximum(padding, 1), padding)
    within = jnp.arange(PAD_BLOCK, dtype=jnp.int32)[None, None, :]
    live = live_block[:, :, None] & ~(closing[:, :, None] & (within >= PAD_BLOCK - padding))
    result = jnp.where(live, first_block[:, :, None], -1)
    return result.reshape(TOKENS).astype(jnp.int32)


def spiked(entries, key, source, target, parts, factor):
    owner, partner = [(jnp.arange(entries.shape[dim]) // (entries.shape[dim] // parts)).reshape([-1 if axis == dim else 1 for axis in range(entries.ndim)]) for dim in (source, target)]
    chosen = jax.random.permutation(key, parts)[partner]
    strong = (owner == chosen) | (owner == (partner + parts // 2) % parts)
    return jnp.where(strong, factor * entries, entries)


def levels(key, extent, cuts, least, high):
    def one(axis_at, shards_of):
        steps = jax.random.uniform(jax.random.fold_in(jax.random.fold_in(key, 6), axis_at), (shards_of,), jnp.float32, least / len(cuts), high / len(cuts))
        return jnp.repeat(jnp.exp(steps), extent[axis_at] // shards_of).reshape((-1,) + (1,) * (len(extent) - axis_at - 1))

    factor_of = one(*cuts[0])
    for cut in cuts[1:]:
        factor_of = factor_of * one(*cut)
    return factor_of


def scatter_about(stream_key, extent, deviation, reach, cuts=(), held_as=jnp.bfloat16):
    values = deviation * jax.random.normal(stream_key, extent, jnp.float32)
    if cuts:
        values = values * levels(stream_key, extent, cuts, -0.22, 0.18)
    return jnp.clip(values, -reach, reach).astype(held_as)


def noise_with(stream_key, dims, deviation, reach, cuts, heavy, held_as=jnp.bfloat16):
    values = deviation * jax.random.normal(stream_key, dims, jnp.float32)
    if cuts:
        values = values * levels(stream_key, dims, cuts, -0.22, 0.18)
    return jnp.clip(spiked(values, jax.random.fold_in(stream_key, 3), *heavy), -reach, reach).astype(held_as)


def setup_inputs(seed: int = 0) -> dict:
    key_list = jax.random.split(jax.random.key(seed), 10)
    tokens = scatter_about(key_list[0], (TOKENS, D), 1.0, 6.0, ((0, 32),))
    segment = draw_segment(jax.random.fold_in(key_list[9], 71), 0)
    norm_attn_gain = jnp.clip(1.0 + 0.18 * jax.random.normal(key_list[2], (D,), jnp.float32), 0.099609375, 1.8984375).astype(jnp.bfloat16)
    qkv_weight = scatter_about(key_list[3], (D, 3, D), D ** -0.5, 0.21875, ((0, 16), (2, 2)))
    attn_out_weight = scatter_about(key_list[4], (D, D), (D // 8) ** -0.5, 0.625, ((0, 2), (1, 16)))
    norm_mlp_gain = jnp.clip(1.0 + 0.18 * jax.random.normal(key_list[5], (D,), jnp.float32), 0.099609375, 1.8984375).astype(jnp.bfloat16)
    in_weight = scatter_about(key_list[6], (D, 2, FF), D ** -0.5, 0.21875, ((0, 16), (2, 2)))
    out_weight = scatter_about(key_list[7], (FF, D), (FF // 2) ** -0.5, 0.25, ((0, 2), (1, 16)))
    cotangent = noise_with(key_list[8], (TOKENS, D), 1.0, 6.0, ((0, 32),), (0, 1, 32, 2.75))
    return dict(tokens=tokens, segment=segment, norm_attn_gain=norm_attn_gain, qkv_weight=qkv_weight, attn_out_weight=attn_out_weight, norm_mlp_gain=norm_mlp_gain, in_weight=in_weight, out_weight=out_weight, cotangent=cotangent)


@jax.custom_vjp
def low(v):
    return lax.optimization_barrier(v.astype(jnp.bfloat16)).astype(jnp.float32)

@jax.custom_vjp
def low_back(v):
    return v

def low_keep(v):
    return (low(v), None)

def low_pass(kept, grad):
    return (grad,)

def back_keep(v):
    return (v, None)

def back_low(kept, grad):
    return (low(grad),)
low.defvjp(low_keep, low_pass)
low_back.defvjp(back_keep, back_low)

def layer_norm(values, gain):
    centred = values - lax.optimization_barrier(jnp.mean(values, axis=-1, keepdims=True))
    spread = lax.optimization_barrier(jnp.mean(centred * centred, axis=-1, keepdims=True))
    return centred * lax.rsqrt(spread + 1e-05) * gain

def slot_position(segment):
    slots = jnp.arange(segment.shape[0], dtype=jnp.int32)
    return jnp.where(segment >= 0, slots - PAD_BLOCK * segment, 0).astype(jnp.int32)

def rope_tables(position):
    half = HEAD_DIM // 2
    exponent = jnp.arange(half).astype(jnp.float32) * (2.0 / HEAD_DIM)
    inverse = jnp.power(10000.0, -exponent)
    angle = position.astype(jnp.float32)[:, None] * inverse[None, :]
    angle = jnp.concatenate([angle, angle], axis=-1)
    return (jnp.cos(angle)[:, None, :], jnp.sin(angle)[:, None, :])

def rotate(values, cosine, sine):
    half = values.shape[-1] // 2
    turned = jnp.concatenate([-values[..., half:], values[..., :half]], axis=-1)
    return values * cosine + turned * sine

def attend_block(start, queries, key_pad, value_pad, segment, seg_pad):
    key_width = QBLOCK + 2 * WINDOW_HALF
    query_blk = lax.dynamic_slice_in_dim(queries, start, QBLOCK, 0)
    key_win = lax.dynamic_slice_in_dim(key_pad, start, key_width, 0)
    value_win = lax.dynamic_slice_in_dim(value_pad, start, key_width, 0)
    seg_query = lax.dynamic_slice_in_dim(segment, start, QBLOCK, 0)
    seg_keys = lax.dynamic_slice_in_dim(seg_pad, start, key_width, 0)
    raw = jnp.einsum('qhd,khd->hqk', query_blk, key_win, precision=lax.Precision.HIGHEST)
    scores = low_back(raw * HEAD_DIM ** (-0.5))
    row_pos = start + jnp.arange(QBLOCK, dtype=jnp.int32)
    col_pos = start - WINDOW_HALF + jnp.arange(key_width, dtype=jnp.int32)
    allowed = (seg_query[:, None] == seg_keys[None, :]) & (jnp.abs(row_pos[:, None] - col_pos[None, :]) <= WINDOW_HALF)
    scores = jnp.where(allowed[None], scores, -1e+30)
    top = lax.optimization_barrier(jnp.max(scores, axis=-1, keepdims=True))
    weights = jnp.exp(scores - top)
    probs = weights / lax.optimization_barrier(jnp.sum(weights, axis=-1, keepdims=True))
    return jnp.einsum('hqk,khd->qhd', low(probs), value_win, precision=lax.Precision.HIGHEST)

def forward_group(inputs, segment, gain_attn, qkv_w, attn_out_w, gain_mlp, in_w, out_w):
    highest = lax.Precision.HIGHEST
    group_rows = inputs.shape[0]
    normed = low(layer_norm(inputs, gain_attn))
    projected = low_back(jnp.einsum('rd,dcf->rcf', normed, qkv_w, precision=highest))
    cosine, sine = rope_tables(slot_position(segment))
    shape = (group_rows, HEADS, HEAD_DIM)
    queries = low(rotate(projected[:, 0].reshape(shape), cosine, sine))
    keys_rot = low(rotate(projected[:, 1].reshape(shape), cosine, sine))
    value_rows = low(projected[:, 2].reshape(shape))
    margin = ((WINDOW_HALF, WINDOW_HALF), (0, 0), (0, 0))
    key_pad = jnp.pad(keys_rot, margin)
    value_pad = jnp.pad(value_rows, margin)
    seg_pad = jnp.pad(segment, (WINDOW_HALF, WINDOW_HALF), constant_values=-2)
    block_fn = jax.checkpoint(attend_block)
    starts = jnp.arange(group_rows // QBLOCK, dtype=jnp.int32) * QBLOCK
    blocks = lax.map(lambda start: block_fn(start, queries, key_pad, value_pad, segment, seg_pad), starts)
    attended = low(low_back(blocks.reshape(group_rows, D)))
    hidden = inputs + low_back(jnp.dot(attended, attn_out_w, precision=highest))
    normed_two = low(layer_norm(hidden, gain_mlp))
    pre_act = low_back(jnp.einsum('rd,dcf->rcf', normed_two, in_w, precision=highest))
    gated = low(jax.nn.gelu(pre_act[:, 0], approximate=False) * pre_act[:, 1])
    return hidden + low_back(jnp.dot(gated, out_w, precision=highest))

def reference(tokens, segment, norm_attn_gain, qkv_weight, attn_out_weight, norm_mlp_gain, in_weight, out_weight, cotangent):
    params = tuple((p.astype(jnp.float32) for p in (norm_attn_gain, qkv_weight, attn_out_weight, norm_mlp_gain, in_weight, out_weight)))
    token_groups = tokens.astype(jnp.float32).reshape(N_DP, GROUP, D)
    seg_groups = segment.reshape(N_DP, GROUP)
    cot_groups = cotangent.astype(jnp.float32).reshape(N_DP, GROUP, D)

    def one_group(totals, item):
        rows, seg, cot = item
        result, pull = jax.vjp(lambda inputs, *weights: forward_group(inputs, seg, *weights), rows, *params)
        grads = pull(cot * (seg >= 0).astype(jnp.float32)[:, None])
        updated = tuple((total + grad for total, grad in zip(totals, grads[1:])))
        return (updated, (result.astype(jnp.bfloat16), grads[0]))
    init = tuple((jnp.zeros(p.shape, jnp.float32) for p in params))
    totals, (outputs, grad_rows) = lax.scan(one_group, init, (token_groups, seg_groups, cot_groups))
    return (outputs.reshape(TOKENS, D), grad_rows.reshape(TOKENS, D), totals[0], totals[1], totals[2], totals[3], totals[4], totals[5])
```

```python
import jax
import jax.numpy as jnp
from jax import lax
from jax.sharding import PartitionSpec as P

HEAD_DIM = 64
WINDOW_HALF = 64
PAD_BLOCK = 128
QBLOCK = 1152


def passed_along(block, axis, distance):
    devices = range(lax.axis_size(axis))
    route = [(i - distance, i) for i in devices if i - distance in devices]
    return lax.ppermute(block, axis, route)


def layer_norm(values, gain):
    centred = values - jnp.mean(values, axis=-1, keepdims=True)
    spread = jnp.mean(centred * centred, axis=-1, keepdims=True)
    return centred * lax.rsqrt(spread + 1e-05) * gain


def rope_tables(position):
    half = HEAD_DIM // 2
    exponent = jnp.arange(half).astype(jnp.float32) * (2.0 / HEAD_DIM)
    inverse = jnp.power(10000.0, -exponent)
    angle = position.astype(jnp.float32)[:, None] * inverse[None, :]
    angle = jnp.concatenate([angle, angle], axis=-1)
    return (jnp.cos(angle)[:, None, :], jnp.sin(angle)[:, None, :])


def rotate(values, cosine, sine):
    half = values.shape[-1] // 2
    turned = jnp.concatenate([-values[..., half:], values[..., :half]], axis=-1)
    return values * cosine + turned * sine


def unrotate(values, cosine, sine):
    half = values.shape[-1] // 2
    scaled = values * sine
    return values * cosine + jnp.concatenate([scaled[..., half:], -scaled[..., :half]], axis=-1)


def split_windows(values):
    subs = QBLOCK // PAD_BLOCK
    lower = values[:QBLOCK].reshape((subs, PAD_BLOCK) + values.shape[1:])
    upper = values[PAD_BLOCK:].reshape((subs, PAD_BLOCK) + values.shape[1:])
    return jnp.concatenate([lower, upper], axis=1)


def merge_windows(values):
    rest = values.shape[2:]
    lower = values[:, :PAD_BLOCK].reshape((QBLOCK,) + rest)
    upper = values[:, PAD_BLOCK:].reshape((QBLOCK,) + rest)
    margin = ((0, 0),) * len(rest)
    return jnp.pad(lower, ((0, PAD_BLOCK),) + margin) + jnp.pad(upper, ((PAD_BLOCK, 0),) + margin)


def windows(queries, key_pad, value_pad, seg_query, seg_pad):
    subs = QBLOCK // PAD_BLOCK
    query_blk = queries.reshape((subs, PAD_BLOCK) + queries.shape[1:])
    key_sub = split_windows(key_pad)
    value_sub = split_windows(value_pad)
    seg_rows = seg_query.reshape(subs, PAD_BLOCK)
    seg_cols = split_windows(seg_pad)
    raw = jnp.einsum("sqhd,skhd->hsqk", query_blk, key_sub, preferred_element_type=jnp.float32)
    row_pos = jnp.arange(PAD_BLOCK, dtype=jnp.int32)[:, None]
    col_pos = jnp.arange(PAD_BLOCK + 2 * WINDOW_HALF, dtype=jnp.int32)[None, :] - WINDOW_HALF
    band = jnp.abs(row_pos - col_pos) <= WINDOW_HALF
    allowed = (seg_rows[:, :, None] == seg_cols[:, None, :]) & band[None]
    scores = jnp.where(allowed[None], raw * HEAD_DIM ** (-0.5), -1e30)
    return (query_blk, key_sub, value_sub, scores)


def attend_forward(queries, key_pad, value_pad, seg_query, seg_pad):

    def one_block(carry, start):
        query_blk, key_sub, value_sub, scores = windows(
            queries, key_pad, value_pad, seg_query, seg_pad
        )
        top = jnp.max(scores, axis=-1, keepdims=True)
        weights = jnp.exp(scores - top)
        total = jnp.sum(weights, axis=-1, keepdims=True)
        probs_low = (weights / total).astype(jnp.bfloat16)
        out_blk = jnp.einsum(
            "hsqk,skhd->sqhd", probs_low, value_sub, preferred_element_type=jnp.float32
        )
        return (
            carry,
            (out_blk.reshape((QBLOCK,) + queries.shape[1:]), (top + jnp.log(total))[..., 0]),
        )

    starts = jnp.arange(queries.shape[0] // QBLOCK, dtype=jnp.int32) * QBLOCK
    unused, (outputs, logsum) = lax.scan(one_block, None, starts)
    return (outputs.reshape(queries.shape), logsum)


def attend_backward(queries, key_pad, value_pad, grad_attended, logsum, seg_query, seg_pad):
    subs = QBLOCK // PAD_BLOCK

    def one_block(carry, item):
        start, logsum_blk = item
        key_acc, value_acc = carry
        query_blk, key_sub, value_sub, scores = windows(
            queries, key_pad, value_pad, seg_query, seg_pad
        )
        probs = jnp.exp(scores - logsum_blk[..., None])
        probs_low = probs.astype(jnp.bfloat16)
        grad_blk = grad_attended.reshape((subs, PAD_BLOCK) + queries.shape[1:])
        grad_probs = jnp.einsum(
            "sqhd,skhd->hsqk", grad_blk, value_sub, preferred_element_type=jnp.float32
        )
        delta = jnp.sum(grad_probs * probs, axis=-1, keepdims=True)
        grad_scores = (probs * (grad_probs - delta)).astype(jnp.bfloat16)
        scale = HEAD_DIM ** (-0.5)
        grad_query = (
            jnp.einsum("hsqk,skhd->sqhd", grad_scores, key_sub, preferred_element_type=jnp.float32)
            * scale
        )
        grad_key_sub = (
            jnp.einsum(
                "hsqk,sqhd->skhd", grad_scores, query_blk, preferred_element_type=jnp.float32
            )
            * scale
        )
        grad_value_sub = jnp.einsum(
            "hsqk,sqhd->skhd", probs_low, grad_blk, preferred_element_type=jnp.float32
        )
        key_acc = key_acc + merge_windows(grad_key_sub)
        value_acc = value_acc + merge_windows(grad_value_sub)
        return ((key_acc, value_acc), grad_query.reshape((QBLOCK,) + queries.shape[1:]))

    starts = jnp.arange(queries.shape[0] // QBLOCK, dtype=jnp.int32) * QBLOCK
    init = (jnp.zeros(key_pad.shape, jnp.float32), jnp.zeros(key_pad.shape, jnp.float32))
    (key_acc, value_acc), grad_queries = lax.scan(one_block, init, (starts, logsum))
    return (grad_queries.reshape(queries.shape), key_acc, value_acc)


def gelu_gate(pre_act):
    return jax.nn.gelu(pre_act[:, 0], approximate=False) * pre_act[:, 1]


def neighbour(piece, by):
    return passed_along(piece.astype(jnp.bfloat16), "tensor", by).astype(piece.dtype)


def steps_of(devices, swapped):
    bits = [1 << i for i in range(devices.bit_length() - 1)]
    near, far = bits[:2], bits[2:]
    return far + (near if swapped else near[::-1])


def exchanged(block, mask):
    devices = lax.axis_size("dp")
    return lax.ppermute(block, "dp", [(i, i ^ mask) for i in range(devices)])


def swapped_cores(block):
    return lax.ppermute(block, "tensor", [(0, 1), (1, 0)])


def gather_rows(shard, swapped):
    devices = lax.axis_size("dp")
    index = lax.axis_index("dp")
    levels = devices.bit_length() - 1
    held = shard.reshape((1,) * levels + shard.shape)
    for mask in steps_of(devices, swapped):
        axis = levels - mask.bit_length()
        other = exchanged(held, mask)
        held = jnp.where(
            (index & mask) == 0,
            jnp.concatenate([held, other], axis=axis),
            jnp.concatenate([other, held], axis=axis),
        )
    return held.reshape(devices * shard.shape[0], shard.shape[1])


def scatter_rows(total, swapped):
    devices = lax.axis_size("dp")
    index = lax.axis_index("dp")
    levels = devices.bit_length() - 1
    rows = total.shape[0] // devices
    held = total.reshape((2,) * levels + (rows, total.shape[1]))
    for mask in reversed(steps_of(devices, swapped)):
        axis = levels - mask.bit_length()
        bit = (index & mask) // mask
        keep = lax.dynamic_slice_in_dim(held, bit, 1, axis)
        send = lax.dynamic_slice_in_dim(held, 1 - bit, 1, axis)
        other = exchanged(send.astype(jnp.bfloat16), mask)
        held = keep.astype(jnp.float32) + other.astype(jnp.float32)
    return held.reshape(rows, total.shape[1])


def both_halves(own):
    other = swapped_cores(own)
    first = lax.axis_index("tensor") == 0
    return jnp.where(first, jnp.stack([own, other]), jnp.stack([other, own]))


def own_half(both):
    index = lax.axis_index("tensor")
    keep = lax.dynamic_index_in_dim(both, index, 0, keepdims=False)
    send = lax.dynamic_index_in_dim(both, 1 - index, 0, keepdims=False)
    return keep.astype(jnp.float32) + swapped_cores(send.astype(jnp.bfloat16)).astype(jnp.float32)


def body(
    tokens,
    segment,
    norm_attn_gain,
    qkv_weight,
    attn_out_weight,
    norm_mlp_gain,
    in_weight,
    out_weight,
    cotangent,
):
    local_rows = tokens.shape[0]
    index = lax.axis_index("tensor")
    own_rows = norm_attn_gain.shape[0]
    half_width = qkv_weight.shape[2]
    half_units = in_weight.shape[2]
    gains = jnp.pad(jnp.stack([norm_attn_gain, norm_mlp_gain], axis=1), ((0, 0), (0, 126)))
    query_key = gather_rows(qkv_weight[:, :2].reshape(own_rows, -1), False)
    value_gain = gather_rows(jnp.concatenate([qkv_weight[:, 2], gains], axis=1), True)
    up = gather_rows(in_weight.reshape(own_rows, -1), False)
    down = gather_rows(jnp.concatenate([attn_out_weight.T, out_weight.T], axis=1), True)
    width = query_key.shape[0]
    gain_one = value_gain[:, half_width]
    gain_two = value_gain[:, half_width + 1]
    query_key = both_halves(query_key)
    value_half = both_halves(value_gain[:, :half_width])
    up = both_halves(up)
    down = both_halves(down)
    weight_qkv = jnp.concatenate(
        [query_key.reshape(2, width, 2, half_width), value_half[:, :, None]], axis=2
    ).transpose(1, 2, 0, 3).reshape(width, 3, 2 * half_width)
    weight_in = up.reshape(2, width, 2, half_units).transpose(1, 2, 0, 3).reshape(
        width, 2, 2 * half_units
    )
    weight_attn = down[:, :, :half_width].transpose(0, 2, 1).reshape(2 * half_width, width)
    weight_out = down[:, :, half_width:].transpose(0, 2, 1).reshape(2 * half_units, width)
    inputs = tokens.astype(jnp.float32)
    own_segment = lax.dynamic_slice_in_dim(segment, index * local_rows, local_rows, 0)
    normed, norm_one_pull = jax.vjp(layer_norm, inputs, gain_one.astype(jnp.float32))
    normed_low = normed.astype(jnp.bfloat16)
    first_slot = index * local_rows
    row_count = normed_low.shape[0]
    local_width = weight_qkv.shape[2]
    heads_here = local_width // HEAD_DIM
    shape = (row_count, heads_here, HEAD_DIM)
    projected = jnp.einsum(
        "rd,dcf->rcf", normed_low, weight_qkv, preferred_element_type=jnp.float32
    )
    slots = first_slot + jnp.arange(row_count, dtype=jnp.int32)
    position = jnp.where(own_segment >= 0, slots - PAD_BLOCK * own_segment, 0)
    cosine, sine = rope_tables(position)
    queries = rotate(projected[:, 0].reshape(shape), cosine, sine).astype(jnp.bfloat16)
    keys_rot = rotate(projected[:, 1].reshape(shape), cosine, sine).astype(jnp.bfloat16)
    value_rows = projected[:, 2].reshape(shape).astype(jnp.bfloat16)
    seg_pad_full = jnp.pad(segment, (WINDOW_HALF, WINDOW_HALF), constant_values=-2)
    paired = jnp.stack([keys_rot, value_rows], axis=1).astype(jnp.float32)
    from_below = neighbour(paired[row_count - WINDOW_HALF :], 1)
    from_above = neighbour(paired[:WINDOW_HALF], -1)
    extended = jnp.concatenate([from_below, paired, from_above], axis=0).astype(jnp.bfloat16)
    key_pad = extended[:, 0]
    value_pad = extended[:, 1]
    seg_pad = lax.dynamic_slice_in_dim(
        seg_pad_full, index * local_rows, local_rows + 2 * WINDOW_HALF, 0
    )
    attended, logsum = attend_forward(queries, key_pad, value_pad, own_segment, seg_pad)
    attended_low = attended.reshape(row_count, local_width).astype(jnp.bfloat16)
    hidden = inputs + jnp.dot(attended_low, weight_attn, preferred_element_type=jnp.float32)
    normed_two, norm_two_pull = jax.vjp(layer_norm, hidden, gain_two.astype(jnp.float32))
    normed_two_low = normed_two.astype(jnp.bfloat16)
    pre_act = jnp.einsum(
        "rd,dcf->rcf", normed_two_low, weight_in, preferred_element_type=jnp.float32
    )
    gated, gate_pull = jax.vjp(gelu_gate, pre_act)
    gated_low = gated.astype(jnp.bfloat16)
    layer_out = (
        hidden + jnp.dot(gated_low, weight_out, preferred_element_type=jnp.float32)
    ).astype(jnp.bfloat16)
    grad_y = cotangent.astype(jnp.float32) * (own_segment >= 0).astype(jnp.float32)[:, None]
    grad_y_rows = grad_y.astype(jnp.bfloat16)
    grad_weight_out = jnp.einsum(
        "rf,rd->fd", gated_low, grad_y_rows, preferred_element_type=jnp.float32
    )
    grad_gated = jnp.einsum(
        "rd,fd->rf", grad_y_rows, weight_out, preferred_element_type=jnp.float32
    )
    grad_pre = gate_pull(grad_gated)[0].astype(jnp.bfloat16)
    grad_weight_in = jnp.einsum(
        "rd,rcf->dcf", normed_two_low, grad_pre, preferred_element_type=jnp.float32
    )
    grad_normed_two = jnp.einsum(
        "rcf,dcf->rd", grad_pre, weight_in, preferred_element_type=jnp.float32
    )
    grad_hidden_norm, grad_gain_two = norm_two_pull(grad_normed_two)
    grad_hidden = grad_y + grad_hidden_norm
    grad_hidden_rows = grad_hidden.astype(jnp.bfloat16)
    grad_weight_attn = jnp.einsum(
        "rf,rd->fd", attended_low, grad_hidden_rows, preferred_element_type=jnp.float32
    )
    grad_attended = jnp.einsum(
        "rd,fd->rf", grad_hidden_rows, weight_attn, preferred_element_type=jnp.float32
    ).astype(jnp.bfloat16)
    grad_queries, key_acc, value_acc = attend_backward(
        queries, key_pad, value_pad, grad_attended.reshape(shape), logsum, own_segment, seg_pad
    )
    paired_grad = jnp.stack([key_acc, value_acc], axis=1)
    from_lower = neighbour(paired_grad[row_count + WINDOW_HALF :], 1)
    from_upper = neighbour(paired_grad[:WINDOW_HALF], -1)
    rest = ((0, 0), (0, 0), (0, 0))
    core = paired_grad[WINDOW_HALF : WINDOW_HALF + row_count]
    core = (
        core
        + jnp.pad(from_lower, ((0, row_count - WINDOW_HALF),) + rest)
        + jnp.pad(from_upper, ((row_count - WINDOW_HALF, 0),) + rest)
    )
    grad_keys = core[:, 0]
    grad_values = core[:, 1]
    grad_queries = unrotate(grad_queries, cosine, sine).reshape(row_count, local_width)
    grad_keys = unrotate(grad_keys, cosine, sine).reshape(row_count, local_width)
    grad_qkv = jnp.stack(
        [grad_queries, grad_keys, grad_values.reshape(row_count, local_width)], axis=1
    ).astype(jnp.bfloat16)
    grad_weight_qkv = jnp.einsum(
        "rd,rcf->dcf", normed_low, grad_qkv, preferred_element_type=jnp.float32
    )
    grad_normed = jnp.einsum(
        "rcf,dcf->rd", grad_qkv, weight_qkv, preferred_element_type=jnp.float32
    )
    grad_input_norm, grad_gain_one = norm_one_pull(grad_normed)
    grad_tokens = grad_hidden + grad_input_norm
    grad_in = grad_weight_in.reshape(width, 2, 2, half_units).transpose(2, 0, 1, 3)
    grad_in = own_half(grad_in.reshape(2, width, 2 * half_units))
    grad_down = jnp.concatenate(
        [
            grad_weight_attn.reshape(2, half_width, width),
            grad_weight_out.reshape(2, half_units, width),
        ],
        axis=1,
    ).transpose(0, 2, 1)
    grad_down = own_half(grad_down)
    grad_parts = grad_weight_qkv.reshape(width, 3, 2, half_width).transpose(2, 0, 1, 3)
    grad_query_key = own_half(grad_parts[:, :, :2].reshape(2, width, 2 * half_width))
    grad_gains = jnp.pad(jnp.stack([grad_gain_one, grad_gain_two], axis=1), ((0, 0), (0, 126)))
    grad_value = own_half(
        jnp.concatenate([grad_parts[:, :, 2], jnp.stack([grad_gains, grad_gains])], axis=2)
    )
    owned_in = scatter_rows(grad_in, False).reshape(own_rows, 2, half_units)
    owned_down = scatter_rows(grad_down, True)
    owned_attn = owned_down[:, :half_width].T
    owned_out = owned_down[:, half_width:].T
    owned_query_key = scatter_rows(grad_query_key, False)
    owned_value = scatter_rows(grad_value, True)
    owned_qkv = jnp.concatenate(
        [
            owned_query_key.reshape(own_rows, 2, half_width),
            owned_value[:, None, :half_width],
        ],
        axis=1,
    )
    owned_gain_one = owned_value[:, half_width]
    owned_gain_two = owned_value[:, half_width + 1]
    return (
        layer_out,
        grad_tokens,
        owned_gain_one,
        owned_qkv,
        owned_attn,
        owned_gain_two,
        owned_in,
        owned_out,
    )


def solution(mesh):
    placed = (
        P(("dp", "tensor"), None),
        P("dp"),
        P("dp"),
        P("dp", None, "tensor"),
        P("tensor", "dp"),
        P("dp"),
        P("dp", None, "tensor"),
        P("tensor", "dp"),
        P(("dp", "tensor"), None),
    )
    return jax.shard_map(
        body,
        mesh=mesh,
        in_specs=placed,
        out_specs=(
            P(("dp", "tensor"), None),
            P(("dp", "tensor"), None),
            P("dp"),
            P("dp", None, "tensor"),
            P("tensor", "dp"),
            P("dp"),
            P("dp", None, "tensor"),
            P("tensor", "dp"),
        ),
        check_vma=False,
    )
```

```python
import jax
import jax.numpy as jnp
from jax import lax
from jax.experimental import pallas as pl
from jax.experimental.pallas import tpu as pltpu
from jax.sharding import PartitionSpec as P

HEAD_DIM = 64
WINDOW_HALF = 64
PAD_BLOCK = 128
WIDTH = 768
ROWS = 1152
HALF = 1152
LANES = 128
PAIRS = 6
SPAN = 2 * LANES
UNITS = 512
FIRST_CUT = 640
DOWN = 384 + UNITS + LANES
VMEM = 58 * 2**20
F32 = jnp.float32
BF16 = jnp.bfloat16


def steps_of(devices, swapped):
    bits = [1 << i for i in range(devices.bit_length() - 1)]
    near, far = bits[:2], bits[2:]
    return far + (near if swapped else near[::-1])


def exchanged(block, mask):
    devices = lax.axis_size("dp")
    return lax.ppermute(block, "dp", [(i, i ^ mask) for i in range(devices)])


def swapped_cores(block):
    return lax.ppermute(block, "tensor", [(0, 1), (1, 0)])


def by_exchange(own_rows):
    devices = lax.axis_size("dp")
    return own_rows % 16 == 0 and devices & (devices - 1) == 0


def relative(own_rows, swapped):
    if not by_exchange(own_rows):
        return list(range(WIDTH // 48))
    order = [0]
    for mask in steps_of(lax.axis_size("dp"), swapped):
        order = order + [r ^ mask for r in order]
    return order


def gather_slots(shard, swapped):
    if not by_exchange(shard.shape[0]):
        whole = lax.all_gather(shard, "dp", axis=0, tiled=True)
        return [whole.reshape(WIDTH // 48, 48, shard.shape[1])]
    held = shard[None]
    masks = steps_of(lax.axis_size("dp"), swapped)
    for mask in masks[:-1]:
        held = jnp.concatenate([held, exchanged(held, mask)], axis=0)
    return [held, exchanged(held, masks[-1])]


def scatter_slots(keep, send, own_rows, swapped):
    other = swapped_cores(send)
    if not by_exchange(own_rows):
        total = keep.astype(F32) + other.astype(F32)
        total = total.reshape(WIDTH, keep.shape[2])
        return lax.psum_scatter(total, "dp", scatter_dimension=0, tiled=True)
    for mask in reversed(steps_of(lax.axis_size("dp"), swapped)):
        middle = keep.shape[0] // 2
        kept = keep[:middle].astype(F32) + other[:middle].astype(F32)
        sent = keep[middle:].astype(F32) + other[middle:].astype(F32)
        other = exchanged(sent.astype(BF16), mask)
        keep = kept
    return (keep + other.astype(F32))[0]


def scatter_gains(first, second):
    devices = lax.axis_size("dp")
    index = lax.axis_index("dp")
    levels = devices.bit_length() - 1
    part = WIDTH // devices
    both = jnp.stack([first, second]).reshape(2, devices, part).transpose(1, 0, 2)
    if devices & (devices - 1):
        both = lax.psum(both, "tensor")
        held = lax.psum_scatter(both, "dp", scatter_dimension=0, tiled=True)[0]
        return held[0], held[1]
    held = jnp.pad(both, ((0, 0), (0, 6), (0, LANES - part)))
    held = held + swapped_cores(held)
    held = held.reshape((2,) * levels + (8, LANES))
    for mask in reversed(steps_of(devices, False)):
        axis = levels - mask.bit_length()
        bit = (index & mask) // mask
        keep = lax.dynamic_slice_in_dim(held, bit, 1, axis)
        held = keep + exchanged(lax.dynamic_slice_in_dim(held, 1 - bit, 1, axis), mask)
    held = held.reshape(8, LANES)
    return held[0, :part], held[1, :part]


def nt(left, right):
    return lax.dot_general(left, right, (((1,), (1,)), ((), ())), preferred_element_type=F32)


def tn(left, right):
    return lax.dot_general(left, right, (((0,), (0,)), ((), ())), preferred_element_type=F32)


def nn(left, right):
    return jnp.dot(left, right, preferred_element_type=F32)


def start_slots(info, pieces, order, segments, sems):
    half = len(pieces) // 2
    slot = 0
    for number, piece in enumerate(pieces):
        if number == half:
            slot = 0
        mine = number < half
        core = info[1] if mine else 1 - info[1]
        rows = piece.shape[1]
        for at in range(piece.shape[0]):
            row = pl.multiple_of((info[0] ^ order[slot]) * rows, 16)
            for begin, width, own, other in segments:
                target = own if mine else other
                if target is None:
                    continue
                ref, sem, stride, offset = target
                column = pl.multiple_of(core * stride + offset, LANES)
                pltpu.make_async_copy(
                    piece.at[at, :, pl.ds(begin, width)],
                    ref.at[pl.ds(row, rows), pl.ds(column, width)],
                    sems.at[sem],
                ).start()
            slot += 1


def wait_whole(ref, sem):
    pltpu.make_async_copy(ref, ref, sem).wait()


def fill_window(info, qkv_ref, edge_ref, window, sems):
    core = info[1]
    first = pl.multiple_of(jnp.where(core == 1, 0, WINDOW_HALF + ROWS), 16)
    last = pl.multiple_of(jnp.where(core == 1, WINDOW_HALF + ROWS, 0), 16)
    copies = [
        pltpu.make_async_copy(edge_ref, window.at[pl.ds(first, WINDOW_HALF), :], sems.at[4])
    ]
    for part in range(2):
        for half in range(2):
            copies.append(
                pltpu.make_async_copy(
                    qkv_ref.at[:, pl.ds(HALF * half + 384 * (part + 1), 384)],
                    window.at[pl.ds(WINDOW_HALF, ROWS), pl.ds(WIDTH * part + 384 * half, 384)],
                    sems.at[2 * part + half],
                )
            )
    for copy in copies:
        copy.start()
    window[pl.ds(last, WINDOW_HALF), :] = jnp.zeros((WINDOW_HALF, 2 * WIDTH), BF16)
    for copy in copies:
        copy.wait()


def normalized(values):
    centred = values - jnp.mean(values, axis=-1, keepdims=True)
    spread = jnp.mean(centred * centred, axis=-1, keepdims=True)
    factor = lax.rsqrt(spread + 1e-05)
    return centred * factor, factor


def norm_backward(grad, unit, factor, gain):
    inner = grad * gain
    mean = jnp.mean(inner, axis=-1, keepdims=True)
    along = jnp.mean(inner * unit, axis=-1, keepdims=True)
    return factor * (inner - mean - unit * along)


def turned(values, cosine, sine):
    lane = lax.broadcasted_iota(jnp.int32, values.shape, 1)
    first = (lane & 32) == 0
    other = jnp.where(first, pltpu.roll(values, 96, 1), pltpu.roll(values, 32, 1))
    return values * cosine + other * sine


def both_heads(block):
    lane = lax.broadcasted_iota(jnp.int32, block.shape, 1)
    first = jnp.where(lane < HEAD_DIM, 1.0, 0.0).astype(block.dtype)
    second = jnp.where(lane < HEAD_DIM, 0.0, 1.0).astype(block.dtype)
    return jnp.concatenate([block * first, block * second], axis=0)


def head_lanes(rows):
    lane = lax.broadcasted_iota(jnp.int32, (LANES, LANES), 1)
    return jnp.where(lane < HEAD_DIM, rows[:LANES], rows[LANES:])


def qkv_kernel(order, pieces_of, info, x_ref, cos_ref, sin_ref, *refs):
    count_a, count_b = pieces_of
    order_a, order_b = order
    part_a, refs = refs[:count_a], refs[count_a:]
    part_b, refs = refs[:count_b], refs[count_b:]
    qkv_ref, normed_ref, gain_ref, edge_ref, weight, gains, sems = refs
    step = pl.program_id(0)
    rows = x_ref.shape[0]

    @pl.when(step == 0)
    def _():
        into = lambda offset: (weight, 0, HALF, offset)
        start_slots(info, part_a, order_a, [(0, FIRST_CUT, into(0), into(0))], sems)
        rest = HALF - FIRST_CUT
        start_slots(
            info,
            part_b,
            order_b,
            [
                (0, rest, into(FIRST_CUT), into(FIRST_CUT)),
                (rest, LANES, (gains, 1, 0, 0), None),
            ],
            sems,
        )
        wait_whole(weight, sems.at[0])
        wait_whole(gains, sems.at[1])
        row = lax.broadcasted_iota(jnp.int32, (16, LANES), 0)
        lane = lax.broadcasted_iota(jnp.int32, (16, LANES), 1)
        pick = jnp.where(row == lane, 1.0, 0.0).astype(BF16)
        gain_ref[...] = nt(pick, gains[...])[:8]

    unit, unused = normalized(x_ref[...].astype(F32))
    normed = (unit * gain_ref[0:1, :]).astype(BF16)
    normed_ref[...] = normed
    cosine, sine = cos_ref[...], sin_ref[...]
    for half in range(2):
        result = nn(normed, weight[:, HALF * half : HALF * (half + 1)])
        for tile in range(9):
            block = result[:, LANES * tile : LANES * (tile + 1)]
            if tile < 6:
                block = turned(block, cosine, sine)
            if tile < 3:
                block = block * (HEAD_DIM**-0.5)
            begin = HALF * half + LANES * tile
            qkv_ref[:, begin : begin + LANES] = block.astype(BF16)

    for core, at_step, begin in ((1, 0, 0), (0, ROWS // rows - 1, rows - WINDOW_HALF)):

        @pl.when((info[1] == core) & (step == at_step))
        def _():
            for part in range(2):
                for half in range(2):
                    source = HALF * half + 384 * (part + 1)
                    target = WIDTH * part + 384 * half
                    edge_ref[:, target : target + 384] = qkv_ref[
                        begin : begin + WINDOW_HALF, source : source + 384
                    ]


def attend_kernel(
    info, row_seg, col_seg, q_ref, qkv_ref, edge_ref, out_ref, probs_ref, window, sems
):
    step = pl.program_id(0)

    @pl.when(step == 0)
    def _():
        fill_window(info, qkv_ref, edge_ref, window, sems)

    start = pl.multiple_of(step * LANES, LANES)
    key_seg = col_seg[pl.ds(start, SPAN), :]
    key_at = lax.broadcasted_iota(jnp.int32, (SPAN, LANES), 0) - WINDOW_HALF
    query_at = lax.broadcasted_iota(jnp.int32, (SPAN, LANES), 1)
    near = jnp.abs(key_at - query_at) <= WINDOW_HALF
    allowed = (key_seg == row_seg[0]) & near
    bias = jnp.where(allowed, 0.0, -1e30)
    bias = jnp.concatenate([bias, bias], axis=1)
    for pair in range(PAIRS):
        half, tile = pair // 3, pair % 3
        begin = HALF * half + LANES * tile
        lanes = slice(LANES * pair, LANES * (pair + 1))
        queries = both_heads(q_ref[:, begin : begin + LANES])
        keys = window[pl.ds(start, SPAN), lanes]
        values = window[pl.ds(start, SPAN), WIDTH + LANES * pair : WIDTH + LANES * (pair + 1)]
        scores = nt(keys, queries) + bias
        weights = jnp.exp(scores - jnp.max(scores, axis=0, keepdims=True))
        total = jnp.sum(weights, axis=0, keepdims=True)
        probs = (weights * (1.0 / total)).astype(BF16)
        probs_ref[0, pair] = probs
        out_ref[:, lanes] = head_lanes(tn(probs, values)).astype(BF16)


def mlp_kernel(order, count, info, x_ref, att_ref, cot_ref, live_ref, gain_ref, *refs):
    order_in, order_down = order
    part_in, refs = refs[: count[0]], refs[count[0] :]
    part_down, refs = refs[: count[1]], refs[count[1] :]
    (
        out_ref,
        hidden_grad_ref,
        att_grad_ref,
        normed_ref,
        gated_ref,
        pre_grad_ref,
        low_grad_ref,
        out_grad_ref,
        gain_grad_ref,
        w_in,
        w_att,
        w_out,
        tail_own,
        tail_other,
        sems,
    ) = refs
    step = pl.program_id(0)

    @pl.when(step == 0)
    def _():
        into = (w_in, 0, HALF, 0)
        start_slots(info, part_in, order_in, [(0, HALF, into, into)], sems)
        att, out = (w_att, 1, 384, 0), (w_out, 2, UNITS, 0)
        start_slots(
            info,
            part_down,
            order_down,
            [
                (0, 384, att, att),
                (384, UNITS, out, out),
                (384 + UNITS, LANES, (tail_own, 3, 0, 0), (tail_other, 4, 0, 0)),
            ],
            sems,
        )
        wait_whole(w_att, sems.at[1])
        wait_whole(w_in, sems.at[0])
        wait_whole(w_out.at[:, pl.ds(0, 2 * UNITS)], sems.at[2])
        wait_whole(tail_own, sems.at[3])
        wait_whole(tail_other, sems.at[4])
        w_out[:, 2 * UNITS :] = tail_own[...] + tail_other[...]
        gain_grad_ref[...] = jnp.zeros_like(gain_grad_ref)

    gain = gain_ref[1:2, :]
    hidden = x_ref[...].astype(F32) + nt(att_ref[...], w_att[...])
    unit, factor = normalized(hidden)
    normed = (unit * gain).astype(BF16)
    normed_ref[...] = normed
    out_grad = cot_ref[...].astype(F32) * live_ref[...]
    out_grad_low = out_grad.astype(BF16)
    out_grad_ref[...] = out_grad_low
    pre = [nn(normed, w_in[:, HALF * half : HALF * (half + 1)]) for half in range(2)]
    tails = [part[:, 2 * UNITS :] for part in pre]
    lane = lax.broadcasted_iota(jnp.int32, tails[0].shape, 1)
    low = lane < HEAD_DIM
    gates = [part[:, :UNITS] for part in pre]
    gates.append(jnp.where(low, tails[0], pltpu.roll(tails[1], 64, 1)))
    ups = [part[:, UNITS : 2 * UNITS] for part in pre]
    ups.append(jnp.where(low, pltpu.roll(tails[0], 64, 1), tails[1]))
    for part, (gate, up) in enumerate(zip(gates, ups)):
        columns = slice(UNITS * part, UNITS * part + gate.shape[1])
        share = 0.5 + 0.5 * lax.erf(gate * (0.5**0.5))
        slope = share + gate * (jnp.exp(-0.5 * gate * gate) * 0.3989422804014327)
        curve = gate * share
        gated_ref[:, columns] = (curve * up).astype(BF16)
        grad = nn(out_grad_low, w_out[:, columns])
        gate_grad = (grad * up * slope).astype(BF16)
        up_grad = (grad * curve).astype(BF16)
        if part < 2:
            begin = HALF * part
            pre_grad_ref[:, begin : begin + UNITS] = gate_grad
            pre_grad_ref[:, begin + UNITS : begin + 2 * UNITS] = up_grad
        else:
            gate_grad = gate_grad.astype(F32)
            up_grad = up_grad.astype(F32)
            pre_grad_ref[:, 2 * UNITS : HALF] = jnp.where(
                low, gate_grad, pltpu.roll(up_grad, 64, 1)
            ).astype(BF16)
            pre_grad_ref[:, HALF + 2 * UNITS :] = jnp.where(
                low, pltpu.roll(gate_grad, 64, 1), up_grad
            ).astype(BF16)
    out_ref[...] = (hidden + nt(gated_ref[...], w_out[...])).astype(BF16)
    normed_grad = nt(pre_grad_ref[...], w_in[...])
    gain_grad_ref[0:1, :] += jnp.sum(normed_grad * unit, axis=0, keepdims=True)
    hidden_grad = out_grad + norm_backward(normed_grad, unit, factor, gain)
    hidden_grad_ref[...] = hidden_grad
    hidden_grad_low = hidden_grad.astype(BF16)
    low_grad_ref[...] = hidden_grad_low
    att_grad_ref[...] = nn(hidden_grad_low, w_att[...]).astype(BF16)


def weight_grad_kernel(lefts, cuts, orders, info, *refs):
    count = max(lefts) + 1
    left, refs = refs[:count], refs[count:]
    right, refs = refs[: len(lefts)], refs[len(lefts) :]
    outs, total = refs[:-1], refs[-1]
    begin = 0
    for which, ref in zip(lefts, right):
        width = ref.shape[1]
        total[:, begin : begin + width] = tn(left[which][...], ref[...]).astype(BF16)
        begin += width
    for out, (start, stop), order in zip(outs, cuts, orders):
        rows = out.shape[1]
        for slot in range(out.shape[0]):
            row = pl.multiple_of((info[0] ^ order[slot]) * rows, 16)
            out[slot] = total[pl.ds(row, rows), start:stop]


def attend_back_kernel(
    info,
    q_ref,
    probs_ref,
    grad_ref,
    cos_ref,
    sin_ref,
    qkv_ref,
    edge_ref,
    out_ref,
    edge_out_ref,
    window,
    key_grad,
    value_grad,
    sems,
):
    step = pl.program_id(0)

    @pl.when(step == 0)
    def _():
        fill_window(info, qkv_ref, edge_ref, window, sems)
        key_grad[...] = jnp.zeros_like(key_grad)
        value_grad[...] = jnp.zeros_like(value_grad)

    start = pl.multiple_of(step * LANES, LANES)
    span = pl.ds(start, SPAN)
    cosine, sine = cos_ref[pl.ds(start, LANES), :], sin_ref[pl.ds(start, LANES), :]
    for pair in range(PAIRS):
        half, tile = pair // 3, pair % 3
        begin = HALF * half + LANES * tile
        lanes = slice(LANES * pair, LANES * (pair + 1))
        queries = both_heads(q_ref[:, begin : begin + LANES])
        grads = both_heads(grad_ref[:, lanes])
        keys = window[span, lanes]
        values = window[span, WIDTH + LANES * pair : WIDTH + LANES * (pair + 1)]
        probs = probs_ref[0, pair]
        probs_wide = probs.astype(F32)
        probs_grad = nt(values, grads)
        weighted = probs_grad * probs_wide
        delta = jnp.sum(weighted, axis=0, keepdims=True)
        score_grad = (weighted - probs_wide * delta).astype(BF16)
        query_grad = head_lanes(tn(score_grad, keys)) * (HEAD_DIM**-0.5)
        out_ref[pl.ds(start, LANES), begin : begin + LANES] = turned(
            query_grad, cosine, -sine
        ).astype(BF16)
        key_grad[span, lanes] += nn(score_grad, queries)
        value_grad[span, lanes] += nn(probs, grads)

    @pl.when(step == ROWS // LANES - 1)
    def _():
        for pair in range(PAIRS):
            half, tile = pair // 3, pair % 3
            begin = HALF * half + LANES * tile
            lanes = slice(LANES * pair, LANES * (pair + 1))
            inside = slice(WINDOW_HALF, WINDOW_HALF + ROWS)
            out_ref[:, begin + 384 : begin + 384 + LANES] = turned(
                key_grad[inside, lanes], cos_ref[...], -sin_ref[...]
            ).astype(BF16)
            out_ref[:, begin + 768 : begin + 768 + LANES] = value_grad[inside, lanes].astype(BF16)
        row = pl.multiple_of(jnp.where(info[1] == 1, 0, WINDOW_HALF + ROWS), 16)
        edge_out_ref[:, :WIDTH] = key_grad[pl.ds(row, WINDOW_HALF), :].astype(BF16)
        edge_out_ref[:, WIDTH:] = value_grad[pl.ds(row, WINDOW_HALF), :].astype(BF16)


def edge_kernel(info, grad_ref, edge_ref, cos_ref, sin_ref, out_ref):
    out_ref[...] = grad_ref[...]
    for pair in range(PAIRS):
        half, tile = pair // 3, pair % 3
        begin = HALF * half + LANES * tile
        keys = turned(
            edge_ref[:, LANES * pair : LANES * (pair + 1)].astype(F32), cos_ref[...], -sin_ref[...]
        )
        values = edge_ref[:, WIDTH + LANES * pair : WIDTH + LANES * (pair + 1)].astype(F32)
        for offset, add in ((384, keys), (768, values)):
            at = slice(begin + offset, begin + offset + LANES)
            out_ref[:, at] = (grad_ref[:, at].astype(F32) + add).astype(BF16)


def input_grad_kernel(
    order, pieces_of, info, x_ref, grad_ref, hidden_grad_ref, gain_ref, *refs
):
    count_a, count_b = pieces_of
    order_a, order_b = order
    part_a, refs = refs[:count_a], refs[count_a:]
    part_b, refs = refs[:count_b], refs[count_b:]
    out_ref, gain_grad_ref, weight, sems = refs

    @pl.when(pl.program_id(0) == 0)
    def _():
        into = lambda offset: (weight, 0, HALF, offset)
        start_slots(info, part_a, order_a, [(0, FIRST_CUT, into(0), into(0))], sems)
        rest = (0, HALF - FIRST_CUT, into(FIRST_CUT), into(FIRST_CUT))
        start_slots(info, part_b, order_b, [rest], sems)
        gain_grad_ref[...] = jnp.zeros_like(gain_grad_ref)
        wait_whole(weight, sems.at[0])

    unit, factor = normalized(x_ref[...].astype(F32))
    normed_grad = nt(grad_ref[...], weight[...])
    gain_grad_ref[0:1, :] += jnp.sum(normed_grad * unit, axis=0, keepdims=True)
    out_ref[...] = hidden_grad_ref[...] + norm_backward(
        normed_grad, unit, factor, gain_ref[0:1, :]
    )


def shape_of(shape, dtype=BF16):
    return jax.ShapeDtypeStruct(shape, dtype)


def call(kernel, info, grid, ins, in_specs, outs, out_specs, scratch, flops, aliases=None):
    moved = sum(a.size * a.dtype.itemsize for a in list(ins) + list(outs))
    return pl.pallas_call(
        kernel,
        out_shape=outs,
        grid_spec=pltpu.PrefetchScalarGridSpec(
            num_scalar_prefetch=1,
            grid=grid,
            in_specs=in_specs,
            out_specs=out_specs,
            scratch_shapes=scratch,
        ),
        input_output_aliases=aliases or {},
        compiler_params=pltpu.CompilerParams(
            dimension_semantics=("arbitrary",), vmem_limit_bytes=VMEM
        ),
        cost_estimate=pl.CostEstimate(
            flops=int(flops), bytes_accessed=int(moved), transcendentals=0
        ),
    )(info, *ins)


def by_rows(rows, columns):
    return pl.BlockSpec((rows, columns), lambda i, s: (i, 0))


def full(*shape):
    return pl.BlockSpec(shape, lambda i, s: (0,) * len(shape))


ANYWHERE = pl.BlockSpec(memory_space=pl.ANY)


def weight_grads(info, lefts, jobs, cuts, orders, slots, send):
    in_specs = [full(ROWS, WIDTH) for unused in lefts]
    for unused, right, width, block in jobs:
        if block is None:
            in_specs.append(pl.BlockSpec((ROWS, width), lambda i, s: (0, s[1] ^ send)))
        else:
            in_specs.append(pl.BlockSpec((ROWS, width), lambda i, s, block=block: (0, block)))
    total = sum(job[2] for job in jobs)
    outs = [shape_of((slots, WIDTH // slots, stop - start)) for start, stop in cuts]
    which = tuple(job[0] for job in jobs)
    return call(
        lambda *refs: weight_grad_kernel(which, cuts, orders, *refs),
        info,
        (1,),
        list(lefts) + [job[1] for job in jobs],
        in_specs,
        outs,
        [full(*out.shape) for out in outs],
        [pltpu.VMEM((WIDTH, total), BF16)],
        2 * ROWS * WIDTH * total,
    )


def body(
    tokens,
    segment,
    norm_attn_gain,
    qkv_weight,
    attn_out_weight,
    norm_mlp_gain,
    in_weight,
    out_weight,
    cotangent,
):
    own_rows = norm_attn_gain.shape[0]
    core = lax.axis_index("tensor")
    place = lax.axis_index("dp") if by_exchange(own_rows) else 0
    info = jnp.stack([jnp.int32(place), core.astype(jnp.int32)])
    order = relative(own_rows, False)
    order_swapped = relative(own_rows, True)
    slots = len(order)

    gains = jnp.pad(jnp.stack([norm_attn_gain, norm_mlp_gain], axis=1), ((0, 0), (0, LANES - 2)))
    flat = qkv_weight.reshape(own_rows, HALF)
    part_a = gather_slots(flat[:, :FIRST_CUT], False)
    part_b = gather_slots(jnp.concatenate([flat[:, FIRST_CUT:], gains], axis=1), True)
    part_a = part_a + [swapped_cores(piece) for piece in part_a]
    part_b = part_b + [swapped_cores(piece) for piece in part_b]
    shard_in = jnp.concatenate(
        [
            in_weight[:, 0, :UNITS],
            in_weight[:, 1, :UNITS],
            in_weight[:, 0, UNITS:],
            in_weight[:, 1, UNITS:],
        ],
        axis=1,
    )
    turned_out = out_weight.T
    tail = turned_out[:, UNITS:]
    blank = jnp.zeros_like(tail)
    tail = jnp.where(
        core == 0,
        jnp.concatenate([tail, blank], axis=1),
        jnp.concatenate([blank, tail], axis=1),
    )
    shard_down = jnp.concatenate([attn_out_weight.T, turned_out[:, :UNITS], tail], axis=1)
    part_in = gather_slots(shard_in, False)
    part_down = gather_slots(shard_down, True)
    part_in = part_in + [swapped_cores(piece) for piece in part_in]
    part_down = part_down + [swapped_cores(piece) for piece in part_down]

    own_segment = lax.dynamic_slice_in_dim(segment, core * ROWS, ROWS, 0)
    slot = core * ROWS + jnp.arange(ROWS, dtype=jnp.int32)
    position = jnp.where(own_segment >= 0, slot - PAD_BLOCK * own_segment, 0)
    lane = jnp.arange(LANES, dtype=jnp.int32)
    exponent = (lane % 32).astype(F32) * (2.0 / HEAD_DIM)
    angle = position.astype(F32)[:, None] * jnp.power(10000.0, -exponent)[None, :]
    cosine = jnp.cos(angle)
    sine = jnp.sin(angle) * jnp.where((lane & 32) == 0, -1.0, 1.0)[None, :]
    seg_pad = jnp.pad(segment, (WINDOW_HALF, WINDOW_HALF), constant_values=-2)
    col_seg = lax.dynamic_slice_in_dim(seg_pad, core * ROWS, ROWS + 2 * WINDOW_HALF, 0)[:, None]
    row_seg = own_segment.reshape(ROWS // LANES, 1, LANES)
    live = (own_segment >= 0).astype(F32)[:, None]

    rows = 384
    steps = ROWS // rows
    pieces_of = (len(part_a), len(part_b))
    qkv, normed, gain_rows, edge = call(
        lambda *refs: qkv_kernel((order, order_swapped), pieces_of, *refs),
        info,
        (steps,),
        [tokens, cosine, sine, *part_a, *part_b],
        [by_rows(rows, WIDTH), by_rows(rows, LANES), by_rows(rows, LANES)]
        + [ANYWHERE] * sum(pieces_of),
        [
            shape_of((ROWS, 2 * HALF)),
            shape_of((ROWS, WIDTH)),
            shape_of((8, WIDTH), F32),
            shape_of((WINDOW_HALF, 2 * WIDTH)),
        ],
        [by_rows(rows, 2 * HALF), by_rows(rows, WIDTH), full(8, WIDTH), full(64, 2 * WIDTH)],
        [
            pltpu.VMEM((WIDTH, 2 * HALF), BF16),
            pltpu.VMEM((WIDTH, LANES), BF16),
            pltpu.SemaphoreType.DMA((2,)),
        ],
        2 * ROWS * WIDTH * 2 * HALF,
    )
    edge = swapped_cores(edge)

    blocks = ROWS // LANES
    window_shape = (ROWS + 2 * WINDOW_HALF, 2 * WIDTH)
    attended, probs = call(
        attend_kernel,
        info,
        (blocks,),
        [row_seg, col_seg, qkv, qkv, edge],
        [
            pl.BlockSpec((1, 1, LANES), lambda i, s: (i, 0, 0)),
            full(ROWS + 2 * WINDOW_HALF, 1),
            by_rows(LANES, 2 * HALF),
            ANYWHERE,
            ANYWHERE,
        ],
        [shape_of((ROWS, WIDTH)), shape_of((blocks, PAIRS, SPAN, SPAN))],
        [
            by_rows(LANES, WIDTH),
            pl.BlockSpec((1, PAIRS, SPAN, SPAN), lambda i, s: (i, 0, 0, 0)),
        ],
        [pltpu.VMEM(window_shape, BF16), pltpu.SemaphoreType.DMA((5,))],
        blocks * PAIRS * 2 * 2 * SPAN * SPAN * LANES,
    )

    (
        layer_out,
        hidden_grad,
        att_grad,
        normed_two,
        gated,
        pre_grad,
        hidden_grad_low,
        out_grad,
        gain_two_grad,
    ) = call(
        lambda *refs: mlp_kernel(
            (order, order_swapped), (len(part_in), len(part_down)), *refs
        ),
        info,
        (steps,),
        [tokens, attended, cotangent, live, gain_rows, *part_in, *part_down],
        [by_rows(rows, WIDTH)] * 3
        + [by_rows(rows, 1), full(8, WIDTH)]
        + [ANYWHERE] * (len(part_in) + len(part_down)),
        [
            shape_of((ROWS, WIDTH)),
            shape_of((ROWS, WIDTH), F32),
            shape_of((ROWS, WIDTH)),
            shape_of((ROWS, WIDTH)),
            shape_of((ROWS, HALF)),
            shape_of((ROWS, 2 * HALF)),
            shape_of((ROWS, WIDTH)),
            shape_of((ROWS, WIDTH)),
            shape_of((8, WIDTH), F32),
        ],
        [by_rows(rows, WIDTH)] * 4
        + [by_rows(rows, HALF), by_rows(rows, 2 * HALF)]
        + [by_rows(rows, WIDTH)] * 2
        + [full(8, WIDTH)],
        [
            pltpu.VMEM((WIDTH, 2 * HALF), BF16),
            pltpu.VMEM((WIDTH, WIDTH), BF16),
            pltpu.VMEM((WIDTH, HALF), BF16),
            pltpu.VMEM((WIDTH, LANES), BF16),
            pltpu.VMEM((WIDTH, LANES), BF16),
            pltpu.SemaphoreType.DMA((5,)),
        ],
        2 * ROWS * WIDTH * (4 * HALF + 2 * HALF + 2 * WIDTH),
    )

    early = (
        info,
        [normed_two, hidden_grad_low, out_grad],
        [
            (0, pre_grad, HALF, None),
            (1, attended, 384, None),
            (2, gated, UNITS, None),
            (2, gated, LANES, 2 * UNITS // LANES),
        ],
        [(0, HALF), (HALF, HALF + DOWN)],
        [order, order_swapped],
        slots,
    )
    send_in, send_down = weight_grads(*early, 1)
    keep_in, keep_down = weight_grads(*early, 0)
    owned_in = scatter_slots(keep_in, send_in, own_rows, False)
    owned_down = scatter_slots(keep_down, send_down, own_rows, True)

    qkv_grad, edge_grad = call(
        attend_back_kernel,
        info,
        (blocks,),
        [qkv, probs, att_grad, cosine, sine, qkv, edge],
        [
            by_rows(LANES, 2 * HALF),
            pl.BlockSpec((1, PAIRS, SPAN, SPAN), lambda i, s: (i, 0, 0, 0)),
            by_rows(LANES, WIDTH),
            full(ROWS, LANES),
            full(ROWS, LANES),
            ANYWHERE,
            ANYWHERE,
        ],
        [shape_of((ROWS, 2 * HALF)), shape_of((WINDOW_HALF, 2 * WIDTH))],
        [full(ROWS, 2 * HALF), full(WINDOW_HALF, 2 * WIDTH)],
        [
            pltpu.VMEM(window_shape, BF16),
            pltpu.VMEM((window_shape[0], WIDTH), F32),
            pltpu.VMEM((window_shape[0], WIDTH), F32),
            pltpu.SemaphoreType.DMA((5,)),
        ],
        blocks * PAIRS * 4 * 2 * SPAN * SPAN * LANES,
    )
    edge_grad = swapped_cores(edge_grad)
    at_edge = lambda i, s: ((1 - s[1]) * (ROWS // WINDOW_HALF - 1), 0)
    (qkv_grad,) = call(
        edge_kernel,
        info,
        (1,),
        [qkv_grad, edge_grad, cosine, sine],
        [
            pl.BlockSpec((WINDOW_HALF, 2 * HALF), at_edge),
            full(WINDOW_HALF, 2 * WIDTH),
            pl.BlockSpec((WINDOW_HALF, LANES), at_edge),
            pl.BlockSpec((WINDOW_HALF, LANES), at_edge),
        ],
        [shape_of((ROWS, 2 * HALF))],
        [pl.BlockSpec((WINDOW_HALF, 2 * HALF), at_edge)],
        [],
        0,
        {1: 0},
    )

    late = (
        info,
        [normed],
        [(0, qkv_grad, HALF, None)],
        [(0, FIRST_CUT), (FIRST_CUT, HALF)],
        [order, order_swapped],
        slots,
    )
    send_a, send_b = weight_grads(*late, 1)
    keep_a, keep_b = weight_grads(*late, 0)
    owned_a = scatter_slots(keep_a, send_a, own_rows, False)
    owned_b = scatter_slots(keep_b, send_b, own_rows, True)

    grad_tokens, gain_one_grad = call(
        lambda *refs: input_grad_kernel((order, order_swapped), pieces_of, *refs),
        info,
        (steps,),
        [tokens, qkv_grad, hidden_grad, gain_rows, *part_a, *part_b],
        [by_rows(rows, WIDTH), by_rows(rows, 2 * HALF), by_rows(rows, WIDTH), full(8, WIDTH)]
        + [ANYWHERE] * sum(pieces_of),
        [shape_of((ROWS, WIDTH), F32), shape_of((8, WIDTH), F32)],
        [by_rows(rows, WIDTH), full(8, WIDTH)],
        [pltpu.VMEM((WIDTH, 2 * HALF), BF16), pltpu.SemaphoreType.DMA((1,))],
        2 * ROWS * WIDTH * 2 * HALF,
    )
    owned_gain_one, owned_gain_two = scatter_gains(gain_one_grad[0], gain_two_grad[0])

    owned_qkv = jnp.concatenate([owned_a, owned_b], axis=1).reshape(own_rows, 3, HALF // 3)
    owned_in = jnp.stack(
        [
            jnp.concatenate([owned_in[:, :UNITS], owned_in[:, 2 * UNITS : -64]], axis=1),
            jnp.concatenate([owned_in[:, UNITS : 2 * UNITS], owned_in[:, -64:]], axis=1),
        ],
        axis=1,
    )
    owned_attn = owned_down[:, :384].T
    tail = jnp.where(core == 0, owned_down[:, -128:-64], owned_down[:, -64:])
    owned_out = jnp.concatenate([owned_down[:, 384 : 384 + UNITS], tail], axis=1).T
    return (
        layer_out,
        grad_tokens,
        owned_gain_one,
        owned_qkv,
        owned_attn,
        owned_gain_two,
        owned_in,
        owned_out,
    )


def solution(mesh):
    placed = (
        P(("dp", "tensor"), None),
        P("dp"),
        P("dp"),
        P("dp", None, "tensor"),
        P("tensor", "dp"),
        P("dp"),
        P("dp", None, "tensor"),
        P("tensor", "dp"),
        P(("dp", "tensor"), None),
    )
    return jax.shard_map(
        body,
        mesh=mesh,
        in_specs=placed,
        out_specs=(
            P(("dp", "tensor"), None),
            P(("dp", "tensor"), None),
            P("dp"),
            P("dp", None, "tensor"),
            P("tensor", "dp"),
            P("dp"),
            P("dp", None, "tensor"),
            P("tensor", "dp"),
        ),
        check_vma=False,
    )
```

```python
import jax
import jax.numpy as jnp
from jax import lax
from jax.experimental import pallas as pl
from jax.experimental.pallas import tpu as pltpu
from jax.sharding import PartitionSpec as P

HEAD_DIM = 64
WINDOW_HALF = 64
PAD_BLOCK = 128
WIDTH = 768
ROWS = 1152
HALF = 1152
LANES = 128
THIRD = 384
PAIRS = 3
SPAN = 2 * LANES
UNITS = 512
FIRST_CUT = 640
DOWN = 384 + UNITS + LANES
VMEM = 58 * 2**20
ANYWHERE = pl.BlockSpec(memory_space=pl.ANY)
F32 = jnp.float32
BF16 = jnp.bfloat16


def steps_of(devices, swapped):
    bits = [1 << i for i in range(devices.bit_length() - 1)]
    near, far = bits[:2], bits[2:]
    return far + (near if swapped else near[::-1])


def exchanged(block, mask):
    devices = lax.axis_size("dp")
    return lax.ppermute(block, "dp", [(i, i ^ mask) for i in range(devices)])


def swapped_cores(block):
    return lax.ppermute(block, "tensor", [(0, 1), (1, 0)])


def by_exchange(own_rows):
    devices = lax.axis_size("dp")
    return own_rows % 16 == 0 and devices & (devices - 1) == 0


def relative(own_rows, swapped):
    if not by_exchange(own_rows):
        return list(range(WIDTH // 48))
    order = [0]
    for mask in steps_of(lax.axis_size("dp"), swapped):
        order = order + [r ^ mask for r in order]
    return order


def held_until(arrays, *gates):
    return lax.optimization_barrier((tuple(arrays), gates))[0]


def gather_start(shard):
    masks = steps_of(lax.axis_size("dp"), False)
    held = shard[None]
    if not by_exchange(shard.shape[0]) or len(masks) <= 3:
        return [held]
    first, second = masks[:2]
    return [held] + [exchanged(held, mask) for mask in (first, second, first ^ second)]


def columns_of(pieces, start, stop):
    return jnp.concatenate([piece[:, :, start:stop] for piece in pieces], axis=0)


def gather_middle(held, swapped):
    arrived = held
    if by_exchange(held.shape[1]):
        masks = steps_of(lax.axis_size("dp"), swapped)
        for mask in masks[held.shape[0].bit_length() - 1 : -1]:
            arrived = exchanged(held, mask)
            held = jnp.concatenate([held, arrived], axis=0)
    return held, arrived


def gather_finish(held, swapped):
    if not by_exchange(held.shape[1]):
        whole = lax.all_gather(held[0], "dp", axis=0, tiled=True)
        return [whole.reshape(WIDTH // 48, 48, held.shape[2])]
    return [held, exchanged(held, steps_of(lax.axis_size("dp"), swapped)[-1])]


def scatter_start(keep, send, own_rows, swapped):
    other = swapped_cores(send)
    arrivals = [other]
    if not by_exchange(own_rows):
        total = keep.astype(F32) + other.astype(F32)
        total = total.reshape(WIDTH, keep.shape[2])
        total = lax.psum_scatter(total, "dp", scatter_dimension=0, tiled=True)
        return total[None], arrivals * 3
    masks = steps_of(lax.axis_size("dp"), swapped)
    last = 2 if len(masks) > 3 else 0
    for mask in reversed(masks[last:]):
        middle = keep.shape[0] // 2
        kept = keep[:middle].astype(F32) + other[:middle].astype(F32)
        sent = keep[middle:].astype(F32) + other[middle:].astype(F32)
        other = exchanged(sent.astype(BF16), mask)
        arrivals.append(other)
        keep = kept
    return keep.astype(F32) + other.astype(F32), arrivals + [other] * 3


def scatter_finish(*totals):
    own = jnp.concatenate([total[0] for total in totals], axis=1)
    if totals[0].shape[0] == 1:
        return own
    first, second = steps_of(lax.axis_size("dp"), False)[:2]
    arrived = []
    for i, mask in enumerate((first, second, first ^ second)):
        low = jnp.concatenate([total[i + 1].astype(BF16) for total in totals], axis=1)
        arrived.append(exchanged(low, mask).astype(F32))
    return own + (arrived[0] + arrived[1] + arrived[2])


def gain_part(weight, grad, gain):
    return jnp.sum(weight.astype(F32) * grad, axis=1) / gain.astype(F32)


def nt(left, right):
    return lax.dot_general(left, right, (((1,), (1,)), ((), ())), preferred_element_type=F32)


def tn(left, right):
    return lax.dot_general(left, right, (((0,), (0,)), ((), ())), preferred_element_type=F32)


def nn(left, right):
    return jnp.dot(left, right, preferred_element_type=F32)


def start_slots(info, pieces, order, segments, sems):
    slot = 0
    for piece in pieces:
        rows = piece.shape[1]
        for at in range(piece.shape[0]):
            row = pl.multiple_of((info[0] ^ order[slot]) * rows, 16)
            for begin, width, target, column, sem in segments:
                pltpu.make_async_copy(
                    piece.at[at, :, pl.ds(begin, width)],
                    target.at[pl.ds(row, rows), pl.ds(column, width)],
                    sems.at[sem],
                ).start()
            slot += 1


def wait_whole(ref, sem):
    pltpu.make_async_copy(ref, ref, sem).wait()


def store_slots(info, value, hold, outs):
    hold[...] = value.astype(F32).T.astype(BF16)
    for out, order in outs:
        rows = WIDTH // len(order)
        for slot, place in enumerate(order):
            row = pl.multiple_of((info[0] ^ place) * rows, 16)
            out[rows * slot : rows * (slot + 1), :] = hold[pl.ds(row, rows), :]


def fill_window(info, qkv_ref, edge_ref, window, sems):
    core = info[1]
    first = pl.multiple_of(jnp.where(core == 1, 0, WINDOW_HALF + ROWS), 16)
    last = pl.multiple_of(jnp.where(core == 1, WINDOW_HALF + ROWS, 0), 16)
    copies = [
        pltpu.make_async_copy(
            edge_ref, window.at[pl.ds(first, WINDOW_HALF), :], sems.at[0]
        ),
        pltpu.make_async_copy(
            qkv_ref.at[:, pl.ds(THIRD, 2 * THIRD)],
            window.at[pl.ds(WINDOW_HALF, ROWS), :],
            sems.at[1],
        ),
    ]
    for copy in copies:
        copy.start()
    window[pl.ds(last, WINDOW_HALF), :] = jnp.zeros((WINDOW_HALF, 2 * THIRD), BF16)
    for copy in copies:
        copy.wait()


def normalized(values):
    centred = values - jnp.mean(values, axis=-1, keepdims=True)
    spread = jnp.mean(centred * centred, axis=-1, keepdims=True)
    factor = lax.rsqrt(spread + 1e-05)
    return centred * factor, factor


def norm_backward(grad, unit, factor, gain):
    inner = grad * gain
    mean = jnp.mean(inner, axis=-1, keepdims=True)
    along = jnp.mean(inner * unit, axis=-1, keepdims=True)
    return factor * (inner - mean - unit * along)


def turned(values, cosine, sine):
    lane = lax.broadcasted_iota(jnp.int32, values.shape, 1)
    first = (lane & 32) == 0
    other = jnp.where(first, pltpu.roll(values, 96, 1), pltpu.roll(values, 32, 1))
    return values * cosine + other * sine


def both_heads(block):
    lane = lax.broadcasted_iota(jnp.int32, block.shape, 1)
    first = jnp.where(lane < HEAD_DIM, 1.0, 0.0).astype(block.dtype)
    second = jnp.where(lane < HEAD_DIM, 0.0, 1.0).astype(block.dtype)
    return jnp.concatenate([block * first, block * second], axis=0)


def head_lanes(rows):
    lane = lax.broadcasted_iota(jnp.int32, (LANES, LANES), 1)
    return jnp.where(lane < HEAD_DIM, rows[:LANES], rows[LANES:])


def qkv_kernel(orders, counts, own, info, x_ref, cos_ref, sin_ref, *refs):
    part_a, refs = refs[: counts[0]], refs[counts[0] :]
    part_b, refs = refs[: counts[1]], refs[counts[1] :]
    if own:
        qkv_ref, edge_ref, weight, gain_ref, turned_a, turned_b, gains, hold, sems = refs
    else:
        gain_ref, qkv_ref, edge_ref, weight, sems = refs
    step = pl.program_id(0)
    rows = x_ref.shape[0]

    @pl.when(step == 0)
    def _():
        rest = HALF - FIRST_CUT
        start_slots(info, part_a, orders[0], [(0, FIRST_CUT, weight, 0, 0)], sems)
        segments = [(0, rest, weight, FIRST_CUT, 0)]
        if own:
            segments.append((rest, LANES, gains, 0, 1))
        start_slots(info, part_b, orders[1], segments, sems)
        if own:
            wait_whole(gains, sems.at[1])
            row = lax.broadcasted_iota(jnp.int32, (16, LANES), 0)
            lane = lax.broadcasted_iota(jnp.int32, (16, LANES), 1)
            pick = jnp.where(row == lane, 1.0, 0.0).astype(BF16)
            gain_ref[...] = nt(pick, gains[...])[:8]
        wait_whole(weight, sems.at[0])

    unit, unused = normalized(x_ref[...].astype(F32))
    normed = (unit * gain_ref[0:1, :]).astype(BF16)
    cosine, sine = cos_ref[...], sin_ref[...]
    result = nn(normed, weight[...])
    for tile in range(9):
        block = result[:, LANES * tile : LANES * (tile + 1)]
        if tile < 6:
            block = turned(block, cosine, sine)
        if tile < 3:
            block = block * (HEAD_DIM**-0.5)
        qkv_ref[:, LANES * tile : LANES * (tile + 1)] = block.astype(BF16)
    if own:
        store_slots(info, normed, hold, [(turned_a, orders[0]), (turned_b, orders[1])])

    for core, at_step, begin in ((1, 0, 0), (0, ROWS // rows - 1, rows - WINDOW_HALF)):

        @pl.when((info[1] == core) & (step == at_step))
        def _():
            edge_ref[...] = qkv_ref[begin : begin + WINDOW_HALF, THIRD:]


def turn_kernel(order, info, cot_ref, live_ref, out_ref, hold):
    grad = cot_ref[...].astype(F32) * live_ref[...]
    store_slots(info, grad, hold, [(out_ref, order)])


def attend_kernel(
    info, row_seg, col_seg, q_ref, qkv_ref, edge_ref, out_ref, probs_ref, window, sems
):
    step = pl.program_id(0)

    @pl.when(step == 0)
    def _():
        fill_window(info, qkv_ref, edge_ref, window, sems)

    start = pl.multiple_of(step * LANES, LANES)
    key_seg = col_seg[pl.ds(start, SPAN), :]
    key_at = lax.broadcasted_iota(jnp.int32, (SPAN, LANES), 0) - WINDOW_HALF
    query_at = lax.broadcasted_iota(jnp.int32, (SPAN, LANES), 1)
    near = jnp.abs(key_at - query_at) <= WINDOW_HALF
    allowed = (key_seg == row_seg[0]) & near
    bias = jnp.where(allowed, 0.0, -1e30)
    bias = jnp.concatenate([bias, bias], axis=1)
    for pair in range(PAIRS):
        lanes = slice(LANES * pair, LANES * (pair + 1))
        queries = both_heads(q_ref[:, lanes])
        keys = window[pl.ds(start, SPAN), lanes]
        values = window[pl.ds(start, SPAN), THIRD + LANES * pair : THIRD + LANES * (pair + 1)]
        scores = nt(keys, queries) + bias
        weights = jnp.exp(scores - jnp.max(scores, axis=0, keepdims=True))
        total = jnp.sum(weights, axis=0, keepdims=True)
        probs = (weights * (1.0 / total)).astype(BF16)
        probs_ref[0, pair] = probs
        out_ref[:, lanes] = head_lanes(tn(probs, values)).astype(BF16)


def mlp_kernel(orders, counts, info, x_ref, att_own, att_other, cot_ref, live_ref, gain_ref, *refs):
    parts = []
    for count in counts:
        parts.append(refs[:count])
        refs = refs[count:]
    in_own, in_other, down_own, down_other = parts
    (
        out_ref,
        hidden_grad_ref,
        att_grad_own,
        att_grad_other,
        gated_ref,
        pre_grad_own,
        pre_grad_other,
        normed_turned,
        grad_turned,
        w_in,
        w_att,
        w_out,
        tail_own,
        tail_other,
        hold,
        sems,
    ) = refs
    step = pl.program_id(0)

    @pl.when(step == 0)
    def _():
        for number, (part, tail) in enumerate(((down_own, tail_own), (down_other, tail_other))):
            segments = [
                (0, THIRD, w_att, THIRD * number, 1),
                (THIRD, UNITS, w_out, UNITS * number, 2),
                (THIRD + UNITS, LANES, tail, 0, 3 + number),
            ]
            start_slots(info, part, orders[1], segments, sems)
        for number, part in enumerate((in_own, in_other)):
            start_slots(info, part, orders[0], [(0, HALF, w_in, HALF * number, 0)], sems)
        wait_whole(w_att, sems.at[1])
        wait_whole(w_out.at[:, pl.ds(0, 2 * UNITS)], sems.at[2])
        wait_whole(tail_own, sems.at[3])
        wait_whole(tail_other, sems.at[4])
        other = pltpu.roll(tail_other[...].astype(F32), HEAD_DIM, 1).astype(BF16)
        w_out[:, 2 * UNITS :] = tail_own[...] + other
        wait_whole(w_in, sems.at[0])

    gain = gain_ref[1:2, :]
    hidden = (
        x_ref[...].astype(F32)
        + nt(att_own[...], w_att[:, :THIRD])
        + nt(att_other[...], w_att[:, THIRD:])
    )
    unit, factor = normalized(hidden)
    normed = (unit * gain).astype(BF16)
    store_slots(info, normed, hold, [(normed_turned, orders[0])])
    out_grad = cot_ref[...].astype(F32) * live_ref[...]
    out_grad_low = out_grad.astype(BF16)
    pre = [nn(normed, w_in[:, HALF * half : HALF * (half + 1)]) for half in range(2)]
    tails = [part[:, 2 * UNITS :] for part in pre]
    lane = lax.broadcasted_iota(jnp.int32, tails[0].shape, 1)
    low = lane < HEAD_DIM
    gates = [part[:, :UNITS] for part in pre]
    gates.append(jnp.where(low, tails[0], pltpu.roll(tails[1], 64, 1)))
    ups = [part[:, UNITS : 2 * UNITS] for part in pre]
    ups.append(jnp.where(low, pltpu.roll(tails[0], 64, 1), tails[1]))
    pre_grads = (pre_grad_own, pre_grad_other)
    for part, (gate, up) in enumerate(zip(gates, ups)):
        columns = slice(UNITS * part, UNITS * part + gate.shape[1])
        share = 0.5 + 0.5 * lax.erf(gate * (0.5**0.5))
        slope = share + gate * (jnp.exp(-0.5 * gate * gate) * 0.3989422804014327)
        curve = gate * share
        gated_ref[:, columns] = (curve * up).astype(BF16)
        grad = nn(out_grad_low, w_out[:, columns])
        gate_grad = grad * up * slope
        up_grad = grad * curve
        if part < 2:
            pre_grads[part][:, :UNITS] = gate_grad.astype(BF16)
            pre_grads[part][:, UNITS : 2 * UNITS] = up_grad.astype(BF16)
        else:
            own = jnp.where(low, gate_grad, pltpu.roll(up_grad, 64, 1))
            other = jnp.where(low, pltpu.roll(gate_grad, 64, 1), up_grad)
            pre_grad_own[:, 2 * UNITS :] = own.astype(BF16)
            pre_grad_other[:, 2 * UNITS :] = other.astype(BF16)
    out_ref[...] = (hidden + nt(gated_ref[...], w_out[...])).astype(BF16)
    normed_grad = nt(pre_grad_own[...], w_in[:, :HALF]) + nt(pre_grad_other[...], w_in[:, HALF:])
    hidden_grad = out_grad + norm_backward(normed_grad, unit, factor, gain)
    hidden_grad_ref[...] = hidden_grad
    hidden_grad_low = hidden_grad.astype(BF16)
    store_slots(info, hidden_grad_low, hold, [(grad_turned, orders[1])])
    att_grad_own[...] = nn(hidden_grad_low, w_att[:, :THIRD]).astype(BF16)
    att_grad_other[...] = nn(hidden_grad_low, w_att[:, THIRD:]).astype(BF16)


def weight_grad_kernel(jobs, count, roll_last, info, *refs):
    left, refs = refs[: count[0]], refs[count[0] :]
    right, outs = refs[: count[1]], refs[count[1] :]
    for which, source, target, column in jobs:
        result = nn(left[which][...], right[source][...])
        if roll_last and source == count[1] - 1:
            result = pltpu.roll(result, HEAD_DIM, 1)
        width = right[source].shape[1]
        outs[target][:, column : column + width] = result.astype(BF16)


def qkv_weight_grad_kernel(info, left_a, left_b, right, edge_ref, out_a, out_b, edge):
    core = info[1]
    edge[...] = jnp.zeros_like(edge)
    row = pl.multiple_of((1 - core) * WINDOW_HALF, 16)
    edge[pl.ds(row, WINDOW_HALF), :] = edge_ref[...]
    column = pl.multiple_of((1 - core) * (ROWS - LANES), LANES)
    near_a = left_a[:, pl.ds(column, LANES)]
    near_b = left_b[:, pl.ds(column, LANES)]
    result = nn(left_a[...], right[:, :FIRST_CUT])
    out_a[:, :THIRD] = result[:, :THIRD].astype(BF16)
    more = nn(near_a, edge[:, : FIRST_CUT - THIRD])
    out_a[:, THIRD:] = (result[:, THIRD:] + more).astype(BF16)
    result = nn(left_b[...], right[:, FIRST_CUT:]) + nn(near_b, edge[:, FIRST_CUT - THIRD :])
    out_b[...] = result.astype(BF16)


def attend_back_kernel(
    info,
    q_ref,
    probs_ref,
    grad_ref,
    cos_ref,
    sin_ref,
    qkv_ref,
    edge_ref,
    out_ref,
    edge_out_ref,
    window,
    key_grad,
    value_grad,
    sems,
):
    step = pl.program_id(0)

    @pl.when(step == 0)
    def _():
        fill_window(info, qkv_ref, edge_ref, window, sems)
        key_grad[...] = jnp.zeros_like(key_grad)
        value_grad[...] = jnp.zeros_like(value_grad)

    start = pl.multiple_of(step * LANES, LANES)
    span = pl.ds(start, SPAN)
    own = pl.ds(pl.multiple_of(start + WINDOW_HALF, WINDOW_HALF), LANES)
    cosine, sine = cos_ref[own, :], sin_ref[own, :]
    for pair in range(PAIRS):
        lanes = slice(LANES * pair, LANES * (pair + 1))
        queries = both_heads(q_ref[:, lanes])
        grads = both_heads(grad_ref[:, lanes])
        keys = window[span, lanes]
        values = window[span, THIRD + LANES * pair : THIRD + LANES * (pair + 1)]
        probs = probs_ref[0, pair]
        probs_wide = probs.astype(F32)
        probs_grad = nt(values, grads)
        weighted = probs_grad * probs_wide
        delta = jnp.sum(weighted, axis=0, keepdims=True)
        score_grad = (weighted - probs_wide * delta).astype(BF16)
        query_grad = head_lanes(tn(score_grad, keys)) * (HEAD_DIM**-0.5)
        out_ref[pl.ds(start, LANES), lanes] = turned(query_grad, cosine, -sine).astype(BF16)
        key_grad[span, lanes] += nn(score_grad, queries)
        value_grad[span, lanes] += nn(probs, grads)

    @pl.when(step == ROWS // LANES - 1)
    def _():
        inside = slice(WINDOW_HALF, WINDOW_HALF + ROWS)
        row = pl.multiple_of(jnp.where(info[1] == 1, 0, WINDOW_HALF + ROWS), 16)
        edge_rows = pl.ds(row, WINDOW_HALF)
        for pair in range(PAIRS):
            lanes = slice(LANES * pair, LANES * (pair + 1))
            out_ref[:, THIRD + LANES * pair : THIRD + LANES * (pair + 1)] = turned(
                key_grad[inside, lanes], cos_ref[inside, :], -sin_ref[inside, :]
            ).astype(BF16)
            edge_out_ref[:, lanes] = turned(
                key_grad[edge_rows, lanes], cos_ref[edge_rows, :], -sin_ref[edge_rows, :]
            ).astype(BF16)
        out_ref[:, 2 * THIRD :] = value_grad[inside, :].astype(BF16)
        edge_out_ref[:, THIRD:] = value_grad[edge_rows, :].astype(BF16)


def input_grad_kernel(
    base, info, x_ref, own_ref, other_ref, edge_own, edge_other, hidden_ref, gain_ref, w_own, w_other, *refs
):
    out_ref, fixed = refs[-2:]
    rows = x_ref.shape[0]
    step = pl.program_id(0) + base
    total = None
    for grad_ref, edge_ref, weight in ((own_ref, edge_own, w_own), (other_ref, edge_other, w_other)):
        fixed[...] = grad_ref[...]
        for core, at_step, begin in ((1, 0, 0), (0, ROWS // rows - 1, rows - WINDOW_HALF)):

            @pl.when((info[1] == core) & (step == at_step))
            def _():
                at = slice(begin, begin + WINDOW_HALF)
                fixed[at, THIRD:] = (
                    fixed[at, THIRD:].astype(F32) + edge_ref[...].astype(F32)
                ).astype(BF16)

        part = nt(fixed[...], weight[...])
        total = part if total is None else total + part
    unit, factor = normalized(x_ref[...].astype(F32))
    out_ref[...] = hidden_ref[...] + norm_backward(total, unit, factor, gain_ref[0:1, :])


def shape_of(shape, dtype=BF16):
    return jax.ShapeDtypeStruct(shape, dtype)


def call(
    kernel, info, grid, ins, in_specs, outs, out_specs, scratch, flops, aliases=None, after=()
):
    moved = sum(a.size * a.dtype.itemsize for a in list(ins) + list(outs))
    first = 1 + len(ins)
    later = first + len(after)
    return pl.pallas_call(
        lambda *refs: kernel(*refs[:first], *refs[later:]),
        out_shape=outs,
        grid_spec=pltpu.PrefetchScalarGridSpec(
            num_scalar_prefetch=1,
            grid=grid,
            in_specs=list(in_specs) + [ANYWHERE] * len(after),
            out_specs=out_specs,
            scratch_shapes=scratch,
        ),
        input_output_aliases=aliases or {},
        compiler_params=pltpu.CompilerParams(
            dimension_semantics=("arbitrary",), vmem_limit_bytes=VMEM
        ),
        cost_estimate=pl.CostEstimate(
            flops=int(flops), bytes_accessed=int(moved), transcendentals=0
        ),
    )(info, *ins, *after)


def by_rows(rows, columns):
    return pl.BlockSpec((rows, columns), lambda i, s: (i, 0))


def full(*shape):
    return pl.BlockSpec(shape, lambda i, s: (0,) * len(shape))


def body(
    tokens,
    segment,
    norm_attn_gain,
    qkv_weight,
    attn_out_weight,
    norm_mlp_gain,
    in_weight,
    out_weight,
    cotangent,
):
    own_rows = norm_attn_gain.shape[0]
    core = lax.axis_index("tensor")
    place = lax.axis_index("dp") if by_exchange(own_rows) else 0
    info = jnp.stack([jnp.int32(place), core.astype(jnp.int32)])
    orders = (relative(own_rows, False), relative(own_rows, True))
    slots = len(orders[0])
    slot_rows = WIDTH // slots

    gains = jnp.pad(jnp.stack([norm_attn_gain, norm_mlp_gain], axis=1), ((0, 0), (0, LANES - 2)))
    flat_qkv = qkv_weight.reshape(own_rows, HALF)
    first_pieces = gather_start(jnp.concatenate([flat_qkv, gains], axis=1))
    shard_in = jnp.concatenate(
        [
            in_weight[:, 0, :UNITS],
            in_weight[:, 1, :UNITS],
            in_weight[:, 0, UNITS:],
            in_weight[:, 1, UNITS:],
        ],
        axis=1,
    )
    turned_out = out_weight.T
    blank = jnp.zeros((own_rows, HEAD_DIM), BF16)
    shard_down = jnp.concatenate([attn_out_weight.T, turned_out, blank], axis=1)
    second_shard = jnp.concatenate([shard_in, shard_down], axis=1)
    second_shard, *first_pieces = held_until([second_shard] + first_pieces)
    second_pieces = gather_start(second_shard)

    own_segment = lax.dynamic_slice_in_dim(segment, core * ROWS, ROWS, 0)
    seg_pad = jnp.pad(segment, (WINDOW_HALF, WINDOW_HALF), constant_values=-2)
    span_segment = lax.dynamic_slice_in_dim(seg_pad, core * ROWS, ROWS + 2 * WINDOW_HALF, 0)
    slot = core * ROWS - WINDOW_HALF + jnp.arange(ROWS + 2 * WINDOW_HALF, dtype=jnp.int32)
    position = jnp.where(span_segment >= 0, slot - PAD_BLOCK * span_segment, 0)
    lane = jnp.arange(LANES, dtype=jnp.int32)
    exponent = (lane % 32).astype(F32) * (2.0 / HEAD_DIM)
    angle = position.astype(F32)[:, None] * jnp.power(10000.0, -exponent)[None, :]
    cos_span = jnp.cos(angle)
    sin_span = jnp.sin(angle) * jnp.where((lane & 32) == 0, -1.0, 1.0)[None, :]
    cosine = cos_span[WINDOW_HALF:-WINDOW_HALF]
    sine = sin_span[WINDOW_HALF:-WINDOW_HALF]
    col_seg = span_segment[:, None]
    row_seg = own_segment.reshape(ROWS // LANES, 1, LANES)
    live = (own_segment >= 0).astype(F32)[:, None]

    rows = 384
    steps = ROWS // rows
    by_column = lambda: pl.BlockSpec((WIDTH, rows), lambda i, s: (0, i))

    (out_grad_turned,) = call(
        lambda *refs: turn_kernel(orders[1], *refs),
        info,
        (steps,),
        [cotangent, live],
        [by_rows(rows, WIDTH), by_rows(rows, 1)],
        [shape_of((WIDTH, ROWS))],
        [by_column()],
        [pltpu.VMEM((WIDTH, rows), BF16)],
        0,
    )

    first_pieces = held_until(first_pieces, out_grad_turned, cos_span, sin_span)
    held_a = columns_of(first_pieces, 0, FIRST_CUT)
    held_b = columns_of(first_pieces, FIRST_CUT, HALF + LANES)
    own_a = gather_finish(gather_middle(held_a, False)[0], False)
    own_b = gather_finish(gather_middle(held_b, True)[0], True)
    other_a = [swapped_cores(piece) for piece in own_a]
    other_b = [swapped_cores(piece) for piece in own_b]
    held_in, arrived_in = gather_middle(columns_of(second_pieces, 0, HALF), False)
    held_down, arrived_down = gather_middle(columns_of(second_pieces, HALF, HALF + DOWN), True)

    token_specs = [by_rows(rows, WIDTH), by_rows(rows, LANES), by_rows(rows, LANES)]
    counts = (len(own_a), len(own_b))
    half_shapes = [shape_of((ROWS, HALF)), shape_of((WINDOW_HALF, 2 * THIRD)), shape_of((WIDTH, HALF))]
    half_specs = [by_rows(rows, HALF), full(WINDOW_HALF, 2 * THIRD), full(WIDTH, HALF)]
    qkv_own, edge_own, w_own, gain_rows, turned_a, turned_b = call(
        lambda *refs: qkv_kernel(orders, counts, True, *refs),
        info,
        (steps,),
        [tokens, cosine, sine, *own_a, *own_b],
        token_specs + [ANYWHERE] * sum(counts),
        half_shapes + [shape_of((8, WIDTH), F32), shape_of((WIDTH, ROWS)), shape_of((WIDTH, ROWS))],
        half_specs + [full(8, WIDTH), by_column(), by_column()],
        [
            pltpu.VMEM((WIDTH, LANES), BF16),
            pltpu.VMEM((WIDTH, rows), BF16),
            pltpu.SemaphoreType.DMA((2,)),
        ],
        2 * ROWS * WIDTH * HALF,
        after=[other_a[0], other_b[0]] if len(other_a) > 1 else [],
    )
    edge_for_other = swapped_cores(edge_own)
    held_in, held_down = held_until((held_in, held_down), qkv_own)
    in_own, down_own = gather_finish(held_in, False), gather_finish(held_down, True)
    qkv_other, edge_other, w_other = call(
        lambda *refs: qkv_kernel(orders, counts, False, *refs),
        info,
        (steps,),
        [tokens, cosine, sine, *other_a, *other_b, gain_rows],
        token_specs + [ANYWHERE] * sum(counts) + [full(8, WIDTH)],
        half_shapes,
        half_specs,
        [pltpu.SemaphoreType.DMA((2,))],
        2 * ROWS * WIDTH * HALF,
    )
    edge_for_own = swapped_cores(edge_other)

    blocks = ROWS // LANES
    window_shape = (ROWS + 2 * WINDOW_HALF, 2 * THIRD)
    by_block = pl.BlockSpec((1, PAIRS, SPAN, SPAN), lambda i, s: (i, 0, 0, 0))

    def attend(qkv, edge, after):
        return call(
            attend_kernel,
            info,
            (blocks,),
            [row_seg, col_seg, qkv, qkv, edge],
            [
                pl.BlockSpec((1, 1, LANES), lambda i, s: (i, 0, 0)),
                full(ROWS + 2 * WINDOW_HALF, 1),
                by_rows(LANES, THIRD),
                ANYWHERE,
                ANYWHERE,
            ],
            [shape_of((ROWS, THIRD)), shape_of((blocks, PAIRS, SPAN, SPAN))],
            [by_rows(LANES, THIRD), by_block],
            [pltpu.VMEM(window_shape, BF16), pltpu.SemaphoreType.DMA((2,))],
            blocks * PAIRS * 2 * 2 * SPAN * SPAN * LANES,
            after=after,
        )

    att_other, probs_other = attend(
        qkv_other, edge_for_other, [arrived_in, arrived_down]
    )
    att_own, probs_own = attend(qkv_own, edge_for_own, [att_other])

    in_own[-1], down_own[-1] = held_until((in_own[-1], down_own[-1]), att_other)
    in_other = [swapped_cores(piece) for piece in in_own]
    down_other = [swapped_cores(piece) for piece in down_own]
    parts = (in_own, in_other, down_own, down_other)
    counts = tuple(len(part) for part in parts)
    (
        layer_out,
        hidden_grad,
        att_grad_own,
        att_grad_other,
        gated,
        pre_grad_own,
        pre_grad_other,
        normed_two_turned,
        hidden_grad_turned,
    ) = call(
        lambda *refs: mlp_kernel(orders, counts, *refs),
        info,
        (steps,),
        [tokens, att_own, att_other, cotangent, live, gain_rows]
        + [piece for part in parts for piece in part],
        [by_rows(rows, WIDTH), by_rows(rows, THIRD), by_rows(rows, THIRD), by_rows(rows, WIDTH)]
        + [by_rows(rows, 1), full(8, WIDTH)]
        + [ANYWHERE] * sum(counts),
        [
            shape_of((ROWS, WIDTH)),
            shape_of((ROWS, WIDTH), F32),
            shape_of((ROWS, THIRD)),
            shape_of((ROWS, THIRD)),
            shape_of((ROWS, HALF)),
            shape_of((ROWS, HALF)),
            shape_of((ROWS, HALF)),
            shape_of((WIDTH, ROWS)),
            shape_of((WIDTH, ROWS)),
        ],
        [by_rows(rows, WIDTH)] * 2
        + [by_rows(rows, THIRD)] * 2
        + [by_rows(rows, HALF)] * 3
        + [by_column()] * 2,
        [
            pltpu.VMEM((WIDTH, 2 * HALF), BF16),
            pltpu.VMEM((WIDTH, WIDTH), BF16),
            pltpu.VMEM((WIDTH, HALF), BF16),
            pltpu.VMEM((WIDTH, LANES), BF16),
            pltpu.VMEM((WIDTH, LANES), BF16),
            pltpu.VMEM((WIDTH, rows), BF16),
            pltpu.SemaphoreType.DMA((5,)),
        ],
        2 * ROWS * WIDTH * (4 * HALF + 2 * HALF + 2 * WIDTH),
    )

    def early_grads(number, pre_grad, att):
        lefts = [normed_two_turned, hidden_grad_turned, out_grad_turned]
        rights = [pre_grad, att, gated, gated]
        jobs = ((0, 0, 0, 0), (1, 1, 1, 0), (2, 2, 1, THIRD), (2, 3, 1, THIRD + UNITS))
        outs = [shape_of((WIDTH, HALF)), shape_of((WIDTH, DOWN))]
        return call(
            lambda *refs: weight_grad_kernel(jobs, (3, 4), number == 1, *refs),
            info,
            (1,),
            lefts + rights,
            [full(WIDTH, ROWS)] * 3
            + [
                full(ROWS, HALF),
                full(ROWS, THIRD),
                pl.BlockSpec((ROWS, UNITS), lambda i, s: (0, number)),
                pl.BlockSpec((ROWS, LANES), lambda i, s: (0, 2 * UNITS // LANES)),
            ],
            outs,
            [full(*out.shape) for out in outs],
            [],
            2 * ROWS * WIDTH * (HALF + DOWN),
        )

    by_slots = lambda array: array.reshape(slots, slot_rows, array.shape[1])
    send_in, send_down = early_grads(1, pre_grad_other, att_other)
    keep_in, keep_down = early_grads(0, pre_grad_own, att_own)
    sum_in, in_back = scatter_start(by_slots(keep_in), by_slots(send_in), own_rows, False)
    sum_down, down_back = scatter_start(by_slots(keep_down), by_slots(send_down), own_rows, True)

    def attend_back(qkv, probs, att_grad, edge, after):
        return call(
            attend_back_kernel,
            info,
            (blocks,),
            [qkv, probs, att_grad, cos_span, sin_span, qkv, edge],
            [
                by_rows(LANES, THIRD),
                by_block,
                by_rows(LANES, THIRD),
                full(*cos_span.shape),
                full(*cos_span.shape),
                ANYWHERE,
                ANYWHERE,
            ],
            [shape_of((ROWS, HALF)), shape_of((WINDOW_HALF, 2 * THIRD))],
            [full(ROWS, HALF), full(WINDOW_HALF, 2 * THIRD)],
            [
                pltpu.VMEM(window_shape, BF16),
                pltpu.VMEM((window_shape[0], THIRD), F32),
                pltpu.VMEM((window_shape[0], THIRD), F32),
                pltpu.SemaphoreType.DMA((2,)),
            ],
            blocks * PAIRS * 4 * 2 * SPAN * SPAN * LANES,
            after=after,
        )

    grad_own, edge_grad = attend_back(qkv_own, probs_own, att_grad_own, edge_for_own, [keep_in])
    edge_grad_other = swapped_cores(edge_grad)
    grad_other, edge_grad = attend_back(
        qkv_other, probs_other, att_grad_other, edge_for_other, [grad_own, in_back[0], down_back[0]]
    )
    edge_grad_own = swapped_cores(edge_grad)

    def late_grads(grad, edge, after):
        outs = [shape_of((WIDTH, FIRST_CUT)), shape_of((WIDTH, HALF - FIRST_CUT))]
        ins = [turned_a, turned_b, grad, edge]
        return call(
            qkv_weight_grad_kernel,
            info,
            (1,),
            ins,
            [full(*array.shape) for array in ins],
            outs,
            [full(*out.shape) for out in outs],
            [pltpu.VMEM((LANES, 2 * THIRD), BF16)],
            2 * ROWS * WIDTH * HALF,
            after=after,
        )

    send_a, send_b = late_grads(grad_other, edge_grad_other, [in_back[1], down_back[1]])
    keep_a, keep_b = late_grads(grad_own, edge_grad_own, [send_a])
    sum_a, a_back = scatter_start(by_slots(keep_a), by_slots(send_a), own_rows, False)
    sum_b, b_back = scatter_start(by_slots(keep_b), by_slots(send_b), own_rows, True)
    sum_in, sum_down = held_until((sum_in, sum_down), a_back[0], b_back[0])
    owned_early = scatter_finish(sum_in, sum_down)
    owned_in, owned_down = owned_early[:, :HALF], owned_early[:, HALF:]

    part_rows = 288
    part_steps = ROWS // part_rows // 2
    grad_tokens = None
    for base in (0, part_steps):
        at_row = lambda width: pl.BlockSpec((part_rows, width), lambda i, s: (i + base, 0))
        ins = [tokens, grad_own, grad_other, edge_grad_own, edge_grad_other, hidden_grad, gain_rows]
        ins += [w_own, w_other]
        specs = [at_row(WIDTH), at_row(HALF), at_row(HALF)]
        specs += [full(WINDOW_HALF, 2 * THIRD)] * 2 + [at_row(WIDTH), full(8, WIDTH)]
        specs += [full(WIDTH, HALF)] * 2
        aliases = None
        if grad_tokens is None:
            after = [keep_a, a_back[0], b_back[0], in_back[2], down_back[2]]
        else:
            after = [grad_tokens, a_back[1], b_back[1], owned_early]
            aliases = {1 + len(ins): 0}
        (grad_tokens,) = call(
            lambda *refs: input_grad_kernel(base, *refs),
            info,
            (part_steps,),
            ins,
            specs,
            [shape_of((ROWS, WIDTH), F32)],
            [at_row(WIDTH)],
            [pltpu.VMEM((part_rows, HALF), BF16)],
            ROWS * WIDTH * 2 * HALF,
            aliases,
            after,
        )

    flat_grad = scatter_finish(sum_a, sum_b)
    gain_grads = jnp.stack(
        [
            gain_part(flat_qkv, flat_grad, norm_attn_gain),
            gain_part(shard_in, owned_in, norm_mlp_gain),
        ]
    )
    (gain_grads,) = held_until((gain_grads,), grad_tokens)
    gain_grads = gain_grads + swapped_cores(gain_grads)
    owned_gain_one, owned_gain_two = gain_grads[0], gain_grads[1]
    owned_qkv = flat_grad.reshape(own_rows, 3, THIRD)
    owned_in = jnp.stack(
        [
            jnp.concatenate([owned_in[:, :UNITS], owned_in[:, 2 * UNITS : -64]], axis=1),
            jnp.concatenate([owned_in[:, UNITS : 2 * UNITS], owned_in[:, -64:]], axis=1),
        ],
        axis=1,
    )
    owned_attn = owned_down[:, :THIRD].T
    owned_out = owned_down[:, THIRD : THIRD + UNITS + HEAD_DIM].T
    return (
        layer_out,
        grad_tokens,
        owned_gain_one,
        owned_qkv,
        owned_attn,
        owned_gain_two,
        owned_in,
        owned_out,
    )


def solution(mesh):
    placed = (
        P(("dp", "tensor"), None),
        P("dp"),
        P("dp"),
        P("dp", None, "tensor"),
        P("tensor", "dp"),
        P("dp"),
        P("dp", None, "tensor"),
        P("tensor", "dp"),
        P(("dp", "tensor"), None),
    )
    return jax.shard_map(
        body,
        mesh=mesh,
        in_specs=placed,
        out_specs=(
            P(("dp", "tensor"), None),
            P(("dp", "tensor"), None),
            P("dp"),
            P("dp", None, "tensor"),
            P("tensor", "dp"),
            P("dp"),
            P("dp", None, "tensor"),
            P("tensor", "dp"),
        ),
        check_vma=False,
    )
```

```python
import jax
import jax.numpy as jnp
from jax import lax
from jax.experimental import pallas as pl
from jax.experimental.pallas import tpu as pltpu
from jax.sharding import PartitionSpec as P

HEAD_DIM = 64
WINDOW_HALF = 64
PAD_BLOCK = 128
WIDTH = 768
ROWS = 1152
HALF = 1152
LANES = 128
THIRD = 384
PAIRS = 6
SPAN = 2 * LANES
UNITS = 512
FIRST_CUT = 640
DOWN = 384 + UNITS + LANES
VMEM = 58 * 2**20
ANYWHERE = pl.BlockSpec(memory_space=pl.ANY)
F32 = jnp.float32
BF16 = jnp.bfloat16


def steps_of(devices, swapped):
    bits = [1 << i for i in range(devices.bit_length() - 1)]
    near, far = bits[:2], bits[2:]
    return far + (near if swapped else near[::-1])


def exchanged(block, mask):
    devices = lax.axis_size("dp")
    return lax.ppermute(block, "dp", [(i, i ^ mask) for i in range(devices)])


def swapped_cores(block):
    return lax.ppermute(block, "tensor", [(0, 1), (1, 0)])


def by_exchange(own_rows):
    devices = lax.axis_size("dp")
    return own_rows % 16 == 0 and devices & (devices - 1) == 0


def relative(own_rows, swapped):
    if not by_exchange(own_rows):
        return list(range(WIDTH // 48))
    order = [0]
    for mask in steps_of(lax.axis_size("dp"), swapped):
        order = order + [r ^ mask for r in order]
    return order


def held_until(arrays, *gates):
    return lax.optimization_barrier((tuple(arrays), gates))[0]


def gather_start(shard):
    masks = steps_of(lax.axis_size("dp"), False)
    held = shard[None]
    if not by_exchange(shard.shape[0]) or len(masks) <= 3:
        return [held]
    first, second = masks[:2]
    return [held] + [exchanged(held, mask) for mask in (first, second, first ^ second)]


def columns_of(pieces, start, stop):
    return jnp.concatenate([piece[:, :, start:stop] for piece in pieces], axis=0)


def gather_middle(held, swapped):
    arrived = held
    if by_exchange(held.shape[1]):
        masks = steps_of(lax.axis_size("dp"), swapped)
        for mask in masks[held.shape[0].bit_length() - 1 : -1]:
            arrived = exchanged(held, mask)
            held = jnp.concatenate([held, arrived], axis=0)
    return held, arrived


def gather_finish(held, swapped):
    if not by_exchange(held.shape[1]):
        whole = lax.all_gather(held[0], "dp", axis=0, tiled=True)
        return [whole.reshape(WIDTH // 48, 48, held.shape[2])]
    return [held, exchanged(held, steps_of(lax.axis_size("dp"), swapped)[-1])]


def scatter_start(keep, other, own_rows, swapped, first_gate=None):
    arrivals = [other]
    if not by_exchange(own_rows):
        total = keep.astype(F32) + other.astype(F32)
        total = lax.psum_scatter(total, "dp", scatter_dimension=0, tiled=True)
        return total[None], arrivals * 3
    devices = lax.axis_size("dp")
    index = lax.axis_index("dp")
    levels = devices.bit_length() - 1
    masks = steps_of(devices, swapped)
    last = 2 if len(masks) > 3 else 0
    shape = (2,) * levels + (own_rows, keep.shape[1])
    keep, other = keep.reshape(shape), other.reshape(shape)
    for mask in reversed(masks[last:]):
        axis = levels - mask.bit_length()
        bit = (index & mask) // mask
        part = lambda array, which: lax.dynamic_slice_in_dim(array, which, 1, axis).astype(F32)
        sent = part(keep, 1 - bit) + part(other, 1 - bit)
        kept = part(keep, bit) + part(other, bit)
        other = exchanged(sent.astype(BF16), mask)
        arrivals.append(other)
        if first_gate is not None and len(arrivals) == 2:
            (other,) = held_until((other,), first_gate)
        keep = kept
    total = keep.astype(F32) + other.astype(F32)
    return total.reshape(2**last, own_rows, -1), arrivals + [other] * 3


def scatter_finish(*totals):
    if totals[0].shape[0] == 1:
        return jnp.concatenate([total[0] for total in totals], axis=1)
    unit = steps_of(lax.axis_size("dp"), False)[0]
    place = (lax.axis_index("dp") // unit) % 4

    def rows_of(which):
        parts = [lax.dynamic_index_in_dim(total, which, 0, keepdims=False) for total in totals]
        return jnp.concatenate(parts, axis=1)

    arrived = [
        exchanged(rows_of(place ^ j).astype(BF16), unit * j).astype(F32) for j in range(1, 4)
    ]
    return rows_of(place) + (arrived[0] + arrived[1] + arrived[2])


def weight_grad(left, right):
    return lax.dot_general(
        left, right, (((0,), (0,)), ((), ())), preferred_element_type=F32
    ).astype(BF16)


def gain_part(weight, grad, gain):
    return jnp.sum(weight.astype(F32) * grad, axis=1) / gain.astype(F32)


def nt(left, right):
    return lax.dot_general(left, right, (((1,), (1,)), ((), ())), preferred_element_type=F32)


def nn(left, right):
    return jnp.dot(left, right, preferred_element_type=F32)


def start_slots(info, pieces, order, segments, sems):
    slot = 0
    for piece in pieces:
        rows = piece.shape[1]
        for at in range(piece.shape[0]):
            row = pl.multiple_of((info[0] ^ order[slot]) * rows, 16)
            for begin, width, target, column, sem in segments:
                pltpu.make_async_copy(
                    piece.at[at, :, pl.ds(begin, width)],
                    target.at[pl.ds(row, rows), pl.ds(column, width)],
                    sems.at[sem],
                ).start()
            slot += 1


def wait_whole(ref, sem):
    pltpu.make_async_copy(ref, ref, sem).wait()


def fill_window(info, qkv_ref, edge_ref, window, sems):
    core = info[1]
    first = pl.multiple_of(jnp.where(core == 1, 0, WINDOW_HALF + ROWS), 16)
    last = pl.multiple_of(jnp.where(core == 1, WINDOW_HALF + ROWS, 0), 16)
    copies = [
        pltpu.make_async_copy(edge_ref, window.at[pl.ds(first, WINDOW_HALF), :], sems.at[4])
    ]
    for part in range(2):
        for half in range(2):
            copies.append(
                pltpu.make_async_copy(
                    qkv_ref.at[:, pl.ds(HALF * half + THIRD * (part + 1), THIRD)],
                    window.at[pl.ds(WINDOW_HALF, ROWS), pl.ds(WIDTH * part + THIRD * half, THIRD)],
                    sems.at[2 * part + half],
                )
            )
    for copy in copies:
        copy.start()
    window[pl.ds(last, WINDOW_HALF), :] = jnp.zeros((WINDOW_HALF, 2 * WIDTH), BF16)
    for copy in copies:
        copy.wait()


def identity():
    row = lax.broadcasted_iota(jnp.int32, (LANES, LANES), 0)
    lane = lax.broadcasted_iota(jnp.int32, (LANES, LANES), 1)
    return jnp.where(row == lane, 1.0, 0.0).astype(BF16)


def turn_rows(unit, window, begin, row, turned_ref):
    for pair in range(PAIRS):
        lanes = slice(LANES * pair, LANES * (pair + 1))
        block = window[pl.ds(row, LANES), begin + LANES * pair : begin + LANES * (pair + 1)]
        turned_ref[lanes, pl.ds(row, LANES)] = nt(unit, block).astype(BF16)


def head_rows(columns):
    return jnp.concatenate([columns[:HEAD_DIM, :LANES], columns[HEAD_DIM:, LANES:]], axis=0)


def normalized(values):
    centred = values - jnp.mean(values, axis=-1, keepdims=True)
    spread = jnp.mean(centred * centred, axis=-1, keepdims=True)
    factor = lax.rsqrt(spread + 1e-05)
    return centred * factor, factor


def norm_backward(grad, unit, factor, gain):
    inner = grad * gain
    mean = jnp.mean(inner, axis=-1, keepdims=True)
    along = jnp.mean(inner * unit, axis=-1, keepdims=True)
    return factor * (inner - mean - unit * along)


def turned(values, cosine, sine):
    lane = lax.broadcasted_iota(jnp.int32, values.shape, 1)
    first = (lane & 32) == 0
    other = jnp.where(first, pltpu.roll(values, 96, 1), pltpu.roll(values, 32, 1))
    return values * cosine + other * sine


def both_heads(block):
    lane = lax.broadcasted_iota(jnp.int32, block.shape, 1)
    first = jnp.where(lane < HEAD_DIM, 1.0, 0.0).astype(block.dtype)
    second = jnp.where(lane < HEAD_DIM, 0.0, 1.0).astype(block.dtype)
    return jnp.concatenate([block * first, block * second], axis=0)


def qkv_kernel(orders, counts, info, x_ref, cos_ref, sin_ref, *refs):
    parts = []
    for count in counts:
        parts.append(refs[:count])
        refs = refs[count:]
    own_a, other_a, own_b, other_b = parts
    qkv_ref, normed_ref, gain_ref, edge_ref, weight, gains, sems = refs
    step = pl.program_id(0)
    rows = x_ref.shape[0]

    @pl.when(step == 0)
    def _():
        rest = HALF - FIRST_CUT
        start_slots(info, own_b, orders[1], [(rest, LANES, gains, 0, 1)], sems)
        for begin, part_a, part_b in ((0, own_a, own_b), (HALF, other_a, other_b)):
            start_slots(info, part_a, orders[0], [(0, FIRST_CUT, weight, begin, 0)], sems)
            start_slots(info, part_b, orders[1], [(0, rest, weight, begin + FIRST_CUT, 0)], sems)
        wait_whole(gains, sems.at[1])
        row = lax.broadcasted_iota(jnp.int32, (16, LANES), 0)
        lane = lax.broadcasted_iota(jnp.int32, (16, LANES), 1)
        pick = jnp.where(row == lane, 1.0, 0.0).astype(BF16)
        gain_ref[...] = nt(pick, gains[...])[:8]
        wait_whole(weight, sems.at[0])

    unit, unused = normalized(x_ref[...].astype(F32))
    normed = (unit * gain_ref[0:1, :]).astype(BF16)
    normed_ref[...] = normed
    cosine, sine = cos_ref[...], sin_ref[...]
    for half in range(2):
        result = nn(normed, weight[:, HALF * half : HALF * (half + 1)])
        for tile in range(9):
            block = result[:, LANES * tile : LANES * (tile + 1)]
            if tile < 6:
                block = turned(block, cosine, sine)
            if tile < 3:
                block = block * (HEAD_DIM**-0.5)
            begin = HALF * half + LANES * tile
            qkv_ref[:, begin : begin + LANES] = block.astype(BF16)

    for core, at_step, begin in ((1, 0, 0), (0, ROWS // rows - 1, rows - WINDOW_HALF)):

        @pl.when((info[1] == core) & (step == at_step))
        def _():
            for part in range(2):
                for half in range(2):
                    source = HALF * half + THIRD * (part + 1)
                    target = WIDTH * part + THIRD * (1 - half)
                    edge_ref[:, target : target + THIRD] = qkv_ref[
                        begin : begin + WINDOW_HALF, source : source + THIRD
                    ]


def attend_kernel(
    info, row_seg, col_seg, q_ref, qkv_ref, edge_ref, own_ref, other_ref, probs_ref, window, turned_values, sems
):
    step = pl.program_id(0)
    unit = identity()

    @pl.when(step == 0)
    def _():
        fill_window(info, qkv_ref, edge_ref, window, sems)
        turn_rows(unit, window, WIDTH, 0, turned_values)

    start = pl.multiple_of(step * LANES, LANES)
    turn_rows(unit, window, WIDTH, pl.multiple_of(start + LANES, LANES), turned_values)
    key_seg = col_seg[pl.ds(start, SPAN), :]
    key_at = lax.broadcasted_iota(jnp.int32, (SPAN, LANES), 0) - WINDOW_HALF
    query_at = lax.broadcasted_iota(jnp.int32, (SPAN, LANES), 1)
    near = jnp.abs(key_at - query_at) <= WINDOW_HALF
    allowed = (key_seg == row_seg[0]) & near
    bias = jnp.where(allowed, 0.0, -1e30)
    bias = jnp.concatenate([bias, bias], axis=1)

    def scores_of(pair):
        begin = HALF * (pair // 3) + LANES * (pair % 3)
        queries = both_heads(q_ref[:, begin : begin + LANES])
        keys = window[pl.ds(start, SPAN), LANES * pair : LANES * (pair + 1)]
        return nt(keys, queries)

    following = scores_of(0)
    for pair in range(PAIRS):
        scores = following + bias
        if pair + 1 < PAIRS:
            following = scores_of(pair + 1)
        weights = jnp.exp(scores - jnp.max(scores, axis=0, keepdims=True))
        total = jnp.sum(weights, axis=0, keepdims=True)
        probs = (weights * (1.0 / total)).astype(BF16)
        probs_ref[0, pair] = probs
        values = turned_values[LANES * pair : LANES * (pair + 1), pl.ds(start, SPAN)]
        result = nt(unit, head_rows(nn(values, probs)).astype(BF16)).astype(BF16)
        out_ref = own_ref if pair < 3 else other_ref
        out_ref[:, LANES * (pair % 3) : LANES * (pair % 3 + 1)] = result


def mlp_kernel(orders, counts, info, x_ref, att_own, att_other, cot_ref, live_ref, gain_ref, *refs):
    parts = []
    for count in counts:
        parts.append(refs[:count])
        refs = refs[count:]
    in_own, in_other, down_own, down_other = parts
    (
        out_ref,
        hidden_grad_ref,
        att_grad_own,
        att_grad_other,
        normed_ref,
        gated_own,
        gated_other,
        pre_grad_own,
        pre_grad_other,
        low_grad_ref,
        out_grad_ref,
        w_in,
        w_att,
        w_out,
        tail_own,
        tail_other,
        sems,
    ) = refs
    step = pl.program_id(0)

    @pl.when(step == 0)
    def _():
        for number, (part, tail) in enumerate(((down_own, tail_own), (down_other, tail_other))):
            segments = [
                (0, THIRD, w_att, THIRD * number, 1),
                (THIRD, UNITS, w_out, UNITS * number, 2),
                (THIRD + UNITS, LANES, tail, 0, 3 + number),
            ]
            start_slots(info, part, orders[1], segments, sems)
        for number, part in enumerate((in_own, in_other)):
            start_slots(info, part, orders[0], [(0, HALF, w_in, HALF * number, 0)], sems)
        wait_whole(w_att, sems.at[1])
        wait_whole(w_out.at[:, pl.ds(0, 2 * UNITS)], sems.at[2])
        wait_whole(tail_own, sems.at[3])
        wait_whole(tail_other, sems.at[4])
        other = pltpu.roll(tail_other[...].astype(F32), HEAD_DIM, 1).astype(BF16)
        w_out[:, 2 * UNITS :] = tail_own[...] + other
        wait_whole(w_in, sems.at[0])

    gain = gain_ref[1:2, :]
    hidden = (
        x_ref[...].astype(F32)
        + nt(att_own[...], w_att[:, :THIRD])
        + nt(att_other[...], w_att[:, THIRD:])
    )
    unit, factor = normalized(hidden)
    normed = (unit * gain).astype(BF16)
    normed_ref[...] = normed
    out_grad = cot_ref[...].astype(F32) * live_ref[...]
    out_grad_low = out_grad.astype(BF16)
    out_grad_ref[...] = out_grad_low
    pre = [nn(normed, w_in[:, HALF * half : HALF * (half + 1)]) for half in range(2)]
    tails = [part[:, 2 * UNITS :] for part in pre]
    lane = lax.broadcasted_iota(jnp.int32, tails[0].shape, 1)
    low = lane < HEAD_DIM
    gates = [part[:, :UNITS] for part in pre]
    gates.append(jnp.where(low, tails[0], pltpu.roll(tails[1], 64, 1)))
    ups = [part[:, UNITS : 2 * UNITS] for part in pre]
    ups.append(jnp.where(low, pltpu.roll(tails[0], 64, 1), tails[1]))
    pre_grads = (pre_grad_own, pre_grad_other)
    for part, (gate, up) in enumerate(zip(gates, ups)):
        columns = slice(UNITS * part, UNITS * part + gate.shape[1])
        share = 0.5 + 0.5 * lax.erf(gate * (0.5**0.5))
        slope = share + gate * (jnp.exp(-0.5 * gate * gate) * 0.3989422804014327)
        curve = gate * share
        gated = curve * up
        grad = nn(out_grad_low, w_out[:, columns])
        gate_grad = grad * up * slope
        up_grad = grad * curve
        if part < 2:
            (gated_own, gated_other)[part][:, :UNITS] = gated.astype(BF16)
            pre_grads[part][:, :UNITS] = gate_grad.astype(BF16)
            pre_grads[part][:, UNITS : 2 * UNITS] = up_grad.astype(BF16)
        else:
            gated_own[:, UNITS:] = gated.astype(BF16)
            gated_other[:, UNITS:] = pltpu.roll(gated, HEAD_DIM, 1).astype(BF16)
            own = jnp.where(low, gate_grad, pltpu.roll(up_grad, 64, 1))
            other = jnp.where(low, pltpu.roll(gate_grad, 64, 1), up_grad)
            pre_grad_own[:, 2 * UNITS :] = own.astype(BF16)
            pre_grad_other[:, 2 * UNITS :] = other.astype(BF16)
    product = (
        nt(gated_own[:, :UNITS], w_out[:, :UNITS])
        + nt(gated_other[:, :UNITS], w_out[:, UNITS : 2 * UNITS])
        + nt(gated_own[:, UNITS:], w_out[:, 2 * UNITS :])
    )
    out_ref[...] = (hidden + product).astype(BF16)
    normed_grad = nt(pre_grad_own[...], w_in[:, :HALF]) + nt(pre_grad_other[...], w_in[:, HALF:])
    hidden_grad = out_grad + norm_backward(normed_grad, unit, factor, gain)
    hidden_grad_ref[...] = hidden_grad
    hidden_grad_low = hidden_grad.astype(BF16)
    low_grad_ref[...] = hidden_grad_low
    att_grad_own[...] = nn(hidden_grad_low, w_att[:, :THIRD]).astype(BF16)
    att_grad_other[...] = nn(hidden_grad_low, w_att[:, THIRD:]).astype(BF16)


def attend_back_kernel(
    info,
    q_ref,
    probs_ref,
    grad_own,
    grad_other,
    cos_ref,
    sin_ref,
    cos_turned,
    sin_turned,
    qkv_ref,
    edge_ref,
    out_own,
    out_other,
    edge_out_ref,
    window,
    turned_keys,
    key_grad,
    value_grad,
    sems,
):
    step = pl.program_id(0)
    unit = identity()

    @pl.when(step == 0)
    def _():
        fill_window(info, qkv_ref, edge_ref, window, sems)
        turn_rows(unit, window, 0, 0, turned_keys)
        key_grad[...] = jnp.zeros_like(key_grad)
        value_grad[...] = jnp.zeros_like(value_grad)

    start = pl.multiple_of(step * LANES, LANES)
    span = pl.ds(start, SPAN)
    turn_rows(unit, window, 0, pl.multiple_of(start + LANES, LANES), turned_keys)
    cosine, sine = cos_turned[...], sin_turned[...]

    def probs_grad_of(pair):
        grad_ref = grad_own if pair < 3 else grad_other
        grads = both_heads(grad_ref[:, LANES * (pair % 3) : LANES * (pair % 3 + 1)])
        values = window[span, WIDTH + LANES * pair : WIDTH + LANES * (pair + 1)]
        return grads, nt(values, grads)

    following = probs_grad_of(0)
    for pair in range(PAIRS):
        lanes = slice(LANES * pair, LANES * (pair + 1))
        place = slice(LANES * (pair % 3), LANES * (pair % 3 + 1))
        begin = HALF * (pair // 3) + LANES * (pair % 3)
        grads, probs_grad = following
        if pair + 1 < PAIRS:
            following = probs_grad_of(pair + 1)
        probs = probs_ref[0, pair]
        probs_wide = probs.astype(F32)
        weighted = probs_grad * probs_wide
        delta = jnp.sum(weighted, axis=0, keepdims=True)
        score_grad = (weighted - probs_wide * delta).astype(BF16)
        value_grad[span, lanes] += nn(probs, grads)
        queries = both_heads(q_ref[:, begin : begin + LANES])
        key_grad[span, lanes] += nn(score_grad, queries)
        query_grad = head_rows(nn(turned_keys[lanes, span], score_grad)) * (HEAD_DIM**-0.5)
        other = jnp.concatenate(
            [query_grad[32:64], query_grad[:32], query_grad[96:], query_grad[64:96]], axis=0
        )
        query_grad = (query_grad * cosine - other * sine).astype(BF16)
        out_ref = out_own if pair < 3 else out_other
        out_ref[pl.ds(start, LANES), place] = nt(unit, query_grad).astype(BF16)

    @pl.when(step == ROWS // LANES - 1)
    def _():
        inside = slice(WINDOW_HALF, WINDOW_HALF + ROWS)
        row = pl.multiple_of(jnp.where(info[1] == 1, 0, WINDOW_HALF + ROWS), 16)
        edge_rows = pl.ds(row, WINDOW_HALF)
        for pair in range(PAIRS):
            out_ref = out_own if pair < 3 else out_other
            lanes = slice(LANES * pair, LANES * (pair + 1))
            begin = LANES * (pair % 3)
            target = (LANES * pair + THIRD) % WIDTH
            out_ref[:, THIRD + begin : THIRD + begin + LANES] = turned(
                key_grad[inside, lanes], cos_ref[inside, :], -sin_ref[inside, :]
            ).astype(BF16)
            out_ref[:, 2 * THIRD + begin : 2 * THIRD + begin + LANES] = value_grad[
                inside, lanes
            ].astype(BF16)
            edge_out_ref[:, target : target + LANES] = turned(
                key_grad[edge_rows, lanes], cos_ref[edge_rows, :], -sin_ref[edge_rows, :]
            ).astype(BF16)
            edge_out_ref[:, WIDTH + target : WIDTH + target + LANES] = value_grad[
                edge_rows, lanes
            ].astype(BF16)


def edge_kernel(info, own_ref, other_ref, edge_ref, own_out, other_out):
    for half, (grad_ref, out_ref) in enumerate(((own_ref, own_out), (other_ref, other_out))):
        out_ref[:, :THIRD] = grad_ref[:, :THIRD]
        for part in range(2):
            at = slice(THIRD * (part + 1), THIRD * (part + 2))
            begin = WIDTH * part + THIRD * half
            add = edge_ref[:, begin : begin + THIRD].astype(F32)
            out_ref[:, at] = (grad_ref[:, at].astype(F32) + add).astype(BF16)


def input_grad_kernel(info, x_ref, own_ref, other_ref, hidden_ref, gain_ref, weight, out_ref):
    grad = nt(own_ref[...], weight[:, :HALF]) + nt(other_ref[...], weight[:, HALF:])
    unit, factor = normalized(x_ref[...].astype(F32))
    out_ref[...] = hidden_ref[...] + norm_backward(grad, unit, factor, gain_ref[0:1, :])


def shape_of(shape, dtype=BF16):
    return jax.ShapeDtypeStruct(shape, dtype)


def call(
    kernel, info, grid, ins, in_specs, outs, out_specs, scratch, flops, aliases=None, after=()
):
    moved = sum(a.size * a.dtype.itemsize for a in list(ins) + list(outs))
    first = 1 + len(ins)
    later = first + len(after)
    return pl.pallas_call(
        lambda *refs: kernel(*refs[:first], *refs[later:]),
        out_shape=outs,
        grid_spec=pltpu.PrefetchScalarGridSpec(
            num_scalar_prefetch=1,
            grid=grid,
            in_specs=list(in_specs) + [ANYWHERE] * len(after),
            out_specs=out_specs,
            scratch_shapes=scratch,
        ),
        input_output_aliases=aliases or {},
        compiler_params=pltpu.CompilerParams(
            dimension_semantics=("arbitrary",), vmem_limit_bytes=VMEM
        ),
        cost_estimate=pl.CostEstimate(
            flops=int(flops), bytes_accessed=int(moved), transcendentals=0
        ),
    )(info, *ins, *after)


def by_rows(rows, columns):
    return pl.BlockSpec((rows, columns), lambda i, s: (i, 0))


def full(*shape):
    return pl.BlockSpec(shape, lambda i, s: (0,) * len(shape))


def body(
    tokens,
    segment,
    norm_attn_gain,
    qkv_weight,
    attn_out_weight,
    norm_mlp_gain,
    in_weight,
    out_weight,
    cotangent,
):
    own_rows = norm_attn_gain.shape[0]
    core = lax.axis_index("tensor")
    place = lax.axis_index("dp") if by_exchange(own_rows) else 0
    info = jnp.stack([jnp.int32(place), core.astype(jnp.int32)])
    orders = (relative(own_rows, False), relative(own_rows, True))

    gains = jnp.pad(jnp.stack([norm_attn_gain, norm_mlp_gain], axis=1), ((0, 0), (0, LANES - 2)))
    flat_qkv = qkv_weight.reshape(own_rows, HALF)
    first_pieces = gather_start(jnp.concatenate([flat_qkv, gains], axis=1))
    shard_in = jnp.concatenate(
        [
            in_weight[:, 0, :UNITS],
            in_weight[:, 1, :UNITS],
            in_weight[:, 0, UNITS:],
            in_weight[:, 1, UNITS:],
        ],
        axis=1,
    )
    turned_out = out_weight.T
    blank = jnp.zeros((own_rows, HEAD_DIM), BF16)
    shard_down = jnp.concatenate([attn_out_weight.T, turned_out, blank], axis=1)
    second_shard = jnp.concatenate([shard_in, shard_down], axis=1)
    second_shard, *first_pieces = held_until([second_shard] + first_pieces)
    second_pieces = gather_start(second_shard)

    own_segment = lax.dynamic_slice_in_dim(segment, core * ROWS, ROWS, 0)
    seg_pad = jnp.pad(segment, (WINDOW_HALF, WINDOW_HALF), constant_values=-2)
    span_segment = lax.dynamic_slice_in_dim(seg_pad, core * ROWS, ROWS + 2 * WINDOW_HALF, 0)
    slot = core * ROWS - WINDOW_HALF + jnp.arange(ROWS + 2 * WINDOW_HALF, dtype=jnp.int32)
    position = jnp.where(span_segment >= 0, slot - PAD_BLOCK * span_segment, 0)
    lane = jnp.arange(LANES, dtype=jnp.int32)
    exponent = (lane % 32).astype(F32) * (2.0 / HEAD_DIM)
    angle = position.astype(F32)[:, None] * jnp.power(10000.0, -exponent)[None, :]
    cos_span = jnp.cos(angle)
    sin_span = jnp.sin(angle) * jnp.where((lane & 32) == 0, -1.0, 1.0)[None, :]
    cosine = cos_span[WINDOW_HALF:-WINDOW_HALF]
    sine = sin_span[WINDOW_HALF:-WINDOW_HALF]
    cos_turned, sin_turned = cosine.T, sine.T
    col_seg = span_segment[:, None]
    row_seg = own_segment.reshape(ROWS // LANES, 1, LANES)
    live = (own_segment >= 0).astype(F32)[:, None]

    rows = 384
    steps = ROWS // rows
    first_pieces = held_until(first_pieces, cos_span, sin_span)
    held_a = columns_of(first_pieces, 0, FIRST_CUT)
    held_b = columns_of(first_pieces, FIRST_CUT, HALF + LANES)
    own_a = gather_finish(gather_middle(held_a, False)[0], False)
    own_b = gather_finish(gather_middle(held_b, True)[0], True)
    other_a = [swapped_cores(piece) for piece in own_a]
    other_b = [swapped_cores(piece) for piece in own_b]
    second_pieces = held_until(second_pieces, other_a[-1], other_b[-1])
    held_in, arrived_in = gather_middle(columns_of(second_pieces, 0, HALF), False)
    held_down, arrived_down = gather_middle(columns_of(second_pieces, HALF, HALF + DOWN), True)

    parts = (own_a, other_a, own_b, other_b)
    counts_qkv = tuple(len(part) for part in parts)
    qkv, normed, gain_rows, edge, weight_qkv = call(
        lambda *refs: qkv_kernel(orders, counts_qkv, *refs),
        info,
        (steps,),
        [tokens, cosine, sine] + [piece for part in parts for piece in part],
        [by_rows(rows, WIDTH), by_rows(rows, LANES), by_rows(rows, LANES)]
        + [ANYWHERE] * sum(counts_qkv),
        [
            shape_of((ROWS, 2 * HALF)),
            shape_of((ROWS, WIDTH)),
            shape_of((8, WIDTH), F32),
            shape_of((WINDOW_HALF, 2 * WIDTH)),
            shape_of((WIDTH, 2 * HALF)),
        ],
        [by_rows(rows, 2 * HALF), by_rows(rows, WIDTH), full(8, WIDTH)]
        + [full(WINDOW_HALF, 2 * WIDTH), full(WIDTH, 2 * HALF)],
        [pltpu.VMEM((WIDTH, LANES), BF16), pltpu.SemaphoreType.DMA((2,))],
        2 * ROWS * WIDTH * 2 * HALF,
    )
    edge = swapped_cores(edge)
    held_in, held_down = held_until((held_in, held_down), qkv)
    in_own, down_own = gather_finish(held_in, False), gather_finish(held_down, True)

    blocks = ROWS // LANES
    window_shape = (ROWS + 2 * WINDOW_HALF, 2 * WIDTH)
    turned_shape = (WIDTH, ROWS + 2 * WINDOW_HALF)
    by_block = pl.BlockSpec((1, PAIRS, SPAN, SPAN), lambda i, s: (i, 0, 0, 0))
    att_own, att_other, probs = call(
        attend_kernel,
        info,
        (blocks,),
        [row_seg, col_seg, qkv, qkv, edge],
        [
            pl.BlockSpec((1, 1, LANES), lambda i, s: (i, 0, 0)),
            full(ROWS + 2 * WINDOW_HALF, 1),
            by_rows(LANES, 2 * HALF),
            ANYWHERE,
            ANYWHERE,
        ],
        [
            shape_of((ROWS, THIRD)),
            shape_of((ROWS, THIRD)),
            shape_of((blocks, PAIRS, SPAN, SPAN)),
        ],
        [by_rows(LANES, THIRD), by_rows(LANES, THIRD), by_block],
        [
            pltpu.VMEM(window_shape, BF16),
            pltpu.VMEM(turned_shape, BF16),
            pltpu.SemaphoreType.DMA((5,)),
        ],
        blocks * PAIRS * 2 * 2 * SPAN * SPAN * LANES,
        after=[arrived_in, arrived_down],
    )

    in_own[-1], down_own[-1] = held_until((in_own[-1], down_own[-1]), att_own)
    in_other = [swapped_cores(piece) for piece in in_own]
    down_other = [swapped_cores(piece) for piece in down_own]
    parts = (in_own, in_other, down_own, down_other)
    counts = tuple(len(part) for part in parts)
    (
        layer_out,
        hidden_grad,
        att_grad_own,
        att_grad_other,
        normed_two,
        gated_own,
        gated_other,
        pre_grad_own,
        pre_grad_other,
        hidden_grad_low,
        out_grad,
    ) = call(
        lambda *refs: mlp_kernel(orders, counts, *refs),
        info,
        (steps,),
        [tokens, att_own, att_other, cotangent, live, gain_rows]
        + [piece for part in parts for piece in part],
        [by_rows(rows, WIDTH), by_rows(rows, THIRD), by_rows(rows, THIRD), by_rows(rows, WIDTH)]
        + [by_rows(rows, 1), full(8, WIDTH)]
        + [ANYWHERE] * sum(counts),
        [
            shape_of((ROWS, WIDTH)),
            shape_of((ROWS, WIDTH), F32),
            shape_of((ROWS, THIRD)),
            shape_of((ROWS, THIRD)),
            shape_of((ROWS, WIDTH)),
            shape_of((ROWS, UNITS + LANES)),
            shape_of((ROWS, UNITS + LANES)),
            shape_of((ROWS, HALF)),
            shape_of((ROWS, HALF)),
            shape_of((ROWS, WIDTH)),
            shape_of((ROWS, WIDTH)),
        ],
        [by_rows(rows, WIDTH)] * 2
        + [by_rows(rows, THIRD)] * 2
        + [by_rows(rows, WIDTH)]
        + [by_rows(rows, UNITS + LANES)] * 2
        + [by_rows(rows, HALF)] * 2
        + [by_rows(rows, WIDTH)] * 2,
        [
            pltpu.VMEM((WIDTH, 2 * HALF), BF16),
            pltpu.VMEM((WIDTH, WIDTH), BF16),
            pltpu.VMEM((WIDTH, HALF), BF16),
            pltpu.VMEM((WIDTH, LANES), BF16),
            pltpu.VMEM((WIDTH, LANES), BF16),
            pltpu.SemaphoreType.DMA((5,)),
        ],
        2 * ROWS * WIDTH * (4 * HALF + 2 * HALF + 2 * WIDTH),
    )

    def down_grads(att, gated):
        parts = [weight_grad(hidden_grad_low, att), weight_grad(out_grad, gated)]
        return jnp.concatenate(parts, axis=1)

    send_in = weight_grad(normed_two, pre_grad_other)
    send_down = down_grads(att_other, gated_other)
    keep_in = weight_grad(normed_two, pre_grad_own)
    keep_down = down_grads(att_own, gated_own)
    sum_in, in_back = scatter_start(keep_in, swapped_cores(send_in), own_rows, False)
    sum_down, down_back = scatter_start(keep_down, swapped_cores(send_down), own_rows, True)

    grad_own, grad_other, edge_grad = call(
        attend_back_kernel,
        info,
        (blocks,),
        [qkv, probs, att_grad_own, att_grad_other, cos_span, sin_span]
        + [cos_turned, sin_turned, qkv, edge],
        [by_rows(LANES, 2 * HALF), by_block, by_rows(LANES, THIRD), by_rows(LANES, THIRD)]
        + [full(*cos_span.shape)] * 2
        + [pl.BlockSpec((LANES, LANES), lambda i, s: (0, i))] * 2
        + [ANYWHERE] * 2,
        [shape_of((ROWS, HALF)), shape_of((ROWS, HALF)), shape_of((WINDOW_HALF, 2 * WIDTH))],
        [full(ROWS, HALF), full(ROWS, HALF), full(WINDOW_HALF, 2 * WIDTH)],
        [
            pltpu.VMEM(window_shape, BF16),
            pltpu.VMEM(turned_shape, BF16),
            pltpu.VMEM((window_shape[0], WIDTH), F32),
            pltpu.VMEM((window_shape[0], WIDTH), F32),
            pltpu.SemaphoreType.DMA((5,)),
        ],
        blocks * PAIRS * 4 * 2 * SPAN * SPAN * LANES,
        after=[send_in, send_down, keep_in, keep_down],
    )
    edge_grad = swapped_cores(edge_grad)
    at_edge = lambda i, s: ((1 - s[1]) * (ROWS // WINDOW_HALF - 1), 0)
    grad_own, grad_other = call(
        edge_kernel,
        info,
        (1,),
        [grad_own, grad_other, edge_grad],
        [pl.BlockSpec((WINDOW_HALF, HALF), at_edge)] * 2 + [full(WINDOW_HALF, 2 * WIDTH)],
        [shape_of((ROWS, HALF))] * 2,
        [pl.BlockSpec((WINDOW_HALF, HALF), at_edge)] * 2,
        [],
        0,
        {1: 0, 2: 1},
        [in_back[1], down_back[1]],
    )

    send_a = weight_grad(normed, grad_other[:, :FIRST_CUT])
    send_b = weight_grad(normed, grad_other[:, FIRST_CUT:])
    keep_a = weight_grad(normed, grad_own[:, :FIRST_CUT])
    keep_b = weight_grad(normed, grad_own[:, FIRST_CUT:])
    late_a, late_b = swapped_cores(send_a), swapped_cores(send_b)

    (grad_tokens,) = call(
        input_grad_kernel,
        info,
        (steps,),
        [tokens, grad_own, grad_other, hidden_grad, gain_rows, weight_qkv],
        [by_rows(rows, WIDTH), by_rows(rows, HALF), by_rows(rows, HALF), by_rows(rows, WIDTH)]
        + [full(8, WIDTH), full(WIDTH, 2 * HALF)],
        [shape_of((ROWS, WIDTH), F32)],
        [by_rows(rows, WIDTH)],
        [],
        2 * ROWS * WIDTH * 2 * HALF,
        after=[keep_a, keep_b, late_a, late_b, in_back[2], down_back[2]],
    )
    sum_a, a_back = scatter_start(keep_a, late_a, own_rows, False, grad_tokens)
    sum_b, b_back = scatter_start(keep_b, late_b, own_rows, True, grad_tokens)
    sum_in, sum_down = held_until((sum_in, sum_down), a_back[0], b_back[0])
    owned_early = scatter_finish(sum_in, sum_down)
    owned_in, owned_down = owned_early[:, :HALF], owned_early[:, HALF:]

    flat_grad = scatter_finish(sum_a, sum_b)
    gain_grads = jnp.stack(
        [
            gain_part(flat_qkv, flat_grad, norm_attn_gain),
            gain_part(shard_in, owned_in, norm_mlp_gain),
        ]
    )
    gain_grads = gain_grads + swapped_cores(gain_grads)
    owned_gain_one, owned_gain_two = gain_grads[0], gain_grads[1]
    owned_qkv = flat_grad.reshape(own_rows, 3, THIRD)
    owned_in = jnp.stack(
        [
            jnp.concatenate([owned_in[:, :UNITS], owned_in[:, 2 * UNITS : -64]], axis=1),
            jnp.concatenate([owned_in[:, UNITS : 2 * UNITS], owned_in[:, -64:]], axis=1),
        ],
        axis=1,
    )
    owned_attn = owned_down[:, :THIRD].T
    owned_out = owned_down[:, THIRD : THIRD + UNITS + HEAD_DIM].T
    return (
        layer_out,
        grad_tokens,
        owned_gain_one,
        owned_qkv,
        owned_attn,
        owned_gain_two,
        owned_in,
        owned_out,
    )


def solution(mesh):
    placed = (
        P(("dp", "tensor"), None),
        P("dp"),
        P("dp"),
        P("dp", None, "tensor"),
        P("tensor", "dp"),
        P("dp"),
        P("dp", None, "tensor"),
        P("tensor", "dp"),
        P(("dp", "tensor"), None),
    )
    return jax.shard_map(
        body,
        mesh=mesh,
        in_specs=placed,
        out_specs=(
            P(("dp", "tensor"), None),
            P(("dp", "tensor"), None),
            P("dp"),
            P("dp", None, "tensor"),
            P("tensor", "dp"),
            P("dp"),
            P("dp", None, "tensor"),
            P("tensor", "dp"),
        ),
        check_vma=False,
    )
```

```python
import jax
import jax.numpy as jnp
from jax import lax
from jax.experimental import pallas as pl
from jax.experimental.pallas import tpu as pltpu
from jax.sharding import PartitionSpec as P

HEAD_DIM = 64
WINDOW_HALF = 64
PAD_BLOCK = 128
WIDTH = 768
ROWS = 1152
MORE_ROWS = ROWS + 64
HALF = 1152
LANES = 128
THIRD = 384
PAIRS = 6
SPAN = 2 * LANES
UNITS = 512
FIRST_CUT = 640
DOWN = 384 + UNITS + LANES
VMEM = 58 * 2**20
ANYWHERE = pl.BlockSpec(memory_space=pl.ANY)
F32 = jnp.float32
BF16 = jnp.bfloat16


def steps_of(devices, swapped):
    bits = [1 << i for i in range(devices.bit_length() - 1)]
    near, far = bits[:2], bits[2:]
    return far + (near if swapped else near[::-1])


def exchanged(block, mask):
    devices = lax.axis_size("dp")
    return lax.ppermute(block, "dp", [(i, i ^ mask) for i in range(devices)])


def swapped_cores(block):
    return lax.ppermute(block, "tensor", [(0, 1), (1, 0)])


def by_exchange(own_rows):
    devices = lax.axis_size("dp")
    return own_rows % 16 == 0 and devices & (devices - 1) == 0


def relative(own_rows, swapped):
    if not by_exchange(own_rows):
        return list(range(WIDTH // 48))
    order = [0]
    for mask in steps_of(lax.axis_size("dp"), swapped):
        order = order + [r ^ mask for r in order]
    return order


def held_until(arrays, *gates):
    return lax.optimization_barrier((tuple(arrays), gates))[0]


def gather_start(shard):
    masks = steps_of(lax.axis_size("dp"), False)
    held = shard[None]
    if not by_exchange(shard.shape[0]) or len(masks) <= 3:
        return [held]
    first, second = masks[:2]
    return [held] + [exchanged(held, mask) for mask in (first, second, first ^ second)]


def columns_of(pieces, start, stop):
    return jnp.concatenate([piece[:, :, start:stop] for piece in pieces], axis=0)


def gather_middle(held, swapped, gate=None):
    if by_exchange(held.shape[1]):
        masks = steps_of(lax.axis_size("dp"), swapped)
        for mask in masks[held.shape[0].bit_length() - 1 : -1]:
            arrived = exchanged(held, mask)
            if gate is not None:
                (arrived,) = held_until((arrived,), gate)
            held = jnp.concatenate([held, arrived], axis=0)
    return held


def gather_finish(held, swapped):
    if not by_exchange(held.shape[1]):
        whole = lax.all_gather(held[0], "dp", axis=0, tiled=True)
        return [whole.reshape(WIDTH // 48, 48, held.shape[2])]
    return [held, exchanged(held, steps_of(lax.axis_size("dp"), swapped)[-1])]


def scatter_start(keep, other, own_rows, swapped, first_gates=None):
    arrivals = [other]
    if not by_exchange(own_rows):
        total = keep.astype(F32) + other.astype(F32)
        total = lax.psum_scatter(total, "dp", scatter_dimension=0, tiled=True)
        return total[None], arrivals * 3
    devices = lax.axis_size("dp")
    index = lax.axis_index("dp")
    levels = devices.bit_length() - 1
    masks = steps_of(devices, swapped)
    last = 2 if len(masks) > 3 else 0
    shape = (2,) * levels + (own_rows, keep.shape[1])
    keep, other = keep.reshape(shape), other.reshape(shape)
    for mask in reversed(masks[last:]):
        axis = levels - mask.bit_length()
        bit = (index & mask) // mask
        part = lambda array, which: lax.dynamic_slice_in_dim(array, which, 1, axis).astype(F32)
        sent = (part(keep, 1 - bit) + part(other, 1 - bit)).astype(BF16)
        kept = (part(keep, bit) + part(other, bit)).astype(BF16)
        other = exchanged(sent, mask)
        arrivals.append(other)
        if first_gates is not None and len(arrivals) == 2:
            (other,) = held_until((other,), *first_gates)
        keep = kept
    total = keep.astype(F32) + other.astype(F32)
    return total.reshape(2**last, own_rows, -1), arrivals + [other] * 3


def scatter_finish(*totals):
    if totals[0].shape[0] == 1:
        return jnp.concatenate([total[0] for total in totals], axis=1)
    unit = steps_of(lax.axis_size("dp"), False)[0]
    place = (lax.axis_index("dp") // unit) % 4

    def rows_of(which):
        parts = [lax.dynamic_index_in_dim(total, which, 0, keepdims=False) for total in totals]
        return jnp.concatenate(parts, axis=1)

    arrived = [
        exchanged(rows_of(place ^ j).astype(BF16), unit * j).astype(F32) for j in range(1, 4)
    ]
    return rows_of(place) + (arrived[0] + arrived[1] + arrived[2])


def weight_grad(left, right):
    return lax.dot_general(
        left, right, (((0,), (0,)), ((), ())), preferred_element_type=F32
    ).astype(BF16)


def gain_part(weight, grad, gain):
    return jnp.sum(weight.astype(F32) * grad, axis=1) / gain.astype(F32)


def nt(left, right):
    return lax.dot_general(left, right, (((1,), (1,)), ((), ())), preferred_element_type=F32)


def nn(left, right):
    return jnp.dot(left, right, preferred_element_type=F32)


def start_slots(info, pieces, order, segments, sems):
    slot = 0
    for piece in pieces:
        rows = piece.shape[1]
        for at in range(piece.shape[0]):
            row = pl.multiple_of((info[0] ^ order[slot]) * rows, 16)
            for begin, width, target, column, sem in segments:
                pltpu.make_async_copy(
                    piece.at[at, :, pl.ds(begin, width)],
                    target.at[pl.ds(row, rows), pl.ds(column, width)],
                    sems.at[sem],
                ).start()
            slot += 1


def wait_whole(ref, sem):
    pltpu.make_async_copy(ref, ref, sem).wait()


def fill_window(info, qkv_ref, edge_ref, window, sems):
    core = info[1]
    first = pl.multiple_of(jnp.where(core == 1, 0, WINDOW_HALF + ROWS), 16)
    last = pl.multiple_of(jnp.where(core == 1, WINDOW_HALF + ROWS, 0), 16)
    copies = [
        pltpu.make_async_copy(
            edge_ref.at[:, pl.ds(0, 2 * WIDTH)],
            window.at[pl.ds(first, WINDOW_HALF), :],
            sems.at[4],
        )
    ]
    for part in range(2):
        for half in range(2):
            copies.append(
                pltpu.make_async_copy(
                    qkv_ref.at[:, pl.ds(HALF * half + THIRD * (part + 1), THIRD)],
                    window.at[pl.ds(WINDOW_HALF, ROWS), pl.ds(WIDTH * part + THIRD * half, THIRD)],
                    sems.at[2 * part + half],
                )
            )
    for copy in copies:
        copy.start()
    window[pl.ds(last, WINDOW_HALF), :] = jnp.zeros((WINDOW_HALF, 2 * WIDTH), BF16)
    for copy in copies:
        copy.wait()


def identity():
    row = lax.broadcasted_iota(jnp.int32, (LANES, LANES), 0)
    lane = lax.broadcasted_iota(jnp.int32, (LANES, LANES), 1)
    return jnp.where(row == lane, 1.0, 0.0).astype(BF16)


def turn_rows(unit, window, begin, row, turned_ref):
    for pair in range(PAIRS):
        lanes = slice(LANES * pair, LANES * (pair + 1))
        block = window[pl.ds(row, LANES), begin + LANES * pair : begin + LANES * (pair + 1)]
        turned_ref[lanes, pl.ds(row, LANES)] = nt(unit, block).astype(BF16)


def head_rows(columns):
    return jnp.concatenate([columns[:HEAD_DIM, :LANES], columns[HEAD_DIM:, LANES:]], axis=0)


def normalized(values):
    centred = values - jnp.mean(values, axis=-1, keepdims=True)
    spread = jnp.mean(centred * centred, axis=-1, keepdims=True)
    factor = lax.rsqrt(spread + 1e-05)
    return centred * factor, factor


def norm_backward(grad, unit, factor, gain):
    inner = grad * gain
    mean = jnp.mean(inner, axis=-1, keepdims=True)
    along = jnp.mean(inner * unit, axis=-1, keepdims=True)
    return factor * (inner - mean - unit * along)


def turned(values, cosine, sine):
    lane = lax.broadcasted_iota(jnp.int32, values.shape, 1)
    first = (lane & 32) == 0
    other = jnp.where(first, pltpu.roll(values, 96, 1), pltpu.roll(values, 32, 1))
    return values * cosine + other * sine


def both_heads(block):
    lane = lax.broadcasted_iota(jnp.int32, block.shape, 1)
    first = jnp.where(lane < HEAD_DIM, 1.0, 0.0).astype(block.dtype)
    second = jnp.where(lane < HEAD_DIM, 0.0, 1.0).astype(block.dtype)
    return jnp.concatenate([block * first, block * second], axis=0)


def qkv_kernel(orders, counts, info, x_ref, cos_ref, sin_ref, *refs):
    parts = []
    for count in counts:
        parts.append(refs[:count])
        refs = refs[count:]
    own_a, other_a, own_b, other_b = parts
    qkv_ref, normed_ref, gain_ref, edge_ref, weight_ref, weight, gains, sems = refs
    step = pl.program_id(0)
    rows = x_ref.shape[0]

    @pl.when(step == 0)
    def _():
        rest = HALF - FIRST_CUT
        start_slots(info, own_b, orders[1], [(rest, LANES, gains, 0, 1)], sems)
        for begin, part_a, part_b in ((0, own_a, own_b), (HALF, other_a, other_b)):
            start_slots(info, part_a, orders[0], [(0, FIRST_CUT, weight, begin, 0)], sems)
            start_slots(info, part_b, orders[1], [(0, rest, weight, begin + FIRST_CUT, 0)], sems)
        wait_whole(gains, sems.at[1])
        row = lax.broadcasted_iota(jnp.int32, (16, LANES), 0)
        lane = lax.broadcasted_iota(jnp.int32, (16, LANES), 1)
        pick = jnp.where(row == lane, 1.0, 0.0).astype(BF16)
        gain_ref[...] = nt(pick, gains[...])[:8]
        wait_whole(weight, sems.at[0])
        pltpu.make_async_copy(weight, weight_ref, sems.at[2]).start()

    unit, unused = normalized(x_ref[...].astype(F32))
    normed = (unit * gain_ref[0:1, :]).astype(BF16)
    normed_ref[...] = normed
    cosine, sine = cos_ref[...], sin_ref[...]
    for half in range(2):
        result = nn(normed, weight[:, HALF * half : HALF * (half + 1)])
        for tile in range(9):
            block = result[:, LANES * tile : LANES * (tile + 1)]
            if tile < 6:
                block = turned(block, cosine, sine)
            if tile < 3:
                block = block * (HEAD_DIM**-0.5)
            begin = HALF * half + LANES * tile
            qkv_ref[:, begin : begin + LANES] = block.astype(BF16)

    for core, at_step, begin in ((1, 0, 0), (0, ROWS // rows - 1, rows - WINDOW_HALF)):

        @pl.when((info[1] == core) & (step == at_step))
        def _():
            for part in range(2):
                for half in range(2):
                    source = HALF * half + THIRD * (part + 1)
                    target = WIDTH * part + THIRD * (1 - half)
                    edge_ref[:, target : target + THIRD] = qkv_ref[
                        begin : begin + WINDOW_HALF, source : source + THIRD
                    ]
            edge_ref[:, 2 * WIDTH :] = normed_ref[begin : begin + WINDOW_HALF, :]

    @pl.when(step == ROWS // rows - 1)
    def _():
        pltpu.make_async_copy(weight, weight_ref, sems.at[2]).wait()


def attend_kernel(
    info, row_seg, col_seg, q_ref, qkv_ref, edge_ref, own_ref, other_ref, probs_ref, window, turned_values, sems
):
    step = pl.program_id(0)
    unit = identity()

    @pl.when(step == 0)
    def _():
        fill_window(info, qkv_ref, edge_ref, window, sems)
        turn_rows(unit, window, WIDTH, 0, turned_values)

    start = pl.multiple_of(step * LANES, LANES)
    turn_rows(unit, window, WIDTH, pl.multiple_of(start + LANES, LANES), turned_values)
    key_seg = col_seg[pl.ds(start, SPAN), :]
    key_at = lax.broadcasted_iota(jnp.int32, (SPAN, LANES), 0) - WINDOW_HALF
    query_at = lax.broadcasted_iota(jnp.int32, (SPAN, LANES), 1)
    near = jnp.abs(key_at - query_at) <= WINDOW_HALF
    allowed = (key_seg == row_seg[0]) & near
    bias = jnp.where(allowed, 0.0, -1e30)
    bias = jnp.concatenate([bias, bias], axis=1)

    scores, probs, results = [], [], []
    for pair in range(PAIRS):
        begin = HALF * (pair // 3) + LANES * (pair % 3)
        queries = both_heads(q_ref[:, begin : begin + LANES])
        keys = window[pl.ds(start, SPAN), LANES * pair : LANES * (pair + 1)]
        scores.append(nt(keys, queries) + bias)
    for pair in range(PAIRS):
        weights = jnp.exp(scores[pair] - jnp.max(scores[pair], axis=0, keepdims=True))
        total = jnp.sum(weights, axis=0, keepdims=True)
        probs.append((weights * (1.0 / total)).astype(BF16))
        probs_ref[0, pair] = probs[pair]
    for pair in range(PAIRS):
        values = turned_values[LANES * pair : LANES * (pair + 1), pl.ds(start, SPAN)]
        results.append(head_rows(nn(values, probs[pair])).astype(BF16))
    for pair in range(PAIRS):
        out_ref = own_ref if pair < 3 else other_ref
        out_ref[:, LANES * (pair % 3) : LANES * (pair % 3 + 1)] = nt(unit, results[pair]).astype(
            BF16
        )


def mlp_kernel(orders, counts, info, x_ref, att_own, att_other, cot_ref, live_ref, gain_ref, *refs):
    parts = []
    for count in counts:
        parts.append(refs[:count])
        refs = refs[count:]
    in_own, in_other, down_own, down_other = parts
    (
        out_ref,
        hidden_grad_ref,
        att_grad_own,
        att_grad_other,
        normed_ref,
        gated_own,
        gated_other,
        pre_grad_own,
        pre_grad_other,
        low_grad_ref,
        out_grad_ref,
        w_in,
        w_att,
        w_out,
        tail_own,
        tail_other,
        sems,
    ) = refs
    step = pl.program_id(0)

    @pl.when(step == 0)
    def _():
        for number, (part, tail) in enumerate(((down_own, tail_own), (down_other, tail_other))):
            segments = [
                (0, THIRD, w_att, THIRD * number, 1),
                (THIRD, UNITS, w_out, UNITS * number, 2),
                (THIRD + UNITS, LANES, tail, 0, 3 + number),
            ]
            start_slots(info, part, orders[1], segments, sems)
        for number, part in enumerate((in_own, in_other)):
            start_slots(info, part, orders[0], [(0, HALF, w_in, HALF * number, 0)], sems)
        wait_whole(w_att, sems.at[1])
        wait_whole(w_out.at[:, pl.ds(0, 2 * UNITS)], sems.at[2])
        wait_whole(tail_own, sems.at[3])
        wait_whole(tail_other, sems.at[4])
        other = pltpu.roll(tail_other[...].astype(F32), HEAD_DIM, 1).astype(BF16)
        w_out[:, 2 * UNITS :] = tail_own[...] + other
        wait_whole(w_in, sems.at[0])

    gain = gain_ref[1:2, :]
    hidden = (
        x_ref[...].astype(F32)
        + nt(att_own[...], w_att[:, :THIRD])
        + nt(att_other[...], w_att[:, THIRD:])
    )
    unit, factor = normalized(hidden)
    normed = (unit * gain).astype(BF16)
    normed_ref[...] = normed
    out_grad = cot_ref[...].astype(F32) * live_ref[...]
    out_grad_low = out_grad.astype(BF16)
    out_grad_ref[...] = out_grad_low
    pre = [nn(normed, w_in[:, HALF * half : HALF * (half + 1)]) for half in range(2)]
    tails = [part[:, 2 * UNITS :] for part in pre]
    lane = lax.broadcasted_iota(jnp.int32, tails[0].shape, 1)
    low = lane < HEAD_DIM
    gates = [part[:, :UNITS] for part in pre]
    gates.append(jnp.where(low, tails[0], pltpu.roll(tails[1], 64, 1)))
    ups = [part[:, UNITS : 2 * UNITS] for part in pre]
    ups.append(jnp.where(low, pltpu.roll(tails[0], 64, 1), tails[1]))
    pre_grads = (pre_grad_own, pre_grad_other)
    for part, (gate, up) in enumerate(zip(gates, ups)):
        columns = slice(UNITS * part, UNITS * part + gate.shape[1])
        share = 0.5 + 0.5 * lax.erf(gate * (0.5**0.5))
        slope = share + gate * (jnp.exp(-0.5 * gate * gate) * 0.3989422804014327)
        curve = gate * share
        gated = curve * up
        grad = nn(out_grad_low, w_out[:, columns])
        gate_grad = grad * up * slope
        up_grad = grad * curve
        if part < 2:
            (gated_own, gated_other)[part][:, :UNITS] = gated.astype(BF16)
            pre_grads[part][:, :UNITS] = gate_grad.astype(BF16)
            pre_grads[part][:, UNITS : 2 * UNITS] = up_grad.astype(BF16)
        else:
            gated_own[:, UNITS:] = gated.astype(BF16)
            gated_other[:, UNITS:] = pltpu.roll(gated, HEAD_DIM, 1).astype(BF16)
            own = jnp.where(low, gate_grad, pltpu.roll(up_grad, 64, 1))
            other = jnp.where(low, pltpu.roll(gate_grad, 64, 1), up_grad)
            pre_grad_own[:, 2 * UNITS :] = own.astype(BF16)
            pre_grad_other[:, 2 * UNITS :] = other.astype(BF16)
    product = (
        nt(gated_own[:, :UNITS], w_out[:, :UNITS])
        + nt(gated_other[:, :UNITS], w_out[:, UNITS : 2 * UNITS])
        + nt(gated_own[:, UNITS:], w_out[:, 2 * UNITS :])
    )
    out_ref[...] = (hidden + product).astype(BF16)
    normed_grad = nt(pre_grad_own[...], w_in[:, :HALF]) + nt(pre_grad_other[...], w_in[:, HALF:])
    hidden_grad = out_grad + norm_backward(normed_grad, unit, factor, gain)
    hidden_grad_ref[...] = hidden_grad
    hidden_grad_low = hidden_grad.astype(BF16)
    low_grad_ref[...] = hidden_grad_low
    att_grad_own[...] = nn(hidden_grad_low, w_att[:, :THIRD]).astype(BF16)
    att_grad_other[...] = nn(hidden_grad_low, w_att[:, THIRD:]).astype(BF16)


def attend_back_kernel(
    info,
    q_ref,
    probs_ref,
    grad_own,
    grad_other,
    cos_ref,
    sin_ref,
    cos_turned,
    sin_turned,
    qkv_ref,
    edge_ref,
    out_own,
    out_other,
    edge_out_ref,
    window,
    turned_keys,
    key_grad,
    value_grad,
    sems,
):
    step = pl.program_id(0)
    unit = identity()

    @pl.when(step == 0)
    def _():
        fill_window(info, qkv_ref, edge_ref, window, sems)
        turn_rows(unit, window, 0, 0, turned_keys)
        key_grad[...] = jnp.zeros_like(key_grad)
        value_grad[...] = jnp.zeros_like(value_grad)

    start = pl.multiple_of(step * LANES, LANES)
    span = pl.ds(start, SPAN)
    turn_rows(unit, window, 0, pl.multiple_of(start + LANES, LANES), turned_keys)
    cosine, sine = cos_turned[...], sin_turned[...]

    all_lanes = [slice(LANES * pair, LANES * (pair + 1)) for pair in range(PAIRS)]
    grads, probs_grads, score_grads, query_grads = [], [], [], []
    for pair, lanes in enumerate(all_lanes):
        grad_ref = grad_own if pair < 3 else grad_other
        grads.append(both_heads(grad_ref[:, LANES * (pair % 3) : LANES * (pair % 3 + 1)]))
        values = window[span, WIDTH + LANES * pair : WIDTH + LANES * (pair + 1)]
        probs_grads.append(nt(values, grads[pair]))
    for pair, lanes in enumerate(all_lanes):
        value_grad[span, lanes] += nn(probs_ref[0, pair], grads[pair])
    for pair in range(PAIRS):
        probs = probs_ref[0, pair].astype(F32)
        weighted = probs_grads[pair] * probs
        delta = jnp.sum(weighted, axis=0, keepdims=True)
        score_grads.append((weighted - probs * delta).astype(BF16))
    for pair, lanes in enumerate(all_lanes):
        query_grads.append(head_rows(nn(turned_keys[lanes, span], score_grads[pair])))
    for pair, lanes in enumerate(all_lanes):
        begin = HALF * (pair // 3) + LANES * (pair % 3)
        queries = both_heads(q_ref[:, begin : begin + LANES])
        key_grad[span, lanes] += nn(score_grads[pair], queries)
    for pair in range(PAIRS):
        grad = query_grads[pair] * (HEAD_DIM**-0.5)
        other = jnp.concatenate([grad[32:64], grad[:32], grad[96:], grad[64:96]], axis=0)
        query_grads[pair] = (grad * cosine - other * sine).astype(BF16)
    for pair in range(PAIRS):
        out_ref = out_own if pair < 3 else out_other
        place = slice(LANES * (pair % 3), LANES * (pair % 3 + 1))
        out_ref[pl.ds(start, LANES), place] = nt(unit, query_grads[pair]).astype(BF16)

    @pl.when(step == ROWS // LANES - 1)
    def _():
        inside = slice(WINDOW_HALF, WINDOW_HALF + ROWS)
        row = pl.multiple_of(jnp.where(info[1] == 1, 0, WINDOW_HALF + ROWS), 16)
        edge_rows = pl.ds(row, WINDOW_HALF)
        for pair in range(PAIRS):
            out_ref = out_own if pair < 3 else out_other
            lanes = slice(LANES * pair, LANES * (pair + 1))
            begin = LANES * (pair % 3)
            target = (LANES * pair + THIRD) % WIDTH
            keys_at = slice(THIRD + begin, THIRD + begin + LANES)
            values_at = slice(2 * THIRD + begin, 2 * THIRD + begin + LANES)
            out_ref[:ROWS, keys_at] = turned(
                key_grad[inside, lanes], cos_ref[inside, :], -sin_ref[inside, :]
            ).astype(BF16)
            out_ref[:ROWS, values_at] = value_grad[inside, lanes].astype(BF16)
            edge_keys = turned(
                key_grad[edge_rows, lanes], cos_ref[edge_rows, :], -sin_ref[edge_rows, :]
            ).astype(BF16)
            edge_values = value_grad[edge_rows, lanes].astype(BF16)
            edge_out_ref[:, target : target + LANES] = edge_keys
            edge_out_ref[:, WIDTH + target : WIDTH + target + LANES] = edge_values
            out_ref[ROWS:, begin : begin + LANES] = jnp.zeros((WINDOW_HALF, LANES), BF16)
            out_ref[ROWS:, keys_at] = edge_keys
            out_ref[ROWS:, values_at] = edge_values


def input_grad_kernel(
    info, x_ref, own_ref, other_ref, edge_ref, hidden_ref, gain_ref, weight, out_ref, fixed
):
    rows = x_ref.shape[0]
    step = pl.program_id(0)
    grad = None
    for half, grad_ref in enumerate((own_ref, other_ref)):
        fixed[...] = grad_ref[...]
        for core, at_step, begin in ((1, 0, 0), (0, ROWS // rows - 1, rows - WINDOW_HALF)):

            @pl.when((info[1] == core) & (step == at_step))
            def _():
                at = slice(begin, begin + WINDOW_HALF)
                for part in range(2):
                    to = slice(THIRD * (part + 1), THIRD * (part + 2))
                    source = WIDTH * part + THIRD * half
                    add = edge_ref[:, source : source + THIRD].astype(F32)
                    fixed[at, to] = (fixed[at, to].astype(F32) + add).astype(BF16)

        part = nt(fixed[...], weight[:, HALF * half : HALF * (half + 1)])
        grad = part if grad is None else grad + part
    unit, factor = normalized(x_ref[...].astype(F32))
    out_ref[...] = hidden_ref[...] + norm_backward(grad, unit, factor, gain_ref[0:1, :])


def shape_of(shape, dtype=BF16):
    return jax.ShapeDtypeStruct(shape, dtype)


def call(
    kernel, info, grid, ins, in_specs, outs, out_specs, scratch, flops, aliases=None, after=()
):
    moved = sum(a.size * a.dtype.itemsize for a in list(ins) + list(outs))
    first = 1 + len(ins)
    later = first + len(after)
    return pl.pallas_call(
        lambda *refs: kernel(*refs[:first], *refs[later:]),
        out_shape=outs,
        grid_spec=pltpu.PrefetchScalarGridSpec(
            num_scalar_prefetch=1,
            grid=grid,
            in_specs=list(in_specs) + [ANYWHERE] * len(after),
            out_specs=out_specs,
            scratch_shapes=scratch,
        ),
        input_output_aliases=aliases or {},
        compiler_params=pltpu.CompilerParams(
            dimension_semantics=("arbitrary",), vmem_limit_bytes=VMEM
        ),
        cost_estimate=pl.CostEstimate(
            flops=int(flops), bytes_accessed=int(moved), transcendentals=0
        ),
    )(info, *ins, *after)


def by_rows(rows, columns):
    return pl.BlockSpec((rows, columns), lambda i, s: (i, 0))


def full(*shape):
    return pl.BlockSpec(shape, lambda i, s: (0,) * len(shape))


def body(
    tokens,
    segment,
    norm_attn_gain,
    qkv_weight,
    attn_out_weight,
    norm_mlp_gain,
    in_weight,
    out_weight,
    cotangent,
):
    own_rows = norm_attn_gain.shape[0]
    core = lax.axis_index("tensor")
    place = lax.axis_index("dp") if by_exchange(own_rows) else 0
    info = jnp.stack([jnp.int32(place), core.astype(jnp.int32)])
    orders = (relative(own_rows, False), relative(own_rows, True))

    gains = jnp.pad(jnp.stack([norm_attn_gain, norm_mlp_gain], axis=1), ((0, 0), (0, LANES - 2)))
    flat_qkv = qkv_weight.reshape(own_rows, HALF)
    first_pieces = gather_start(jnp.concatenate([flat_qkv, gains], axis=1))
    shard_in = jnp.concatenate(
        [
            in_weight[:, 0, :UNITS],
            in_weight[:, 1, :UNITS],
            in_weight[:, 0, UNITS:],
            in_weight[:, 1, UNITS:],
        ],
        axis=1,
    )
    turned_out = out_weight.T
    blank = jnp.zeros((own_rows, HEAD_DIM), BF16)
    shard_down = jnp.concatenate([attn_out_weight.T, turned_out, blank], axis=1)
    second_shard = jnp.concatenate([shard_in, shard_down], axis=1)
    second_shard, *first_pieces = held_until([second_shard] + first_pieces)
    second_pieces = gather_start(second_shard)

    own_segment = lax.dynamic_slice_in_dim(segment, core * ROWS, ROWS, 0)
    seg_pad = jnp.pad(segment, (WINDOW_HALF, WINDOW_HALF), constant_values=-2)
    span_segment = lax.dynamic_slice_in_dim(seg_pad, core * ROWS, ROWS + 2 * WINDOW_HALF, 0)
    slot = core * ROWS - WINDOW_HALF + jnp.arange(ROWS + 2 * WINDOW_HALF, dtype=jnp.int32)
    position = jnp.where(span_segment >= 0, slot - PAD_BLOCK * span_segment, 0)
    lane = jnp.arange(LANES, dtype=jnp.int32)
    exponent = (lane % 32).astype(F32) * (2.0 / HEAD_DIM)
    angle = position.astype(F32)[:, None] * jnp.power(10000.0, -exponent)[None, :]
    cos_span = jnp.cos(angle)
    sin_span = jnp.sin(angle) * jnp.where((lane & 32) == 0, -1.0, 1.0)[None, :]
    cosine = cos_span[WINDOW_HALF:-WINDOW_HALF]
    sine = sin_span[WINDOW_HALF:-WINDOW_HALF]
    cos_turned, sin_turned = cosine.T, sine.T
    col_seg = span_segment[:, None]
    row_seg = own_segment.reshape(ROWS // LANES, 1, LANES)
    live = (own_segment >= 0).astype(F32)[:, None]

    rows = 384
    steps = ROWS // rows
    first_pieces = held_until(first_pieces, cos_span, sin_span)
    held_a = columns_of(first_pieces, 0, FIRST_CUT)
    held_b = columns_of(first_pieces, FIRST_CUT, HALF + LANES)
    own_a = gather_finish(gather_middle(held_a, False), False)
    own_b = gather_finish(gather_middle(held_b, True), True)
    second_pieces = held_until(second_pieces, own_a[-1], own_b[-1])
    own_a, own_b = [jnp.concatenate(own_a, axis=0)], [jnp.concatenate(own_b, axis=0)]
    other_a, other_b = [swapped_cores(own_a[0])], [swapped_cores(own_b[0])]

    parts = (own_a, other_a, own_b, other_b)
    counts_qkv = tuple(len(part) for part in parts)
    qkv, normed, gain_rows, edge, weight_qkv = call(
        lambda *refs: qkv_kernel(orders, counts_qkv, *refs),
        info,
        (steps,),
        [tokens, cosine, sine] + [piece for part in parts for piece in part],
        [by_rows(rows, WIDTH), by_rows(rows, LANES), by_rows(rows, LANES)]
        + [ANYWHERE] * sum(counts_qkv),
        [
            shape_of((ROWS, 2 * HALF)),
            shape_of((MORE_ROWS, WIDTH)),
            shape_of((8, WIDTH), F32),
            shape_of((WINDOW_HALF, 3 * WIDTH)),
            shape_of((WIDTH, 2 * HALF)),
        ],
        [by_rows(rows, 2 * HALF), by_rows(rows, WIDTH), full(8, WIDTH)]
        + [full(WINDOW_HALF, 3 * WIDTH), ANYWHERE],
        [
            pltpu.VMEM((WIDTH, 2 * HALF), BF16),
            pltpu.VMEM((WIDTH, LANES), BF16),
            pltpu.SemaphoreType.DMA((3,)),
        ],
        2 * ROWS * WIDTH * 2 * HALF,
    )
    edge = swapped_cores(edge)
    normed = lax.dynamic_update_slice(normed, edge[:, 2 * WIDTH :], (ROWS, 0))
    held_in = gather_middle(columns_of(second_pieces, 0, HALF), False, qkv)
    held_down = gather_middle(columns_of(second_pieces, HALF, HALF + DOWN), True, qkv)
    in_own, down_own = gather_finish(held_in, False), gather_finish(held_down, True)

    blocks = ROWS // LANES
    window_shape = (ROWS + 2 * WINDOW_HALF, 2 * WIDTH)
    turned_shape = (WIDTH, ROWS + 2 * WINDOW_HALF)
    by_block = pl.BlockSpec((1, PAIRS, SPAN, SPAN), lambda i, s: (i, 0, 0, 0))
    att_own, att_other, probs = call(
        attend_kernel,
        info,
        (blocks,),
        [row_seg, col_seg, qkv, qkv, edge],
        [
            pl.BlockSpec((1, 1, LANES), lambda i, s: (i, 0, 0)),
            full(ROWS + 2 * WINDOW_HALF, 1),
            by_rows(LANES, 2 * HALF),
            ANYWHERE,
            ANYWHERE,
        ],
        [
            shape_of((ROWS, THIRD)),
            shape_of((ROWS, THIRD)),
            shape_of((blocks, PAIRS, SPAN, SPAN)),
        ],
        [by_rows(LANES, THIRD), by_rows(LANES, THIRD), by_block],
        [
            pltpu.VMEM(window_shape, BF16),
            pltpu.VMEM(turned_shape, BF16),
            pltpu.SemaphoreType.DMA((5,)),
        ],
        blocks * PAIRS * 2 * 2 * SPAN * SPAN * LANES,
        after=[held_in, held_down],
    )

    in_own[-1], down_own[-1] = held_until((in_own[-1], down_own[-1]), att_own)
    in_other = [swapped_cores(piece) for piece in in_own]
    down_other = [swapped_cores(piece) for piece in down_own]
    parts = (in_own, in_other, down_own, down_other)
    counts = tuple(len(part) for part in parts)
    (
        layer_out,
        hidden_grad,
        att_grad_own,
        att_grad_other,
        normed_two,
        gated_own,
        gated_other,
        pre_grad_own,
        pre_grad_other,
        hidden_grad_low,
        out_grad,
    ) = call(
        lambda *refs: mlp_kernel(orders, counts, *refs),
        info,
        (steps,),
        [tokens, att_own, att_other, cotangent, live, gain_rows]
        + [piece for part in parts for piece in part],
        [by_rows(rows, WIDTH), by_rows(rows, THIRD), by_rows(rows, THIRD), by_rows(rows, WIDTH)]
        + [by_rows(rows, 1), full(8, WIDTH)]
        + [ANYWHERE] * sum(counts),
        [
            shape_of((ROWS, WIDTH)),
            shape_of((ROWS, WIDTH), F32),
            shape_of((ROWS, THIRD)),
            shape_of((ROWS, THIRD)),
            shape_of((ROWS, WIDTH)),
            shape_of((ROWS, UNITS + LANES)),
            shape_of((ROWS, UNITS + LANES)),
            shape_of((ROWS, HALF)),
            shape_of((ROWS, HALF)),
            shape_of((ROWS, WIDTH)),
            shape_of((ROWS, WIDTH)),
        ],
        [by_rows(rows, WIDTH)] * 2
        + [by_rows(rows, THIRD)] * 2
        + [by_rows(rows, WIDTH)]
        + [by_rows(rows, UNITS + LANES)] * 2
        + [by_rows(rows, HALF)] * 2
        + [by_rows(rows, WIDTH)] * 2,
        [
            pltpu.VMEM((WIDTH, 2 * HALF), BF16),
            pltpu.VMEM((WIDTH, WIDTH), BF16),
            pltpu.VMEM((WIDTH, HALF), BF16),
            pltpu.VMEM((WIDTH, LANES), BF16),
            pltpu.VMEM((WIDTH, LANES), BF16),
            pltpu.SemaphoreType.DMA((5,)),
        ],
        2 * ROWS * WIDTH * (4 * HALF + 2 * HALF + 2 * WIDTH),
    )

    def down_grads(att, gated):
        parts = [weight_grad(hidden_grad_low, att), weight_grad(out_grad, gated)]
        return jnp.concatenate(parts, axis=1)

    send_in = weight_grad(normed_two, pre_grad_other)
    send_down = down_grads(att_other, gated_other)
    keep_in = weight_grad(normed_two, pre_grad_own)
    keep_down = down_grads(att_own, gated_own)
    sum_in, in_back = scatter_start(keep_in, swapped_cores(send_in), own_rows, False)
    sum_down, down_back = scatter_start(keep_down, swapped_cores(send_down), own_rows, True)

    grad_own, grad_other, edge_grad = call(
        attend_back_kernel,
        info,
        (blocks,),
        [qkv, probs, att_grad_own, att_grad_other, cos_span, sin_span]
        + [cos_turned, sin_turned, qkv, edge],
        [by_rows(LANES, 2 * HALF), by_block, by_rows(LANES, THIRD), by_rows(LANES, THIRD)]
        + [full(*cos_span.shape)] * 2
        + [pl.BlockSpec((LANES, LANES), lambda i, s: (0, i))] * 2
        + [ANYWHERE] * 2,
        [shape_of((MORE_ROWS, HALF))] * 2 + [shape_of((WINDOW_HALF, 2 * WIDTH))],
        [full(MORE_ROWS, HALF)] * 2 + [full(WINDOW_HALF, 2 * WIDTH)],
        [
            pltpu.VMEM(window_shape, BF16),
            pltpu.VMEM(turned_shape, BF16),
            pltpu.VMEM((window_shape[0], WIDTH), F32),
            pltpu.VMEM((window_shape[0], WIDTH), F32),
            pltpu.SemaphoreType.DMA((5,)),
        ],
        blocks * PAIRS * 4 * 2 * SPAN * SPAN * LANES,
        after=[keep_in, keep_down, in_back[0], down_back[0]],
    )
    edge_grad = swapped_cores(edge_grad)

    send_a = weight_grad(normed, grad_other[:, :FIRST_CUT])
    send_b = weight_grad(normed, grad_other[:, FIRST_CUT:])
    keep_a = weight_grad(normed, grad_own[:, :FIRST_CUT])
    keep_b = weight_grad(normed, grad_own[:, FIRST_CUT:])
    late_a, late_b = swapped_cores(send_a), swapped_cores(send_b)

    (grad_tokens,) = call(
        input_grad_kernel,
        info,
        (steps,),
        [tokens, grad_own, grad_other, edge_grad, hidden_grad, gain_rows, weight_qkv],
        [by_rows(rows, WIDTH), by_rows(rows, HALF), by_rows(rows, HALF)]
        + [full(WINDOW_HALF, 2 * WIDTH), by_rows(rows, WIDTH)]
        + [full(8, WIDTH), full(WIDTH, 2 * HALF)],
        [shape_of((ROWS, WIDTH), F32)],
        [by_rows(rows, WIDTH)],
        [pltpu.VMEM((rows, HALF), BF16)],
        2 * ROWS * WIDTH * 2 * HALF,
        after=[keep_a, keep_b, late_a, late_b, in_back[2], down_back[2]],
    )
    sum_in, sum_down = held_until((sum_in, sum_down), late_a, late_b)
    owned_early = scatter_finish(sum_in, sum_down)
    gates = (grad_tokens, owned_early)
    sum_a, unused = scatter_start(keep_a, late_a, own_rows, False, gates)
    sum_b, unused = scatter_start(keep_b, late_b, own_rows, True, gates)
    owned_in, owned_down = owned_early[:, :HALF], owned_early[:, HALF:]

    flat_grad = scatter_finish(sum_a, sum_b)
    gain_grads = jnp.stack(
        [
            gain_part(flat_qkv, flat_grad, norm_attn_gain),
            gain_part(shard_in, owned_in, norm_mlp_gain),
        ]
    )
    gain_grads = gain_grads + swapped_cores(gain_grads)
    owned_gain_one, owned_gain_two = gain_grads[0], gain_grads[1]
    owned_qkv = flat_grad.reshape(own_rows, 3, THIRD)
    owned_in = jnp.stack(
        [
            jnp.concatenate([owned_in[:, :UNITS], owned_in[:, 2 * UNITS : -64]], axis=1),
            jnp.concatenate([owned_in[:, UNITS : 2 * UNITS], owned_in[:, -64:]], axis=1),
        ],
        axis=1,
    )
    owned_attn = owned_down[:, :THIRD].T
    owned_out = owned_down[:, THIRD : THIRD + UNITS + HEAD_DIM].T
    return (
        layer_out,
        grad_tokens,
        owned_gain_one,
        owned_qkv,
        owned_attn,
        owned_gain_two,
        owned_in,
        owned_out,
    )


def solution(mesh):
    placed = (
        P(("dp", "tensor"), None),
        P("dp"),
        P("dp"),
        P("dp", None, "tensor"),
        P("tensor", "dp"),
        P("dp"),
        P("dp", None, "tensor"),
        P("tensor", "dp"),
        P(("dp", "tensor"), None),
    )
    return jax.shard_map(
        body,
        mesh=mesh,
        in_specs=placed,
        out_specs=(
            P(("dp", "tensor"), None),
            P(("dp", "tensor"), None),
            P("dp"),
            P("dp", None, "tensor"),
            P("tensor", "dp"),
            P("dp"),
            P("dp", None, "tensor"),
            P("tensor", "dp"),
        ),
        check_vma=False,
    )
```

```python
import jax
import jax.numpy as jnp
from jax import lax
from jax.experimental import pallas as pl
from jax.experimental.pallas import tpu as pltpu
from jax.sharding import PartitionSpec as P

HEAD_DIM = 64
WINDOW_HALF = 64
PAD_BLOCK = 128
WIDTH = 768
ROWS = 1152
MORE_ROWS = ROWS + 64
HALF = 1152
LANES = 128
THIRD = 384
PAIRS = 6
SPAN = 2 * LANES
UNITS = 512
FIRST_CUT = 640
DOWN = 384 + UNITS + LANES
VMEM = 58 * 2**20
ANYWHERE = pl.BlockSpec(memory_space=pl.ANY)
F32 = jnp.float32
BF16 = jnp.bfloat16


def steps_of(devices, swapped):
    bits = [1 << i for i in range(devices.bit_length() - 1)]
    near, far = bits[:2], bits[2:]
    return far + (near if swapped else near[::-1])


def exchanged(block, mask):
    devices = lax.axis_size("dp")
    return lax.ppermute(block, "dp", [(i, i ^ mask) for i in range(devices)])


def swapped_cores(block):
    return lax.ppermute(block, "tensor", [(0, 1), (1, 0)])


def by_exchange(own_rows):
    devices = lax.axis_size("dp")
    return own_rows % 16 == 0 and devices & (devices - 1) == 0


def relative(own_rows, swapped):
    if not by_exchange(own_rows):
        return list(range(WIDTH // 48))
    order = [0]
    for mask in steps_of(lax.axis_size("dp"), swapped):
        order = order + [r ^ mask for r in order]
    return order


def held_until(arrays, *gates):
    return lax.optimization_barrier((tuple(arrays), gates))[0]


def gather_start(shard):
    masks = steps_of(lax.axis_size("dp"), False)
    held = shard[None]
    if not by_exchange(shard.shape[0]) or len(masks) <= 3:
        return [held]
    first, second = masks[:2]
    return [held] + [exchanged(held, mask) for mask in (first, second, first ^ second)]


def joined(pieces):
    return lax.optimization_barrier(jnp.concatenate(pieces, axis=0))


def gather_middle(held, swapped, gate=None):
    if by_exchange(held.shape[1]):
        masks = steps_of(lax.axis_size("dp"), swapped)
        for mask in masks[held.shape[0].bit_length() - 1 : -1]:
            arrived = exchanged(held, mask)
            if gate is not None:
                (arrived,) = held_until((arrived,), gate)
            held = jnp.concatenate([held, arrived], axis=0)
    return held


def gather_finish(held, swapped):
    if not by_exchange(held.shape[1]):
        whole = lax.all_gather(held[0], "dp", axis=0, tiled=True)
        return [whole.reshape(WIDTH // 48, 48, held.shape[2])]
    return [held, exchanged(held, steps_of(lax.axis_size("dp"), swapped)[-1])]


def scatter_start(keep, other, own_rows, swapped, first_gates=None):
    arrivals = [other]
    if not by_exchange(own_rows):
        total = keep.astype(F32) + other.astype(F32)
        total = lax.psum_scatter(total, "dp", scatter_dimension=0, tiled=True)
        return total[None], arrivals * 3
    devices = lax.axis_size("dp")
    index = lax.axis_index("dp")
    levels = devices.bit_length() - 1
    masks = steps_of(devices, swapped)
    last = 2 if len(masks) > 3 else 0
    shape = (2,) * levels + (own_rows, keep.shape[1])
    keep, other = keep.reshape(shape), other.reshape(shape)
    for mask in reversed(masks[last:]):
        axis = levels - mask.bit_length()
        bit = (index & mask) // mask
        part = lambda array, which: lax.dynamic_slice_in_dim(array, which, 1, axis).astype(F32)
        sent = (part(keep, 1 - bit) + part(other, 1 - bit)).astype(BF16)
        kept = (part(keep, bit) + part(other, bit)).astype(BF16)
        other = exchanged(sent, mask)
        arrivals.append(other)
        if first_gates is not None and len(arrivals) == 2:
            (other,) = held_until((other,), *first_gates)
        keep = kept
    total = keep.astype(F32) + other.astype(F32)
    return total.reshape(2**last, own_rows, -1), arrivals + [other] * 3


def scatter_finish(*totals):
    if totals[0].shape[0] == 1:
        return jnp.concatenate([total[0] for total in totals], axis=1)
    unit = steps_of(lax.axis_size("dp"), False)[0]
    place = (lax.axis_index("dp") // unit) % 4

    def rows_of(which):
        parts = [lax.dynamic_index_in_dim(total, which, 0, keepdims=False) for total in totals]
        return jnp.concatenate(parts, axis=1)

    arrived = [
        exchanged(rows_of(place ^ j).astype(BF16), unit * j).astype(F32) for j in range(1, 4)
    ]
    return rows_of(place) + (arrived[0] + arrived[1] + arrived[2])


def weight_grad(left, right):
    return lax.dot_general(
        left, right, (((0,), (0,)), ((), ())), preferred_element_type=F32
    ).astype(BF16)


def gain_part(weight, grad, gain):
    return jnp.sum(weight.astype(F32) * grad, axis=1) / gain.astype(F32)


def nt(left, right):
    return lax.dot_general(left, right, (((1,), (1,)), ((), ())), preferred_element_type=F32)


def nn(left, right):
    return jnp.dot(left, right, preferred_element_type=F32)


def start_slots(info, pieces, order, segments, sems):
    slot = 0
    for piece in pieces:
        rows = piece.shape[1]
        for at in range(piece.shape[0]):
            row = pl.multiple_of((info[0] ^ order[slot]) * rows, 16)
            for begin, width, target, column, sem in segments:
                pltpu.make_async_copy(
                    piece.at[at, :, pl.ds(begin, width)],
                    target.at[pl.ds(row, rows), pl.ds(column, width)],
                    sems.at[sem],
                ).start()
            slot += 1


def wait_whole(ref, sem):
    pltpu.make_async_copy(ref, ref, sem).wait()


def fill_window(info, qkv_ref, edge_ref, window, sems):
    core = info[1]
    first = pl.multiple_of(jnp.where(core == 1, 0, WINDOW_HALF + ROWS), 16)
    last = pl.multiple_of(jnp.where(core == 1, WINDOW_HALF + ROWS, 0), 16)
    copies = [
        pltpu.make_async_copy(
            edge_ref.at[:, pl.ds(0, 2 * WIDTH)],
            window.at[pl.ds(first, WINDOW_HALF), :],
            sems.at[4],
        )
    ]
    for part in range(2):
        for half in range(2):
            copies.append(
                pltpu.make_async_copy(
                    qkv_ref.at[:, pl.ds(HALF * half + THIRD * (part + 1), THIRD)],
                    window.at[pl.ds(WINDOW_HALF, ROWS), pl.ds(WIDTH * part + THIRD * half, THIRD)],
                    sems.at[2 * part + half],
                )
            )
    for copy in copies:
        copy.start()
    window[pl.ds(last, WINDOW_HALF), :] = jnp.zeros((WINDOW_HALF, 2 * WIDTH), BF16)
    for copy in copies:
        copy.wait()


def identity():
    row = lax.broadcasted_iota(jnp.int32, (LANES, LANES), 0)
    lane = lax.broadcasted_iota(jnp.int32, (LANES, LANES), 1)
    return jnp.where(row == lane, 1.0, 0.0).astype(BF16)


def turn_rows(unit, window, begin, row, turned_ref):
    for pair in range(PAIRS):
        lanes = slice(LANES * pair, LANES * (pair + 1))
        block = window[pl.ds(row, LANES), begin + LANES * pair : begin + LANES * (pair + 1)]
        turned_ref[lanes, pl.ds(row, LANES)] = nt(unit, block).astype(BF16)


def head_rows(columns):
    return jnp.concatenate([columns[:HEAD_DIM, :LANES], columns[HEAD_DIM:, LANES:]], axis=0)


def normalized(values):
    centred = values - jnp.mean(values, axis=-1, keepdims=True)
    spread = jnp.mean(centred * centred, axis=-1, keepdims=True)
    factor = lax.rsqrt(spread + 1e-05)
    return centred * factor, factor


def norm_backward(grad, unit, factor, gain):
    inner = grad * gain
    mean = jnp.mean(inner, axis=-1, keepdims=True)
    along = jnp.mean(inner * unit, axis=-1, keepdims=True)
    return factor * (inner - mean - unit * along)


def turned(values, cosine, sine):
    lane = lax.broadcasted_iota(jnp.int32, values.shape, 1)
    first = (lane & 32) == 0
    other = jnp.where(first, pltpu.roll(values, 96, 1), pltpu.roll(values, 32, 1))
    return values * cosine + other * sine


def both_heads(block):
    lane = lax.broadcasted_iota(jnp.int32, block.shape, 1)
    first = jnp.where(lane < HEAD_DIM, 1.0, 0.0).astype(block.dtype)
    second = jnp.where(lane < HEAD_DIM, 0.0, 1.0).astype(block.dtype)
    return jnp.concatenate([block * first, block * second], axis=0)


def qkv_kernel(orders, counts, info, x_ref, cos_ref, sin_ref, *refs):
    parts = []
    for count in counts:
        parts.append(refs[:count])
        refs = refs[count:]
    own_a, other_a, own_b, other_b = parts
    qkv_ref, normed_ref, gain_ref, edge_ref, weight_ref, weight, gains, sems = refs
    step = pl.program_id(0)
    rows = x_ref.shape[0]

    @pl.when(step == 0)
    def _():
        rest = HALF - FIRST_CUT
        start_slots(info, own_b, orders[1], [(rest, LANES, gains, 0, 1)], sems)
        for begin, part_a, part_b in ((0, own_a, own_b), (HALF, other_a, other_b)):
            start_slots(info, part_a, orders[0], [(0, FIRST_CUT, weight, begin, 0)], sems)
            start_slots(info, part_b, orders[1], [(0, rest, weight, begin + FIRST_CUT, 0)], sems)
        wait_whole(gains, sems.at[1])
        row = lax.broadcasted_iota(jnp.int32, (16, LANES), 0)
        lane = lax.broadcasted_iota(jnp.int32, (16, LANES), 1)
        pick = jnp.where(row == lane, 1.0, 0.0).astype(BF16)
        gain_ref[...] = nt(pick, gains[...])[:8]
        wait_whole(weight, sems.at[0])
        pltpu.make_async_copy(weight, weight_ref, sems.at[2]).start()

    unit, unused = normalized(x_ref[...].astype(F32))
    normed = (unit * gain_ref[0:1, :]).astype(BF16)
    normed_ref[...] = normed
    table_rows = pl.ds(pl.multiple_of(WINDOW_HALF + step * rows, WINDOW_HALF), rows)
    cosine, sine = cos_ref[table_rows, :], sin_ref[table_rows, :]
    for half in range(2):
        result = nn(normed, weight[:, HALF * half : HALF * (half + 1)])
        for tile in range(9):
            block = result[:, LANES * tile : LANES * (tile + 1)]
            if tile < 6:
                block = turned(block, cosine, sine)
            if tile < 3:
                block = block * (HEAD_DIM**-0.5)
            begin = HALF * half + LANES * tile
            qkv_ref[:, begin : begin + LANES] = block.astype(BF16)

    for core, at_step, begin in ((1, 0, 0), (0, ROWS // rows - 1, rows - WINDOW_HALF)):

        @pl.when((info[1] == core) & (step == at_step))
        def _():
            for part in range(2):
                for half in range(2):
                    source = HALF * half + THIRD * (part + 1)
                    target = WIDTH * part + THIRD * (1 - half)
                    edge_ref[:, target : target + THIRD] = qkv_ref[
                        begin : begin + WINDOW_HALF, source : source + THIRD
                    ]
            edge_ref[:, 2 * WIDTH :] = normed_ref[begin : begin + WINDOW_HALF, :]

    @pl.when(step == ROWS // rows - 1)
    def _():
        pltpu.make_async_copy(weight, weight_ref, sems.at[2]).wait()


def attend_kernel(
    info, row_seg, col_seg, q_ref, qkv_ref, edge_ref, own_ref, other_ref, probs_ref, window, turned_values, sems
):
    step = pl.program_id(0)
    unit = identity()

    @pl.when(step == 0)
    def _():
        fill_window(info, qkv_ref, edge_ref, window, sems)
        turn_rows(unit, window, WIDTH, 0, turned_values)

    start = pl.multiple_of(step * LANES, LANES)
    turn_rows(unit, window, WIDTH, pl.multiple_of(start + LANES, LANES), turned_values)
    key_seg = col_seg[pl.ds(start, SPAN), :]
    key_at = lax.broadcasted_iota(jnp.int32, (SPAN, LANES), 0) - WINDOW_HALF
    query_at = lax.broadcasted_iota(jnp.int32, (SPAN, LANES), 1)
    near = jnp.abs(key_at - query_at) <= WINDOW_HALF
    allowed = (key_seg == row_seg[0]) & near
    bias = jnp.where(allowed, 0.0, -1e30)
    bias = jnp.concatenate([bias, bias], axis=1)

    scores, probs, results = [], [], []
    for pair in range(PAIRS):
        begin = HALF * (pair // 3) + LANES * (pair % 3)
        queries = both_heads(q_ref[:, begin : begin + LANES])
        keys = window[pl.ds(start, SPAN), LANES * pair : LANES * (pair + 1)]
        scores.append(nt(keys, queries) + bias)
    for pair in range(PAIRS):
        weights = jnp.exp(scores[pair] - jnp.max(scores[pair], axis=0, keepdims=True))
        total = jnp.sum(weights, axis=0, keepdims=True)
        probs.append((weights * (1.0 / total)).astype(BF16))
        probs_ref[0, pair] = probs[pair]
    for pair in range(PAIRS):
        values = turned_values[LANES * pair : LANES * (pair + 1), pl.ds(start, SPAN)]
        results.append(head_rows(nn(values, probs[pair])).astype(BF16))
    for pair in range(PAIRS):
        out_ref = own_ref if pair < 3 else other_ref
        out_ref[:, LANES * (pair % 3) : LANES * (pair % 3 + 1)] = nt(unit, results[pair]).astype(
            BF16
        )


def mlp_kernel(orders, counts, info, x_ref, att_own, att_other, cot_ref, live_ref, gain_ref, *refs):
    parts = []
    for count in counts:
        parts.append(refs[:count])
        refs = refs[count:]
    in_own, in_other, down_own, down_other = parts
    (
        out_ref,
        hidden_grad_ref,
        att_grad_own,
        att_grad_other,
        normed_ref,
        gated_own,
        gated_other,
        pre_grad_own,
        pre_grad_other,
        low_grad_ref,
        out_grad_ref,
        w_in,
        w_att,
        w_out,
        tail_own,
        tail_other,
        sems,
    ) = refs
    step = pl.program_id(0)

    @pl.when(step == 0)
    def _():
        for number, (part, tail) in enumerate(((down_own, tail_own), (down_other, tail_other))):
            segments = [
                (0, THIRD, w_att, THIRD * number, 1),
                (THIRD, UNITS, w_out, UNITS * number, 2),
                (THIRD + UNITS, LANES, tail, 0, 3 + number),
            ]
            start_slots(info, part, orders[1], segments, sems)
        for number, part in enumerate((in_own, in_other)):
            start_slots(info, part, orders[0], [(0, HALF, w_in, HALF * number, 0)], sems)
        wait_whole(w_att, sems.at[1])
        wait_whole(w_out.at[:, pl.ds(0, 2 * UNITS)], sems.at[2])
        wait_whole(tail_own, sems.at[3])
        wait_whole(tail_other, sems.at[4])
        other = pltpu.roll(tail_other[...].astype(F32), HEAD_DIM, 1).astype(BF16)
        w_out[:, 2 * UNITS :] = tail_own[...] + other
        wait_whole(w_in, sems.at[0])

    gain = gain_ref[1:2, :]
    hidden = (
        x_ref[...].astype(F32)
        + nt(att_own[...], w_att[:, :THIRD])
        + nt(att_other[...], w_att[:, THIRD:])
    )
    unit, factor = normalized(hidden)
    normed = (unit * gain).astype(BF16)
    normed_ref[...] = normed
    out_grad = cot_ref[...].astype(F32) * live_ref[...]
    out_grad_low = out_grad.astype(BF16)
    out_grad_ref[...] = out_grad_low
    pre = [nn(normed, w_in[:, HALF * half : HALF * (half + 1)]) for half in range(2)]
    tails = [part[:, 2 * UNITS :] for part in pre]
    lane = lax.broadcasted_iota(jnp.int32, tails[0].shape, 1)
    low = lane < HEAD_DIM
    gates = [part[:, :UNITS] for part in pre]
    gates.append(jnp.where(low, tails[0], pltpu.roll(tails[1], 64, 1)))
    ups = [part[:, UNITS : 2 * UNITS] for part in pre]
    ups.append(jnp.where(low, pltpu.roll(tails[0], 64, 1), tails[1]))
    pre_grads = (pre_grad_own, pre_grad_other)
    for part, (gate, up) in enumerate(zip(gates, ups)):
        columns = slice(UNITS * part, UNITS * part + gate.shape[1])
        share = 0.5 + 0.5 * lax.erf(gate * (0.5**0.5))
        slope = share + gate * (jnp.exp(-0.5 * gate * gate) * 0.3989422804014327)
        curve = gate * share
        gated = curve * up
        grad = nn(out_grad_low, w_out[:, columns])
        gate_grad = grad * up * slope
        up_grad = grad * curve
        if part < 2:
            (gated_own, gated_other)[part][:, :UNITS] = gated.astype(BF16)
            pre_grads[part][:, :UNITS] = gate_grad.astype(BF16)
            pre_grads[part][:, UNITS : 2 * UNITS] = up_grad.astype(BF16)
        else:
            gated_own[:, UNITS:] = gated.astype(BF16)
            gated_other[:, UNITS:] = pltpu.roll(gated, HEAD_DIM, 1).astype(BF16)
            own = jnp.where(low, gate_grad, pltpu.roll(up_grad, 64, 1))
            other = jnp.where(low, pltpu.roll(gate_grad, 64, 1), up_grad)
            pre_grad_own[:, 2 * UNITS :] = own.astype(BF16)
            pre_grad_other[:, 2 * UNITS :] = other.astype(BF16)
    product = (
        nt(gated_own[:, :UNITS], w_out[:, :UNITS])
        + nt(gated_other[:, :UNITS], w_out[:, UNITS : 2 * UNITS])
        + nt(gated_own[:, UNITS:], w_out[:, 2 * UNITS :])
    )
    out_ref[...] = (hidden + product).astype(BF16)
    normed_grad = nt(pre_grad_own[...], w_in[:, :HALF]) + nt(pre_grad_other[...], w_in[:, HALF:])
    hidden_grad = out_grad + norm_backward(normed_grad, unit, factor, gain)
    hidden_grad_ref[...] = hidden_grad
    hidden_grad_low = hidden_grad.astype(BF16)
    low_grad_ref[...] = hidden_grad_low
    att_grad_own[...] = nn(hidden_grad_low, w_att[:, :THIRD]).astype(BF16)
    att_grad_other[...] = nn(hidden_grad_low, w_att[:, THIRD:]).astype(BF16)


def attend_back_kernel(
    info,
    q_ref,
    probs_ref,
    grad_own,
    grad_other,
    cos_ref,
    sin_ref,
    cos_turned,
    sin_turned,
    qkv_ref,
    edge_ref,
    out_own,
    out_other,
    edge_out_ref,
    window,
    turned_keys,
    key_grad,
    value_grad,
    sems,
):
    step = pl.program_id(0)
    unit = identity()

    @pl.when(step == 0)
    def _():
        fill_window(info, qkv_ref, edge_ref, window, sems)
        turn_rows(unit, window, 0, 0, turned_keys)
        key_grad[...] = jnp.zeros_like(key_grad)
        value_grad[...] = jnp.zeros_like(value_grad)

    start = pl.multiple_of(step * LANES, LANES)
    span = pl.ds(start, SPAN)
    turn_rows(unit, window, 0, pl.multiple_of(start + LANES, LANES), turned_keys)
    cosine, sine = cos_turned[...], sin_turned[...]

    all_lanes = [slice(LANES * pair, LANES * (pair + 1)) for pair in range(PAIRS)]
    grads, probs_grads, score_grads, query_grads = [], [], [], []
    for pair, lanes in enumerate(all_lanes):
        grad_ref = grad_own if pair < 3 else grad_other
        grads.append(both_heads(grad_ref[:, LANES * (pair % 3) : LANES * (pair % 3 + 1)]))
        values = window[span, WIDTH + LANES * pair : WIDTH + LANES * (pair + 1)]
        probs_grads.append(nt(values, grads[pair]))
    for pair, lanes in enumerate(all_lanes):
        value_grad[span, lanes] += nn(probs_ref[0, pair], grads[pair])
    for pair in range(PAIRS):
        probs = probs_ref[0, pair].astype(F32)
        weighted = probs_grads[pair] * probs
        delta = jnp.sum(weighted, axis=0, keepdims=True)
        score_grads.append((weighted - probs * delta).astype(BF16))
    for pair, lanes in enumerate(all_lanes):
        query_grads.append(head_rows(nn(turned_keys[lanes, span], score_grads[pair])))
    for pair, lanes in enumerate(all_lanes):
        begin = HALF * (pair // 3) + LANES * (pair % 3)
        queries = both_heads(q_ref[:, begin : begin + LANES])
        key_grad[span, lanes] += nn(score_grads[pair], queries)
    for pair in range(PAIRS):
        grad = query_grads[pair] * (HEAD_DIM**-0.5)
        other = jnp.concatenate([grad[32:64], grad[:32], grad[96:], grad[64:96]], axis=0)
        query_grads[pair] = (grad * cosine - other * sine).astype(BF16)
    for pair in range(PAIRS):
        out_ref = out_own if pair < 3 else out_other
        place = slice(LANES * (pair % 3), LANES * (pair % 3 + 1))
        out_ref[pl.ds(start, LANES), place] = nt(unit, query_grads[pair]).astype(BF16)

    @pl.when(step == ROWS // LANES - 1)
    def _():
        inside = slice(WINDOW_HALF, WINDOW_HALF + ROWS)
        row = pl.multiple_of(jnp.where(info[1] == 1, 0, WINDOW_HALF + ROWS), 16)
        edge_rows = pl.ds(row, WINDOW_HALF)
        for pair in range(PAIRS):
            out_ref = out_own if pair < 3 else out_other
            lanes = slice(LANES * pair, LANES * (pair + 1))
            begin = LANES * (pair % 3)
            target = (LANES * pair + THIRD) % WIDTH
            keys_at = slice(THIRD + begin, THIRD + begin + LANES)
            values_at = slice(2 * THIRD + begin, 2 * THIRD + begin + LANES)
            out_ref[:ROWS, keys_at] = turned(
                key_grad[inside, lanes], cos_ref[inside, :], -sin_ref[inside, :]
            ).astype(BF16)
            out_ref[:ROWS, values_at] = value_grad[inside, lanes].astype(BF16)
            edge_keys = turned(
                key_grad[edge_rows, lanes], cos_ref[edge_rows, :], -sin_ref[edge_rows, :]
            ).astype(BF16)
            edge_values = value_grad[edge_rows, lanes].astype(BF16)
            edge_out_ref[:, target : target + LANES] = edge_keys
            edge_out_ref[:, WIDTH + target : WIDTH + target + LANES] = edge_values
            out_ref[ROWS:, begin : begin + LANES] = jnp.zeros((WINDOW_HALF, LANES), BF16)
            out_ref[ROWS:, keys_at] = edge_keys
            out_ref[ROWS:, values_at] = edge_values


def input_grad_kernel(
    info, x_ref, own_ref, other_ref, edge_ref, hidden_ref, gain_ref, weight, out_ref, fixed
):
    rows = x_ref.shape[0]
    step = pl.program_id(0)
    grad = None
    for half, grad_ref in enumerate((own_ref, other_ref)):
        fixed[...] = grad_ref[...]
        for core, at_step, begin in ((1, 0, 0), (0, ROWS // rows - 1, rows - WINDOW_HALF)):

            @pl.when((info[1] == core) & (step == at_step))
            def _():
                at = slice(begin, begin + WINDOW_HALF)
                for part in range(2):
                    to = slice(THIRD * (part + 1), THIRD * (part + 2))
                    source = WIDTH * part + THIRD * half
                    add = edge_ref[:, source : source + THIRD].astype(F32)
                    fixed[at, to] = (fixed[at, to].astype(F32) + add).astype(BF16)

        part = nt(fixed[...], weight[:, HALF * half : HALF * (half + 1)])
        grad = part if grad is None else grad + part
    unit, factor = normalized(x_ref[...].astype(F32))
    out_ref[...] = hidden_ref[...] + norm_backward(grad, unit, factor, gain_ref[0:1, :])


def shape_of(shape, dtype=BF16):
    return jax.ShapeDtypeStruct(shape, dtype)


def call(
    kernel, info, grid, ins, in_specs, outs, out_specs, scratch, flops, aliases=None, after=()
):
    moved = sum(a.size * a.dtype.itemsize for a in list(ins) + list(outs))
    first = 1 + len(ins)
    later = first + len(after)
    return pl.pallas_call(
        lambda *refs: kernel(*refs[:first], *refs[later:]),
        out_shape=outs,
        grid_spec=pltpu.PrefetchScalarGridSpec(
            num_scalar_prefetch=1,
            grid=grid,
            in_specs=list(in_specs) + [ANYWHERE] * len(after),
            out_specs=out_specs,
            scratch_shapes=scratch,
        ),
        input_output_aliases=aliases or {},
        compiler_params=pltpu.CompilerParams(
            dimension_semantics=("arbitrary",), vmem_limit_bytes=VMEM
        ),
        cost_estimate=pl.CostEstimate(
            flops=int(flops), bytes_accessed=int(moved), transcendentals=0
        ),
    )(info, *ins, *after)


def by_rows(rows, columns):
    return pl.BlockSpec((rows, columns), lambda i, s: (i, 0))


def full(*shape):
    return pl.BlockSpec(shape, lambda i, s: (0,) * len(shape))


def body(
    tokens,
    segment,
    norm_attn_gain,
    qkv_weight,
    attn_out_weight,
    norm_mlp_gain,
    in_weight,
    out_weight,
    cotangent,
):
    own_rows = norm_attn_gain.shape[0]
    core = lax.axis_index("tensor")
    place = lax.axis_index("dp") if by_exchange(own_rows) else 0
    info = jnp.stack([jnp.int32(place), core.astype(jnp.int32)])
    orders = (relative(own_rows, False), relative(own_rows, True))

    gains = jnp.pad(jnp.stack([norm_attn_gain, norm_mlp_gain], axis=1), ((0, 0), (0, LANES - 2)))
    flat_qkv = qkv_weight.reshape(own_rows, HALF)
    first_pieces = gather_start(jnp.concatenate([flat_qkv, gains], axis=1))
    shard_in = jnp.concatenate(
        [
            in_weight[:, 0, :UNITS],
            in_weight[:, 1, :UNITS],
            in_weight[:, 0, UNITS:],
            in_weight[:, 1, UNITS:],
        ],
        axis=1,
    )
    turned_out = out_weight.T
    blank = jnp.zeros((own_rows, HEAD_DIM), BF16)
    shard_down = jnp.concatenate([attn_out_weight.T, turned_out, blank], axis=1)
    second_shard = jnp.concatenate([shard_in, shard_down], axis=1)
    second_shard, *first_pieces = held_until([second_shard] + first_pieces)
    second_pieces = gather_start(second_shard)

    own_segment = lax.dynamic_slice_in_dim(segment, core * ROWS, ROWS, 0)
    seg_pad = jnp.pad(segment, (WINDOW_HALF, WINDOW_HALF), constant_values=-2)
    span_segment = lax.dynamic_slice_in_dim(seg_pad, core * ROWS, ROWS + 2 * WINDOW_HALF, 0)
    slot = core * ROWS - WINDOW_HALF + jnp.arange(ROWS + 2 * WINDOW_HALF, dtype=jnp.int32)
    position = jnp.where(span_segment >= 0, slot - PAD_BLOCK * span_segment, 0)
    lane = jnp.arange(LANES, dtype=jnp.int32)
    exponent = (lane % 32).astype(F32) * (2.0 / HEAD_DIM)
    angle = position.astype(F32)[:, None] * jnp.power(10000.0, -exponent)[None, :]
    cos_span = jnp.cos(angle)
    sin_span = jnp.sin(angle) * jnp.where((lane & 32) == 0, -1.0, 1.0)[None, :]
    cos_turned = cos_span[WINDOW_HALF:-WINDOW_HALF].T
    sin_turned = sin_span[WINDOW_HALF:-WINDOW_HALF].T
    col_seg = span_segment[:, None]
    row_seg = own_segment.reshape(ROWS // LANES, 1, LANES)
    live = (own_segment >= 0).astype(F32)[:, None]

    rows = 384
    steps = ROWS // rows
    first_pieces = held_until(
        first_pieces, cos_span, sin_span, col_seg, row_seg, live, info
    )
    first_held = joined(first_pieces)
    held_a, held_b = first_held[:, :, :FIRST_CUT], first_held[:, :, FIRST_CUT:]
    own_a = gather_finish(gather_middle(held_a, False), False)
    own_b = gather_finish(gather_middle(held_b, True), True)
    second_held = joined(second_pieces)
    held_in, held_down = second_held[:, :, :HALF], second_held[:, :, HALF:]
    own_a[-1], own_b[-1] = held_until((own_a[-1], own_b[-1]), held_in, held_down)
    own_a, own_b = [jnp.concatenate(own_a, axis=0)], [jnp.concatenate(own_b, axis=0)]
    other_a, other_b = [swapped_cores(own_a[0])], [swapped_cores(own_b[0])]

    parts = (own_a, other_a, own_b, other_b)
    counts_qkv = tuple(len(part) for part in parts)
    qkv, normed, gain_rows, edge, weight_qkv = call(
        lambda *refs: qkv_kernel(orders, counts_qkv, *refs),
        info,
        (steps,),
        [tokens, cos_span, sin_span] + [piece for part in parts for piece in part],
        [by_rows(rows, WIDTH), full(*cos_span.shape), full(*cos_span.shape)]
        + [ANYWHERE] * sum(counts_qkv),
        [
            shape_of((ROWS, 2 * HALF)),
            shape_of((MORE_ROWS, WIDTH)),
            shape_of((8, WIDTH), F32),
            shape_of((WINDOW_HALF, 3 * WIDTH)),
            shape_of((WIDTH, 2 * HALF)),
        ],
        [by_rows(rows, 2 * HALF), by_rows(rows, WIDTH), full(8, WIDTH)]
        + [full(WINDOW_HALF, 3 * WIDTH), ANYWHERE],
        [
            pltpu.VMEM((WIDTH, 2 * HALF), BF16),
            pltpu.VMEM((WIDTH, LANES), BF16),
            pltpu.SemaphoreType.DMA((3,)),
        ],
        2 * ROWS * WIDTH * 2 * HALF,
    )
    edge = swapped_cores(edge)
    normed = lax.dynamic_update_slice(normed, edge[:, 2 * WIDTH :], (ROWS, 0))
    held_in = gather_middle(held_in, False, qkv)
    held_down = gather_middle(held_down, True, qkv)
    in_own, down_own = gather_finish(held_in, False), gather_finish(held_down, True)

    blocks = ROWS // LANES
    window_shape = (ROWS + 2 * WINDOW_HALF, 2 * WIDTH)
    turned_shape = (WIDTH, ROWS + 2 * WINDOW_HALF)
    by_block = pl.BlockSpec((1, PAIRS, SPAN, SPAN), lambda i, s: (i, 0, 0, 0))
    att_own, att_other, probs = call(
        attend_kernel,
        info,
        (blocks,),
        [row_seg, col_seg, qkv, qkv, edge],
        [
            pl.BlockSpec((1, 1, LANES), lambda i, s: (i, 0, 0)),
            full(ROWS + 2 * WINDOW_HALF, 1),
            by_rows(LANES, 2 * HALF),
            ANYWHERE,
            ANYWHERE,
        ],
        [
            shape_of((ROWS, THIRD)),
            shape_of((ROWS, THIRD)),
            shape_of((blocks, PAIRS, SPAN, SPAN)),
        ],
        [by_rows(LANES, THIRD), by_rows(LANES, THIRD), by_block],
        [
            pltpu.VMEM(window_shape, BF16),
            pltpu.VMEM(turned_shape, BF16),
            pltpu.SemaphoreType.DMA((5,)),
        ],
        blocks * PAIRS * 2 * 2 * SPAN * SPAN * LANES,
        after=[held_in, held_down],
    )

    in_own[-1], down_own[-1] = held_until((in_own[-1], down_own[-1]), att_own)
    in_other = [swapped_cores(piece) for piece in in_own]
    down_other = [swapped_cores(piece) for piece in down_own]
    parts = (in_own, in_other, down_own, down_other)
    counts = tuple(len(part) for part in parts)
    (
        layer_out,
        hidden_grad,
        att_grad_own,
        att_grad_other,
        normed_two,
        gated_own,
        gated_other,
        pre_grad_own,
        pre_grad_other,
        hidden_grad_low,
        out_grad,
    ) = call(
        lambda *refs: mlp_kernel(orders, counts, *refs),
        info,
        (steps,),
        [tokens, att_own, att_other, cotangent, live, gain_rows]
        + [piece for part in parts for piece in part],
        [by_rows(rows, WIDTH), by_rows(rows, THIRD), by_rows(rows, THIRD), by_rows(rows, WIDTH)]
        + [by_rows(rows, 1), full(8, WIDTH)]
        + [ANYWHERE] * sum(counts),
        [
            shape_of((ROWS, WIDTH)),
            shape_of((ROWS, WIDTH), F32),
            shape_of((ROWS, THIRD)),
            shape_of((ROWS, THIRD)),
            shape_of((ROWS, WIDTH)),
            shape_of((ROWS, UNITS + LANES)),
            shape_of((ROWS, UNITS + LANES)),
            shape_of((ROWS, HALF)),
            shape_of((ROWS, HALF)),
            shape_of((ROWS, WIDTH)),
            shape_of((ROWS, WIDTH)),
        ],
        [by_rows(rows, WIDTH)] * 2
        + [by_rows(rows, THIRD)] * 2
        + [by_rows(rows, WIDTH)]
        + [by_rows(rows, UNITS + LANES)] * 2
        + [by_rows(rows, HALF)] * 2
        + [by_rows(rows, WIDTH)] * 2,
        [
            pltpu.VMEM((WIDTH, 2 * HALF), BF16),
            pltpu.VMEM((WIDTH, WIDTH), BF16),
            pltpu.VMEM((WIDTH, HALF), BF16),
            pltpu.VMEM((WIDTH, LANES), BF16),
            pltpu.VMEM((WIDTH, LANES), BF16),
            pltpu.SemaphoreType.DMA((5,)),
        ],
        2 * ROWS * WIDTH * (4 * HALF + 2 * HALF + 2 * WIDTH),
    )

    def down_grads(att, gated):
        parts = [weight_grad(hidden_grad_low, att), weight_grad(out_grad, gated)]
        return jnp.concatenate(parts, axis=1)

    send_in = weight_grad(normed_two, pre_grad_other)
    send_down = down_grads(att_other, gated_other)
    keep_in = weight_grad(normed_two, pre_grad_own)
    keep_down = down_grads(att_own, gated_own)
    sum_in, in_back = scatter_start(keep_in, swapped_cores(send_in), own_rows, False)
    sum_down, down_back = scatter_start(keep_down, swapped_cores(send_down), own_rows, True)

    grad_own, grad_other, edge_grad = call(
        attend_back_kernel,
        info,
        (blocks,),
        [qkv, probs, att_grad_own, att_grad_other, cos_span, sin_span]
        + [cos_turned, sin_turned, qkv, edge],
        [by_rows(LANES, 2 * HALF), by_block, by_rows(LANES, THIRD), by_rows(LANES, THIRD)]
        + [full(*cos_span.shape)] * 2
        + [pl.BlockSpec((LANES, LANES), lambda i, s: (0, i))] * 2
        + [ANYWHERE] * 2,
        [shape_of((MORE_ROWS, HALF))] * 2 + [shape_of((WINDOW_HALF, 2 * WIDTH))],
        [full(MORE_ROWS, HALF)] * 2 + [full(WINDOW_HALF, 2 * WIDTH)],
        [
            pltpu.VMEM(window_shape, BF16),
            pltpu.VMEM(turned_shape, BF16),
            pltpu.VMEM((window_shape[0], WIDTH), F32),
            pltpu.VMEM((window_shape[0], WIDTH), F32),
            pltpu.SemaphoreType.DMA((5,)),
        ],
        blocks * PAIRS * 4 * 2 * SPAN * SPAN * LANES,
        after=[send_in, send_down, keep_in, keep_down],
    )
    edge_grad = swapped_cores(edge_grad)
    (normed,) = held_until((normed,), in_back[1], down_back[1])

    send_a = weight_grad(normed, grad_other[:, :FIRST_CUT])
    send_b = weight_grad(normed, grad_other[:, FIRST_CUT:])
    keep_a = weight_grad(normed, grad_own[:, :FIRST_CUT])
    keep_b = weight_grad(normed, grad_own[:, FIRST_CUT:])
    late_a, late_b = swapped_cores(send_a), swapped_cores(send_b)

    (grad_tokens,) = call(
        input_grad_kernel,
        info,
        (steps,),
        [tokens, grad_own, grad_other, edge_grad, hidden_grad, gain_rows, weight_qkv],
        [by_rows(rows, WIDTH), by_rows(rows, HALF), by_rows(rows, HALF)]
        + [full(WINDOW_HALF, 2 * WIDTH), by_rows(rows, WIDTH)]
        + [full(8, WIDTH), full(WIDTH, 2 * HALF)],
        [shape_of((ROWS, WIDTH), F32)],
        [by_rows(rows, WIDTH)],
        [pltpu.VMEM((rows, HALF), BF16)],
        2 * ROWS * WIDTH * 2 * HALF,
        after=[keep_a, keep_b, late_a, late_b, in_back[2], down_back[2]],
    )
    sum_in, sum_down = held_until((sum_in, sum_down), late_a, late_b)
    owned_early = scatter_finish(sum_in, sum_down)
    gates = (grad_tokens, owned_early)
    sum_a, unused = scatter_start(keep_a, late_a, own_rows, False, gates)
    sum_b, unused = scatter_start(keep_b, late_b, own_rows, True, gates)
    owned_in, owned_down = owned_early[:, :HALF], owned_early[:, HALF:]

    flat_grad = scatter_finish(sum_a, sum_b)
    gain_grads = jnp.stack(
        [
            gain_part(flat_qkv, flat_grad, norm_attn_gain),
            gain_part(shard_in, owned_in, norm_mlp_gain),
        ]
    )
    gain_grads = gain_grads + swapped_cores(gain_grads)
    owned_gain_one, owned_gain_two = gain_grads[0], gain_grads[1]
    owned_qkv = flat_grad.reshape(own_rows, 3, THIRD)
    owned_in = jnp.stack(
        [
            jnp.concatenate([owned_in[:, :UNITS], owned_in[:, 2 * UNITS : -64]], axis=1),
            jnp.concatenate([owned_in[:, UNITS : 2 * UNITS], owned_in[:, -64:]], axis=1),
        ],
        axis=1,
    )
    owned_attn = owned_down[:, :THIRD].T
    owned_out = owned_down[:, THIRD : THIRD + UNITS + HEAD_DIM].T
    return (
        layer_out,
        grad_tokens,
        owned_gain_one,
        owned_qkv,
        owned_attn,
        owned_gain_two,
        owned_in,
        owned_out,
    )


def solution(mesh):
    placed = (
        P(("dp", "tensor"), None),
        P("dp"),
        P("dp"),
        P("dp", None, "tensor"),
        P("tensor", "dp"),
        P("dp"),
        P("dp", None, "tensor"),
        P("tensor", "dp"),
        P(("dp", "tensor"), None),
    )
    return jax.shard_map(
        body,
        mesh=mesh,
        in_specs=placed,
        out_specs=(
            P(("dp", "tensor"), None),
            P(("dp", "tensor"), None),
            P("dp"),
            P("dp", None, "tensor"),
            P("tensor", "dp"),
            P("dp"),
            P("dp", None, "tensor"),
            P("tensor", "dp"),
        ),
        check_vma=False,
    )
```

```python
import jax
import jax.numpy as jnp
from jax import lax
from jax.experimental import pallas as pl
from jax.experimental.pallas import tpu as pltpu
from jax.sharding import PartitionSpec as P

HEAD_DIM = 64
WINDOW_HALF = 64
PAD_BLOCK = 128
WIDTH = 768
ROWS = 1152
MORE_ROWS = ROWS + 64
HALF = 1152
LANES = 128
THIRD = 384
PAIRS = 6
SPAN = 2 * LANES
UNITS = 512
FIRST_CUT = 640
WIDE = HALF + LANES
DOWN = 384 + UNITS + LANES
MIB = 2**20
ANYWHERE = pl.BlockSpec(memory_space=pl.ANY)
F32 = jnp.float32
BF16 = jnp.bfloat16


def steps_of(devices, swapped):
    bits = [1 << i for i in range(devices.bit_length() - 1)]
    near, far = bits[:2], bits[2:]
    return far + (near if swapped else near[::-1])


def exchanged(block, mask):
    devices = lax.axis_size("dp")
    return lax.ppermute(block, "dp", [(i, i ^ mask) for i in range(devices)])


def swapped_cores(block):
    return lax.ppermute(block, "tensor", [(0, 1), (1, 0)])


def by_exchange(own_rows):
    devices = lax.axis_size("dp")
    return own_rows % 16 == 0 and devices & (devices - 1) == 0


def relative(own_rows, swapped):
    if not by_exchange(own_rows):
        return list(range(WIDTH // 48))
    order = [0]
    for mask in steps_of(lax.axis_size("dp"), swapped):
        order = order + [r ^ mask for r in order]
    return order


def held_until(arrays, *gates):
    return lax.optimization_barrier((tuple(arrays), gates))[0]


def gather_start(shard):
    masks = steps_of(lax.axis_size("dp"), False)
    held = shard[None]
    if not by_exchange(shard.shape[0]) or len(masks) <= 3:
        return [held]
    first, second = masks[:2]
    return [held] + [exchanged(held, mask) for mask in (first, second, first ^ second)]


def joined(pieces):
    return lax.optimization_barrier(jnp.concatenate(pieces, axis=0))


def gather_middle(held, swapped, gate=None):
    if by_exchange(held.shape[1]):
        masks = steps_of(lax.axis_size("dp"), swapped)
        for mask in masks[held.shape[0].bit_length() - 1 : -1]:
            arrived = exchanged(held, mask)
            if gate is not None:
                (arrived,) = held_until((arrived,), gate)
            held = jnp.concatenate([held, arrived], axis=0)
    return held


def gather_finish(held, swapped):
    if not by_exchange(held.shape[1]):
        whole = lax.all_gather(held[0], "dp", axis=0, tiled=True)
        return [whole.reshape(WIDTH // 48, 48, held.shape[2])]
    return [held, exchanged(held, steps_of(lax.axis_size("dp"), swapped)[-1])]


def scatter_start(keep, other, own_rows, swapped, first_gates=None):
    arrivals, sents = [other], [other]
    if not by_exchange(own_rows):
        total = keep.astype(F32) + other.astype(F32)
        total = lax.psum_scatter(total, "dp", scatter_dimension=0, tiled=True)
        return total[None], arrivals * 3, sents * 3
    devices = lax.axis_size("dp")
    index = lax.axis_index("dp")
    levels = devices.bit_length() - 1
    masks = steps_of(devices, swapped)
    last = 2 if len(masks) > 3 else 0
    shape = (2,) * levels + (own_rows, keep.shape[1])
    keep, other = keep.reshape(shape), other.reshape(shape)
    for mask in reversed(masks[last:]):
        axis = levels - mask.bit_length()
        bit = (index & mask) // mask
        part = lambda array, which: lax.dynamic_slice_in_dim(array, which, 1, axis).astype(F32)
        sent = (part(keep, 1 - bit) + part(other, 1 - bit)).astype(BF16)
        kept = (part(keep, bit) + part(other, bit)).astype(BF16)
        other = exchanged(sent, mask)
        arrivals.append(other)
        sents.append(sent)
        if first_gates is not None and len(arrivals) == 2:
            (other,) = held_until((other,), *first_gates)
        keep = kept
    total = keep.astype(F32) + other.astype(F32)
    return total.reshape(2**last, own_rows, -1), arrivals + [other] * 3, sents + [other] * 3


def scatter_finish(*totals):
    if totals[0].shape[0] == 1:
        return jnp.concatenate([total[0] for total in totals], axis=1)
    unit = steps_of(lax.axis_size("dp"), False)[0]
    place = (lax.axis_index("dp") // unit) % 4

    def rows_of(which):
        parts = [lax.dynamic_index_in_dim(total, which, 0, keepdims=False) for total in totals]
        return jnp.concatenate(parts, axis=1)

    arrived = [
        exchanged(rows_of(place ^ j).astype(BF16), unit * j).astype(F32) for j in range(1, 4)
    ]
    return rows_of(place) + (arrived[0] + arrived[1] + arrived[2])


def weight_grad(left, right):
    return lax.dot_general(
        left, right, (((0,), (0,)), ((), ())), preferred_element_type=F32
    ).astype(BF16)


def gain_part(weight, grad, gain):
    return jnp.sum(weight.astype(F32) * grad, axis=1) / gain.astype(F32)


def nt(left, right):
    return lax.dot_general(left, right, (((1,), (1,)), ((), ())), preferred_element_type=F32)


def nn(left, right):
    return jnp.dot(left, right, preferred_element_type=F32)


def start_slots(info, pieces, order, segments, sems):
    slot = 0
    for piece in pieces:
        rows = piece.shape[1]
        for at in range(piece.shape[0]):
            row = pl.multiple_of((info[0] ^ order[slot]) * rows, 16)
            for begin, width, target, column, sem in segments:
                pltpu.make_async_copy(
                    piece.at[at, :, pl.ds(begin, width)],
                    target.at[pl.ds(row, rows), pl.ds(column, width)],
                    sems.at[sem],
                ).start()
            slot += 1


def wait_whole(ref, sem):
    pltpu.make_async_copy(ref, ref, sem).wait()


def fill_window(info, qkv_ref, edge_ref, window, sems):
    core = info[1]
    first = pl.multiple_of(jnp.where(core == 1, 0, WINDOW_HALF + ROWS), 16)
    last = pl.multiple_of(jnp.where(core == 1, WINDOW_HALF + ROWS, 0), 16)
    copies = [
        pltpu.make_async_copy(
            edge_ref.at[:, pl.ds(0, 2 * WIDTH)],
            window.at[pl.ds(first, WINDOW_HALF), :],
            sems.at[4],
        )
    ]
    for part in range(2):
        for half in range(2):
            copies.append(
                pltpu.make_async_copy(
                    qkv_ref.at[:, pl.ds(HALF * half + THIRD * (part + 1), THIRD)],
                    window.at[pl.ds(WINDOW_HALF, ROWS), pl.ds(WIDTH * part + THIRD * half, THIRD)],
                    sems.at[2 * part + half],
                )
            )
    for copy in copies:
        copy.start()
    window[pl.ds(last, WINDOW_HALF), :] = jnp.zeros((WINDOW_HALF, 2 * WIDTH), BF16)
    for copy in copies:
        copy.wait()


def identity():
    row = lax.broadcasted_iota(jnp.int32, (LANES, LANES), 0)
    lane = lax.broadcasted_iota(jnp.int32, (LANES, LANES), 1)
    return jnp.where(row == lane, 1.0, 0.0).astype(BF16)


def turn_rows(unit, window, begin, row, turned_ref):
    for pair in range(PAIRS):
        lanes = slice(LANES * pair, LANES * (pair + 1))
        block = window[pl.ds(row, LANES), begin + LANES * pair : begin + LANES * (pair + 1)]
        turned_ref[lanes, pl.ds(row, LANES)] = nt(unit, block).astype(BF16)


def head_rows(columns):
    return jnp.concatenate([columns[:HEAD_DIM, :LANES], columns[HEAD_DIM:, LANES:]], axis=0)


def normalized(values):
    centred = values - jnp.mean(values, axis=-1, keepdims=True)
    spread = jnp.mean(centred * centred, axis=-1, keepdims=True)
    factor = lax.rsqrt(spread + 1e-05)
    return centred * factor, factor


def norm_backward(grad, unit, factor, gain):
    inner = grad * gain
    mean = jnp.mean(inner, axis=-1, keepdims=True)
    along = jnp.mean(inner * unit, axis=-1, keepdims=True)
    return factor * (inner - mean - unit * along)


def turned(values, cosine, sine):
    lane = lax.broadcasted_iota(jnp.int32, values.shape, 1)
    first = (lane & 32) == 0
    other = jnp.where(first, pltpu.roll(values, 96, 1), pltpu.roll(values, 32, 1))
    return values * cosine + other * sine


def both_heads(block):
    lane = lax.broadcasted_iota(jnp.int32, block.shape, 1)
    first = jnp.where(lane < HEAD_DIM, 1.0, 0.0).astype(block.dtype)
    second = jnp.where(lane < HEAD_DIM, 0.0, 1.0).astype(block.dtype)
    return jnp.concatenate([block * first, block * second], axis=0)


def qkv_kernel(orders, counts, info, x_ref, cos_ref, sin_ref, *refs):
    parts = []
    for count in counts:
        parts.append(refs[:count])
        refs = refs[count:]
    own_a, other_a, own_b, other_b = parts
    qkv_ref, normed_ref, gain_ref, edge_ref, weight_ref, weight, sems = refs
    step = pl.program_id(0)
    rows = x_ref.shape[0]

    @pl.when(step == 0)
    def _():
        for begin, part_a, part_b in ((0, own_a, own_b), (WIDE, other_a, other_b)):
            start_slots(info, part_a, orders[0], [(0, FIRST_CUT, weight, begin, 0)], sems)
            start_slots(
                info,
                part_b,
                orders[1],
                [(0, WIDE - FIRST_CUT, weight, begin + FIRST_CUT, 0)],
                sems,
            )
        wait_whole(weight, sems.at[0])
        pltpu.make_async_copy(weight, weight_ref, sems.at[1]).start()
        row = lax.broadcasted_iota(jnp.int32, (16, LANES), 0)
        lane = lax.broadcasted_iota(jnp.int32, (16, LANES), 1)
        pick = jnp.where(row == lane, 1.0, 0.0).astype(BF16)
        gain_ref[...] = nt(pick, weight[:, HALF:WIDE])[:8]

    unit, unused = normalized(x_ref[...].astype(F32))
    normed = (unit * gain_ref[0:1, :]).astype(BF16)
    normed_ref[...] = normed
    table_rows = pl.ds(pl.multiple_of(WINDOW_HALF + step * rows, WINDOW_HALF), rows)
    cosine, sine = cos_ref[table_rows, :], sin_ref[table_rows, :]
    for half in range(2):
        result = nn(normed, weight[:, WIDE * half : WIDE * half + HALF])
        for tile in range(9):
            block = result[:, LANES * tile : LANES * (tile + 1)]
            if tile < 6:
                block = turned(block, cosine, sine)
            if tile < 3:
                block = block * (HEAD_DIM**-0.5)
            begin = HALF * half + LANES * tile
            qkv_ref[:, begin : begin + LANES] = block.astype(BF16)

    for core, at_step, begin in ((1, 0, 0), (0, ROWS // rows - 1, rows - WINDOW_HALF)):

        @pl.when((info[1] == core) & (step == at_step))
        def _():
            for part in range(2):
                for half in range(2):
                    source = HALF * half + THIRD * (part + 1)
                    target = WIDTH * part + THIRD * (1 - half)
                    edge_ref[:, target : target + THIRD] = qkv_ref[
                        begin : begin + WINDOW_HALF, source : source + THIRD
                    ]
            edge_ref[:, 2 * WIDTH :] = normed_ref[begin : begin + WINDOW_HALF, :]

    @pl.when(step == ROWS // rows - 1)
    def _():
        pltpu.make_async_copy(weight, weight_ref, sems.at[1]).wait()


def attend_kernel(
    info, row_seg, col_seg, q_ref, qkv_ref, edge_ref, own_ref, other_ref, probs_ref, window, turned_values, sems
):
    step = pl.program_id(0)
    unit = identity()

    @pl.when(step == 0)
    def _():
        fill_window(info, qkv_ref, edge_ref, window, sems)
        turn_rows(unit, window, WIDTH, 0, turned_values)

    start = pl.multiple_of(step * LANES, LANES)
    turn_rows(unit, window, WIDTH, pl.multiple_of(start + LANES, LANES), turned_values)
    key_seg = col_seg[pl.ds(start, SPAN), :]
    key_at = lax.broadcasted_iota(jnp.int32, (SPAN, LANES), 0) - WINDOW_HALF
    query_at = lax.broadcasted_iota(jnp.int32, (SPAN, LANES), 1)
    near = jnp.abs(key_at - query_at) <= WINDOW_HALF
    allowed = (key_seg == row_seg[0]) & near
    bias = jnp.where(allowed, 0.0, -1e30)
    bias = jnp.concatenate([bias, bias], axis=1)

    scores, probs, results = [], [], []
    for pair in range(PAIRS):
        begin = HALF * (pair // 3) + LANES * (pair % 3)
        queries = both_heads(q_ref[:, begin : begin + LANES])
        keys = window[pl.ds(start, SPAN), LANES * pair : LANES * (pair + 1)]
        scores.append(nt(keys, queries) + bias)
    for pair in range(PAIRS):
        weights = jnp.exp(scores[pair] - jnp.max(scores[pair], axis=0, keepdims=True))
        total = jnp.sum(weights, axis=0, keepdims=True)
        probs.append((weights * (1.0 / total)).astype(BF16))
        probs_ref[0, pair] = probs[pair]
    for pair in range(PAIRS):
        values = turned_values[LANES * pair : LANES * (pair + 1), pl.ds(start, SPAN)]
        results.append(head_rows(nn(values, probs[pair])).astype(BF16))
    for pair in range(PAIRS):
        out_ref = own_ref if pair < 3 else other_ref
        out_ref[:, LANES * (pair % 3) : LANES * (pair % 3 + 1)] = nt(unit, results[pair]).astype(
            BF16
        )


def mlp_kernel(orders, counts, info, x_ref, att_own, att_other, cot_ref, live_ref, gain_ref, *refs):
    parts = []
    for count in counts:
        parts.append(refs[:count])
        refs = refs[count:]
    in_own, in_other, down_own, down_other = parts
    (
        out_ref,
        hidden_grad_ref,
        att_grad_own,
        att_grad_other,
        normed_ref,
        gated_own,
        gated_other,
        pre_grad_own,
        pre_grad_other,
        low_grad_ref,
        out_grad_ref,
        w_in,
        w_down,
        sems,
    ) = refs
    step = pl.program_id(0)

    @pl.when(step == 0)
    def _():
        for number, part in enumerate((down_own, down_other)):
            start_slots(info, part, orders[1], [(0, DOWN, w_down, DOWN * number, 0)], sems)
        for number, part in enumerate((in_own, in_other)):
            start_slots(info, part, orders[0], [(0, HALF, w_in, HALF * number, 1)], sems)
        wait_whole(w_down, sems.at[0])
        other = pltpu.roll(w_down[:, 2 * DOWN - LANES :].astype(F32), HEAD_DIM, 1).astype(BF16)
        w_down[:, DOWN - LANES : DOWN] += other

    gain = gain_ref[1:2, :]
    hidden = (
        x_ref[...].astype(F32)
        + nt(att_own[...], w_down[:, :THIRD])
        + nt(att_other[...], w_down[:, DOWN : DOWN + THIRD])
    )
    unit, factor = normalized(hidden)
    normed = (unit * gain).astype(BF16)
    normed_ref[...] = normed
    out_grad = cot_ref[...].astype(F32) * live_ref[...]
    out_grad_low = out_grad.astype(BF16)
    out_grad_ref[...] = out_grad_low

    @pl.when(step == 0)
    def _():
        wait_whole(w_in, sems.at[1])

    pre = [nn(normed, w_in[:, HALF * half : HALF * (half + 1)]) for half in range(2)]
    tails = [part[:, 2 * UNITS :] for part in pre]
    lane = lax.broadcasted_iota(jnp.int32, tails[0].shape, 1)
    low = lane < HEAD_DIM
    gates = [part[:, :UNITS] for part in pre]
    gates.append(jnp.where(low, tails[0], pltpu.roll(tails[1], 64, 1)))
    ups = [part[:, UNITS : 2 * UNITS] for part in pre]
    ups.append(jnp.where(low, pltpu.roll(tails[0], 64, 1), tails[1]))
    pre_grads = (pre_grad_own, pre_grad_other)
    unit_columns = (
        slice(THIRD, THIRD + UNITS),
        slice(DOWN + THIRD, DOWN + THIRD + UNITS),
        slice(DOWN - LANES, DOWN),
    )
    for part, (gate, up) in enumerate(zip(gates, ups)):
        share = 0.5 + 0.5 * lax.erf(gate * (0.5**0.5))
        slope = share + gate * (jnp.exp(-0.5 * gate * gate) * 0.3989422804014327)
        curve = gate * share
        gated = curve * up
        grad = nn(out_grad_low, w_down[:, unit_columns[part]])
        gate_grad = grad * up * slope
        up_grad = grad * curve
        if part < 2:
            (gated_own, gated_other)[part][:, :UNITS] = gated.astype(BF16)
            pre_grads[part][:, :UNITS] = gate_grad.astype(BF16)
            pre_grads[part][:, UNITS : 2 * UNITS] = up_grad.astype(BF16)
        else:
            gated_own[:, UNITS:] = gated.astype(BF16)
            gated_other[:, UNITS:] = pltpu.roll(gated, HEAD_DIM, 1).astype(BF16)
            own = jnp.where(low, gate_grad, pltpu.roll(up_grad, 64, 1))
            other = jnp.where(low, pltpu.roll(gate_grad, 64, 1), up_grad)
            pre_grad_own[:, 2 * UNITS :] = own.astype(BF16)
            pre_grad_other[:, 2 * UNITS :] = other.astype(BF16)
    product = (
        nt(gated_own[...], w_down[:, THIRD:DOWN])
        + nt(gated_other[:, :UNITS], w_down[:, unit_columns[1]])
    )
    out_ref[...] = (hidden + product).astype(BF16)
    normed_grad = nt(pre_grad_own[...], w_in[:, :HALF]) + nt(pre_grad_other[...], w_in[:, HALF:])
    hidden_grad = out_grad + norm_backward(normed_grad, unit, factor, gain)
    hidden_grad_ref[...] = hidden_grad
    hidden_grad_low = hidden_grad.astype(BF16)
    low_grad_ref[...] = hidden_grad_low
    att_grad_own[...] = nn(hidden_grad_low, w_down[:, :THIRD]).astype(BF16)
    att_grad_other[...] = nn(hidden_grad_low, w_down[:, DOWN : DOWN + THIRD]).astype(BF16)


def attend_back_kernel(
    info,
    q_ref,
    probs_ref,
    grad_own,
    grad_other,
    cos_ref,
    sin_ref,
    cos_turned,
    sin_turned,
    qkv_ref,
    edge_ref,
    out_own,
    out_other,
    edge_out_ref,
    window,
    turned_keys,
    key_grad,
    value_grad,
    sems,
):
    step = pl.program_id(0)
    unit = identity()

    @pl.when(step == 0)
    def _():
        fill_window(info, qkv_ref, edge_ref, window, sems)
        turn_rows(unit, window, 0, 0, turned_keys)
        key_grad[...] = jnp.zeros_like(key_grad)
        value_grad[...] = jnp.zeros_like(value_grad)

    start = pl.multiple_of(step * LANES, LANES)
    span = pl.ds(start, SPAN)
    turn_rows(unit, window, 0, pl.multiple_of(start + LANES, LANES), turned_keys)
    cosine, sine = cos_turned[...], sin_turned[...]

    all_lanes = [slice(LANES * pair, LANES * (pair + 1)) for pair in range(PAIRS)]
    grads, probs_grads, score_grads, query_grads = [], [], [], []
    for pair, lanes in enumerate(all_lanes):
        grad_ref = grad_own if pair < 3 else grad_other
        grads.append(both_heads(grad_ref[:, LANES * (pair % 3) : LANES * (pair % 3 + 1)]))
        values = window[span, WIDTH + LANES * pair : WIDTH + LANES * (pair + 1)]
        probs_grads.append(nt(values, grads[pair]))
    for pair, lanes in enumerate(all_lanes):
        value_grad[span, lanes] += nn(probs_ref[0, pair], grads[pair])
    for pair in range(PAIRS):
        probs = probs_ref[0, pair].astype(F32)
        weighted = probs_grads[pair] * probs
        delta = jnp.sum(weighted, axis=0, keepdims=True)
        score_grads.append((weighted - probs * delta).astype(BF16))
    for pair, lanes in enumerate(all_lanes):
        query_grads.append(head_rows(nn(turned_keys[lanes, span], score_grads[pair])))
    for pair, lanes in enumerate(all_lanes):
        begin = HALF * (pair // 3) + LANES * (pair % 3)
        queries = both_heads(q_ref[:, begin : begin + LANES])
        key_grad[span, lanes] += nn(score_grads[pair], queries)
    for pair in range(PAIRS):
        grad = query_grads[pair] * (HEAD_DIM**-0.5)
        other = jnp.concatenate([grad[32:64], grad[:32], grad[96:], grad[64:96]], axis=0)
        query_grads[pair] = (grad * cosine - other * sine).astype(BF16)
    for pair in range(PAIRS):
        out_ref = out_own if pair < 3 else out_other
        place = slice(LANES * (pair % 3), LANES * (pair % 3 + 1))
        out_ref[pl.ds(start, LANES), place] = nt(unit, query_grads[pair]).astype(BF16)

    @pl.when(step == ROWS // LANES - 1)
    def _():
        inside = slice(WINDOW_HALF, WINDOW_HALF + ROWS)
        row = pl.multiple_of(jnp.where(info[1] == 1, 0, WINDOW_HALF + ROWS), 16)
        edge_rows = pl.ds(row, WINDOW_HALF)
        for pair in range(PAIRS):
            out_ref = out_own if pair < 3 else out_other
            lanes = slice(LANES * pair, LANES * (pair + 1))
            begin = LANES * (pair % 3)
            target = (LANES * pair + THIRD) % WIDTH
            keys_at = slice(THIRD + begin, THIRD + begin + LANES)
            values_at = slice(2 * THIRD + begin, 2 * THIRD + begin + LANES)
            out_ref[:ROWS, keys_at] = turned(
                key_grad[inside, lanes], cos_ref[inside, :], -sin_ref[inside, :]
            ).astype(BF16)
            out_ref[:ROWS, values_at] = value_grad[inside, lanes].astype(BF16)
            edge_keys = turned(
                key_grad[edge_rows, lanes], cos_ref[edge_rows, :], -sin_ref[edge_rows, :]
            ).astype(BF16)
            edge_values = value_grad[edge_rows, lanes].astype(BF16)
            edge_out_ref[:, target : target + LANES] = edge_keys
            edge_out_ref[:, WIDTH + target : WIDTH + target + LANES] = edge_values
            out_ref[ROWS:, begin : begin + LANES] = jnp.zeros((WINDOW_HALF, LANES), BF16)
            out_ref[ROWS:, keys_at] = edge_keys
            out_ref[ROWS:, values_at] = edge_values


def input_grad_kernel(
    info, x_ref, own_ref, other_ref, edge_ref, hidden_ref, gain_ref, weight, out_ref, fixed
):
    rows = x_ref.shape[0]
    step = pl.program_id(0)
    grad = None
    for half, grad_ref in enumerate((own_ref, other_ref)):
        fixed[...] = grad_ref[...]
        for core, at_step, begin in ((1, 0, 0), (0, ROWS // rows - 1, rows - WINDOW_HALF)):

            @pl.when((info[1] == core) & (step == at_step))
            def _():
                at = slice(begin, begin + WINDOW_HALF)
                for part in range(2):
                    to = slice(THIRD * (part + 1), THIRD * (part + 2))
                    source = WIDTH * part + THIRD * half
                    add = edge_ref[:, source : source + THIRD].astype(F32)
                    fixed[at, to] = (fixed[at, to].astype(F32) + add).astype(BF16)

        part = nt(fixed[...], weight[:, WIDE * half : WIDE * half + HALF])
        grad = part if grad is None else grad + part
    unit, factor = normalized(x_ref[...].astype(F32))
    out_ref[...] = hidden_ref[...] + norm_backward(grad, unit, factor, gain_ref[0:1, :])


def shape_of(shape, dtype=BF16):
    return jax.ShapeDtypeStruct(shape, dtype)


def call(
    kernel, info, grid, ins, in_specs, outs, out_specs, scratch, flops, vmem, after=()
):
    moved = sum(a.size * a.dtype.itemsize for a in list(ins) + list(outs))
    first = 1 + len(ins)
    later = first + len(after)
    return pl.pallas_call(
        lambda *refs: kernel(*refs[:first], *refs[later:]),
        out_shape=outs,
        grid_spec=pltpu.PrefetchScalarGridSpec(
            num_scalar_prefetch=1,
            grid=grid,
            in_specs=list(in_specs) + [ANYWHERE] * len(after),
            out_specs=out_specs,
            scratch_shapes=scratch,
        ),
        compiler_params=pltpu.CompilerParams(
            dimension_semantics=("arbitrary",), vmem_limit_bytes=vmem * MIB
        ),
        cost_estimate=pl.CostEstimate(
            flops=int(flops), bytes_accessed=int(moved), transcendentals=0
        ),
    )(info, *ins, *after)


def by_rows(rows, columns):
    return pl.BlockSpec((rows, columns), lambda i, s: (i, 0))


def full(*shape):
    return pl.BlockSpec(shape, lambda i, s: (0,) * len(shape))


def body(
    tokens,
    segment,
    norm_attn_gain,
    qkv_weight,
    attn_out_weight,
    norm_mlp_gain,
    in_weight,
    out_weight,
    cotangent,
):
    own_rows = norm_attn_gain.shape[0]
    core = lax.axis_index("tensor")
    place = lax.axis_index("dp") if by_exchange(own_rows) else 0
    info = jnp.stack([jnp.int32(place), core.astype(jnp.int32)])
    orders = (relative(own_rows, False), relative(own_rows, True))

    gains = jnp.pad(jnp.stack([norm_attn_gain, norm_mlp_gain], axis=1), ((0, 0), (0, LANES - 2)))
    flat_qkv = qkv_weight.reshape(own_rows, HALF)
    first_pieces = gather_start(jnp.concatenate([flat_qkv, gains], axis=1))
    shard_in = jnp.concatenate(
        [
            in_weight[:, 0, :UNITS],
            in_weight[:, 1, :UNITS],
            in_weight[:, 0, UNITS:],
            in_weight[:, 1, UNITS:],
        ],
        axis=1,
    )
    turned_out = out_weight.T
    blank = jnp.zeros((own_rows, HEAD_DIM), BF16)
    shard_down = jnp.concatenate([attn_out_weight.T, turned_out, blank], axis=1)
    second_shard = jnp.concatenate([shard_in, shard_down], axis=1)
    second_shard, *first_pieces = held_until([second_shard] + first_pieces)
    second_pieces = gather_start(second_shard)

    own_segment = lax.dynamic_slice_in_dim(segment, core * ROWS, ROWS, 0)
    seg_pad = jnp.pad(segment, (WINDOW_HALF, WINDOW_HALF), constant_values=-2)
    span_segment = lax.dynamic_slice_in_dim(seg_pad, core * ROWS, ROWS + 2 * WINDOW_HALF, 0)
    slot = core * ROWS - WINDOW_HALF + jnp.arange(ROWS + 2 * WINDOW_HALF, dtype=jnp.int32)
    position = jnp.where(span_segment >= 0, slot - PAD_BLOCK * span_segment, 0)
    lane = jnp.arange(LANES, dtype=jnp.int32)
    exponent = (lane % 32).astype(F32) * (2.0 / HEAD_DIM)
    angle = position.astype(F32)[:, None] * jnp.power(10000.0, -exponent)[None, :]
    cos_span = jnp.cos(angle)
    sin_span = jnp.sin(angle) * jnp.where((lane & 32) == 0, -1.0, 1.0)[None, :]
    cos_turned = cos_span[WINDOW_HALF:-WINDOW_HALF].T
    sin_turned = sin_span[WINDOW_HALF:-WINDOW_HALF].T
    col_seg = span_segment[:, None]
    row_seg = own_segment.reshape(ROWS // LANES, 1, LANES)
    live = (own_segment >= 0).astype(F32)[:, None]

    rows = 384
    steps = ROWS // rows
    first_pieces = held_until(
        first_pieces, cos_span, sin_span, cos_turned, sin_turned, col_seg, row_seg, live, info
    )
    first_held = joined(first_pieces)
    held_a, held_b = first_held[:, :, :FIRST_CUT], first_held[:, :, FIRST_CUT:]
    own_a = gather_finish(gather_middle(held_a, False), False)
    own_b = gather_finish(gather_middle(held_b, True), True)
    second_held = joined(second_pieces)
    held_in, held_down = second_held[:, :, :HALF], second_held[:, :, HALF:]
    own_a[-1], own_b[-1] = held_until((own_a[-1], own_b[-1]), held_in, held_down)
    own_a, own_b = [jnp.concatenate(own_a, axis=0)], [jnp.concatenate(own_b, axis=0)]
    other_a, other_b = [swapped_cores(own_a[0])], [swapped_cores(own_b[0])]

    parts = (own_a, other_a, own_b, other_b)
    counts_qkv = tuple(len(part) for part in parts)
    qkv, normed, gain_rows, edge, weight_qkv = call(
        lambda *refs: qkv_kernel(orders, counts_qkv, *refs),
        info,
        (steps,),
        [tokens, cos_span, sin_span] + [piece for part in parts for piece in part],
        [by_rows(rows, WIDTH), full(*cos_span.shape), full(*cos_span.shape)]
        + [ANYWHERE] * sum(counts_qkv),
        [
            shape_of((ROWS, 2 * HALF)),
            shape_of((MORE_ROWS, WIDTH)),
            shape_of((8, WIDTH), F32),
            shape_of((WINDOW_HALF, 3 * WIDTH)),
            shape_of((WIDTH, 2 * WIDE)),
        ],
        [by_rows(rows, 2 * HALF), by_rows(rows, WIDTH), full(8, WIDTH)]
        + [full(WINDOW_HALF, 3 * WIDTH), ANYWHERE],
        [
            pltpu.VMEM((WIDTH, 2 * WIDE), BF16),
            pltpu.SemaphoreType.DMA((2,)),
        ],
        2 * ROWS * WIDTH * 2 * HALF,
        28,
    )
    edge = swapped_cores(edge)
    normed = lax.dynamic_update_slice(normed, edge[:, 2 * WIDTH :], (ROWS, 0))
    held_in = gather_middle(held_in, False, qkv)
    held_down = gather_middle(held_down, True, qkv)
    in_own, down_own = gather_finish(held_in, False), gather_finish(held_down, True)

    blocks = ROWS // LANES
    window_shape = (ROWS + 2 * WINDOW_HALF, 2 * WIDTH)
    turned_shape = (WIDTH, ROWS + 2 * WINDOW_HALF)
    by_block = pl.BlockSpec((1, PAIRS, SPAN, SPAN), lambda i, s: (i, 0, 0, 0))
    att_own, att_other, probs = call(
        attend_kernel,
        info,
        (blocks,),
        [row_seg, col_seg, qkv, qkv, edge],
        [
            pl.BlockSpec((1, 1, LANES), lambda i, s: (i, 0, 0)),
            full(ROWS + 2 * WINDOW_HALF, 1),
            by_rows(LANES, 2 * HALF),
            ANYWHERE,
            ANYWHERE,
        ],
        [
            shape_of((ROWS, THIRD)),
            shape_of((ROWS, THIRD)),
            shape_of((blocks, PAIRS, SPAN, SPAN)),
        ],
        [by_rows(LANES, THIRD), by_rows(LANES, THIRD), by_block],
        [
            pltpu.VMEM(window_shape, BF16),
            pltpu.VMEM(turned_shape, BF16),
            pltpu.SemaphoreType.DMA((5,)),
        ],
        blocks * PAIRS * 2 * 2 * SPAN * SPAN * LANES,
        28,
        after=[held_in, held_down],
    )

    in_own[-1], down_own[-1] = held_until((in_own[-1], down_own[-1]), att_own)
    in_other = [swapped_cores(piece) for piece in in_own]
    down_other = [swapped_cores(piece) for piece in down_own]
    parts = (in_own, in_other, down_own, down_other)
    counts = tuple(len(part) for part in parts)
    (
        layer_out,
        hidden_grad,
        att_grad_own,
        att_grad_other,
        normed_two,
        gated_own,
        gated_other,
        pre_grad_own,
        pre_grad_other,
        hidden_grad_low,
        out_grad,
    ) = call(
        lambda *refs: mlp_kernel(orders, counts, *refs),
        info,
        (steps,),
        [tokens, att_own, att_other, cotangent, live, gain_rows]
        + [piece for part in parts for piece in part],
        [by_rows(rows, WIDTH), by_rows(rows, THIRD), by_rows(rows, THIRD), by_rows(rows, WIDTH)]
        + [by_rows(rows, 1), full(8, WIDTH)]
        + [ANYWHERE] * sum(counts),
        [
            shape_of((ROWS, WIDTH)),
            shape_of((ROWS, WIDTH), F32),
            shape_of((ROWS, THIRD)),
            shape_of((ROWS, THIRD)),
            shape_of((ROWS, WIDTH)),
            shape_of((ROWS, UNITS + LANES)),
            shape_of((ROWS, UNITS + LANES)),
            shape_of((ROWS, HALF)),
            shape_of((ROWS, HALF)),
            shape_of((ROWS, WIDTH)),
            shape_of((ROWS, WIDTH)),
        ],
        [by_rows(rows, WIDTH)] * 2
        + [by_rows(rows, THIRD)] * 2
        + [by_rows(rows, WIDTH)]
        + [by_rows(rows, UNITS + LANES)] * 2
        + [by_rows(rows, HALF)] * 2
        + [by_rows(rows, WIDTH)] * 2,
        [
            pltpu.VMEM((WIDTH, 2 * HALF), BF16),
            pltpu.VMEM((WIDTH, 2 * DOWN), BF16),
            pltpu.SemaphoreType.DMA((2,)),
        ],
        2 * ROWS * WIDTH * (4 * HALF + 2 * HALF + 2 * WIDTH),
        46,
    )

    def down_grads(att, gated):
        parts = [weight_grad(hidden_grad_low, att), weight_grad(out_grad, gated)]
        return jnp.concatenate(parts, axis=1)

    send_in = weight_grad(normed_two, pre_grad_other)
    send_down = down_grads(att_other, gated_other)
    keep_in = weight_grad(normed_two, pre_grad_own)
    keep_down = down_grads(att_own, gated_own)
    sum_in, in_back, in_sent = scatter_start(keep_in, swapped_cores(send_in), own_rows, False)
    sum_down, down_back, down_sent = scatter_start(keep_down, swapped_cores(send_down), own_rows, True)

    grad_own, grad_other, edge_grad = call(
        attend_back_kernel,
        info,
        (blocks,),
        [qkv, probs, att_grad_own, att_grad_other, cos_span, sin_span]
        + [cos_turned, sin_turned, qkv, edge],
        [by_rows(LANES, 2 * HALF), by_block, by_rows(LANES, THIRD), by_rows(LANES, THIRD)]
        + [full(*cos_span.shape)] * 2
        + [pl.BlockSpec((LANES, LANES), lambda i, s: (0, i))] * 2
        + [ANYWHERE] * 2,
        [shape_of((MORE_ROWS, HALF))] * 2 + [shape_of((WINDOW_HALF, 2 * WIDTH))],
        [full(MORE_ROWS, HALF)] * 2 + [full(WINDOW_HALF, 2 * WIDTH)],
        [
            pltpu.VMEM(window_shape, BF16),
            pltpu.VMEM(turned_shape, BF16),
            pltpu.VMEM((window_shape[0], WIDTH), F32),
            pltpu.VMEM((window_shape[0], WIDTH), F32),
            pltpu.SemaphoreType.DMA((5,)),
        ],
        blocks * PAIRS * 4 * 2 * SPAN * SPAN * LANES,
        46,
        after=[send_in, send_down, keep_in, keep_down],
    )
    edge_grad = swapped_cores(edge_grad)
    (normed,) = held_until((normed,), in_sent[2], down_sent[2])

    send_a = weight_grad(normed, grad_other[:, :FIRST_CUT])
    send_b = weight_grad(normed, grad_other[:, FIRST_CUT:])
    keep_a = weight_grad(normed, grad_own[:, :FIRST_CUT])
    keep_b = weight_grad(normed, grad_own[:, FIRST_CUT:])
    late_a, late_b = swapped_cores(send_a), swapped_cores(send_b)

    (grad_tokens,) = call(
        input_grad_kernel,
        info,
        (steps,),
        [tokens, grad_own, grad_other, edge_grad, hidden_grad, gain_rows, weight_qkv],
        [by_rows(rows, WIDTH), by_rows(rows, HALF), by_rows(rows, HALF)]
        + [full(WINDOW_HALF, 2 * WIDTH), by_rows(rows, WIDTH)]
        + [full(8, WIDTH), full(WIDTH, 2 * WIDE)],
        [shape_of((ROWS, WIDTH), F32)],
        [by_rows(rows, WIDTH)],
        [pltpu.VMEM((rows, HALF), BF16)],
        2 * ROWS * WIDTH * 2 * HALF,
        28,
        after=[keep_a, keep_b, late_a, late_b, in_back[2], down_back[2]],
    )
    sum_in, sum_down = held_until((sum_in, sum_down), late_a, late_b)
    owned_early = scatter_finish(sum_in, sum_down)
    gates = (grad_tokens, owned_early)
    sum_a, unused, unused = scatter_start(keep_a, late_a, own_rows, False, gates)
    sum_b, unused, unused = scatter_start(keep_b, late_b, own_rows, True, gates)
    owned_in, owned_down = owned_early[:, :HALF], owned_early[:, HALF:]

    flat_grad = scatter_finish(sum_a, sum_b)
    gain_grads = jnp.stack(
        [
            gain_part(flat_qkv, flat_grad, norm_attn_gain),
            gain_part(shard_in, owned_in, norm_mlp_gain),
        ]
    )
    gain_grads = gain_grads + swapped_cores(gain_grads)
    owned_gain_one, owned_gain_two = gain_grads[0], gain_grads[1]
    owned_qkv = flat_grad.reshape(own_rows, 3, THIRD)
    owned_in = jnp.stack(
        [
            jnp.concatenate([owned_in[:, :UNITS], owned_in[:, 2 * UNITS : -64]], axis=1),
            jnp.concatenate([owned_in[:, UNITS : 2 * UNITS], owned_in[:, -64:]], axis=1),
        ],
        axis=1,
    )
    owned_attn = owned_down[:, :THIRD].T
    owned_out = owned_down[:, THIRD : THIRD + UNITS + HEAD_DIM].T
    return (
        layer_out,
        grad_tokens,
        owned_gain_one,
        owned_qkv,
        owned_attn,
        owned_gain_two,
        owned_in,
        owned_out,
    )


def solution(mesh):
    placed = (
        P(("dp", "tensor"), None),
        P("dp"),
        P("dp"),
        P("dp", None, "tensor"),
        P("tensor", "dp"),
        P("dp"),
        P("dp", None, "tensor"),
        P("tensor", "dp"),
        P(("dp", "tensor"), None),
    )
    return jax.shard_map(
        body,
        mesh=mesh,
        in_specs=placed,
        out_specs=(
            P(("dp", "tensor"), None),
            P(("dp", "tensor"), None),
            P("dp"),
            P("dp", None, "tensor"),
            P("tensor", "dp"),
            P("dp"),
            P("dp", None, "tensor"),
            P("tensor", "dp"),
        ),
        check_vma=False,
    )
```

```python
import jax
import jax.numpy as jnp
from jax import lax
from jax.experimental import pallas as pl
from jax.experimental.pallas import tpu as pltpu
from jax.sharding import PartitionSpec as P

HEAD_DIM = 64
WINDOW_HALF = 64
PAD_BLOCK = 128
WIDTH = 768
ROWS = 1152
MORE_ROWS = ROWS + 64
HALF = 1152
LANES = 128
THIRD = 384
PAIRS = 6
SPAN = 2 * LANES
PIECES = ROWS // LANES + 1
UNITS = 512
FIRST_CUT = 640
WIDE = HALF + LANES
DOWN = 384 + UNITS + LANES
MIB = 2**20
ANYWHERE = pl.BlockSpec(memory_space=pl.ANY)
F32 = jnp.float32
BF16 = jnp.bfloat16


def steps_of(devices, swapped):
    bits = [1 << i for i in range(devices.bit_length() - 1)]
    near, far = bits[:2], bits[2:]
    return far + (near if swapped else near[::-1])


def exchanged(block, mask):
    devices = lax.axis_size("dp")
    return lax.ppermute(block, "dp", [(i, i ^ mask) for i in range(devices)])


def swapped_cores(block):
    return lax.ppermute(block, "tensor", [(0, 1), (1, 0)])


def by_exchange(own_rows):
    devices = lax.axis_size("dp")
    return own_rows % 16 == 0 and devices & (devices - 1) == 0


def relative(own_rows, swapped):
    if not by_exchange(own_rows):
        return list(range(WIDTH // 48))
    order = [0]
    for mask in steps_of(lax.axis_size("dp"), swapped):
        order = order + [r ^ mask for r in order]
    return order


def held_until(arrays, *gates):
    return lax.optimization_barrier((tuple(arrays), gates))[0]


def gather_start(shard):
    masks = steps_of(lax.axis_size("dp"), False)
    held = shard[None]
    if not by_exchange(shard.shape[0]) or len(masks) <= 3:
        return [held]
    first, second = masks[:2]
    return [held] + [exchanged(held, mask) for mask in (first, second, first ^ second)]


def joined(pieces):
    return lax.optimization_barrier(jnp.concatenate(pieces, axis=0))


def gather_middle(held, swapped, gate=None):
    if by_exchange(held.shape[1]):
        masks = steps_of(lax.axis_size("dp"), swapped)
        for mask in masks[held.shape[0].bit_length() - 1 : -1]:
            arrived = exchanged(held, mask)
            if gate is not None:
                (arrived,) = held_until((arrived,), gate)
            held = jnp.concatenate([held, arrived], axis=0)
    return held


def gather_finish(held, swapped):
    if not by_exchange(held.shape[1]):
        whole = lax.all_gather(held[0], "dp", axis=0, tiled=True)
        return [whole.reshape(WIDTH // 48, 48, held.shape[2])]
    return [held, exchanged(held, steps_of(lax.axis_size("dp"), swapped)[-1])]


def scatter_start(keep, other, own_rows, swapped, first_gates=None):
    arrivals, sents = [other], [other]
    if not by_exchange(own_rows):
        total = keep.astype(F32) + other.astype(F32)
        total = lax.psum_scatter(total, "dp", scatter_dimension=0, tiled=True)
        return total[None], arrivals * 3, sents * 3
    devices = lax.axis_size("dp")
    index = lax.axis_index("dp")
    levels = devices.bit_length() - 1
    masks = steps_of(devices, swapped)
    last = 2 if len(masks) > 3 else 0
    shape = (2,) * levels + (own_rows, keep.shape[1])
    keep, other = keep.reshape(shape), other.reshape(shape)
    for mask in reversed(masks[last:]):
        axis = levels - mask.bit_length()
        bit = (index & mask) // mask
        part = lambda array, which: lax.dynamic_slice_in_dim(array, which, 1, axis).astype(F32)
        sent = (part(keep, 1 - bit) + part(other, 1 - bit)).astype(BF16)
        kept = (part(keep, bit) + part(other, bit)).astype(BF16)
        other = exchanged(sent, mask)
        arrivals.append(other)
        sents.append(sent)
        if first_gates is not None and len(arrivals) == 2:
            (other,) = held_until((other,), *first_gates)
        keep = kept
    total = keep.astype(F32) + other.astype(F32)
    return total.reshape(2**last, own_rows, -1), arrivals + [other] * 3, sents + [other] * 3


def scatter_finish(*totals):
    if totals[0].shape[0] == 1:
        return jnp.concatenate([total[0] for total in totals], axis=1)
    unit = steps_of(lax.axis_size("dp"), False)[0]
    place = (lax.axis_index("dp") // unit) % 4

    def rows_of(which):
        parts = [lax.dynamic_index_in_dim(total, which, 0, keepdims=False) for total in totals]
        return jnp.concatenate(parts, axis=1)

    arrived = [
        exchanged(rows_of(place ^ j).astype(BF16), unit * j).astype(F32) for j in range(1, 4)
    ]
    return rows_of(place) + (arrived[0] + arrived[1] + arrived[2])


def weight_grad(left, right):
    return lax.dot_general(
        left, right, (((0,), (0,)), ((), ())), preferred_element_type=F32
    ).astype(BF16)


def gain_part(weight, grad, gain):
    return jnp.sum(weight.astype(F32) * grad, axis=1) / gain.astype(F32)


def nt(left, right):
    return lax.dot_general(left, right, (((1,), (1,)), ((), ())), preferred_element_type=F32)


def nn(left, right):
    return jnp.dot(left, right, preferred_element_type=F32)


def start_slots(info, pieces, order, segments, sems):
    slot = 0
    for piece in pieces:
        rows = piece.shape[1]
        for at in range(piece.shape[0]):
            row = pl.multiple_of((info[0] ^ order[slot]) * rows, 16)
            for begin, width, target, column, sem in segments:
                pltpu.make_async_copy(
                    piece.at[at, :, pl.ds(begin, width)],
                    target.at[pl.ds(row, rows), pl.ds(column, width)],
                    sems.at[sem],
                ).start()
            slot += 1


def wait_whole(ref, sem):
    pltpu.make_async_copy(ref, ref, sem).wait()


def start_window(info, qkv_ref, edge_ref, window, sems):
    core = info[1]
    first = pl.multiple_of(jnp.where(core == 1, 0, WINDOW_HALF + ROWS), 16)
    last = pl.multiple_of(jnp.where(core == 1, WINDOW_HALF + ROWS, 0), 16)
    edge = pltpu.make_async_copy(
        edge_ref.at[:, pl.ds(0, 2 * WIDTH)],
        window.at[pl.ds(first, WINDOW_HALF), :],
        sems.at[PIECES],
    )
    edge.start()
    for piece in range(PIECES):
        begin, stop = piece_rows(piece)
        for part in range(2):
            for half in range(2):
                source = HALF * half + THIRD * (part + 1)
                target = WIDTH * part + THIRD * half
                pltpu.make_async_copy(
                    qkv_ref.at[pl.ds(begin - WINDOW_HALF, stop - begin), pl.ds(source, THIRD)],
                    window.at[pl.ds(begin, stop - begin), pl.ds(target, THIRD)],
                    sems.at[piece],
                ).start()
    window[pl.ds(last, WINDOW_HALF), :] = jnp.zeros((WINDOW_HALF, 2 * WIDTH), BF16)
    edge.wait()


def piece_rows(piece):
    return max(LANES * piece, WINDOW_HALF), min(LANES * (piece + 1), WINDOW_HALF + ROWS)


def wait_window(window, step, sems):
    @pl.when(step == 0)
    def _():
        for piece in range(2):
            begin, stop = piece_rows(piece)
            wait_whole(window.at[pl.ds(begin, stop - begin), :], sems.at[piece])

    @pl.when((step > 0) & (step < PIECES - 2))
    def _():
        row = pl.multiple_of((step + 1) * LANES, LANES)
        wait_whole(window.at[pl.ds(row, LANES), :], sems.at[step + 1])

    @pl.when(step == PIECES - 2)
    def _():
        begin, stop = piece_rows(PIECES - 1)
        wait_whole(window.at[pl.ds(begin, stop - begin), :], sems.at[PIECES - 1])


def identity():
    row = lax.broadcasted_iota(jnp.int32, (LANES, LANES), 0)
    lane = lax.broadcasted_iota(jnp.int32, (LANES, LANES), 1)
    return jnp.where(row == lane, 1.0, 0.0).astype(BF16)


def turn_rows(unit, window, begin, row, turned_ref):
    for pair in range(PAIRS):
        lanes = slice(LANES * pair, LANES * (pair + 1))
        block = window[pl.ds(row, LANES), begin + LANES * pair : begin + LANES * (pair + 1)]
        turned_ref[lanes, pl.ds(row, LANES)] = nt(unit, block).astype(BF16)


def head_rows(columns):
    return jnp.concatenate([columns[:HEAD_DIM, :LANES], columns[HEAD_DIM:, LANES:]], axis=0)


def normalized(values):
    centred = values - jnp.mean(values, axis=-1, keepdims=True)
    spread = jnp.mean(centred * centred, axis=-1, keepdims=True)
    factor = lax.rsqrt(spread + 1e-05)
    return centred * factor, factor


def norm_backward(grad, unit, factor, gain):
    inner = grad * gain
    mean = jnp.mean(inner, axis=-1, keepdims=True)
    along = jnp.mean(inner * unit, axis=-1, keepdims=True)
    return factor * (inner - mean - unit * along)


def turned(values, cosine, sine):
    lane = lax.broadcasted_iota(jnp.int32, values.shape, 1)
    first = (lane & 32) == 0
    other = jnp.where(first, pltpu.roll(values, 96, 1), pltpu.roll(values, 32, 1))
    return values * cosine + other * sine


def both_heads(block):
    lane = lax.broadcasted_iota(jnp.int32, block.shape, 1)
    first = jnp.where(lane < HEAD_DIM, 1.0, 0.0).astype(block.dtype)
    second = jnp.where(lane < HEAD_DIM, 0.0, 1.0).astype(block.dtype)
    return jnp.concatenate([block * first, block * second], axis=0)


def table_kernel(cos_in, sin_in, seg_ref, cos_ref, sin_ref, cos_turned, sin_turned, col_ref):
    cos_ref[...] = cos_in[...]
    sin_ref[...] = sin_in[...]
    for block in range(ROWS // LANES):
        rows = slice(WINDOW_HALF + LANES * block, WINDOW_HALF + LANES * (block + 1))
        lanes = slice(LANES * block, LANES * (block + 1))
        cos_turned[:, lanes] = cos_in[rows, :].T
        sin_turned[:, lanes] = sin_in[rows, :].T
    for block in range(PIECES):
        row = jnp.broadcast_to(seg_ref[block : block + 1, :].astype(F32), (LANES, LANES))
        col_ref[LANES * block : LANES * (block + 1), :] = row.T.astype(jnp.int32)


def qkv_kernel(orders, counts, info, x_ref, cos_ref, sin_ref, *refs):
    parts = []
    for count in counts:
        parts.append(refs[:count])
        refs = refs[count:]
    own_a, other_a, own_b, other_b = parts
    qkv_ref, normed_ref, gain_ref, edge_ref, weight_ref, weight, sems = refs
    step = pl.program_id(0)
    rows = x_ref.shape[0]

    @pl.when(step == 0)
    def _():
        for begin, part_a, part_b in ((0, own_a, own_b), (WIDE, other_a, other_b)):
            start_slots(info, part_a, orders[0], [(0, FIRST_CUT, weight, begin, 0)], sems)
            start_slots(
                info,
                part_b,
                orders[1],
                [(0, WIDE - FIRST_CUT, weight, begin + FIRST_CUT, 0)],
                sems,
            )
        wait_whole(weight, sems.at[0])
        pltpu.make_async_copy(weight, weight_ref, sems.at[1]).start()
        row = lax.broadcasted_iota(jnp.int32, (16, LANES), 0)
        lane = lax.broadcasted_iota(jnp.int32, (16, LANES), 1)
        pick = jnp.where(row == lane, 1.0, 0.0).astype(BF16)
        gain_ref[...] = nt(pick, weight[:, HALF:WIDE])[:8]

    unit, unused = normalized(x_ref[...].astype(F32))
    normed = (unit * gain_ref[0:1, :]).astype(BF16)
    normed_ref[...] = normed
    table_rows = pl.ds(pl.multiple_of(WINDOW_HALF + step * rows, WINDOW_HALF), rows)
    cosine, sine = cos_ref[table_rows, :], sin_ref[table_rows, :]
    for half in range(2):
        result = nn(normed, weight[:, WIDE * half : WIDE * half + HALF])
        for tile in range(9):
            block = result[:, LANES * tile : LANES * (tile + 1)]
            if tile < 6:
                block = turned(block, cosine, sine)
            if tile < 3:
                block = block * (HEAD_DIM**-0.5)
            begin = HALF * half + LANES * tile
            qkv_ref[:, begin : begin + LANES] = block.astype(BF16)

    for core, at_step, begin in ((1, 0, 0), (0, ROWS // rows - 1, rows - WINDOW_HALF)):

        @pl.when((info[1] == core) & (step == at_step))
        def _():
            for part in range(2):
                for half in range(2):
                    source = HALF * half + THIRD * (part + 1)
                    target = WIDTH * part + THIRD * (1 - half)
                    edge_ref[:, target : target + THIRD] = qkv_ref[
                        begin : begin + WINDOW_HALF, source : source + THIRD
                    ]
            edge_ref[:, 2 * WIDTH :] = normed_ref[begin : begin + WINDOW_HALF, :]

    @pl.when(step == ROWS // rows - 1)
    def _():
        pltpu.make_async_copy(weight, weight_ref, sems.at[1]).wait()


def attend_kernel(
    info, row_seg, col_seg, q_ref, qkv_ref, edge_ref, own_ref, other_ref, probs_ref, window, turned_values, sems
):
    step = pl.program_id(0)
    unit = identity()

    @pl.when(step == 0)
    def _():
        start_window(info, qkv_ref, edge_ref, window, sems)

    wait_window(window, step, sems)

    @pl.when(step == 0)
    def _():
        turn_rows(unit, window, WIDTH, 0, turned_values)

    start = pl.multiple_of(step * LANES, LANES)
    turn_rows(unit, window, WIDTH, pl.multiple_of(start + LANES, LANES), turned_values)
    key_seg = col_seg[pl.ds(start, SPAN), :]
    key_at = lax.broadcasted_iota(jnp.int32, (SPAN, LANES), 0) - WINDOW_HALF
    query_at = lax.broadcasted_iota(jnp.int32, (SPAN, LANES), 1)
    near = jnp.abs(key_at - query_at) <= WINDOW_HALF
    allowed = (key_seg == row_seg[0]) & near
    bias = jnp.where(allowed, 0.0, -1e30)
    bias = jnp.concatenate([bias, bias], axis=1)

    scores, probs, results = [], [], []
    for pair in range(PAIRS):
        begin = HALF * (pair // 3) + LANES * (pair % 3)
        queries = both_heads(q_ref[:, begin : begin + LANES])
        keys = window[pl.ds(start, SPAN), LANES * pair : LANES * (pair + 1)]
        scores.append(nt(keys, queries) + bias)
    for pair in range(PAIRS):
        weights = jnp.exp(scores[pair] - jnp.max(scores[pair], axis=0, keepdims=True))
        total = jnp.sum(weights, axis=0, keepdims=True)
        probs.append((weights * (1.0 / total)).astype(BF16))
        probs_ref[0, pair] = probs[pair]
    for pair in range(PAIRS):
        values = turned_values[LANES * pair : LANES * (pair + 1), pl.ds(start, SPAN)]
        results.append(head_rows(nn(values, probs[pair])).astype(BF16))
    for pair in range(PAIRS):
        out_ref = own_ref if pair < 3 else other_ref
        out_ref[:, LANES * (pair % 3) : LANES * (pair % 3 + 1)] = nt(unit, results[pair]).astype(
            BF16
        )


def mlp_kernel(orders, counts, info, x_ref, att_own, att_other, cot_ref, col_seg, gain_ref, *refs):
    parts = []
    for count in counts:
        parts.append(refs[:count])
        refs = refs[count:]
    in_own, in_other, down_own, down_other = parts
    (
        out_ref,
        hidden_grad_ref,
        att_grad_own,
        att_grad_other,
        normed_ref,
        gated_own,
        gated_other,
        pre_grad_own,
        pre_grad_other,
        low_grad_ref,
        out_grad_ref,
        w_in,
        w_down,
        sems,
    ) = refs
    step = pl.program_id(0)

    @pl.when(step == 0)
    def _():
        for number, part in enumerate((down_own, down_other)):
            start_slots(info, part, orders[1], [(0, DOWN, w_down, DOWN * number, 0)], sems)
        for number, part in enumerate((in_own, in_other)):
            start_slots(info, part, orders[0], [(0, HALF, w_in, HALF * number, 1)], sems)
        wait_whole(w_down, sems.at[0])
        other = pltpu.roll(w_down[:, 2 * DOWN - LANES :].astype(F32), HEAD_DIM, 1).astype(BF16)
        w_down[:, DOWN - LANES : DOWN] += other

    gain = gain_ref[1:2, :]
    hidden = (
        x_ref[...].astype(F32)
        + nt(att_own[...], w_down[:, :THIRD])
        + nt(att_other[...], w_down[:, DOWN : DOWN + THIRD])
    )
    unit, factor = normalized(hidden)
    normed = (unit * gain).astype(BF16)
    normed_ref[...] = normed
    seg_rows = pl.ds(pl.multiple_of(WINDOW_HALF + step * x_ref.shape[0], WINDOW_HALF), x_ref.shape[0])
    live = jnp.where(col_seg[seg_rows, :] >= 0, 1.0, 0.0)
    live = jnp.concatenate([live] * (WIDTH // LANES), axis=1)
    out_grad = cot_ref[...].astype(F32) * live
    out_grad_low = out_grad.astype(BF16)
    out_grad_ref[...] = out_grad_low

    @pl.when(step == 0)
    def _():
        wait_whole(w_in, sems.at[1])

    pre = [nn(normed, w_in[:, HALF * half : HALF * (half + 1)]) for half in range(2)]
    tails = [part[:, 2 * UNITS :] for part in pre]
    lane = lax.broadcasted_iota(jnp.int32, tails[0].shape, 1)
    low = lane < HEAD_DIM
    gates = [part[:, :UNITS] for part in pre]
    gates.append(jnp.where(low, tails[0], pltpu.roll(tails[1], 64, 1)))
    ups = [part[:, UNITS : 2 * UNITS] for part in pre]
    ups.append(jnp.where(low, pltpu.roll(tails[0], 64, 1), tails[1]))
    pre_grads = (pre_grad_own, pre_grad_other)
    unit_columns = (
        slice(THIRD, THIRD + UNITS),
        slice(DOWN + THIRD, DOWN + THIRD + UNITS),
        slice(DOWN - LANES, DOWN),
    )
    for part, (gate, up) in enumerate(zip(gates, ups)):
        share = 0.5 + 0.5 * lax.erf(gate * (0.5**0.5))
        slope = share + gate * (jnp.exp(-0.5 * gate * gate) * 0.3989422804014327)
        curve = gate * share
        gated = curve * up
        grad = nn(out_grad_low, w_down[:, unit_columns[part]])
        gate_grad = grad * up * slope
        up_grad = grad * curve
        if part < 2:
            (gated_own, gated_other)[part][:, :UNITS] = gated.astype(BF16)
            pre_grads[part][:, :UNITS] = gate_grad.astype(BF16)
            pre_grads[part][:, UNITS : 2 * UNITS] = up_grad.astype(BF16)
        else:
            gated_own[:, UNITS:] = gated.astype(BF16)
            gated_other[:, UNITS:] = pltpu.roll(gated, HEAD_DIM, 1).astype(BF16)
            own = jnp.where(low, gate_grad, pltpu.roll(up_grad, 64, 1))
            other = jnp.where(low, pltpu.roll(gate_grad, 64, 1), up_grad)
            pre_grad_own[:, 2 * UNITS :] = own.astype(BF16)
            pre_grad_other[:, 2 * UNITS :] = other.astype(BF16)
    product = (
        nt(gated_own[...], w_down[:, THIRD:DOWN])
        + nt(gated_other[:, :UNITS], w_down[:, unit_columns[1]])
    )
    out_ref[...] = (hidden + product).astype(BF16)
    normed_grad = nt(pre_grad_own[...], w_in[:, :HALF]) + nt(pre_grad_other[...], w_in[:, HALF:])
    hidden_grad = out_grad + norm_backward(normed_grad, unit, factor, gain)
    hidden_grad_ref[...] = hidden_grad
    hidden_grad_low = hidden_grad.astype(BF16)
    low_grad_ref[...] = hidden_grad_low
    att_grad_own[...] = nn(hidden_grad_low, w_down[:, :THIRD]).astype(BF16)
    att_grad_other[...] = nn(hidden_grad_low, w_down[:, DOWN : DOWN + THIRD]).astype(BF16)


def attend_back_kernel(
    info,
    q_ref,
    probs_ref,
    grad_own,
    grad_other,
    cos_ref,
    sin_ref,
    cos_turned,
    sin_turned,
    qkv_ref,
    edge_ref,
    out_own,
    out_other,
    edge_out_ref,
    window,
    turned_keys,
    key_grad,
    value_grad,
    sems,
):
    step = pl.program_id(0)
    unit = identity()

    @pl.when(step == 0)
    def _():
        start_window(info, qkv_ref, edge_ref, window, sems)
        key_grad[...] = jnp.zeros_like(key_grad)
        value_grad[...] = jnp.zeros_like(value_grad)

    wait_window(window, step, sems)

    @pl.when(step == 0)
    def _():
        turn_rows(unit, window, 0, 0, turned_keys)

    start = pl.multiple_of(step * LANES, LANES)
    span = pl.ds(start, SPAN)
    turn_rows(unit, window, 0, pl.multiple_of(start + LANES, LANES), turned_keys)
    cosine, sine = cos_turned[...], sin_turned[...]

    all_lanes = [slice(LANES * pair, LANES * (pair + 1)) for pair in range(PAIRS)]
    grads, probs_grads, score_grads, query_grads = [], [], [], []
    for pair, lanes in enumerate(all_lanes):
        grad_ref = grad_own if pair < 3 else grad_other
        grads.append(both_heads(grad_ref[:, LANES * (pair % 3) : LANES * (pair % 3 + 1)]))
        values = window[span, WIDTH + LANES * pair : WIDTH + LANES * (pair + 1)]
        probs_grads.append(nt(values, grads[pair]))
    for pair, lanes in enumerate(all_lanes):
        value_grad[span, lanes] += nn(probs_ref[0, pair], grads[pair])
    for pair in range(PAIRS):
        probs = probs_ref[0, pair].astype(F32)
        weighted = probs_grads[pair] * probs
        delta = jnp.sum(weighted, axis=0, keepdims=True)
        score_grads.append((weighted - probs * delta).astype(BF16))
    for pair, lanes in enumerate(all_lanes):
        query_grads.append(head_rows(nn(turned_keys[lanes, span], score_grads[pair])))
    for pair, lanes in enumerate(all_lanes):
        begin = HALF * (pair // 3) + LANES * (pair % 3)
        queries = both_heads(q_ref[:, begin : begin + LANES])
        key_grad[span, lanes] += nn(score_grads[pair], queries)
    for pair in range(PAIRS):
        grad = query_grads[pair] * (HEAD_DIM**-0.5)
        other = jnp.concatenate([grad[32:64], grad[:32], grad[96:], grad[64:96]], axis=0)
        query_grads[pair] = (grad * cosine - other * sine).astype(BF16)
    for pair in range(PAIRS):
        out_ref = out_own if pair < 3 else out_other
        place = slice(LANES * (pair % 3), LANES * (pair % 3 + 1))
        out_ref[pl.ds(start, LANES), place] = nt(unit, query_grads[pair]).astype(BF16)

    @pl.when(step == ROWS // LANES - 1)
    def _():
        inside = slice(WINDOW_HALF, WINDOW_HALF + ROWS)
        row = pl.multiple_of(jnp.where(info[1] == 1, 0, WINDOW_HALF + ROWS), 16)
        edge_rows = pl.ds(row, WINDOW_HALF)
        for pair in range(PAIRS):
            out_ref = out_own if pair < 3 else out_other
            lanes = slice(LANES * pair, LANES * (pair + 1))
            begin = LANES * (pair % 3)
            target = (LANES * pair + THIRD) % WIDTH
            keys_at = slice(THIRD + begin, THIRD + begin + LANES)
            values_at = slice(2 * THIRD + begin, 2 * THIRD + begin + LANES)
            out_ref[:ROWS, keys_at] = turned(
                key_grad[inside, lanes], cos_ref[inside, :], -sin_ref[inside, :]
            ).astype(BF16)
            out_ref[:ROWS, values_at] = value_grad[inside, lanes].astype(BF16)
            edge_keys = turned(
                key_grad[edge_rows, lanes], cos_ref[edge_rows, :], -sin_ref[edge_rows, :]
            ).astype(BF16)
            edge_values = value_grad[edge_rows, lanes].astype(BF16)
            edge_out_ref[:, target : target + LANES] = edge_keys
            edge_out_ref[:, WIDTH + target : WIDTH + target + LANES] = edge_values
            out_ref[ROWS:, begin : begin + LANES] = jnp.zeros((WINDOW_HALF, LANES), BF16)
            out_ref[ROWS:, keys_at] = edge_keys
            out_ref[ROWS:, values_at] = edge_values


def input_grad_kernel(
    info, x_ref, own_ref, other_ref, edge_ref, hidden_ref, gain_ref, weight, out_ref, fixed
):
    rows = x_ref.shape[0]
    step = pl.program_id(0)
    grad = None
    for half, grad_ref in enumerate((own_ref, other_ref)):
        fixed[...] = grad_ref[...]
        for core, at_step, begin in ((1, 0, 0), (0, ROWS // rows - 1, rows - WINDOW_HALF)):

            @pl.when((info[1] == core) & (step == at_step))
            def _():
                at = slice(begin, begin + WINDOW_HALF)
                for part in range(2):
                    to = slice(THIRD * (part + 1), THIRD * (part + 2))
                    source = WIDTH * part + THIRD * half
                    add = edge_ref[:, source : source + THIRD].astype(F32)
                    fixed[at, to] = (fixed[at, to].astype(F32) + add).astype(BF16)

        part = nt(fixed[...], weight[:, WIDE * half : WIDE * half + HALF])
        grad = part if grad is None else grad + part
    unit, factor = normalized(x_ref[...].astype(F32))
    out_ref[...] = hidden_ref[...] + norm_backward(grad, unit, factor, gain_ref[0:1, :])


def shape_of(shape, dtype=BF16):
    return jax.ShapeDtypeStruct(shape, dtype)


def call(
    kernel, info, grid, ins, in_specs, outs, out_specs, scratch, flops, vmem, after=()
):
    moved = sum(a.size * a.dtype.itemsize for a in list(ins) + list(outs))
    first = 1 + len(ins)
    later = first + len(after)
    return pl.pallas_call(
        lambda *refs: kernel(*refs[:first], *refs[later:]),
        out_shape=outs,
        grid_spec=pltpu.PrefetchScalarGridSpec(
            num_scalar_prefetch=1,
            grid=grid,
            in_specs=list(in_specs) + [ANYWHERE] * len(after),
            out_specs=out_specs,
            scratch_shapes=scratch,
        ),
        compiler_params=pltpu.CompilerParams(
            dimension_semantics=("arbitrary",), vmem_limit_bytes=vmem * MIB
        ),
        cost_estimate=pl.CostEstimate(
            flops=int(flops), bytes_accessed=int(moved), transcendentals=0
        ),
    )(info, *ins, *after)


def by_rows(rows, columns):
    return pl.BlockSpec((rows, columns), lambda i, s: (i, 0))


def full(*shape):
    return pl.BlockSpec(shape, lambda i, s: (0,) * len(shape))


def body(
    tokens,
    segment,
    norm_attn_gain,
    qkv_weight,
    attn_out_weight,
    norm_mlp_gain,
    in_weight,
    out_weight,
    cotangent,
):
    own_rows = norm_attn_gain.shape[0]
    core = lax.axis_index("tensor")
    place = lax.axis_index("dp") if by_exchange(own_rows) else 0
    info = jnp.stack([jnp.int32(place), core.astype(jnp.int32)])
    orders = (relative(own_rows, False), relative(own_rows, True))

    gains = jnp.pad(jnp.stack([norm_attn_gain, norm_mlp_gain], axis=1), ((0, 0), (0, LANES - 2)))
    flat_qkv = qkv_weight.reshape(own_rows, HALF)
    first_pieces = gather_start(jnp.concatenate([flat_qkv, gains], axis=1))
    shard_in = jnp.concatenate(
        [
            in_weight[:, 0, :UNITS],
            in_weight[:, 1, :UNITS],
            in_weight[:, 0, UNITS:],
            in_weight[:, 1, UNITS:],
        ],
        axis=1,
    )
    turned_out = out_weight.T
    blank = jnp.zeros((own_rows, HEAD_DIM), BF16)
    shard_down = jnp.concatenate([attn_out_weight.T, turned_out, blank], axis=1)
    second_shard = jnp.concatenate([shard_in, shard_down], axis=1)
    second_shard, *first_pieces = held_until([second_shard] + first_pieces)
    second_pieces = gather_start(second_shard)

    own_segment = lax.dynamic_slice_in_dim(segment, core * ROWS, ROWS, 0)
    seg_pad = jnp.pad(segment, (WINDOW_HALF, WINDOW_HALF), constant_values=-2)
    span_segment = lax.dynamic_slice_in_dim(seg_pad, core * ROWS, ROWS + 2 * WINDOW_HALF, 0)
    slot = core * ROWS - WINDOW_HALF + jnp.arange(ROWS + 2 * WINDOW_HALF, dtype=jnp.int32)
    position = jnp.where(span_segment >= 0, slot - PAD_BLOCK * span_segment, 0)
    lane = jnp.arange(LANES, dtype=jnp.int32)
    exponent = (lane % 32).astype(F32) * (2.0 / HEAD_DIM)
    angle = position.astype(F32)[:, None] * jnp.power(10000.0, -exponent)[None, :]
    cos_span = jnp.cos(angle)
    sin_span = jnp.sin(angle) * jnp.where((lane & 32) == 0, -1.0, 1.0)[None, :]
    table_shape = shape_of(cos_span.shape, F32)
    turned_table = shape_of((LANES, ROWS), F32)
    cos_span, sin_span, cos_turned, sin_turned, col_seg = pl.pallas_call(
        table_kernel,
        out_shape=[
            table_shape,
            table_shape,
            turned_table,
            turned_table,
            shape_of(cos_span.shape, jnp.int32),
        ],
        compiler_params=pltpu.CompilerParams(vmem_limit_bytes=58 * MIB),
    )(cos_span, sin_span, span_segment.reshape(PIECES, LANES))
    row_seg = own_segment.reshape(ROWS // LANES, 1, LANES)

    rows = 384
    steps = ROWS // rows
    first_pieces = held_until(
        first_pieces, cos_span, row_seg, info
    )
    first_held = joined(first_pieces)
    held_a, held_b = first_held[:, :, :FIRST_CUT], first_held[:, :, FIRST_CUT:]
    own_a = gather_finish(gather_middle(held_a, False), False)
    own_b = gather_finish(gather_middle(held_b, True), True)
    second_held = joined(second_pieces)
    held_in, held_down = second_held[:, :, :HALF], second_held[:, :, HALF:]
    own_a[-1], own_b[-1] = held_until((own_a[-1], own_b[-1]), held_in, held_down)
    own_a, own_b = [jnp.concatenate(own_a, axis=0)], [jnp.concatenate(own_b, axis=0)]
    other_a, other_b = [swapped_cores(own_a[0])], [swapped_cores(own_b[0])]

    parts = (own_a, other_a, own_b, other_b)
    counts_qkv = tuple(len(part) for part in parts)
    qkv, normed, gain_rows, edge, weight_qkv = call(
        lambda *refs: qkv_kernel(orders, counts_qkv, *refs),
        info,
        (steps,),
        [tokens, cos_span, sin_span] + [piece for part in parts for piece in part],
        [by_rows(rows, WIDTH), full(*cos_span.shape), full(*cos_span.shape)]
        + [ANYWHERE] * sum(counts_qkv),
        [
            shape_of((ROWS, 2 * HALF)),
            shape_of((MORE_ROWS, WIDTH)),
            shape_of((8, WIDTH), F32),
            shape_of((WINDOW_HALF, 3 * WIDTH)),
            shape_of((WIDTH, 2 * WIDE)),
        ],
        [by_rows(rows, 2 * HALF), by_rows(rows, WIDTH), full(8, WIDTH)]
        + [full(WINDOW_HALF, 3 * WIDTH), ANYWHERE],
        [
            pltpu.VMEM((WIDTH, 2 * WIDE), BF16),
            pltpu.SemaphoreType.DMA((2,)),
        ],
        2 * ROWS * WIDTH * 2 * HALF,
        58,
    )
    edge = swapped_cores(edge)
    normed = lax.dynamic_update_slice(normed, edge[:, 2 * WIDTH :], (ROWS, 0))
    held_in = gather_middle(held_in, False, qkv)
    held_down = gather_middle(held_down, True, qkv)
    in_own, down_own = gather_finish(held_in, False), gather_finish(held_down, True)

    blocks = ROWS // LANES
    window_shape = (ROWS + 2 * WINDOW_HALF, 2 * WIDTH)
    turned_shape = (WIDTH, ROWS + 2 * WINDOW_HALF)
    by_block = pl.BlockSpec((1, PAIRS, SPAN, SPAN), lambda i, s: (i, 0, 0, 0))
    att_own, att_other, probs = call(
        attend_kernel,
        info,
        (blocks,),
        [row_seg, col_seg, qkv, qkv, edge],
        [
            pl.BlockSpec((1, 1, LANES), lambda i, s: (i, 0, 0)),
            full(ROWS + 2 * WINDOW_HALF, LANES),
            by_rows(LANES, 2 * HALF),
            ANYWHERE,
            ANYWHERE,
        ],
        [
            shape_of((ROWS, THIRD)),
            shape_of((ROWS, THIRD)),
            shape_of((blocks, PAIRS, SPAN, SPAN)),
        ],
        [by_rows(LANES, THIRD), by_rows(LANES, THIRD), by_block],
        [
            pltpu.VMEM(window_shape, BF16),
            pltpu.VMEM(turned_shape, BF16),
            pltpu.SemaphoreType.DMA((PIECES + 1,)),
        ],
        blocks * PAIRS * 2 * 2 * SPAN * SPAN * LANES,
        58,
        after=[held_in, held_down],
    )

    in_own[-1], down_own[-1] = held_until((in_own[-1], down_own[-1]), att_own)
    in_other = [swapped_cores(piece) for piece in in_own]
    down_other = [swapped_cores(piece) for piece in down_own]
    parts = (in_own, in_other, down_own, down_other)
    counts = tuple(len(part) for part in parts)
    (
        layer_out,
        hidden_grad,
        att_grad_own,
        att_grad_other,
        normed_two,
        gated_own,
        gated_other,
        pre_grad_own,
        pre_grad_other,
        hidden_grad_low,
        out_grad,
    ) = call(
        lambda *refs: mlp_kernel(orders, counts, *refs),
        info,
        (steps,),
        [tokens, att_own, att_other, cotangent, col_seg, gain_rows]
        + [piece for part in parts for piece in part],
        [by_rows(rows, WIDTH), by_rows(rows, THIRD), by_rows(rows, THIRD), by_rows(rows, WIDTH)]
        + [full(*cos_span.shape), full(8, WIDTH)]
        + [ANYWHERE] * sum(counts),
        [
            shape_of((ROWS, WIDTH)),
            shape_of((ROWS, WIDTH), F32),
            shape_of((ROWS, THIRD)),
            shape_of((ROWS, THIRD)),
            shape_of((ROWS, WIDTH)),
            shape_of((ROWS, UNITS + LANES)),
            shape_of((ROWS, UNITS + LANES)),
            shape_of((ROWS, HALF)),
            shape_of((ROWS, HALF)),
            shape_of((ROWS, WIDTH)),
            shape_of((ROWS, WIDTH)),
        ],
        [by_rows(rows, WIDTH)] * 2
        + [by_rows(rows, THIRD)] * 2
        + [by_rows(rows, WIDTH)]
        + [by_rows(rows, UNITS + LANES)] * 2
        + [by_rows(rows, HALF)] * 2
        + [by_rows(rows, WIDTH)] * 2,
        [
            pltpu.VMEM((WIDTH, 2 * HALF), BF16),
            pltpu.VMEM((WIDTH, 2 * DOWN), BF16),
            pltpu.SemaphoreType.DMA((2,)),
        ],
        2 * ROWS * WIDTH * (4 * HALF + 2 * HALF + 2 * WIDTH),
        58,
    )

    def down_grads(att, gated):
        parts = [weight_grad(hidden_grad_low, att), weight_grad(out_grad, gated)]
        return jnp.concatenate(parts, axis=1)

    send_in = weight_grad(normed_two, pre_grad_other)
    send_down = down_grads(att_other, gated_other)
    keep_in = weight_grad(normed_two, pre_grad_own)
    keep_down = down_grads(att_own, gated_own)
    sum_in, in_back, in_sent = scatter_start(keep_in, swapped_cores(send_in), own_rows, False)
    sum_down, down_back, down_sent = scatter_start(keep_down, swapped_cores(send_down), own_rows, True)

    grad_own, grad_other, edge_grad = call(
        attend_back_kernel,
        info,
        (blocks,),
        [qkv, probs, att_grad_own, att_grad_other, cos_span, sin_span]
        + [cos_turned, sin_turned, qkv, edge],
        [by_rows(LANES, 2 * HALF), by_block, by_rows(LANES, THIRD), by_rows(LANES, THIRD)]
        + [full(*cos_span.shape)] * 2
        + [pl.BlockSpec((LANES, LANES), lambda i, s: (0, i))] * 2
        + [ANYWHERE] * 2,
        [shape_of((MORE_ROWS, HALF))] * 2 + [shape_of((WINDOW_HALF, 2 * WIDTH))],
        [full(MORE_ROWS, HALF)] * 2 + [full(WINDOW_HALF, 2 * WIDTH)],
        [
            pltpu.VMEM(window_shape, BF16),
            pltpu.VMEM(turned_shape, BF16),
            pltpu.VMEM((window_shape[0], WIDTH), F32),
            pltpu.VMEM((window_shape[0], WIDTH), F32),
            pltpu.SemaphoreType.DMA((PIECES + 1,)),
        ],
        blocks * PAIRS * 4 * 2 * SPAN * SPAN * LANES,
        58,
        after=[send_in, send_down, keep_in, keep_down],
    )
    edge_grad = swapped_cores(edge_grad)
    (normed,) = held_until((normed,), in_sent[2], down_sent[2])

    send_a = weight_grad(normed, grad_other[:, :FIRST_CUT])
    send_b = weight_grad(normed, grad_other[:, FIRST_CUT:])
    keep_a = weight_grad(normed, grad_own[:, :FIRST_CUT])
    keep_b = weight_grad(normed, grad_own[:, FIRST_CUT:])
    late_a, late_b = swapped_cores(send_a), swapped_cores(send_b)

    (late_info,) = held_until(
        (info,), keep_a, keep_b, late_a, late_b, in_back[2], down_back[2]
    )
    (grad_tokens,) = call(
        input_grad_kernel,
        late_info,
        (steps,),
        [tokens, grad_own, grad_other, edge_grad, hidden_grad, gain_rows, weight_qkv],
        [by_rows(rows, WIDTH), by_rows(rows, HALF), by_rows(rows, HALF)]
        + [full(WINDOW_HALF, 2 * WIDTH), by_rows(rows, WIDTH)]
        + [full(8, WIDTH), full(WIDTH, 2 * WIDE)],
        [shape_of((ROWS, WIDTH), F32)],
        [by_rows(rows, WIDTH)],
        [pltpu.VMEM((rows, HALF), BF16)],
        2 * ROWS * WIDTH * 2 * HALF,
        28,
    )
    sent_a = scatter_start(keep_a, late_a, own_rows, False)[2][1]
    sent_b = scatter_start(keep_b, late_b, own_rows, True)[2][1]
    sum_in, sum_down = held_until((sum_in, sum_down), sent_a, sent_b)
    owned_early = scatter_finish(sum_in, sum_down)
    gates = (grad_tokens, owned_early)
    sum_a, unused, unused = scatter_start(keep_a, late_a, own_rows, False, gates)
    sum_b, unused, unused = scatter_start(keep_b, late_b, own_rows, True, gates)
    owned_in, owned_down = owned_early[:, :HALF], owned_early[:, HALF:]

    flat_grad = scatter_finish(sum_a, sum_b)
    gain_grads = jnp.stack(
        [
            gain_part(flat_qkv, flat_grad, norm_attn_gain),
            gain_part(shard_in, owned_in, norm_mlp_gain),
        ]
    )
    gain_grads = gain_grads + swapped_cores(gain_grads)
    owned_gain_one, owned_gain_two = gain_grads[0], gain_grads[1]
    owned_qkv = flat_grad.reshape(own_rows, 3, THIRD)
    owned_in = jnp.stack(
        [
            jnp.concatenate([owned_in[:, :UNITS], owned_in[:, 2 * UNITS : -64]], axis=1),
            jnp.concatenate([owned_in[:, UNITS : 2 * UNITS], owned_in[:, -64:]], axis=1),
        ],
        axis=1,
    )
    owned_attn = owned_down[:, :THIRD].T
    owned_out = owned_down[:, THIRD : THIRD + UNITS + HEAD_DIM].T
    return (
        layer_out,
        grad_tokens,
        owned_gain_one,
        owned_qkv,
        owned_attn,
        owned_gain_two,
        owned_in,
        owned_out,
    )


def solution(mesh):
    placed = (
        P(("dp", "tensor"), None),
        P("dp"),
        P("dp"),
        P("dp", None, "tensor"),
        P("tensor", "dp"),
        P("dp"),
        P("dp", None, "tensor"),
        P("tensor", "dp"),
        P(("dp", "tensor"), None),
    )
    return jax.shard_map(
        body,
        mesh=mesh,
        in_specs=placed,
        out_specs=(
            P(("dp", "tensor"), None),
            P(("dp", "tensor"), None),
            P("dp"),
            P("dp", None, "tensor"),
            P("tensor", "dp"),
            P("dp"),
            P("dp", None, "tensor"),
            P("tensor", "dp"),
        ),
        check_vma=False,
    )
```

```python
import jax
import jax.numpy as jnp
from jax import lax
from jax.experimental import pallas as pl
from jax.experimental.pallas import tpu as pltpu
from jax.sharding import PartitionSpec as P

HEAD_DIM = 64
WINDOW_HALF = 64
PAD_BLOCK = 128
WIDTH = 768
ROWS = 1152
MORE_ROWS = ROWS + 64
HALF = 1152
LANES = 128
THIRD = 384
PAIRS = 6
SPAN = 2 * LANES
PIECES = ROWS // LANES + 1
UNITS = 512
FIRST_CUT = 640
WIDE = HALF + LANES
DOWN = 384 + UNITS + LANES
MIB = 2**20
ANYWHERE = pl.BlockSpec(memory_space=pl.ANY)
F32 = jnp.float32
BF16 = jnp.bfloat16


def steps_of(devices, swapped):
    bits = [1 << i for i in range(devices.bit_length() - 1)]
    near, far = bits[:2], bits[2:]
    return far + (near if swapped else near[::-1])


def exchanged(block, mask):
    devices = lax.axis_size("dp")
    return lax.ppermute(block, "dp", [(i, i ^ mask) for i in range(devices)])


def swapped_cores(block):
    return lax.ppermute(block, "tensor", [(0, 1), (1, 0)])


def by_exchange(own_rows):
    devices = lax.axis_size("dp")
    return own_rows % 16 == 0 and devices & (devices - 1) == 0


def relative(own_rows, swapped):
    if not by_exchange(own_rows):
        return list(range(WIDTH // 48))
    order = [0]
    for mask in steps_of(lax.axis_size("dp"), swapped):
        order = order + [r ^ mask for r in order]
    return order


def held_until(arrays, *gates):
    return lax.optimization_barrier((tuple(arrays), gates))[0]


def gather_start(shard):
    masks = steps_of(lax.axis_size("dp"), False)
    held = shard[None]
    if not by_exchange(shard.shape[0]) or len(masks) <= 3:
        return [held]
    first, second = masks[:2]
    return [held] + [exchanged(held, mask) for mask in (first, second, first ^ second)]


def joined(pieces):
    return lax.optimization_barrier(jnp.concatenate(pieces, axis=0))


def gather_middle(held, swapped, gate=None):
    if by_exchange(held.shape[1]):
        masks = steps_of(lax.axis_size("dp"), swapped)
        for mask in masks[held.shape[0].bit_length() - 1 : -1]:
            arrived = exchanged(held, mask)
            if gate is not None:
                (arrived,) = held_until((arrived,), gate)
            held = jnp.concatenate([held, arrived], axis=0)
    return held


def gather_finish(held, swapped):
    if not by_exchange(held.shape[1]):
        whole = lax.all_gather(held[0], "dp", axis=0, tiled=True)
        return [whole.reshape(WIDTH // 48, 48, held.shape[2])]
    return [held, exchanged(held, steps_of(lax.axis_size("dp"), swapped)[-1])]


def scatter_start(keep, other, own_rows, swapped, first_gates=None):
    arrivals, sents = [other], [other]
    if not by_exchange(own_rows):
        total = keep.astype(F32) + other.astype(F32)
        total = lax.psum_scatter(total, "dp", scatter_dimension=0, tiled=True)
        return total[None], arrivals * 3, sents * 3
    devices = lax.axis_size("dp")
    index = lax.axis_index("dp")
    levels = devices.bit_length() - 1
    masks = steps_of(devices, swapped)
    last = 2 if len(masks) > 3 else 0
    shape = (2,) * levels + (own_rows, keep.shape[1])
    keep, other = keep.reshape(shape), other.reshape(shape)
    for mask in reversed(masks[last:]):
        axis = levels - mask.bit_length()
        bit = (index & mask) // mask
        part = lambda array, which: lax.dynamic_slice_in_dim(array, which, 1, axis).astype(F32)
        sent = (part(keep, 1 - bit) + part(other, 1 - bit)).astype(BF16)
        kept = (part(keep, bit) + part(other, bit)).astype(BF16)
        other = exchanged(sent, mask)
        arrivals.append(other)
        sents.append(sent)
        if first_gates is not None and len(arrivals) == 2:
            (other,) = held_until((other,), *first_gates)
        keep = kept
    total = keep.astype(F32) + other.astype(F32)
    return total.reshape(2**last, own_rows, -1), arrivals + [other] * 3, sents + [other] * 3


def scatter_finish(*totals):
    if totals[0].shape[0] == 1:
        return jnp.concatenate([total[0] for total in totals], axis=1)
    unit = steps_of(lax.axis_size("dp"), False)[0]
    place = (lax.axis_index("dp") // unit) % 4

    def rows_of(which):
        parts = [lax.dynamic_index_in_dim(total, which, 0, keepdims=False) for total in totals]
        return jnp.concatenate(parts, axis=1)

    arrived = [
        exchanged(rows_of(place ^ j).astype(BF16), unit * j).astype(F32) for j in range(1, 4)
    ]
    return rows_of(place) + (arrived[0] + arrived[1] + arrived[2])


def weight_grad(left, right):
    return lax.dot_general(
        left, right, (((0,), (0,)), ((), ())), preferred_element_type=F32
    ).astype(BF16)


def gain_part(weight, grad, gain):
    return jnp.sum(weight.astype(F32) * grad, axis=1) / gain.astype(F32)


def nt(left, right):
    return lax.dot_general(left, right, (((1,), (1,)), ((), ())), preferred_element_type=F32)


def nn(left, right):
    return jnp.dot(left, right, preferred_element_type=F32)


def start_slots(info, pieces, order, segments, sems):
    slot = 0
    for piece in pieces:
        rows = piece.shape[1]
        for at in range(piece.shape[0]):
            row = pl.multiple_of((info[0] ^ order[slot]) * rows, 16)
            for begin, width, target, column, sem in segments:
                pltpu.make_async_copy(
                    piece.at[at, :, pl.ds(begin, width)],
                    target.at[pl.ds(row, rows), pl.ds(column, width)],
                    sems.at[sem],
                ).start()
            slot += 1


def wait_whole(ref, sem):
    pltpu.make_async_copy(ref, ref, sem).wait()


def start_window(info, qkv_ref, edge_ref, window, sems):
    core = info[1]
    first = pl.multiple_of(jnp.where(core == 1, 0, WINDOW_HALF + ROWS), 16)
    last = pl.multiple_of(jnp.where(core == 1, WINDOW_HALF + ROWS, 0), 16)
    edge = pltpu.make_async_copy(
        edge_ref.at[:, pl.ds(0, 2 * WIDTH)],
        window.at[pl.ds(first, WINDOW_HALF), :],
        sems.at[PIECES],
    )
    edge.start()
    for piece in range(PIECES):
        begin, stop = piece_rows(piece)
        for part in range(2):
            for half in range(2):
                source = HALF * half + THIRD * (part + 1)
                target = WIDTH * part + THIRD * half
                pltpu.make_async_copy(
                    qkv_ref.at[pl.ds(begin - WINDOW_HALF, stop - begin), pl.ds(source, THIRD)],
                    window.at[pl.ds(begin, stop - begin), pl.ds(target, THIRD)],
                    sems.at[piece],
                ).start()
    window[pl.ds(last, WINDOW_HALF), :] = jnp.zeros((WINDOW_HALF, 2 * WIDTH), BF16)
    edge.wait()


def piece_rows(piece):
    return max(LANES * piece, WINDOW_HALF), min(LANES * (piece + 1), WINDOW_HALF + ROWS)


def wait_window(window, step, sems):
    @pl.when(step == 0)
    def _():
        for piece in range(2):
            begin, stop = piece_rows(piece)
            wait_whole(window.at[pl.ds(begin, stop - begin), :], sems.at[piece])

    @pl.when((step > 0) & (step < PIECES - 2))
    def _():
        row = pl.multiple_of((step + 1) * LANES, LANES)
        wait_whole(window.at[pl.ds(row, LANES), :], sems.at[step + 1])

    @pl.when(step == PIECES - 2)
    def _():
        begin, stop = piece_rows(PIECES - 1)
        wait_whole(window.at[pl.ds(begin, stop - begin), :], sems.at[PIECES - 1])


def identity():
    row = lax.broadcasted_iota(jnp.int32, (LANES, LANES), 0)
    lane = lax.broadcasted_iota(jnp.int32, (LANES, LANES), 1)
    return jnp.where(row == lane, 1.0, 0.0).astype(BF16)


def turn_rows(unit, window, begin, row, turned_ref):
    for pair in range(PAIRS):
        lanes = slice(LANES * pair, LANES * (pair + 1))
        block = window[pl.ds(row, LANES), begin + LANES * pair : begin + LANES * (pair + 1)]
        turned_ref[lanes, pl.ds(row, LANES)] = nt(unit, block).astype(BF16)


def head_rows(columns):
    return jnp.concatenate([columns[:HEAD_DIM, :LANES], columns[HEAD_DIM:, LANES:]], axis=0)


def normalized(values):
    centred = values - jnp.mean(values, axis=-1, keepdims=True)
    spread = jnp.mean(centred * centred, axis=-1, keepdims=True)
    factor = lax.rsqrt(spread + 1e-05)
    return centred * factor, factor


def norm_backward(grad, unit, factor, gain):
    inner = grad * gain
    mean = jnp.mean(inner, axis=-1, keepdims=True)
    along = jnp.mean(inner * unit, axis=-1, keepdims=True)
    return factor * (inner - mean - unit * along)


def turned(values, cosine, sine):
    lane = lax.broadcasted_iota(jnp.int32, values.shape, 1)
    first = (lane & 32) == 0
    other = jnp.where(first, pltpu.roll(values, 96, 1), pltpu.roll(values, 32, 1))
    return values * cosine + other * sine


def both_heads(block):
    lane = lax.broadcasted_iota(jnp.int32, block.shape, 1)
    first = jnp.where(lane < HEAD_DIM, 1.0, 0.0).astype(block.dtype)
    second = jnp.where(lane < HEAD_DIM, 0.0, 1.0).astype(block.dtype)
    return jnp.concatenate([block * first, block * second], axis=0)


def table_kernel(cos_in, sin_in, seg_ref, cos_ref, sin_ref, cos_turned, sin_turned, col_ref):
    cos_ref[...] = cos_in[...]
    sin_ref[...] = sin_in[...]
    for block in range(ROWS // LANES):
        rows = slice(WINDOW_HALF + LANES * block, WINDOW_HALF + LANES * (block + 1))
        lanes = slice(LANES * block, LANES * (block + 1))
        cos_turned[:, lanes] = cos_in[rows, :].T
        sin_turned[:, lanes] = sin_in[rows, :].T
    for block in range(PIECES):
        row = jnp.broadcast_to(seg_ref[block : block + 1, :].astype(F32), (LANES, LANES))
        col_ref[LANES * block : LANES * (block + 1), :] = row.T.astype(jnp.int32)


def qkv_kernel(orders, counts, info, x_ref, cos_ref, sin_ref, *refs):
    parts = []
    for count in counts:
        parts.append(refs[:count])
        refs = refs[count:]
    own_a, other_a, own_b, other_b = parts
    qkv_ref, normed_ref, gain_ref, edge_ref, weight_ref, weight, sems = refs
    step = pl.program_id(0)
    rows = x_ref.shape[0]

    @pl.when(step == 0)
    def _():
        for begin, part_a, part_b in ((0, own_a, own_b), (WIDE, other_a, other_b)):
            start_slots(info, part_a, orders[0], [(0, FIRST_CUT, weight, begin, 0)], sems)
            start_slots(
                info,
                part_b,
                orders[1],
                [(0, WIDE - FIRST_CUT, weight, begin + FIRST_CUT, 0)],
                sems,
            )
        wait_whole(weight, sems.at[0])
        pltpu.make_async_copy(weight, weight_ref, sems.at[1]).start()
        row = lax.broadcasted_iota(jnp.int32, (16, LANES), 0)
        lane = lax.broadcasted_iota(jnp.int32, (16, LANES), 1)
        pick = jnp.where(row == lane, 1.0, 0.0).astype(BF16)
        gain_ref[...] = nt(pick, weight[:, HALF:WIDE])[:8]

    unit, unused = normalized(x_ref[...].astype(F32))
    normed = (unit * gain_ref[0:1, :]).astype(BF16)
    normed_ref[...] = normed
    table_rows = pl.ds(pl.multiple_of(WINDOW_HALF + step * rows, WINDOW_HALF), rows)
    cosine, sine = cos_ref[table_rows, :], sin_ref[table_rows, :]
    for half in range(2):
        result = nn(normed, weight[:, WIDE * half : WIDE * half + HALF])
        for tile in range(9):
            block = result[:, LANES * tile : LANES * (tile + 1)]
            if tile < 6:
                block = turned(block, cosine, sine)
            if tile < 3:
                block = block * (HEAD_DIM**-0.5)
            begin = HALF * half + LANES * tile
            qkv_ref[:, begin : begin + LANES] = block.astype(BF16)

    for core, at_step, begin in ((1, 0, 0), (0, ROWS // rows - 1, rows - WINDOW_HALF)):

        @pl.when((info[1] == core) & (step == at_step))
        def _():
            for part in range(2):
                for half in range(2):
                    source = HALF * half + THIRD * (part + 1)
                    target = WIDTH * part + THIRD * (1 - half)
                    edge_ref[:, target : target + THIRD] = qkv_ref[
                        begin : begin + WINDOW_HALF, source : source + THIRD
                    ]
            edge_ref[:, 2 * WIDTH :] = normed_ref[begin : begin + WINDOW_HALF, :]

    @pl.when(step == ROWS // rows - 1)
    def _():
        pltpu.make_async_copy(weight, weight_ref, sems.at[1]).wait()


def attend_kernel(
    info,
    row_seg,
    col_seg,
    q_own,
    q_other,
    qkv_ref,
    edge_ref,
    own_ref,
    other_ref,
    probs_ref,
    window,
    turned_values,
    sems,
):
    step = pl.program_id(0)
    unit = identity()

    @pl.when(step == 0)
    def _():
        start_window(info, qkv_ref, edge_ref, window, sems)

    wait_window(window, step, sems)

    @pl.when(step == 0)
    def _():
        turn_rows(unit, window, WIDTH, 0, turned_values)

    start = pl.multiple_of(step * LANES, LANES)
    turn_rows(unit, window, WIDTH, pl.multiple_of(start + LANES, LANES), turned_values)
    key_seg = col_seg[pl.ds(start, SPAN), :]
    key_at = lax.broadcasted_iota(jnp.int32, (SPAN, LANES), 0) - WINDOW_HALF
    query_at = lax.broadcasted_iota(jnp.int32, (SPAN, LANES), 1)
    near = jnp.abs(key_at - query_at) <= WINDOW_HALF
    allowed = (key_seg == row_seg[0]) & near
    bias = jnp.where(allowed, 0.0, -1e30)
    bias = jnp.concatenate([bias, bias], axis=1)

    scores, probs, results = [], [], []
    for pair in range(PAIRS):
        q_ref = q_own if pair < 3 else q_other
        queries = both_heads(q_ref[:, LANES * (pair % 3) : LANES * (pair % 3 + 1)])
        keys = window[pl.ds(start, SPAN), LANES * pair : LANES * (pair + 1)]
        scores.append(nt(keys, queries) + bias)
    for pair in range(PAIRS):
        weights = jnp.exp(scores[pair] - jnp.max(scores[pair], axis=0, keepdims=True))
        total = jnp.sum(weights, axis=0, keepdims=True)
        probs.append((weights * (1.0 / total)).astype(BF16))
        probs_ref[0, pair] = probs[pair]
    for pair in range(PAIRS):
        values = turned_values[LANES * pair : LANES * (pair + 1), pl.ds(start, SPAN)]
        results.append(head_rows(nn(values, probs[pair])).astype(BF16))
    for pair in range(PAIRS):
        out_ref = own_ref if pair < 3 else other_ref
        out_ref[:, LANES * (pair % 3) : LANES * (pair % 3 + 1)] = nt(unit, results[pair]).astype(
            BF16
        )


def mlp_kernel(orders, counts, info, x_ref, att_own, att_other, cot_ref, col_seg, gain_ref, *refs):
    parts = []
    for count in counts:
        parts.append(refs[:count])
        refs = refs[count:]
    in_own, in_other, down_own, down_other = parts
    (
        out_ref,
        hidden_grad_ref,
        att_grad_own,
        att_grad_other,
        normed_ref,
        gated_own,
        gated_other,
        pre_grad_own,
        pre_grad_other,
        low_grad_ref,
        out_grad_ref,
        w_in,
        w_down,
        sems,
    ) = refs
    step = pl.program_id(0)

    @pl.when(step == 0)
    def _():
        for number, part in enumerate((down_own, down_other)):
            start_slots(info, part, orders[1], [(0, DOWN, w_down, DOWN * number, 0)], sems)
        for number, part in enumerate((in_own, in_other)):
            start_slots(info, part, orders[0], [(0, HALF, w_in, HALF * number, 1)], sems)
        wait_whole(w_down, sems.at[0])
        other = pltpu.roll(w_down[:, 2 * DOWN - LANES :].astype(F32), HEAD_DIM, 1).astype(BF16)
        w_down[:, DOWN - LANES : DOWN] += other

    gain = gain_ref[1:2, :]
    hidden = (
        x_ref[...].astype(F32)
        + nt(att_own[...], w_down[:, :THIRD])
        + nt(att_other[...], w_down[:, DOWN : DOWN + THIRD])
    )
    unit, factor = normalized(hidden)
    normed = (unit * gain).astype(BF16)
    normed_ref[...] = normed
    seg_rows = pl.ds(pl.multiple_of(WINDOW_HALF + step * x_ref.shape[0], WINDOW_HALF), x_ref.shape[0])
    live = jnp.where(col_seg[seg_rows, :] >= 0, 1.0, 0.0)
    live = jnp.concatenate([live] * (WIDTH // LANES), axis=1)
    out_grad = cot_ref[...].astype(F32) * live
    out_grad_low = out_grad.astype(BF16)
    out_grad_ref[...] = out_grad_low

    @pl.when(step == 0)
    def _():
        wait_whole(w_in, sems.at[1])

    pre = [nn(normed, w_in[:, HALF * half : HALF * (half + 1)]) for half in range(2)]
    tails = [part[:, 2 * UNITS :] for part in pre]
    lane = lax.broadcasted_iota(jnp.int32, tails[0].shape, 1)
    low = lane < HEAD_DIM
    gates = [part[:, :UNITS] for part in pre]
    gates.append(jnp.where(low, tails[0], pltpu.roll(tails[1], 64, 1)))
    ups = [part[:, UNITS : 2 * UNITS] for part in pre]
    ups.append(jnp.where(low, pltpu.roll(tails[0], 64, 1), tails[1]))
    pre_grads = (pre_grad_own, pre_grad_other)
    unit_columns = (
        slice(THIRD, THIRD + UNITS),
        slice(DOWN + THIRD, DOWN + THIRD + UNITS),
        slice(DOWN - LANES, DOWN),
    )
    for part, (gate, up) in enumerate(zip(gates, ups)):
        share = 0.5 + 0.5 * lax.erf(gate * (0.5**0.5))
        slope = share + gate * (jnp.exp(-0.5 * gate * gate) * 0.3989422804014327)
        curve = gate * share
        gated = curve * up
        grad = nn(out_grad_low, w_down[:, unit_columns[part]])
        gate_grad = grad * up * slope
        up_grad = grad * curve
        if part < 2:
            (gated_own, gated_other)[part][:, :UNITS] = gated.astype(BF16)
            pre_grads[part][:, :UNITS] = gate_grad.astype(BF16)
            pre_grads[part][:, UNITS : 2 * UNITS] = up_grad.astype(BF16)
        else:
            gated_own[:, UNITS:] = gated.astype(BF16)
            gated_other[:, UNITS:] = pltpu.roll(gated, HEAD_DIM, 1).astype(BF16)
            own = jnp.where(low, gate_grad, pltpu.roll(up_grad, 64, 1))
            other = jnp.where(low, pltpu.roll(gate_grad, 64, 1), up_grad)
            pre_grad_own[:, 2 * UNITS :] = own.astype(BF16)
            pre_grad_other[:, 2 * UNITS :] = other.astype(BF16)
    product = (
        nt(gated_own[...], w_down[:, THIRD:DOWN])
        + nt(gated_other[:, :UNITS], w_down[:, unit_columns[1]])
    )
    out_ref[...] = (hidden + product).astype(BF16)
    normed_grad = nt(pre_grad_own[...], w_in[:, :HALF]) + nt(pre_grad_other[...], w_in[:, HALF:])
    hidden_grad = out_grad + norm_backward(normed_grad, unit, factor, gain)
    hidden_grad_ref[...] = hidden_grad
    hidden_grad_low = hidden_grad.astype(BF16)
    low_grad_ref[...] = hidden_grad_low
    att_grad_own[...] = nn(hidden_grad_low, w_down[:, :THIRD]).astype(BF16)
    att_grad_other[...] = nn(hidden_grad_low, w_down[:, DOWN : DOWN + THIRD]).astype(BF16)


def attend_back_kernel(
    info,
    q_own,
    q_other,
    probs_ref,
    grad_own,
    grad_other,
    cos_ref,
    sin_ref,
    cos_turned,
    sin_turned,
    qkv_ref,
    edge_ref,
    out_own,
    out_other,
    edge_out_ref,
    window,
    turned_keys,
    key_grad,
    value_grad,
    sems,
):
    step = pl.program_id(0)
    unit = identity()

    @pl.when(step == 0)
    def _():
        start_window(info, qkv_ref, edge_ref, window, sems)
        key_grad[...] = jnp.zeros_like(key_grad)
        value_grad[...] = jnp.zeros_like(value_grad)

    wait_window(window, step, sems)

    @pl.when(step == 0)
    def _():
        turn_rows(unit, window, 0, 0, turned_keys)

    start = pl.multiple_of(step * LANES, LANES)
    span = pl.ds(start, SPAN)
    turn_rows(unit, window, 0, pl.multiple_of(start + LANES, LANES), turned_keys)
    cosine, sine = cos_turned[...], sin_turned[...]

    all_lanes = [slice(LANES * pair, LANES * (pair + 1)) for pair in range(PAIRS)]
    grads, probs_grads, score_grads, query_grads = [], [], [], []
    for pair, lanes in enumerate(all_lanes):
        grad_ref = grad_own if pair < 3 else grad_other
        grads.append(both_heads(grad_ref[:, LANES * (pair % 3) : LANES * (pair % 3 + 1)]))
        values = window[span, WIDTH + LANES * pair : WIDTH + LANES * (pair + 1)]
        probs_grads.append(nt(values, grads[pair]))
    for pair, lanes in enumerate(all_lanes):
        value_grad[span, lanes] += nn(probs_ref[0, pair], grads[pair])
    for pair in range(PAIRS):
        probs = probs_ref[0, pair].astype(F32)
        weighted = probs_grads[pair] * probs
        delta = jnp.sum(weighted, axis=0, keepdims=True)
        score_grads.append((weighted - probs * delta).astype(BF16))
    for pair, lanes in enumerate(all_lanes):
        query_grads.append(head_rows(nn(turned_keys[lanes, span], score_grads[pair])))
    for pair, lanes in enumerate(all_lanes):
        q_ref = q_own if pair < 3 else q_other
        queries = both_heads(q_ref[:, LANES * (pair % 3) : LANES * (pair % 3 + 1)])
        key_grad[span, lanes] += nn(score_grads[pair], queries)
    for pair in range(PAIRS):
        grad = query_grads[pair] * (HEAD_DIM**-0.5)
        other = jnp.concatenate([grad[32:64], grad[:32], grad[96:], grad[64:96]], axis=0)
        query_grads[pair] = (grad * cosine - other * sine).astype(BF16)
    for pair in range(PAIRS):
        out_ref = out_own if pair < 3 else out_other
        place = slice(LANES * (pair % 3), LANES * (pair % 3 + 1))
        out_ref[pl.ds(start, LANES), place] = nt(unit, query_grads[pair]).astype(BF16)

    @pl.when(step == ROWS // LANES - 1)
    def _():
        inside = slice(WINDOW_HALF, WINDOW_HALF + ROWS)
        row = pl.multiple_of(jnp.where(info[1] == 1, 0, WINDOW_HALF + ROWS), 16)
        edge_rows = pl.ds(row, WINDOW_HALF)
        for pair in range(PAIRS):
            out_ref = out_own if pair < 3 else out_other
            lanes = slice(LANES * pair, LANES * (pair + 1))
            begin = LANES * (pair % 3)
            target = (LANES * pair + THIRD) % WIDTH
            keys_at = slice(THIRD + begin, THIRD + begin + LANES)
            values_at = slice(2 * THIRD + begin, 2 * THIRD + begin + LANES)
            out_ref[:ROWS, keys_at] = turned(
                key_grad[inside, lanes], cos_ref[inside, :], -sin_ref[inside, :]
            ).astype(BF16)
            out_ref[:ROWS, values_at] = value_grad[inside, lanes].astype(BF16)
            edge_keys = turned(
                key_grad[edge_rows, lanes], cos_ref[edge_rows, :], -sin_ref[edge_rows, :]
            ).astype(BF16)
            edge_values = value_grad[edge_rows, lanes].astype(BF16)
            edge_out_ref[:, target : target + LANES] = edge_keys
            edge_out_ref[:, WIDTH + target : WIDTH + target + LANES] = edge_values
            out_ref[ROWS:, begin : begin + LANES] = jnp.zeros((WINDOW_HALF, LANES), BF16)
            out_ref[ROWS:, keys_at] = edge_keys
            out_ref[ROWS:, values_at] = edge_values


def input_grad_kernel(
    info, x_ref, own_ref, other_ref, edge_ref, hidden_ref, gain_ref, weight, out_ref, fixed
):
    rows = x_ref.shape[0]
    step = pl.program_id(0)
    grad = None
    for half, grad_ref in enumerate((own_ref, other_ref)):
        fixed[...] = grad_ref[...]
        for core, at_step, begin in ((1, 0, 0), (0, ROWS // rows - 1, rows - WINDOW_HALF)):

            @pl.when((info[1] == core) & (step == at_step))
            def _():
                at = slice(begin, begin + WINDOW_HALF)
                for part in range(2):
                    to = slice(THIRD * (part + 1), THIRD * (part + 2))
                    source = WIDTH * part + THIRD * half
                    add = edge_ref[:, source : source + THIRD].astype(F32)
                    fixed[at, to] = (fixed[at, to].astype(F32) + add).astype(BF16)

        part = nt(fixed[...], weight[:, WIDE * half : WIDE * half + HALF])
        grad = part if grad is None else grad + part
    unit, factor = normalized(x_ref[...].astype(F32))
    out_ref[...] = hidden_ref[...] + norm_backward(grad, unit, factor, gain_ref[0:1, :])


def shape_of(shape, dtype=BF16):
    return jax.ShapeDtypeStruct(shape, dtype)


def call(
    kernel, info, grid, ins, in_specs, outs, out_specs, scratch, flops, vmem, after=()
):
    moved = sum(a.size * a.dtype.itemsize for a in list(ins) + list(outs))
    first = 1 + len(ins)
    later = first + len(after)
    return pl.pallas_call(
        lambda *refs: kernel(*refs[:first], *refs[later:]),
        out_shape=outs,
        grid_spec=pltpu.PrefetchScalarGridSpec(
            num_scalar_prefetch=1,
            grid=grid,
            in_specs=list(in_specs) + [ANYWHERE] * len(after),
            out_specs=out_specs,
            scratch_shapes=scratch,
        ),
        compiler_params=pltpu.CompilerParams(
            dimension_semantics=("arbitrary",), vmem_limit_bytes=vmem * MIB
        ),
        cost_estimate=pl.CostEstimate(
            flops=int(flops), bytes_accessed=int(moved), transcendentals=0
        ),
    )(info, *ins, *after)


def by_rows(rows, columns):
    return pl.BlockSpec((rows, columns), lambda i, s: (i, 0))


def full(*shape):
    return pl.BlockSpec(shape, lambda i, s: (0,) * len(shape))


def body(
    tokens,
    segment,
    norm_attn_gain,
    qkv_weight,
    attn_out_weight,
    norm_mlp_gain,
    in_weight,
    out_weight,
    cotangent,
):
    own_rows = norm_attn_gain.shape[0]
    core = lax.axis_index("tensor")
    place = lax.axis_index("dp") if by_exchange(own_rows) else 0
    info = jnp.stack([jnp.int32(place), core.astype(jnp.int32)])
    orders = (relative(own_rows, False), relative(own_rows, True))

    gains = jnp.pad(jnp.stack([norm_attn_gain, norm_mlp_gain], axis=1), ((0, 0), (0, LANES - 2)))
    flat_qkv = qkv_weight.reshape(own_rows, HALF)
    first_pieces = gather_start(jnp.concatenate([flat_qkv, gains], axis=1))
    shard_in = jnp.concatenate(
        [
            in_weight[:, 0, :UNITS],
            in_weight[:, 1, :UNITS],
            in_weight[:, 0, UNITS:],
            in_weight[:, 1, UNITS:],
        ],
        axis=1,
    )
    turned_out = out_weight.T
    blank = jnp.zeros((own_rows, HEAD_DIM), BF16)
    shard_down = jnp.concatenate([attn_out_weight.T, turned_out, blank], axis=1)
    second_shard = jnp.concatenate([shard_in, shard_down], axis=1)
    second_shard, *first_pieces = held_until([second_shard] + first_pieces)
    second_pieces = gather_start(second_shard)

    own_segment = lax.dynamic_slice_in_dim(segment, core * ROWS, ROWS, 0)
    seg_pad = jnp.pad(segment, (WINDOW_HALF, WINDOW_HALF), constant_values=-2)
    span_segment = lax.dynamic_slice_in_dim(seg_pad, core * ROWS, ROWS + 2 * WINDOW_HALF, 0)
    slot = core * ROWS - WINDOW_HALF + jnp.arange(ROWS + 2 * WINDOW_HALF, dtype=jnp.int32)
    position = jnp.where(span_segment >= 0, slot - PAD_BLOCK * span_segment, 0)
    lane = jnp.arange(LANES, dtype=jnp.int32)
    exponent = (lane % 32).astype(F32) * (2.0 / HEAD_DIM)
    angle = position.astype(F32)[:, None] * jnp.power(10000.0, -exponent)[None, :]
    cos_span = jnp.cos(angle)
    sin_span = jnp.sin(angle) * jnp.where((lane & 32) == 0, -1.0, 1.0)[None, :]
    table_shape = shape_of(cos_span.shape, F32)
    turned_table = shape_of((LANES, ROWS), F32)
    cos_span, sin_span, cos_turned, sin_turned, col_seg = pl.pallas_call(
        table_kernel,
        out_shape=[
            table_shape,
            table_shape,
            turned_table,
            turned_table,
            shape_of(cos_span.shape, jnp.int32),
        ],
        compiler_params=pltpu.CompilerParams(vmem_limit_bytes=58 * MIB),
    )(cos_span, sin_span, span_segment.reshape(PIECES, LANES))
    row_seg = own_segment.reshape(ROWS // LANES, 1, LANES)

    rows = 384
    steps = ROWS // rows
    first_held = joined(first_pieces)
    held_a, held_b = first_held[:, :, :FIRST_CUT], first_held[:, :, FIRST_CUT:]
    own_a = gather_finish(gather_middle(held_a, False), False)
    own_b = gather_finish(gather_middle(held_b, True), True)
    second_held = joined(second_pieces)
    held_in, held_down = second_held[:, :, :HALF], second_held[:, :, HALF:]
    own_a[-1], own_b[-1] = held_until(
        (own_a[-1], own_b[-1]), held_in, held_down, cos_span, row_seg, info
    )
    own_a, own_b = [jnp.concatenate(own_a, axis=0)], [jnp.concatenate(own_b, axis=0)]
    other_a, other_b = [swapped_cores(own_a[0])], [swapped_cores(own_b[0])]

    parts = (own_a, other_a, own_b, other_b)
    counts_qkv = tuple(len(part) for part in parts)
    qkv, normed, gain_rows, edge, weight_qkv = call(
        lambda *refs: qkv_kernel(orders, counts_qkv, *refs),
        info,
        (steps,),
        [tokens, cos_span, sin_span] + [piece for part in parts for piece in part],
        [by_rows(rows, WIDTH), full(*cos_span.shape), full(*cos_span.shape)]
        + [ANYWHERE] * sum(counts_qkv),
        [
            shape_of((ROWS, 2 * HALF)),
            shape_of((MORE_ROWS, WIDTH)),
            shape_of((8, WIDTH), F32),
            shape_of((WINDOW_HALF, 3 * WIDTH)),
            shape_of((WIDTH, 2 * WIDE)),
        ],
        [by_rows(rows, 2 * HALF), by_rows(rows, WIDTH), full(8, WIDTH)]
        + [full(WINDOW_HALF, 3 * WIDTH), ANYWHERE],
        [
            pltpu.VMEM((WIDTH, 2 * WIDE), BF16),
            pltpu.SemaphoreType.DMA((2,)),
        ],
        2 * ROWS * WIDTH * 2 * HALF,
        58,
    )
    edge = swapped_cores(edge)
    normed = lax.dynamic_update_slice(normed, edge[:, 2 * WIDTH :], (ROWS, 0))
    held_in = gather_middle(held_in, False, qkv)
    held_down = gather_middle(held_down, True, qkv)
    in_own, down_own = gather_finish(held_in, False), gather_finish(held_down, True)

    blocks = ROWS // LANES
    window_shape = (ROWS + 2 * WINDOW_HALF, 2 * WIDTH)
    turned_shape = (WIDTH, ROWS + 2 * WINDOW_HALF)
    other_queries = pl.BlockSpec((LANES, THIRD), lambda i, s: (i, HALF // THIRD))
    by_block = pl.BlockSpec((1, PAIRS, SPAN, SPAN), lambda i, s: (i, 0, 0, 0))
    att_own, att_other, probs = call(
        attend_kernel,
        info,
        (blocks,),
        [row_seg, col_seg, qkv, qkv, qkv, edge],
        [
            pl.BlockSpec((1, 1, LANES), lambda i, s: (i, 0, 0)),
            full(ROWS + 2 * WINDOW_HALF, LANES),
            by_rows(LANES, THIRD),
            other_queries,
            ANYWHERE,
            ANYWHERE,
        ],
        [
            shape_of((ROWS, THIRD)),
            shape_of((ROWS, THIRD)),
            shape_of((blocks, PAIRS, SPAN, SPAN)),
        ],
        [by_rows(LANES, THIRD), by_rows(LANES, THIRD), by_block],
        [
            pltpu.VMEM(window_shape, BF16),
            pltpu.VMEM(turned_shape, BF16),
            pltpu.SemaphoreType.DMA((PIECES + 1,)),
        ],
        blocks * PAIRS * 2 * 2 * SPAN * SPAN * LANES,
        58,
        after=[held_in, held_down],
    )

    in_own[-1], down_own[-1] = held_until((in_own[-1], down_own[-1]), att_own)
    in_other = [swapped_cores(piece) for piece in in_own]
    down_other = [swapped_cores(piece) for piece in down_own]
    (mlp_info,) = held_until((info,), normed)
    many = ROWS // 2
    parts = (in_own, in_other, down_own, down_other)
    counts = tuple(len(part) for part in parts)
    (
        layer_out,
        hidden_grad,
        att_grad_own,
        att_grad_other,
        normed_two,
        gated_own,
        gated_other,
        pre_grad_own,
        pre_grad_other,
        hidden_grad_low,
        out_grad,
    ) = call(
        lambda *refs: mlp_kernel(orders, counts, *refs),
        mlp_info,
        (ROWS // many,),
        [tokens, att_own, att_other, cotangent, col_seg, gain_rows]
        + [piece for part in parts for piece in part],
        [by_rows(many, WIDTH), by_rows(many, THIRD), by_rows(many, THIRD), by_rows(many, WIDTH)]
        + [full(*cos_span.shape), full(8, WIDTH)]
        + [ANYWHERE] * sum(counts),
        [
            shape_of((ROWS, WIDTH)),
            shape_of((ROWS, WIDTH), F32),
            shape_of((ROWS, THIRD)),
            shape_of((ROWS, THIRD)),
            shape_of((ROWS, WIDTH)),
            shape_of((ROWS, UNITS + LANES)),
            shape_of((ROWS, UNITS + LANES)),
            shape_of((ROWS, HALF)),
            shape_of((ROWS, HALF)),
            shape_of((ROWS, WIDTH)),
            shape_of((ROWS, WIDTH)),
        ],
        [by_rows(many, WIDTH)] * 2
        + [by_rows(many, THIRD)] * 2
        + [by_rows(many, WIDTH)]
        + [by_rows(many, UNITS + LANES)] * 2
        + [by_rows(many, HALF)] * 2
        + [by_rows(many, WIDTH)] * 2,
        [
            pltpu.VMEM((WIDTH, 2 * HALF), BF16),
            pltpu.VMEM((WIDTH, 2 * DOWN), BF16),
            pltpu.SemaphoreType.DMA((2,)),
        ],
        2 * ROWS * WIDTH * (4 * HALF + 2 * HALF + 2 * WIDTH),
        58,
    )

    def down_grads(att, gated):
        parts = [weight_grad(hidden_grad_low, att), weight_grad(out_grad, gated)]
        return jnp.concatenate(parts, axis=1)

    send_in = weight_grad(normed_two, pre_grad_other)
    send_down = down_grads(att_other, gated_other)
    keep_in = weight_grad(normed_two, pre_grad_own)
    keep_down = down_grads(att_own, gated_own)
    sum_in, in_back, in_sent = scatter_start(keep_in, swapped_cores(send_in), own_rows, False)
    sum_down, down_back, down_sent = scatter_start(keep_down, swapped_cores(send_down), own_rows, True)

    grad_own, grad_other, edge_grad = call(
        attend_back_kernel,
        info,
        (blocks,),
        [qkv, qkv, probs, att_grad_own, att_grad_other, cos_span, sin_span]
        + [cos_turned, sin_turned, qkv, edge],
        [by_rows(LANES, THIRD), other_queries, by_block, by_rows(LANES, THIRD), by_rows(LANES, THIRD)]
        + [full(*cos_span.shape)] * 2
        + [pl.BlockSpec((LANES, LANES), lambda i, s: (0, i))] * 2
        + [ANYWHERE] * 2,
        [shape_of((MORE_ROWS, HALF))] * 2 + [shape_of((WINDOW_HALF, 2 * WIDTH))],
        [full(MORE_ROWS, HALF)] * 2 + [full(WINDOW_HALF, 2 * WIDTH)],
        [
            pltpu.VMEM(window_shape, BF16),
            pltpu.VMEM(turned_shape, BF16),
            pltpu.VMEM((window_shape[0], WIDTH), F32),
            pltpu.VMEM((window_shape[0], WIDTH), F32),
            pltpu.SemaphoreType.DMA((PIECES + 1,)),
        ],
        blocks * PAIRS * 4 * 2 * SPAN * SPAN * LANES,
        58,
        after=[send_in, send_down, keep_in, keep_down],
    )
    edge_grad = swapped_cores(edge_grad)
    (normed,) = held_until((normed,), in_sent[2], down_sent[2])

    send_a = weight_grad(normed, grad_other[:, :FIRST_CUT])
    send_b = weight_grad(normed, grad_other[:, FIRST_CUT:])
    keep_a = weight_grad(normed, grad_own[:, :FIRST_CUT])
    keep_b = weight_grad(normed, grad_own[:, FIRST_CUT:])
    late_a, late_b = swapped_cores(send_a), swapped_cores(send_b)

    (late_info,) = held_until(
        (info,), keep_a, keep_b, late_a, late_b, in_back[2], down_back[2]
    )
    (grad_tokens,) = call(
        input_grad_kernel,
        late_info,
        (steps,),
        [tokens, grad_own, grad_other, edge_grad, hidden_grad, gain_rows, weight_qkv],
        [by_rows(rows, WIDTH), by_rows(rows, HALF), by_rows(rows, HALF)]
        + [full(WINDOW_HALF, 2 * WIDTH), by_rows(rows, WIDTH)]
        + [full(8, WIDTH), full(WIDTH, 2 * WIDE)],
        [shape_of((ROWS, WIDTH), F32)],
        [by_rows(rows, WIDTH)],
        [pltpu.VMEM((rows, HALF), BF16)],
        2 * ROWS * WIDTH * 2 * HALF,
        28,
    )
    sent_a = scatter_start(keep_a, late_a, own_rows, False)[2][1]
    sent_b = scatter_start(keep_b, late_b, own_rows, True)[2][1]
    sum_in, sum_down = held_until((sum_in, sum_down), sent_a, sent_b)
    owned_early = scatter_finish(sum_in, sum_down)
    gates = (grad_tokens, owned_early)
    sum_a, unused, unused = scatter_start(keep_a, late_a, own_rows, False, gates)
    sum_b, unused, unused = scatter_start(keep_b, late_b, own_rows, True, gates)
    owned_in, owned_down = owned_early[:, :HALF], owned_early[:, HALF:]

    flat_grad = scatter_finish(sum_a, sum_b)
    gain_grads = jnp.stack(
        [
            gain_part(flat_qkv, flat_grad, norm_attn_gain),
            gain_part(shard_in, owned_in, norm_mlp_gain),
        ]
    )
    owned_qkv = flat_grad.reshape(own_rows, 3, THIRD)
    owned_in = jnp.stack(
        [
            jnp.concatenate([owned_in[:, :UNITS], owned_in[:, 2 * UNITS : -64]], axis=1),
            jnp.concatenate([owned_in[:, UNITS : 2 * UNITS], owned_in[:, -64:]], axis=1),
        ],
        axis=1,
    )
    owned_attn = owned_down[:, :THIRD].T
    owned_out = owned_down[:, THIRD : THIRD + UNITS + HEAD_DIM].T
    (gain_grads,) = held_until((gain_grads,), owned_in, owned_attn, owned_out)
    gain_grads = gain_grads + swapped_cores(gain_grads)
    owned_gain_one, owned_gain_two = gain_grads[0], gain_grads[1]
    return (
        layer_out,
        grad_tokens,
        owned_gain_one,
        owned_qkv,
        owned_attn,
        owned_gain_two,
        owned_in,
        owned_out,
    )


def solution(mesh):
    placed = (
        P(("dp", "tensor"), None),
        P("dp"),
        P("dp"),
        P("dp", None, "tensor"),
        P("tensor", "dp"),
        P("dp"),
        P("dp", None, "tensor"),
        P("tensor", "dp"),
        P(("dp", "tensor"), None),
    )
    return jax.shard_map(
        body,
        mesh=mesh,
        in_specs=placed,
        out_specs=(
            P(("dp", "tensor"), None),
            P(("dp", "tensor"), None),
            P("dp"),
            P("dp", None, "tensor"),
            P("tensor", "dp"),
            P("dp"),
            P("dp", None, "tensor"),
            P("tensor", "dp"),
        ),
        check_vma=False,
    )
```

```python
import jax
import jax.numpy as jnp
from jax import lax
from jax.experimental import pallas as pl
from jax.experimental.pallas import tpu as pltpu
from jax.sharding import PartitionSpec as P

HEAD_DIM = 64
WINDOW_HALF = 64
PAD_BLOCK = 128
WIDTH = 768
ROWS = 1152
MORE_ROWS = ROWS + 64
HALF = 1152
LANES = 128
THIRD = 384
PAIRS = 6
SPAN = 2 * LANES
PIECES = ROWS // LANES + 1
BLOCKS = 3
STEPS = ROWS // LANES // BLOCKS
UNITS = 512
FIRST_CUT = 640
WIDE = HALF + LANES
DOWN = 384 + UNITS + LANES
MIB = 2**20
ANYWHERE = pl.BlockSpec(memory_space=pl.ANY)
F32 = jnp.float32
BF16 = jnp.bfloat16


def steps_of(devices, swapped):
    bits = [1 << i for i in range(devices.bit_length() - 1)]
    near, far = bits[:2], bits[2:]
    return far + (near if swapped else near[::-1])


def exchanged(block, mask):
    devices = lax.axis_size("dp")
    return lax.ppermute(block, "dp", [(i, i ^ mask) for i in range(devices)])


def swapped_cores(block):
    return lax.ppermute(block, "tensor", [(0, 1), (1, 0)])


def by_exchange(own_rows):
    devices = lax.axis_size("dp")
    return own_rows % 16 == 0 and devices & (devices - 1) == 0


def relative(own_rows, swapped):
    if not by_exchange(own_rows):
        return list(range(WIDTH // 48))
    order = [0]
    for mask in steps_of(lax.axis_size("dp"), swapped):
        order = order + [r ^ mask for r in order]
    return order


def held_until(arrays, *gates):
    return lax.optimization_barrier((tuple(arrays), gates))[0]


def gather_start(shard):
    masks = steps_of(lax.axis_size("dp"), False)
    held = shard[None]
    if not by_exchange(shard.shape[0]) or len(masks) <= 3:
        return [held]
    first, second = masks[:2]
    return [held] + [exchanged(held, mask) for mask in (first, second, first ^ second)]


def joined(pieces):
    return lax.optimization_barrier(jnp.concatenate(pieces, axis=0))


def gather_middle(held, swapped, gate=None):
    if by_exchange(held.shape[1]):
        masks = steps_of(lax.axis_size("dp"), swapped)
        for mask in masks[held.shape[0].bit_length() - 1 : -1]:
            arrived = exchanged(held, mask)
            if gate is not None:
                (arrived,) = held_until((arrived,), gate)
            held = jnp.concatenate([held, arrived], axis=0)
    return held


def gather_finish(held, swapped):
    if not by_exchange(held.shape[1]):
        whole = lax.all_gather(held[0], "dp", axis=0, tiled=True)
        return [whole.reshape(WIDTH // 48, 48, held.shape[2])]
    return [held, exchanged(held, steps_of(lax.axis_size("dp"), swapped)[-1])]


def scatter_start(keep, other, own_rows, swapped, first_gates=None):
    arrivals, sents = [other], [other]
    if not by_exchange(own_rows):
        total = keep.astype(F32) + other.astype(F32)
        total = lax.psum_scatter(total, "dp", scatter_dimension=0, tiled=True)
        return total[None], arrivals * 3, sents * 3
    devices = lax.axis_size("dp")
    index = lax.axis_index("dp")
    levels = devices.bit_length() - 1
    masks = steps_of(devices, swapped)
    last = 2 if len(masks) > 3 else 0
    shape = (2,) * levels + (own_rows, keep.shape[1])
    keep, other = keep.reshape(shape), other.reshape(shape)
    for mask in reversed(masks[last:]):
        axis = levels - mask.bit_length()
        bit = (index & mask) // mask
        part = lambda array, which: lax.dynamic_slice_in_dim(array, which, 1, axis).astype(F32)
        sent = (part(keep, 1 - bit) + part(other, 1 - bit)).astype(BF16)
        kept = (part(keep, bit) + part(other, bit)).astype(BF16)
        other = exchanged(sent, mask)
        arrivals.append(other)
        sents.append(sent)
        if first_gates is not None and len(arrivals) == 2:
            (other,) = held_until((other,), *first_gates)
        keep = kept
    total = keep.astype(F32) + other.astype(F32)
    return total.reshape(2**last, own_rows, -1), arrivals + [other] * 3, sents + [other] * 3


def scatter_finish(*totals):
    if totals[0].shape[0] == 1:
        return jnp.concatenate([total[0] for total in totals], axis=1)
    unit = steps_of(lax.axis_size("dp"), False)[0]
    place = (lax.axis_index("dp") // unit) % 4

    def rows_of(which):
        parts = [lax.dynamic_index_in_dim(total, which, 0, keepdims=False) for total in totals]
        return jnp.concatenate(parts, axis=1)

    arrived = [
        exchanged(rows_of(place ^ j).astype(BF16), unit * j).astype(F32) for j in range(1, 4)
    ]
    return rows_of(place) + (arrived[0] + arrived[1] + arrived[2])


def weight_grad(left, right):
    return lax.dot_general(
        left, right, (((0,), (0,)), ((), ())), preferred_element_type=F32
    ).astype(BF16)


def gain_part(weight, grad, gain):
    return jnp.sum(weight.astype(F32) * grad, axis=1) / gain.astype(F32)


def nt(left, right):
    return lax.dot_general(left, right, (((1,), (1,)), ((), ())), preferred_element_type=F32)


def nn(left, right):
    return jnp.dot(left, right, preferred_element_type=F32)


def start_slots(info, pieces, order, segments, sems):
    slot = 0
    for piece in pieces:
        rows = piece.shape[1]
        for at in range(piece.shape[0]):
            row = pl.multiple_of((info[0] ^ order[slot]) * rows, 16)
            for begin, width, target, column, sem in segments:
                pltpu.make_async_copy(
                    piece.at[at, :, pl.ds(begin, width)],
                    target.at[pl.ds(row, rows), pl.ds(column, width)],
                    sems.at[sem],
                ).start()
            slot += 1


def wait_whole(ref, sem):
    pltpu.make_async_copy(ref, ref, sem).wait()


def start_window(info, qkv_ref, edge_ref, window, sems):
    core = info[1]
    first = pl.multiple_of(jnp.where(core == 1, 0, WINDOW_HALF + ROWS), 16)
    last = pl.multiple_of(jnp.where(core == 1, WINDOW_HALF + ROWS, 0), 16)
    edge = pltpu.make_async_copy(
        edge_ref.at[:, pl.ds(0, 2 * WIDTH)],
        window.at[pl.ds(first, WINDOW_HALF), :],
        sems.at[PIECES],
    )
    edge.start()
    for piece in range(PIECES):
        begin, stop = piece_rows(piece)
        for part in range(2):
            for half in range(2):
                source = HALF * half + THIRD * (part + 1)
                target = WIDTH * part + THIRD * half
                pltpu.make_async_copy(
                    qkv_ref.at[pl.ds(begin - WINDOW_HALF, stop - begin), pl.ds(source, THIRD)],
                    window.at[pl.ds(begin, stop - begin), pl.ds(target, THIRD)],
                    sems.at[piece],
                ).start()
    window[pl.ds(last, WINDOW_HALF), :] = jnp.zeros((WINDOW_HALF, 2 * WIDTH), BF16)
    edge.wait()


def piece_rows(piece):
    return max(LANES * piece, WINDOW_HALF), min(LANES * (piece + 1), WINDOW_HALF + ROWS)


def wait_window(window, step, sems):
    for number in range(STEPS):
        first = BLOCKS * number + 1 if number else 0

        @pl.when(step == number)
        def _():
            for piece in range(first, BLOCKS * (number + 1) + 1):
                begin, stop = piece_rows(piece)
                wait_whole(window.at[pl.ds(begin, stop - begin), :], sems.at[piece])


def identity():
    row = lax.broadcasted_iota(jnp.int32, (LANES, LANES), 0)
    lane = lax.broadcasted_iota(jnp.int32, (LANES, LANES), 1)
    return jnp.where(row == lane, 1.0, 0.0).astype(BF16)


def turn_rows(unit, window, begin, row, turned_ref):
    for pair in range(PAIRS):
        lanes = slice(LANES * pair, LANES * (pair + 1))
        block = window[pl.ds(row, LANES), begin + LANES * pair : begin + LANES * (pair + 1)]
        turned_ref[lanes, pl.ds(row, LANES)] = nt(unit, block).astype(BF16)


def head_rows(columns):
    return jnp.concatenate([columns[:HEAD_DIM, :LANES], columns[HEAD_DIM:, LANES:]], axis=0)


def normalized(values):
    centred = values - jnp.mean(values, axis=-1, keepdims=True)
    spread = jnp.mean(centred * centred, axis=-1, keepdims=True)
    factor = lax.rsqrt(spread + 1e-05)
    return centred * factor, factor


def norm_backward(grad, unit, factor, gain):
    inner = grad * gain
    mean = jnp.mean(inner, axis=-1, keepdims=True)
    along = jnp.mean(inner * unit, axis=-1, keepdims=True)
    return factor * (inner - mean - unit * along)


def turned(values, cosine, sine):
    lane = lax.broadcasted_iota(jnp.int32, values.shape, 1)
    first = (lane & 32) == 0
    other = jnp.where(first, pltpu.roll(values, 96, 1), pltpu.roll(values, 32, 1))
    return values * cosine + other * sine


def both_heads(block):
    lane = lax.broadcasted_iota(jnp.int32, block.shape, 1)
    first = jnp.where(lane < HEAD_DIM, 1.0, 0.0).astype(block.dtype)
    second = jnp.where(lane < HEAD_DIM, 0.0, 1.0).astype(block.dtype)
    return jnp.concatenate([block * first, block * second], axis=0)


def table_kernel(cos_in, sin_in, seg_ref, cos_ref, sin_ref, cos_turned, sin_turned, col_ref):
    cos_ref[...] = cos_in[...]
    sin_ref[...] = sin_in[...]
    for block in range(ROWS // LANES):
        rows = slice(WINDOW_HALF + LANES * block, WINDOW_HALF + LANES * (block + 1))
        lanes = slice(LANES * block, LANES * (block + 1))
        cos_turned[:, lanes] = cos_in[rows, :].T
        sin_turned[:, lanes] = sin_in[rows, :].T
    for block in range(PIECES):
        row = jnp.broadcast_to(seg_ref[block : block + 1, :].astype(F32), (LANES, LANES))
        col_ref[LANES * block : LANES * (block + 1), :] = row.T.astype(jnp.int32)


def qkv_kernel(orders, counts, info, x_ref, cos_ref, sin_ref, *refs):
    parts = []
    for count in counts:
        parts.append(refs[:count])
        refs = refs[count:]
    own_a, other_a, own_b, other_b = parts
    qkv_ref, normed_ref, gain_ref, edge_ref, weight_ref, weight, sems = refs
    step = pl.program_id(0)
    rows = x_ref.shape[0]

    @pl.when(step == 0)
    def _():
        for begin, part_a, part_b in ((0, own_a, own_b), (WIDE, other_a, other_b)):
            start_slots(info, part_a, orders[0], [(0, FIRST_CUT, weight, begin, 0)], sems)
            start_slots(
                info,
                part_b,
                orders[1],
                [(0, WIDE - FIRST_CUT, weight, begin + FIRST_CUT, 0)],
                sems,
            )
        wait_whole(weight, sems.at[0])
        pltpu.make_async_copy(weight, weight_ref, sems.at[1]).start()
        row = lax.broadcasted_iota(jnp.int32, (16, LANES), 0)
        lane = lax.broadcasted_iota(jnp.int32, (16, LANES), 1)
        pick = jnp.where(row == lane, 1.0, 0.0).astype(BF16)
        gain_ref[...] = nt(pick, weight[:, HALF:WIDE])[:8]

    unit, unused = normalized(x_ref[...].astype(F32))
    normed = (unit * gain_ref[0:1, :]).astype(BF16)
    normed_ref[...] = normed
    table_rows = pl.ds(pl.multiple_of(WINDOW_HALF + step * rows, WINDOW_HALF), rows)
    cosine, sine = cos_ref[table_rows, :], sin_ref[table_rows, :]
    for half in range(2):
        result = nn(normed, weight[:, WIDE * half : WIDE * half + HALF])
        for tile in range(9):
            block = result[:, LANES * tile : LANES * (tile + 1)]
            if tile < 6:
                block = turned(block, cosine, sine)
            if tile < 3:
                block = block * (HEAD_DIM**-0.5)
            begin = HALF * half + LANES * tile
            qkv_ref[:, begin : begin + LANES] = block.astype(BF16)

    for core, at_step, begin in ((1, 0, 0), (0, ROWS // rows - 1, rows - WINDOW_HALF)):

        @pl.when((info[1] == core) & (step == at_step))
        def _():
            for part in range(2):
                for half in range(2):
                    source = HALF * half + THIRD * (part + 1)
                    target = WIDTH * part + THIRD * (1 - half)
                    edge_ref[:, target : target + THIRD] = qkv_ref[
                        begin : begin + WINDOW_HALF, source : source + THIRD
                    ]
            edge_ref[:, 2 * WIDTH :] = normed_ref[begin : begin + WINDOW_HALF, :]

    @pl.when(step == ROWS // rows - 1)
    def _():
        pltpu.make_async_copy(weight, weight_ref, sems.at[1]).wait()


def attend_kernel(
    info,
    row_seg,
    col_seg,
    q_own,
    q_other,
    qkv_ref,
    edge_ref,
    own_ref,
    other_ref,
    probs_ref,
    window,
    turned_values,
    sems,
):
    step = pl.program_id(0)
    unit = identity()

    @pl.when(step == 0)
    def _():
        start_window(info, qkv_ref, edge_ref, window, sems)

    wait_window(window, step, sems)

    @pl.when(step == 0)
    def _():
        turn_rows(unit, window, WIDTH, 0, turned_values)

    for block in range(BLOCKS):
        rows = slice(LANES * block, LANES * (block + 1))
        start = pl.multiple_of((step * BLOCKS + block) * LANES, LANES)
        turn_rows(unit, window, WIDTH, pl.multiple_of(start + LANES, LANES), turned_values)
        key_seg = col_seg[pl.ds(start, SPAN), :]
        key_at = lax.broadcasted_iota(jnp.int32, (SPAN, LANES), 0) - WINDOW_HALF
        query_at = lax.broadcasted_iota(jnp.int32, (SPAN, LANES), 1)
        near = jnp.abs(key_at - query_at) <= WINDOW_HALF
        allowed = (key_seg == row_seg[block]) & near
        bias = jnp.where(allowed, 0.0, -1e30)
        bias = jnp.concatenate([bias, bias], axis=1)

        scores, probs, results = [], [], []
        for pair in range(PAIRS):
            q_ref = q_own if pair < 3 else q_other
            queries = both_heads(q_ref[rows, LANES * (pair % 3) : LANES * (pair % 3 + 1)])
            keys = window[pl.ds(start, SPAN), LANES * pair : LANES * (pair + 1)]
            scores.append(nt(keys, queries) + bias)
        for pair in range(PAIRS):
            weights = jnp.exp(scores[pair] - jnp.max(scores[pair], axis=0, keepdims=True))
            total = jnp.sum(weights, axis=0, keepdims=True)
            probs.append((weights * (1.0 / total)).astype(BF16))
            probs_ref[block, pair] = probs[pair]
        for pair in range(PAIRS):
            values = turned_values[LANES * pair : LANES * (pair + 1), pl.ds(start, SPAN)]
            results.append(head_rows(nn(values, probs[pair])).astype(BF16))
        for pair in range(PAIRS):
            out_ref = own_ref if pair < 3 else other_ref
            out_ref[rows, LANES * (pair % 3) : LANES * (pair % 3 + 1)] = nt(unit, results[pair]).astype(
                BF16
            )


def mlp_kernel(orders, counts, info, x_ref, att_own, att_other, cot_ref, col_seg, gain_ref, *refs):
    parts = []
    for count in counts:
        parts.append(refs[:count])
        refs = refs[count:]
    in_own, in_other, down_own, down_other = parts
    (
        out_ref,
        hidden_grad_ref,
        att_grad_own,
        att_grad_other,
        normed_ref,
        gated_own,
        gated_other,
        pre_grad_own,
        pre_grad_other,
        low_grad_ref,
        out_grad_ref,
        w_in,
        w_down,
        sems,
    ) = refs
    step = pl.program_id(0)

    @pl.when(step == 0)
    def _():
        for number, part in enumerate((down_own, down_other)):
            start_slots(info, part, orders[1], [(0, DOWN, w_down, DOWN * number, 0)], sems)
        for number, part in enumerate((in_own, in_other)):
            start_slots(info, part, orders[0], [(0, HALF, w_in, HALF * number, 1)], sems)
        wait_whole(w_down, sems.at[0])
        other = pltpu.roll(w_down[:, 2 * DOWN - LANES :].astype(F32), HEAD_DIM, 1).astype(BF16)
        w_down[:, DOWN - LANES : DOWN] += other

    gain = gain_ref[1:2, :]
    hidden = (
        x_ref[...].astype(F32)
        + nt(att_own[...], w_down[:, :THIRD])
        + nt(att_other[...], w_down[:, DOWN : DOWN + THIRD])
    )
    unit, factor = normalized(hidden)
    normed = (unit * gain).astype(BF16)
    normed_ref[...] = normed
    seg_rows = pl.ds(pl.multiple_of(WINDOW_HALF + step * x_ref.shape[0], WINDOW_HALF), x_ref.shape[0])
    live = jnp.where(col_seg[seg_rows, :] >= 0, 1.0, 0.0)
    live = jnp.concatenate([live] * (WIDTH // LANES), axis=1)
    out_grad = cot_ref[...].astype(F32) * live
    out_grad_low = out_grad.astype(BF16)
    out_grad_ref[...] = out_grad_low

    @pl.when(step == 0)
    def _():
        wait_whole(w_in, sems.at[1])

    pre = [nn(normed, w_in[:, HALF * half : HALF * (half + 1)]) for half in range(2)]
    tails = [part[:, 2 * UNITS :] for part in pre]
    lane = lax.broadcasted_iota(jnp.int32, tails[0].shape, 1)
    low = lane < HEAD_DIM
    gates = [part[:, :UNITS] for part in pre]
    gates.append(jnp.where(low, tails[0], pltpu.roll(tails[1], 64, 1)))
    ups = [part[:, UNITS : 2 * UNITS] for part in pre]
    ups.append(jnp.where(low, pltpu.roll(tails[0], 64, 1), tails[1]))
    pre_grads = (pre_grad_own, pre_grad_other)
    unit_columns = (
        slice(THIRD, THIRD + UNITS),
        slice(DOWN + THIRD, DOWN + THIRD + UNITS),
        slice(DOWN - LANES, DOWN),
    )
    for part, (gate, up) in enumerate(zip(gates, ups)):
        share = 0.5 + 0.5 * lax.erf(gate * (0.5**0.5))
        slope = share + gate * (jnp.exp(-0.5 * gate * gate) * 0.3989422804014327)
        curve = gate * share
        gated = curve * up
        grad = nn(out_grad_low, w_down[:, unit_columns[part]])
        gate_grad = grad * up * slope
        up_grad = grad * curve
        if part < 2:
            (gated_own, gated_other)[part][:, :UNITS] = gated.astype(BF16)
            pre_grads[part][:, :UNITS] = gate_grad.astype(BF16)
            pre_grads[part][:, UNITS : 2 * UNITS] = up_grad.astype(BF16)
        else:
            gated_own[:, UNITS:] = gated.astype(BF16)
            gated_other[:, UNITS:] = pltpu.roll(gated, HEAD_DIM, 1).astype(BF16)
            own = jnp.where(low, gate_grad, pltpu.roll(up_grad, 64, 1))
            other = jnp.where(low, pltpu.roll(gate_grad, 64, 1), up_grad)
            pre_grad_own[:, 2 * UNITS :] = own.astype(BF16)
            pre_grad_other[:, 2 * UNITS :] = other.astype(BF16)
    product = (
        nt(gated_own[...], w_down[:, THIRD:DOWN])
        + nt(gated_other[:, :UNITS], w_down[:, unit_columns[1]])
    )
    out_ref[...] = (hidden + product).astype(BF16)
    normed_grad = nt(pre_grad_own[...], w_in[:, :HALF]) + nt(pre_grad_other[...], w_in[:, HALF:])
    hidden_grad = out_grad + norm_backward(normed_grad, unit, factor, gain)
    hidden_grad_ref[...] = hidden_grad
    hidden_grad_low = hidden_grad.astype(BF16)
    low_grad_ref[...] = hidden_grad_low
    att_grad_own[...] = nn(hidden_grad_low, w_down[:, :THIRD]).astype(BF16)
    att_grad_other[...] = nn(hidden_grad_low, w_down[:, DOWN : DOWN + THIRD]).astype(BF16)


def attend_back_kernel(
    info,
    q_own,
    q_other,
    probs_ref,
    grad_own,
    grad_other,
    cos_ref,
    sin_ref,
    cos_turned,
    sin_turned,
    qkv_ref,
    edge_ref,
    out_own,
    out_other,
    edge_out_ref,
    window,
    turned_keys,
    key_grad,
    value_grad,
    sems,
):
    step = pl.program_id(0)
    unit = identity()

    @pl.when(step == 0)
    def _():
        start_window(info, qkv_ref, edge_ref, window, sems)
        key_grad[...] = jnp.zeros_like(key_grad)
        value_grad[...] = jnp.zeros_like(value_grad)

    wait_window(window, step, sems)

    @pl.when(step == 0)
    def _():
        turn_rows(unit, window, 0, 0, turned_keys)

    for block in range(BLOCKS):
        rows = slice(LANES * block, LANES * (block + 1))
        start = pl.multiple_of((step * BLOCKS + block) * LANES, LANES)
        span = pl.ds(start, SPAN)
        turn_rows(unit, window, 0, pl.multiple_of(start + LANES, LANES), turned_keys)
        cosine, sine = cos_turned[:, rows], sin_turned[:, rows]

        all_lanes = [slice(LANES * pair, LANES * (pair + 1)) for pair in range(PAIRS)]
        grads, probs_grads, score_grads, query_grads = [], [], [], []
        for pair, lanes in enumerate(all_lanes):
            grad_ref = grad_own if pair < 3 else grad_other
            grads.append(both_heads(grad_ref[rows, LANES * (pair % 3) : LANES * (pair % 3 + 1)]))
            values = window[span, WIDTH + LANES * pair : WIDTH + LANES * (pair + 1)]
            probs_grads.append(nt(values, grads[pair]))
        for pair, lanes in enumerate(all_lanes):
            value_grad[span, lanes] += nn(probs_ref[block, pair], grads[pair])
        for pair in range(PAIRS):
            probs = probs_ref[block, pair].astype(F32)
            weighted = probs_grads[pair] * probs
            delta = jnp.sum(weighted, axis=0, keepdims=True)
            score_grads.append((weighted - probs * delta).astype(BF16))
        for pair, lanes in enumerate(all_lanes):
            query_grads.append(head_rows(nn(turned_keys[lanes, span], score_grads[pair])))
        for pair, lanes in enumerate(all_lanes):
            q_ref = q_own if pair < 3 else q_other
            queries = both_heads(q_ref[rows, LANES * (pair % 3) : LANES * (pair % 3 + 1)])
            key_grad[span, lanes] += nn(score_grads[pair], queries)
        for pair in range(PAIRS):
            grad = query_grads[pair] * (HEAD_DIM**-0.5)
            other = jnp.concatenate([grad[32:64], grad[:32], grad[96:], grad[64:96]], axis=0)
            query_grads[pair] = (grad * cosine - other * sine).astype(BF16)
        for pair in range(PAIRS):
            out_ref = out_own if pair < 3 else out_other
            place = slice(LANES * (pair % 3), LANES * (pair % 3 + 1))
            out_ref[pl.ds(start, LANES), place] = nt(unit, query_grads[pair]).astype(BF16)

    @pl.when(step == STEPS - 1)
    def _():
        inside = slice(WINDOW_HALF, WINDOW_HALF + ROWS)
        row = pl.multiple_of(jnp.where(info[1] == 1, 0, WINDOW_HALF + ROWS), 16)
        edge_rows = pl.ds(row, WINDOW_HALF)
        for pair in range(PAIRS):
            out_ref = out_own if pair < 3 else out_other
            lanes = slice(LANES * pair, LANES * (pair + 1))
            begin = LANES * (pair % 3)
            target = (LANES * pair + THIRD) % WIDTH
            keys_at = slice(THIRD + begin, THIRD + begin + LANES)
            values_at = slice(2 * THIRD + begin, 2 * THIRD + begin + LANES)
            out_ref[:ROWS, keys_at] = turned(
                key_grad[inside, lanes], cos_ref[inside, :], -sin_ref[inside, :]
            ).astype(BF16)
            out_ref[:ROWS, values_at] = value_grad[inside, lanes].astype(BF16)
            edge_keys = turned(
                key_grad[edge_rows, lanes], cos_ref[edge_rows, :], -sin_ref[edge_rows, :]
            ).astype(BF16)
            edge_values = value_grad[edge_rows, lanes].astype(BF16)
            edge_out_ref[:, target : target + LANES] = edge_keys
            edge_out_ref[:, WIDTH + target : WIDTH + target + LANES] = edge_values
            out_ref[ROWS:, begin : begin + LANES] = jnp.zeros((WINDOW_HALF, LANES), BF16)
            out_ref[ROWS:, keys_at] = edge_keys
            out_ref[ROWS:, values_at] = edge_values


def input_grad_kernel(
    info, x_ref, own_ref, other_ref, edge_ref, hidden_ref, gain_ref, weight, out_ref, fixed
):
    rows = x_ref.shape[0]
    step = pl.program_id(0)
    grad = None
    for half, grad_ref in enumerate((own_ref, other_ref)):
        fixed[...] = grad_ref[...]
        for core, at_step, begin in ((1, 0, 0), (0, ROWS // rows - 1, rows - WINDOW_HALF)):

            @pl.when((info[1] == core) & (step == at_step))
            def _():
                at = slice(begin, begin + WINDOW_HALF)
                for part in range(2):
                    to = slice(THIRD * (part + 1), THIRD * (part + 2))
                    source = WIDTH * part + THIRD * half
                    add = edge_ref[:, source : source + THIRD].astype(F32)
                    fixed[at, to] = (fixed[at, to].astype(F32) + add).astype(BF16)

        part = nt(fixed[...], weight[:, WIDE * half : WIDE * half + HALF])
        grad = part if grad is None else grad + part
    unit, factor = normalized(x_ref[...].astype(F32))
    out_ref[...] = hidden_ref[...] + norm_backward(grad, unit, factor, gain_ref[0:1, :])


def shape_of(shape, dtype=BF16):
    return jax.ShapeDtypeStruct(shape, dtype)


def call(
    kernel, info, grid, ins, in_specs, outs, out_specs, scratch, flops, vmem, after=()
):
    moved = sum(a.size * a.dtype.itemsize for a in list(ins) + list(outs))
    first = 1 + len(ins)
    later = first + len(after)
    return pl.pallas_call(
        lambda *refs: kernel(*refs[:first], *refs[later:]),
        out_shape=outs,
        grid_spec=pltpu.PrefetchScalarGridSpec(
            num_scalar_prefetch=1,
            grid=grid,
            in_specs=list(in_specs) + [ANYWHERE] * len(after),
            out_specs=out_specs,
            scratch_shapes=scratch,
        ),
        compiler_params=pltpu.CompilerParams(
            dimension_semantics=("arbitrary",), vmem_limit_bytes=vmem * MIB
        ),
        cost_estimate=pl.CostEstimate(
            flops=int(flops), bytes_accessed=int(moved), transcendentals=0
        ),
    )(info, *ins, *after)


def by_rows(rows, columns):
    return pl.BlockSpec((rows, columns), lambda i, s: (i, 0))


def full(*shape):
    return pl.BlockSpec(shape, lambda i, s: (0,) * len(shape))


def body(
    tokens,
    segment,
    norm_attn_gain,
    qkv_weight,
    attn_out_weight,
    norm_mlp_gain,
    in_weight,
    out_weight,
    cotangent,
):
    own_rows = norm_attn_gain.shape[0]
    core = lax.axis_index("tensor")
    place = lax.axis_index("dp") if by_exchange(own_rows) else 0
    info = jnp.stack([jnp.int32(place), core.astype(jnp.int32)])
    orders = (relative(own_rows, False), relative(own_rows, True))

    gains = jnp.pad(jnp.stack([norm_attn_gain, norm_mlp_gain], axis=1), ((0, 0), (0, LANES - 2)))
    flat_qkv = qkv_weight.reshape(own_rows, HALF)
    first_pieces = gather_start(jnp.concatenate([flat_qkv, gains], axis=1))
    shard_in = jnp.concatenate(
        [
            in_weight[:, 0, :UNITS],
            in_weight[:, 1, :UNITS],
            in_weight[:, 0, UNITS:],
            in_weight[:, 1, UNITS:],
        ],
        axis=1,
    )
    turned_out = out_weight.T
    blank = jnp.zeros((own_rows, HEAD_DIM), BF16)
    shard_down = jnp.concatenate([attn_out_weight.T, turned_out, blank], axis=1)
    second_shard = jnp.concatenate([shard_in, shard_down], axis=1)
    second_shard, *first_pieces = held_until([second_shard] + first_pieces)
    second_pieces = gather_start(second_shard)

    own_segment = lax.dynamic_slice_in_dim(segment, core * ROWS, ROWS, 0)
    seg_pad = jnp.pad(segment, (WINDOW_HALF, WINDOW_HALF), constant_values=-2)
    span_segment = lax.dynamic_slice_in_dim(seg_pad, core * ROWS, ROWS + 2 * WINDOW_HALF, 0)
    slot = core * ROWS - WINDOW_HALF + jnp.arange(ROWS + 2 * WINDOW_HALF, dtype=jnp.int32)
    position = jnp.where(span_segment >= 0, slot - PAD_BLOCK * span_segment, 0)
    lane = jnp.arange(LANES, dtype=jnp.int32)
    exponent = (lane % 32).astype(F32) * (2.0 / HEAD_DIM)
    angle = position.astype(F32)[:, None] * jnp.power(10000.0, -exponent)[None, :]
    cos_span = jnp.cos(angle)
    sin_span = jnp.sin(angle) * jnp.where((lane & 32) == 0, -1.0, 1.0)[None, :]
    table_shape = shape_of(cos_span.shape, F32)
    turned_table = shape_of((LANES, ROWS), F32)
    cos_span, sin_span, cos_turned, sin_turned, col_seg = pl.pallas_call(
        table_kernel,
        out_shape=[
            table_shape,
            table_shape,
            turned_table,
            turned_table,
            shape_of(cos_span.shape, jnp.int32),
        ],
        compiler_params=pltpu.CompilerParams(vmem_limit_bytes=58 * MIB),
    )(cos_span, sin_span, span_segment.reshape(PIECES, LANES))
    row_seg = own_segment.reshape(ROWS // LANES, 1, LANES)

    rows = 384
    steps = ROWS // rows
    first_held = joined(first_pieces)
    held_a, held_b = first_held[:, :, :FIRST_CUT], first_held[:, :, FIRST_CUT:]
    own_a = gather_finish(gather_middle(held_a, False), False)
    own_b = gather_finish(gather_middle(held_b, True), True)
    second_held = joined(second_pieces)
    held_in, held_down = second_held[:, :, :HALF], second_held[:, :, HALF:]
    own_a[-1], own_b[-1] = held_until(
        (own_a[-1], own_b[-1]), held_in, held_down, cos_span, row_seg, info
    )
    own_a, own_b = [jnp.concatenate(own_a, axis=0)], [jnp.concatenate(own_b, axis=0)]
    other_a, other_b = [swapped_cores(own_a[0])], [swapped_cores(own_b[0])]

    parts = (own_a, other_a, own_b, other_b)
    counts_qkv = tuple(len(part) for part in parts)
    qkv, normed, gain_rows, edge, weight_qkv = call(
        lambda *refs: qkv_kernel(orders, counts_qkv, *refs),
        info,
        (steps,),
        [tokens, cos_span, sin_span] + [piece for part in parts for piece in part],
        [by_rows(rows, WIDTH), full(*cos_span.shape), full(*cos_span.shape)]
        + [ANYWHERE] * sum(counts_qkv),
        [
            shape_of((ROWS, 2 * HALF)),
            shape_of((MORE_ROWS, WIDTH)),
            shape_of((8, WIDTH), F32),
            shape_of((WINDOW_HALF, 3 * WIDTH)),
            shape_of((WIDTH, 2 * WIDE)),
        ],
        [by_rows(rows, 2 * HALF), by_rows(rows, WIDTH), full(8, WIDTH)]
        + [full(WINDOW_HALF, 3 * WIDTH), ANYWHERE],
        [
            pltpu.VMEM((WIDTH, 2 * WIDE), BF16),
            pltpu.SemaphoreType.DMA((2,)),
        ],
        2 * ROWS * WIDTH * 2 * HALF,
        58,
    )
    edge = swapped_cores(edge)
    normed = lax.dynamic_update_slice(normed, edge[:, 2 * WIDTH :], (ROWS, 0))
    held_in = gather_middle(held_in, False, qkv)
    held_down = gather_middle(held_down, True, qkv)
    in_own, down_own = gather_finish(held_in, False), gather_finish(held_down, True)

    blocks = ROWS // LANES
    window_shape = (ROWS + 2 * WINDOW_HALF, 2 * WIDTH)
    turned_shape = (WIDTH, ROWS + 2 * WINDOW_HALF)
    step_rows = BLOCKS * LANES
    other_queries = pl.BlockSpec((step_rows, THIRD), lambda i, s: (i, HALF // THIRD))
    by_block = pl.BlockSpec((BLOCKS, PAIRS, SPAN, SPAN), lambda i, s: (i, 0, 0, 0))
    att_own, att_other, probs = call(
        attend_kernel,
        info,
        (STEPS,),
        [row_seg, col_seg, qkv, qkv, qkv, edge],
        [
            pl.BlockSpec((BLOCKS, 1, LANES), lambda i, s: (i, 0, 0)),
            full(ROWS + 2 * WINDOW_HALF, LANES),
            by_rows(step_rows, THIRD),
            other_queries,
            ANYWHERE,
            ANYWHERE,
        ],
        [
            shape_of((ROWS, THIRD)),
            shape_of((ROWS, THIRD)),
            shape_of((blocks, PAIRS, SPAN, SPAN)),
        ],
        [by_rows(step_rows, THIRD), by_rows(step_rows, THIRD), by_block],
        [
            pltpu.VMEM(window_shape, BF16),
            pltpu.VMEM(turned_shape, BF16),
            pltpu.SemaphoreType.DMA((PIECES + 1,)),
        ],
        blocks * PAIRS * 2 * 2 * SPAN * SPAN * LANES,
        58,
        after=[held_in, held_down],
    )

    in_own[-1], down_own[-1] = held_until((in_own[-1], down_own[-1]), att_own)
    in_other = [swapped_cores(piece) for piece in in_own]
    down_other = [swapped_cores(piece) for piece in down_own]
    (mlp_info,) = held_until((info,), normed)
    parts = (in_own, in_other, down_own, down_other)
    counts = tuple(len(part) for part in parts)
    (
        layer_out,
        hidden_grad,
        att_grad_own,
        att_grad_other,
        normed_two,
        gated_own,
        gated_other,
        pre_grad_own,
        pre_grad_other,
        hidden_grad_low,
        out_grad,
    ) = call(
        lambda *refs: mlp_kernel(orders, counts, *refs),
        mlp_info,
        (steps,),
        [tokens, att_own, att_other, cotangent, col_seg, gain_rows]
        + [piece for part in parts for piece in part],
        [by_rows(rows, WIDTH), by_rows(rows, THIRD), by_rows(rows, THIRD), by_rows(rows, WIDTH)]
        + [full(*cos_span.shape), full(8, WIDTH)]
        + [ANYWHERE] * sum(counts),
        [
            shape_of((ROWS, WIDTH)),
            shape_of((ROWS, WIDTH), F32),
            shape_of((ROWS, THIRD)),
            shape_of((ROWS, THIRD)),
            shape_of((ROWS, WIDTH)),
            shape_of((ROWS, UNITS + LANES)),
            shape_of((ROWS, UNITS + LANES)),
            shape_of((ROWS, HALF)),
            shape_of((ROWS, HALF)),
            shape_of((ROWS, WIDTH)),
            shape_of((ROWS, WIDTH)),
        ],
        [by_rows(rows, WIDTH)] * 2
        + [by_rows(rows, THIRD)] * 2
        + [by_rows(rows, WIDTH)]
        + [by_rows(rows, UNITS + LANES)] * 2
        + [by_rows(rows, HALF)] * 2
        + [by_rows(rows, WIDTH)] * 2,
        [
            pltpu.VMEM((WIDTH, 2 * HALF), BF16),
            pltpu.VMEM((WIDTH, 2 * DOWN), BF16),
            pltpu.SemaphoreType.DMA((2,)),
        ],
        2 * ROWS * WIDTH * (4 * HALF + 2 * HALF + 2 * WIDTH),
        58,
    )

    def down_grads(att, gated):
        parts = [weight_grad(hidden_grad_low, att), weight_grad(out_grad, gated)]
        return jnp.concatenate(parts, axis=1)

    send_in = weight_grad(normed_two, pre_grad_other)
    send_down = down_grads(att_other, gated_other)
    keep_in = weight_grad(normed_two, pre_grad_own)
    keep_down = down_grads(att_own, gated_own)
    sum_in, in_back, in_sent = scatter_start(keep_in, swapped_cores(send_in), own_rows, False)
    sum_down, down_back, down_sent = scatter_start(keep_down, swapped_cores(send_down), own_rows, True)

    grad_own, grad_other, edge_grad = call(
        attend_back_kernel,
        info,
        (STEPS,),
        [qkv, qkv, probs, att_grad_own, att_grad_other, cos_span, sin_span]
        + [cos_turned, sin_turned, qkv, edge],
        [by_rows(step_rows, THIRD), other_queries, by_block]
        + [by_rows(step_rows, THIRD)] * 2
        + [full(*cos_span.shape)] * 2
        + [pl.BlockSpec((LANES, step_rows), lambda i, s: (0, i))] * 2
        + [ANYWHERE] * 2,
        [shape_of((MORE_ROWS, HALF))] * 2 + [shape_of((WINDOW_HALF, 2 * WIDTH))],
        [full(MORE_ROWS, HALF)] * 2 + [full(WINDOW_HALF, 2 * WIDTH)],
        [
            pltpu.VMEM(window_shape, BF16),
            pltpu.VMEM(turned_shape, BF16),
            pltpu.VMEM((window_shape[0], WIDTH), F32),
            pltpu.VMEM((window_shape[0], WIDTH), F32),
            pltpu.SemaphoreType.DMA((PIECES + 1,)),
        ],
        blocks * PAIRS * 4 * 2 * SPAN * SPAN * LANES,
        58,
        after=[send_in, send_down, keep_in, keep_down],
    )
    edge_grad = swapped_cores(edge_grad)
    (normed,) = held_until((normed,), in_sent[2], down_sent[2])

    send_a = weight_grad(normed, grad_other[:, :FIRST_CUT])
    send_b = weight_grad(normed, grad_other[:, FIRST_CUT:])
    keep_a = weight_grad(normed, grad_own[:, :FIRST_CUT])
    keep_b = weight_grad(normed, grad_own[:, FIRST_CUT:])
    late_a, late_b = swapped_cores(send_a), swapped_cores(send_b)

    (late_info,) = held_until(
        (info,), keep_a, keep_b, late_a, late_b, in_back[2], down_back[2]
    )
    (grad_tokens,) = call(
        input_grad_kernel,
        late_info,
        (steps,),
        [tokens, grad_own, grad_other, edge_grad, hidden_grad, gain_rows, weight_qkv],
        [by_rows(rows, WIDTH), by_rows(rows, HALF), by_rows(rows, HALF)]
        + [full(WINDOW_HALF, 2 * WIDTH), by_rows(rows, WIDTH)]
        + [full(8, WIDTH), full(WIDTH, 2 * WIDE)],
        [shape_of((ROWS, WIDTH), F32)],
        [by_rows(rows, WIDTH)],
        [pltpu.VMEM((rows, HALF), BF16)],
        2 * ROWS * WIDTH * 2 * HALF,
        28,
    )
    sent_a = scatter_start(keep_a, late_a, own_rows, False)[2][1]
    sent_b = scatter_start(keep_b, late_b, own_rows, True)[2][1]
    sum_in, sum_down = held_until((sum_in, sum_down), sent_a, sent_b)
    owned_early = scatter_finish(sum_in, sum_down)
    gates = (grad_tokens, owned_early)
    sum_a, unused, unused = scatter_start(keep_a, late_a, own_rows, False, gates)
    sum_b, unused, unused = scatter_start(keep_b, late_b, own_rows, True, gates)
    owned_in, owned_down = owned_early[:, :HALF], owned_early[:, HALF:]

    flat_grad = scatter_finish(sum_a, sum_b)
    gain_grads = jnp.stack(
        [
            gain_part(flat_qkv, flat_grad, norm_attn_gain),
            gain_part(shard_in, owned_in, norm_mlp_gain),
        ]
    )
    owned_qkv = flat_grad.reshape(own_rows, 3, THIRD)
    owned_in = jnp.stack(
        [
            jnp.concatenate([owned_in[:, :UNITS], owned_in[:, 2 * UNITS : -64]], axis=1),
            jnp.concatenate([owned_in[:, UNITS : 2 * UNITS], owned_in[:, -64:]], axis=1),
        ],
        axis=1,
    )
    owned_attn = owned_down[:, :THIRD].T
    owned_out = owned_down[:, THIRD : THIRD + UNITS + HEAD_DIM].T
    (gain_grads,) = held_until((gain_grads,), owned_in, owned_attn, owned_out)
    gain_grads = gain_grads + swapped_cores(gain_grads)
    owned_gain_one, owned_gain_two = gain_grads[0], gain_grads[1]
    return (
        layer_out,
        grad_tokens,
        owned_gain_one,
        owned_qkv,
        owned_attn,
        owned_gain_two,
        owned_in,
        owned_out,
    )


def solution(mesh):
    placed = (
        P(("dp", "tensor"), None),
        P("dp"),
        P("dp"),
        P("dp", None, "tensor"),
        P("tensor", "dp"),
        P("dp"),
        P("dp", None, "tensor"),
        P("tensor", "dp"),
        P(("dp", "tensor"), None),
    )
    return jax.shard_map(
        body,
        mesh=mesh,
        in_specs=placed,
        out_specs=(
            P(("dp", "tensor"), None),
            P(("dp", "tensor"), None),
            P("dp"),
            P("dp", None, "tensor"),
            P("tensor", "dp"),
            P("dp"),
            P("dp", None, "tensor"),
            P("tensor", "dp"),
        ),
        check_vma=False,
    )
```

```python
import jax
import jax.numpy as jnp
from jax import lax
from jax.experimental import pallas as pl
from jax.experimental.pallas import tpu as pltpu
from jax.sharding import PartitionSpec as P

HEAD_DIM = 64
WINDOW_HALF = 64
PAD_BLOCK = 128
WIDTH = 768
ROWS = 1152
MORE_ROWS = ROWS + 64
HALF = 1152
LANES = 128
THIRD = 384
PAIRS = 6
SPAN = 2 * LANES
PIECES = ROWS // LANES + 1
BLOCKS = 3
STEPS = ROWS // LANES // BLOCKS
UNITS = 512
FIRST_CUT = 640
WIDE = HALF + LANES
DOWN = 384 + UNITS + LANES
MIB = 2**20
ANYWHERE = pl.BlockSpec(memory_space=pl.ANY)
F32 = jnp.float32
BF16 = jnp.bfloat16


def steps_of(devices, swapped):
    bits = [1 << i for i in range(devices.bit_length() - 1)]
    near, far = bits[:2], bits[2:]
    return far + (near if swapped else near[::-1])


def exchanged(block, mask):
    devices = lax.axis_size("dp")
    return lax.ppermute(block, "dp", [(i, i ^ mask) for i in range(devices)])


def swapped_cores(block):
    return lax.ppermute(block, "tensor", [(0, 1), (1, 0)])


def by_exchange(own_rows):
    devices = lax.axis_size("dp")
    return own_rows % 16 == 0 and devices & (devices - 1) == 0


def relative(own_rows, swapped):
    if not by_exchange(own_rows):
        return list(range(WIDTH // 48))
    order = [0]
    for mask in steps_of(lax.axis_size("dp"), swapped):
        order = order + [r ^ mask for r in order]
    return order


def held_until(arrays, *gates):
    return lax.optimization_barrier((tuple(arrays), gates))[0]


def gather_start(shard):
    masks = steps_of(lax.axis_size("dp"), False)
    held = shard[None]
    if not by_exchange(shard.shape[0]) or len(masks) <= 3:
        return [held]
    first, second = masks[:2]
    return [held] + [exchanged(held, mask) for mask in (first, second, first ^ second)]


def joined(pieces):
    return lax.optimization_barrier(jnp.concatenate(pieces, axis=0))


def gather_middle(held, swapped, gate=None):
    if by_exchange(held.shape[1]):
        masks = steps_of(lax.axis_size("dp"), swapped)
        for mask in masks[held.shape[0].bit_length() - 1 : -1]:
            arrived = exchanged(held, mask)
            if gate is not None:
                (arrived,) = held_until((arrived,), gate)
            held = jnp.concatenate([held, arrived], axis=0)
    return held


def gather_finish(held, swapped):
    if not by_exchange(held.shape[1]):
        whole = lax.all_gather(held[0], "dp", axis=0, tiled=True)
        return [whole.reshape(WIDTH // 48, 48, held.shape[2])]
    return [held, exchanged(held, steps_of(lax.axis_size("dp"), swapped)[-1])]


def scatter_rounds(keep, other, own_rows, swapped):
    if not by_exchange(own_rows):
        total = keep.astype(F32) + other.astype(F32)
        total = lax.psum_scatter(total, "dp", scatter_dimension=0, tiled=True)
        while True:
            yield total[None]
    devices = lax.axis_size("dp")
    index = lax.axis_index("dp")
    levels = devices.bit_length() - 1
    masks = steps_of(devices, swapped)
    last = 2 if len(masks) > 3 else 0
    shape = (2,) * levels + (own_rows, keep.shape[1])
    keep, other = keep.reshape(shape), other.reshape(shape)
    for mask in reversed(masks[last:]):
        axis = levels - mask.bit_length()
        bit = (index & mask) // mask
        part = lambda array, which: lax.dynamic_slice_in_dim(array, which, 1, axis).astype(F32)
        sent = (part(keep, 1 - bit) + part(other, 1 - bit)).astype(BF16)
        keep = (part(keep, bit) + part(other, bit)).astype(BF16)
        gates = yield sent
        other = exchanged(sent, mask)
        if gates:
            (other,) = held_until((other,), *gates)
    total = (keep.astype(F32) + other.astype(F32)).reshape(2**last, own_rows, -1)
    while True:
        yield total


def scatter_finish(*totals, gates=()):
    if totals[0].shape[0] == 1:
        return jnp.concatenate([total[0] for total in totals], axis=1)
    unit = steps_of(lax.axis_size("dp"), False)[0]
    place = (lax.axis_index("dp") // unit) % 4

    def rows_of(which):
        parts = [lax.dynamic_index_in_dim(total, which, 0, keepdims=False) for total in totals]
        return jnp.concatenate(parts, axis=1)

    arrived = [exchanged(rows_of(place ^ j).astype(BF16), unit * j) for j in range(1, 4)]
    if gates:
        arrived = held_until(arrived, *gates)
    arrived = [part.astype(F32) for part in arrived]
    return rows_of(place) + (arrived[0] + arrived[1] + arrived[2])


def weight_grad(left, right):
    return lax.dot_general(
        left, right, (((0,), (0,)), ((), ())), preferred_element_type=F32
    ).astype(BF16)


def gain_part(weight, grad, gain):
    return jnp.sum(weight.astype(F32) * grad, axis=1) / gain.astype(F32)


def nt(left, right):
    return lax.dot_general(left, right, (((1,), (1,)), ((), ())), preferred_element_type=F32)


def nn(left, right):
    return jnp.dot(left, right, preferred_element_type=F32)


def start_slots(info, pieces, order, segments, sems):
    slot = 0
    for piece in pieces:
        rows = piece.shape[1]
        for at in range(piece.shape[0]):
            row = pl.multiple_of((info[0] ^ order[slot]) * rows, 16)
            for begin, width, target, column, sem in segments:
                pltpu.make_async_copy(
                    piece.at[at, :, pl.ds(begin, width)],
                    target.at[pl.ds(row, rows), pl.ds(column, width)],
                    sems.at[sem],
                ).start()
            slot += 1


def wait_whole(ref, sem):
    pltpu.make_async_copy(ref, ref, sem).wait()


def start_window(info, qkv_ref, edge_ref, window, sems):
    core = info[1]
    first = pl.multiple_of(jnp.where(core == 1, 0, WINDOW_HALF + ROWS), 16)
    last = pl.multiple_of(jnp.where(core == 1, WINDOW_HALF + ROWS, 0), 16)
    edge = pltpu.make_async_copy(
        edge_ref.at[:, pl.ds(0, 2 * WIDTH)],
        window.at[pl.ds(first, WINDOW_HALF), :],
        sems.at[PIECES],
    )
    edge.start()
    for piece in range(PIECES):
        begin, stop = piece_rows(piece)
        for part in range(2):
            for half in range(2):
                source = HALF * half + THIRD * (part + 1)
                target = WIDTH * part + THIRD * half
                pltpu.make_async_copy(
                    qkv_ref.at[pl.ds(begin - WINDOW_HALF, stop - begin), pl.ds(source, THIRD)],
                    window.at[pl.ds(begin, stop - begin), pl.ds(target, THIRD)],
                    sems.at[piece],
                ).start()
    window[pl.ds(last, WINDOW_HALF), :] = jnp.zeros((WINDOW_HALF, 2 * WIDTH), BF16)
    edge.wait()


def piece_rows(piece):
    return max(LANES * piece, WINDOW_HALF), min(LANES * (piece + 1), WINDOW_HALF + ROWS)


def wait_window(window, step, sems):
    for number in range(STEPS):
        first = BLOCKS * number + 1 if number else 0

        @pl.when(step == number)
        def _():
            for piece in range(first, BLOCKS * (number + 1) + 1):
                begin, stop = piece_rows(piece)
                wait_whole(window.at[pl.ds(begin, stop - begin), :], sems.at[piece])


def identity():
    row = lax.broadcasted_iota(jnp.int32, (LANES, LANES), 0)
    lane = lax.broadcasted_iota(jnp.int32, (LANES, LANES), 1)
    return jnp.where(row == lane, 1.0, 0.0).astype(BF16)


def turn_rows(unit, window, begin, row, turned_ref):
    for pair in range(PAIRS):
        lanes = slice(LANES * pair, LANES * (pair + 1))
        block = window[pl.ds(row, LANES), begin + LANES * pair : begin + LANES * (pair + 1)]
        turned_ref[lanes, pl.ds(row, LANES)] = nt(unit, block).astype(BF16)


def head_rows(columns):
    return jnp.concatenate([columns[:HEAD_DIM, :LANES], columns[HEAD_DIM:, LANES:]], axis=0)


def normalized(values):
    centred = values - jnp.mean(values, axis=-1, keepdims=True)
    spread = jnp.mean(centred * centred, axis=-1, keepdims=True)
    factor = lax.rsqrt(spread + 1e-05)
    return centred * factor, factor


def norm_backward(grad, unit, factor, gain):
    inner = grad * gain
    mean = jnp.mean(inner, axis=-1, keepdims=True)
    along = jnp.mean(inner * unit, axis=-1, keepdims=True)
    return factor * (inner - mean - unit * along)


def turned(values, cosine, sine):
    lane = lax.broadcasted_iota(jnp.int32, values.shape, 1)
    first = (lane & 32) == 0
    other = jnp.where(first, pltpu.roll(values, 96, 1), pltpu.roll(values, 32, 1))
    return values * cosine + other * sine


def both_heads(block):
    lane = lax.broadcasted_iota(jnp.int32, block.shape, 1)
    first = jnp.where(lane < HEAD_DIM, 1.0, 0.0).astype(block.dtype)
    second = jnp.where(lane < HEAD_DIM, 0.0, 1.0).astype(block.dtype)
    return jnp.concatenate([block * first, block * second], axis=0)


def table_kernel(cos_in, sin_in, seg_ref, cos_ref, sin_ref, cos_turned, sin_turned, col_ref):
    cos_ref[...] = cos_in[...]
    sin_ref[...] = sin_in[...]
    for block in range(ROWS // LANES):
        rows = slice(WINDOW_HALF + LANES * block, WINDOW_HALF + LANES * (block + 1))
        lanes = slice(LANES * block, LANES * (block + 1))
        cos_turned[:, lanes] = cos_in[rows, :].T
        sin_turned[:, lanes] = sin_in[rows, :].T
    for block in range(PIECES):
        row = jnp.broadcast_to(seg_ref[block : block + 1, :].astype(F32), (LANES, LANES))
        col_ref[LANES * block : LANES * (block + 1), :] = row.T.astype(jnp.int32)


def qkv_kernel(orders, counts, info, x_ref, cos_ref, sin_ref, *refs):
    parts = []
    for count in counts:
        parts.append(refs[:count])
        refs = refs[count:]
    own_a, other_a, own_b, other_b = parts
    qkv_ref, normed_ref, gain_ref, edge_ref, weight_ref, weight, sems = refs
    step = pl.program_id(0)
    rows = x_ref.shape[0]

    @pl.when(step == 0)
    def _():
        for begin, part_a, part_b in ((0, own_a, own_b), (WIDE, other_a, other_b)):
            start_slots(info, part_a, orders[0], [(0, FIRST_CUT, weight, begin, 0)], sems)
            start_slots(
                info,
                part_b,
                orders[1],
                [(0, WIDE - FIRST_CUT, weight, begin + FIRST_CUT, 0)],
                sems,
            )
        wait_whole(weight, sems.at[0])
        pltpu.make_async_copy(weight, weight_ref, sems.at[1]).start()
        row = lax.broadcasted_iota(jnp.int32, (16, LANES), 0)
        lane = lax.broadcasted_iota(jnp.int32, (16, LANES), 1)
        pick = jnp.where(row == lane, 1.0, 0.0).astype(BF16)
        gain_ref[...] = nt(pick, weight[:, HALF:WIDE])[:8]

    unit, unused = normalized(x_ref[...].astype(F32))
    normed = (unit * gain_ref[0:1, :]).astype(BF16)
    normed_ref[...] = normed
    table_rows = pl.ds(pl.multiple_of(WINDOW_HALF + step * rows, WINDOW_HALF), rows)
    cosine, sine = cos_ref[table_rows, :], sin_ref[table_rows, :]
    for half in range(2):
        result = nn(normed, weight[:, WIDE * half : WIDE * half + HALF])
        for tile in range(9):
            block = result[:, LANES * tile : LANES * (tile + 1)]
            if tile < 6:
                block = turned(block, cosine, sine)
            if tile < 3:
                block = block * (HEAD_DIM**-0.5)
            begin = HALF * half + LANES * tile
            qkv_ref[:, begin : begin + LANES] = block.astype(BF16)

    for core, at_step, begin in ((1, 0, 0), (0, ROWS // rows - 1, rows - WINDOW_HALF)):

        @pl.when((info[1] == core) & (step == at_step))
        def _():
            for part in range(2):
                for half in range(2):
                    source = HALF * half + THIRD * (part + 1)
                    target = WIDTH * part + THIRD * (1 - half)
                    edge_ref[:, target : target + THIRD] = qkv_ref[
                        begin : begin + WINDOW_HALF, source : source + THIRD
                    ]
            edge_ref[:, 2 * WIDTH :] = normed_ref[begin : begin + WINDOW_HALF, :]

    @pl.when(step == ROWS // rows - 1)
    def _():
        pltpu.make_async_copy(weight, weight_ref, sems.at[1]).wait()


def attend_kernel(
    info,
    row_seg,
    col_seg,
    q_own,
    q_other,
    qkv_ref,
    edge_ref,
    own_ref,
    other_ref,
    probs_ref,
    window,
    turned_values,
    sems,
):
    step = pl.program_id(0)
    unit = identity()

    @pl.when(step == 0)
    def _():
        start_window(info, qkv_ref, edge_ref, window, sems)

    wait_window(window, step, sems)

    @pl.when(step == 0)
    def _():
        turn_rows(unit, window, WIDTH, 0, turned_values)

    for block in range(BLOCKS):
        rows = slice(LANES * block, LANES * (block + 1))
        start = pl.multiple_of((step * BLOCKS + block) * LANES, LANES)
        turn_rows(unit, window, WIDTH, pl.multiple_of(start + LANES, LANES), turned_values)
        key_seg = col_seg[pl.ds(start, SPAN), :]
        key_at = lax.broadcasted_iota(jnp.int32, (SPAN, LANES), 0) - WINDOW_HALF
        query_at = lax.broadcasted_iota(jnp.int32, (SPAN, LANES), 1)
        near = jnp.abs(key_at - query_at) <= WINDOW_HALF
        allowed = (key_seg == row_seg[block]) & near
        bias = jnp.where(allowed, 0.0, -1e30)
        bias = jnp.concatenate([bias, bias], axis=1)

        scores, probs, results = [], [], []
        for pair in range(PAIRS):
            q_ref = q_own if pair < 3 else q_other
            queries = both_heads(q_ref[rows, LANES * (pair % 3) : LANES * (pair % 3 + 1)])
            keys = window[pl.ds(start, SPAN), LANES * pair : LANES * (pair + 1)]
            scores.append(nt(keys, queries) + bias)
        for pair in range(PAIRS):
            weights = jnp.exp(scores[pair] - jnp.max(scores[pair], axis=0, keepdims=True))
            total = jnp.sum(weights, axis=0, keepdims=True)
            probs.append((weights * (1.0 / total)).astype(BF16))
            probs_ref[block, pair] = probs[pair]
        for pair in range(PAIRS):
            values = turned_values[LANES * pair : LANES * (pair + 1), pl.ds(start, SPAN)]
            results.append(head_rows(nn(values, probs[pair])).astype(BF16))
        for pair in range(PAIRS):
            out_ref = own_ref if pair < 3 else other_ref
            out_ref[rows, LANES * (pair % 3) : LANES * (pair % 3 + 1)] = nt(unit, results[pair]).astype(
                BF16
            )


def mlp_kernel(orders, counts, info, x_ref, att_own, att_other, cot_ref, col_seg, gain_ref, *refs):
    parts = []
    for count in counts:
        parts.append(refs[:count])
        refs = refs[count:]
    in_own, in_other, down_own, down_other = parts
    (
        out_ref,
        hidden_grad_ref,
        att_grad_own,
        att_grad_other,
        normed_ref,
        gated_own,
        gated_other,
        pre_grad_own,
        pre_grad_other,
        low_grad_ref,
        out_grad_ref,
        w_in,
        w_down,
        sems,
    ) = refs
    step = pl.program_id(0)

    @pl.when(step == 0)
    def _():
        for number, part in enumerate((down_own, down_other)):
            start_slots(info, part, orders[1], [(0, DOWN, w_down, DOWN * number, 0)], sems)
        for number, part in enumerate((in_own, in_other)):
            start_slots(info, part, orders[0], [(0, HALF, w_in, HALF * number, 1)], sems)
        wait_whole(w_down, sems.at[0])
        other = pltpu.roll(w_down[:, 2 * DOWN - LANES :].astype(F32), HEAD_DIM, 1).astype(BF16)
        w_down[:, DOWN - LANES : DOWN] += other

    gain = gain_ref[1:2, :]
    hidden = (
        x_ref[...].astype(F32)
        + nt(att_own[...], w_down[:, :THIRD])
        + nt(att_other[...], w_down[:, DOWN : DOWN + THIRD])
    )
    unit, factor = normalized(hidden)
    normed = (unit * gain).astype(BF16)
    normed_ref[...] = normed
    seg_rows = pl.ds(pl.multiple_of(WINDOW_HALF + step * x_ref.shape[0], WINDOW_HALF), x_ref.shape[0])
    live = jnp.where(col_seg[seg_rows, :] >= 0, 1.0, 0.0)
    live = jnp.concatenate([live] * (WIDTH // LANES), axis=1)
    out_grad = cot_ref[...].astype(F32) * live
    out_grad_low = out_grad.astype(BF16)
    out_grad_ref[...] = out_grad_low

    @pl.when(step == 0)
    def _():
        wait_whole(w_in, sems.at[1])

    pre = [nn(normed, w_in[:, HALF * half : HALF * (half + 1)]) for half in range(2)]
    tails = [part[:, 2 * UNITS :] for part in pre]
    lane = lax.broadcasted_iota(jnp.int32, tails[0].shape, 1)
    low = lane < HEAD_DIM
    gates = [part[:, :UNITS] for part in pre]
    gates.append(jnp.where(low, tails[0], pltpu.roll(tails[1], 64, 1)))
    ups = [part[:, UNITS : 2 * UNITS] for part in pre]
    ups.append(jnp.where(low, pltpu.roll(tails[0], 64, 1), tails[1]))
    pre_grads = (pre_grad_own, pre_grad_other)
    unit_columns = (
        slice(THIRD, THIRD + UNITS),
        slice(DOWN + THIRD, DOWN + THIRD + UNITS),
        slice(DOWN - LANES, DOWN),
    )
    for part, (gate, up) in enumerate(zip(gates, ups)):
        share = 0.5 + 0.5 * lax.erf(gate * (0.5**0.5))
        slope = share + gate * (jnp.exp(-0.5 * gate * gate) * 0.3989422804014327)
        curve = gate * share
        gated = curve * up
        grad = nn(out_grad_low, w_down[:, unit_columns[part]])
        gate_grad = grad * up * slope
        up_grad = grad * curve
        if part < 2:
            (gated_own, gated_other)[part][:, :UNITS] = gated.astype(BF16)
            pre_grads[part][:, :UNITS] = gate_grad.astype(BF16)
            pre_grads[part][:, UNITS : 2 * UNITS] = up_grad.astype(BF16)
        else:
            gated_own[:, UNITS:] = gated.astype(BF16)
            gated_other[:, UNITS:] = pltpu.roll(gated, HEAD_DIM, 1).astype(BF16)
            own = jnp.where(low, gate_grad, pltpu.roll(up_grad, 64, 1))
            other = jnp.where(low, pltpu.roll(gate_grad, 64, 1), up_grad)
            pre_grad_own[:, 2 * UNITS :] = own.astype(BF16)
            pre_grad_other[:, 2 * UNITS :] = other.astype(BF16)
    product = (
        nt(gated_own[...], w_down[:, THIRD:DOWN])
        + nt(gated_other[:, :UNITS], w_down[:, unit_columns[1]])
    )
    out_ref[...] = (hidden + product).astype(BF16)
    normed_grad = nt(pre_grad_own[...], w_in[:, :HALF]) + nt(pre_grad_other[...], w_in[:, HALF:])
    hidden_grad = out_grad + norm_backward(normed_grad, unit, factor, gain)
    hidden_grad_ref[...] = hidden_grad
    hidden_grad_low = hidden_grad.astype(BF16)
    low_grad_ref[...] = hidden_grad_low
    att_grad_own[...] = nn(hidden_grad_low, w_down[:, :THIRD]).astype(BF16)
    att_grad_other[...] = nn(hidden_grad_low, w_down[:, DOWN : DOWN + THIRD]).astype(BF16)


def attend_back_kernel(
    info,
    q_own,
    q_other,
    probs_ref,
    grad_own,
    grad_other,
    cos_ref,
    sin_ref,
    cos_turned,
    sin_turned,
    qkv_ref,
    edge_ref,
    out_own,
    out_other,
    edge_out_ref,
    window,
    turned_keys,
    key_grad,
    value_grad,
    sems,
):
    step = pl.program_id(0)
    unit = identity()

    @pl.when(step == 0)
    def _():
        start_window(info, qkv_ref, edge_ref, window, sems)
        key_grad[...] = jnp.zeros_like(key_grad)
        value_grad[...] = jnp.zeros_like(value_grad)

    wait_window(window, step, sems)

    @pl.when(step == 0)
    def _():
        turn_rows(unit, window, 0, 0, turned_keys)

    for block in range(BLOCKS):
        rows = slice(LANES * block, LANES * (block + 1))
        start = pl.multiple_of((step * BLOCKS + block) * LANES, LANES)
        span = pl.ds(start, SPAN)
        turn_rows(unit, window, 0, pl.multiple_of(start + LANES, LANES), turned_keys)
        cosine, sine = cos_turned[:, rows], sin_turned[:, rows]

        all_lanes = [slice(LANES * pair, LANES * (pair + 1)) for pair in range(PAIRS)]
        grads, probs_grads, score_grads, query_grads = [], [], [], []
        for pair, lanes in enumerate(all_lanes):
            grad_ref = grad_own if pair < 3 else grad_other
            grads.append(both_heads(grad_ref[rows, LANES * (pair % 3) : LANES * (pair % 3 + 1)]))
            values = window[span, WIDTH + LANES * pair : WIDTH + LANES * (pair + 1)]
            probs_grads.append(nt(values, grads[pair]))
        for pair, lanes in enumerate(all_lanes):
            value_grad[span, lanes] += nn(probs_ref[block, pair], grads[pair])
        for pair in range(PAIRS):
            probs = probs_ref[block, pair].astype(F32)
            weighted = probs_grads[pair] * probs
            delta = jnp.sum(weighted, axis=0, keepdims=True)
            score_grads.append((weighted - probs * delta).astype(BF16))
        for pair, lanes in enumerate(all_lanes):
            query_grads.append(head_rows(nn(turned_keys[lanes, span], score_grads[pair])))
        for pair, lanes in enumerate(all_lanes):
            q_ref = q_own if pair < 3 else q_other
            queries = both_heads(q_ref[rows, LANES * (pair % 3) : LANES * (pair % 3 + 1)])
            key_grad[span, lanes] += nn(score_grads[pair], queries)
        for pair in range(PAIRS):
            grad = query_grads[pair] * (HEAD_DIM**-0.5)
            other = jnp.concatenate([grad[32:64], grad[:32], grad[96:], grad[64:96]], axis=0)
            query_grads[pair] = (grad * cosine - other * sine).astype(BF16)
        for pair in range(PAIRS):
            out_ref = out_own if pair < 3 else out_other
            place = slice(LANES * (pair % 3), LANES * (pair % 3 + 1))
            out_ref[pl.ds(start, LANES), place] = nt(unit, query_grads[pair]).astype(BF16)

    @pl.when(step == STEPS - 1)
    def _():
        inside = slice(WINDOW_HALF, WINDOW_HALF + ROWS)
        row = pl.multiple_of(jnp.where(info[1] == 1, 0, WINDOW_HALF + ROWS), 16)
        edge_rows = pl.ds(row, WINDOW_HALF)
        for pair in range(PAIRS):
            out_ref = out_own if pair < 3 else out_other
            lanes = slice(LANES * pair, LANES * (pair + 1))
            begin = LANES * (pair % 3)
            target = (LANES * pair + THIRD) % WIDTH
            keys_at = slice(THIRD + begin, THIRD + begin + LANES)
            values_at = slice(2 * THIRD + begin, 2 * THIRD + begin + LANES)
            out_ref[:ROWS, keys_at] = turned(
                key_grad[inside, lanes], cos_ref[inside, :], -sin_ref[inside, :]
            ).astype(BF16)
            out_ref[:ROWS, values_at] = value_grad[inside, lanes].astype(BF16)
            edge_keys = turned(
                key_grad[edge_rows, lanes], cos_ref[edge_rows, :], -sin_ref[edge_rows, :]
            ).astype(BF16)
            edge_values = value_grad[edge_rows, lanes].astype(BF16)
            edge_out_ref[:, target : target + LANES] = edge_keys
            edge_out_ref[:, WIDTH + target : WIDTH + target + LANES] = edge_values
            out_ref[ROWS:, begin : begin + LANES] = jnp.zeros((WINDOW_HALF, LANES), BF16)
            out_ref[ROWS:, keys_at] = edge_keys
            out_ref[ROWS:, values_at] = edge_values


def input_grad_kernel(
    info, x_ref, own_ref, other_ref, edge_ref, hidden_ref, gain_ref, weight, out_ref, fixed
):
    rows = x_ref.shape[0]
    step = pl.program_id(0)
    grad = None
    for half, grad_ref in enumerate((own_ref, other_ref)):
        fixed[...] = grad_ref[...]
        for core, at_step, begin in ((1, 0, 0), (0, ROWS // rows - 1, rows - WINDOW_HALF)):

            @pl.when((info[1] == core) & (step == at_step))
            def _():
                at = slice(begin, begin + WINDOW_HALF)
                for part in range(2):
                    to = slice(THIRD * (part + 1), THIRD * (part + 2))
                    source = WIDTH * part + THIRD * half
                    add = edge_ref[:, source : source + THIRD].astype(F32)
                    fixed[at, to] = (fixed[at, to].astype(F32) + add).astype(BF16)

        part = nt(fixed[...], weight[:, WIDE * half : WIDE * half + HALF])
        grad = part if grad is None else grad + part
    unit, factor = normalized(x_ref[...].astype(F32))
    out_ref[...] = hidden_ref[...] + norm_backward(grad, unit, factor, gain_ref[0:1, :])


def shape_of(shape, dtype=BF16):
    return jax.ShapeDtypeStruct(shape, dtype)


def call(
    kernel, info, grid, ins, in_specs, outs, out_specs, scratch, flops, vmem, after=()
):
    moved = sum(a.size * a.dtype.itemsize for a in list(ins) + list(outs))
    first = 1 + len(ins)
    later = first + len(after)
    return pl.pallas_call(
        lambda *refs: kernel(*refs[:first], *refs[later:]),
        out_shape=outs,
        grid_spec=pltpu.PrefetchScalarGridSpec(
            num_scalar_prefetch=1,
            grid=grid,
            in_specs=list(in_specs) + [ANYWHERE] * len(after),
            out_specs=out_specs,
            scratch_shapes=scratch,
        ),
        compiler_params=pltpu.CompilerParams(
            dimension_semantics=("arbitrary",), vmem_limit_bytes=vmem * MIB
        ),
        cost_estimate=pl.CostEstimate(
            flops=int(flops), bytes_accessed=int(moved), transcendentals=0
        ),
    )(info, *ins, *after)


def by_rows(rows, columns):
    return pl.BlockSpec((rows, columns), lambda i, s: (i, 0))


def full(*shape):
    return pl.BlockSpec(shape, lambda i, s: (0,) * len(shape))


def body(
    tokens,
    segment,
    norm_attn_gain,
    qkv_weight,
    attn_out_weight,
    norm_mlp_gain,
    in_weight,
    out_weight,
    cotangent,
):
    own_rows = norm_attn_gain.shape[0]
    core = lax.axis_index("tensor")
    place = lax.axis_index("dp") if by_exchange(own_rows) else 0
    info = jnp.stack([jnp.int32(place), core.astype(jnp.int32)])
    orders = (relative(own_rows, False), relative(own_rows, True))

    gains = jnp.pad(jnp.stack([norm_attn_gain, norm_mlp_gain], axis=1), ((0, 0), (0, LANES - 2)))
    flat_qkv = qkv_weight.reshape(own_rows, HALF)
    first_pieces = gather_start(jnp.concatenate([flat_qkv, gains], axis=1))
    shard_in = jnp.concatenate(
        [
            in_weight[:, 0, :UNITS],
            in_weight[:, 1, :UNITS],
            in_weight[:, 0, UNITS:],
            in_weight[:, 1, UNITS:],
        ],
        axis=1,
    )
    turned_out = out_weight.T
    blank = jnp.zeros((own_rows, HEAD_DIM), BF16)
    shard_down = jnp.concatenate([attn_out_weight.T, turned_out, blank], axis=1)
    second_shard = jnp.concatenate([shard_in, shard_down], axis=1)
    second_shard, *first_pieces = held_until([second_shard] + first_pieces)
    second_pieces = gather_start(second_shard)

    own_segment = lax.dynamic_slice_in_dim(segment, core * ROWS, ROWS, 0)
    seg_pad = jnp.pad(segment, (WINDOW_HALF, WINDOW_HALF), constant_values=-2)
    span_segment = lax.dynamic_slice_in_dim(seg_pad, core * ROWS, ROWS + 2 * WINDOW_HALF, 0)
    slot = core * ROWS - WINDOW_HALF + jnp.arange(ROWS + 2 * WINDOW_HALF, dtype=jnp.int32)
    position = jnp.where(span_segment >= 0, slot - PAD_BLOCK * span_segment, 0)
    lane = jnp.arange(LANES, dtype=jnp.int32)
    exponent = (lane % 32).astype(F32) * (2.0 / HEAD_DIM)
    angle = position.astype(F32)[:, None] * jnp.power(10000.0, -exponent)[None, :]
    cos_span = jnp.cos(angle)
    sin_span = jnp.sin(angle) * jnp.where((lane & 32) == 0, -1.0, 1.0)[None, :]
    table_shape = shape_of(cos_span.shape, F32)
    turned_table = shape_of((LANES, ROWS), F32)
    cos_span, sin_span, cos_turned, sin_turned, col_seg = pl.pallas_call(
        table_kernel,
        out_shape=[
            table_shape,
            table_shape,
            turned_table,
            turned_table,
            shape_of(cos_span.shape, jnp.int32),
        ],
        compiler_params=pltpu.CompilerParams(vmem_limit_bytes=58 * MIB),
    )(cos_span, sin_span, span_segment.reshape(PIECES, LANES))
    row_seg = own_segment.reshape(ROWS // LANES, 1, LANES)

    rows = 384
    steps = ROWS // rows
    first_held = joined(first_pieces)
    held_a, held_b = first_held[:, :, :FIRST_CUT], first_held[:, :, FIRST_CUT:]
    own_a = gather_finish(gather_middle(held_a, False), False)
    own_b = gather_finish(gather_middle(held_b, True), True)
    second_held = joined(second_pieces)
    held_in, held_down = second_held[:, :, :HALF], second_held[:, :, HALF:]
    own_a[-1], own_b[-1] = held_until(
        (own_a[-1], own_b[-1]), held_in, held_down, cos_span, row_seg, info
    )
    own_a, own_b = [jnp.concatenate(own_a, axis=0)], [jnp.concatenate(own_b, axis=0)]
    other_a, other_b = [swapped_cores(own_a[0])], [swapped_cores(own_b[0])]

    parts = (own_a, other_a, own_b, other_b)
    counts_qkv = tuple(len(part) for part in parts)
    qkv, normed, gain_rows, edge, weight_qkv = call(
        lambda *refs: qkv_kernel(orders, counts_qkv, *refs),
        info,
        (steps,),
        [tokens, cos_span, sin_span] + [piece for part in parts for piece in part],
        [by_rows(rows, WIDTH), full(*cos_span.shape), full(*cos_span.shape)]
        + [ANYWHERE] * sum(counts_qkv),
        [
            shape_of((ROWS, 2 * HALF)),
            shape_of((MORE_ROWS, WIDTH)),
            shape_of((8, WIDTH), F32),
            shape_of((WINDOW_HALF, 3 * WIDTH)),
            shape_of((WIDTH, 2 * WIDE)),
        ],
        [by_rows(rows, 2 * HALF), by_rows(rows, WIDTH), full(8, WIDTH)]
        + [full(WINDOW_HALF, 3 * WIDTH), ANYWHERE],
        [
            pltpu.VMEM((WIDTH, 2 * WIDE), BF16),
            pltpu.SemaphoreType.DMA((2,)),
        ],
        2 * ROWS * WIDTH * 2 * HALF,
        58,
    )
    edge = swapped_cores(edge)
    normed = lax.dynamic_update_slice(normed, edge[:, 2 * WIDTH :], (ROWS, 0))
    held_in = gather_middle(held_in, False, qkv)
    held_down = gather_middle(held_down, True, qkv)
    in_own, down_own = gather_finish(held_in, False), gather_finish(held_down, True)

    blocks = ROWS // LANES
    window_shape = (ROWS + 2 * WINDOW_HALF, 2 * WIDTH)
    turned_shape = (WIDTH, ROWS + 2 * WINDOW_HALF)
    step_rows = BLOCKS * LANES
    other_queries = pl.BlockSpec((step_rows, THIRD), lambda i, s: (i, HALF // THIRD))
    by_block = pl.BlockSpec((BLOCKS, PAIRS, SPAN, SPAN), lambda i, s: (i, 0, 0, 0))
    att_own, att_other, probs = call(
        attend_kernel,
        info,
        (STEPS,),
        [row_seg, col_seg, qkv, qkv, qkv, edge],
        [
            pl.BlockSpec((BLOCKS, 1, LANES), lambda i, s: (i, 0, 0)),
            full(ROWS + 2 * WINDOW_HALF, LANES),
            by_rows(step_rows, THIRD),
            other_queries,
            ANYWHERE,
            ANYWHERE,
        ],
        [
            shape_of((ROWS, THIRD)),
            shape_of((ROWS, THIRD)),
            shape_of((blocks, PAIRS, SPAN, SPAN)),
        ],
        [by_rows(step_rows, THIRD), by_rows(step_rows, THIRD), by_block],
        [
            pltpu.VMEM(window_shape, BF16),
            pltpu.VMEM(turned_shape, BF16),
            pltpu.SemaphoreType.DMA((PIECES + 1,)),
        ],
        blocks * PAIRS * 2 * 2 * SPAN * SPAN * LANES,
        58,
        after=[held_in, held_down],
    )

    in_own[-1], down_own[-1] = held_until((in_own[-1], down_own[-1]), att_own)
    in_other = [swapped_cores(piece) for piece in in_own]
    down_other = [swapped_cores(piece) for piece in down_own]
    (mlp_info,) = held_until((info,), normed)
    parts = (in_own, in_other, down_own, down_other)
    counts = tuple(len(part) for part in parts)
    (
        layer_out,
        hidden_grad,
        att_grad_own,
        att_grad_other,
        normed_two,
        gated_own,
        gated_other,
        pre_grad_own,
        pre_grad_other,
        hidden_grad_low,
        out_grad,
    ) = call(
        lambda *refs: mlp_kernel(orders, counts, *refs),
        mlp_info,
        (steps,),
        [tokens, att_own, att_other, cotangent, col_seg, gain_rows]
        + [piece for part in parts for piece in part],
        [by_rows(rows, WIDTH), by_rows(rows, THIRD), by_rows(rows, THIRD), by_rows(rows, WIDTH)]
        + [full(*cos_span.shape), full(8, WIDTH)]
        + [ANYWHERE] * sum(counts),
        [
            shape_of((ROWS, WIDTH)),
            shape_of((ROWS, WIDTH), F32),
            shape_of((ROWS, THIRD)),
            shape_of((ROWS, THIRD)),
            shape_of((ROWS, WIDTH)),
            shape_of((ROWS, UNITS + LANES)),
            shape_of((ROWS, UNITS + LANES)),
            shape_of((ROWS, HALF)),
            shape_of((ROWS, HALF)),
            shape_of((ROWS, WIDTH)),
            shape_of((ROWS, WIDTH)),
        ],
        [by_rows(rows, WIDTH)] * 2
        + [by_rows(rows, THIRD)] * 2
        + [by_rows(rows, WIDTH)]
        + [by_rows(rows, UNITS + LANES)] * 2
        + [by_rows(rows, HALF)] * 2
        + [by_rows(rows, WIDTH)] * 2,
        [
            pltpu.VMEM((WIDTH, 2 * HALF), BF16),
            pltpu.VMEM((WIDTH, 2 * DOWN), BF16),
            pltpu.SemaphoreType.DMA((2,)),
        ],
        2 * ROWS * WIDTH * (4 * HALF + 2 * HALF + 2 * WIDTH),
        58,
    )

    def down_grads(att, gated):
        parts = [weight_grad(hidden_grad_low, att), weight_grad(out_grad, gated)]
        return jnp.concatenate(parts, axis=1)

    send_in = weight_grad(normed_two, pre_grad_other)
    send_down = down_grads(att_other, gated_other)
    keep_in = weight_grad(normed_two, pre_grad_own)
    keep_down = down_grads(att_own, gated_own)
    rounds_in = scatter_rounds(keep_in, swapped_cores(send_in), own_rows, False)
    rounds_down = scatter_rounds(keep_down, swapped_cores(send_down), own_rows, True)
    next(rounds_in), next(rounds_down)
    second_in, second_down = rounds_in.send(()), rounds_down.send(())
    sum_in, sum_down = rounds_in.send(()), rounds_down.send(())

    grad_own, grad_other, edge_grad = call(
        attend_back_kernel,
        info,
        (STEPS,),
        [qkv, qkv, probs, att_grad_own, att_grad_other, cos_span, sin_span]
        + [cos_turned, sin_turned, qkv, edge],
        [by_rows(step_rows, THIRD), other_queries, by_block]
        + [by_rows(step_rows, THIRD)] * 2
        + [full(*cos_span.shape)] * 2
        + [pl.BlockSpec((LANES, step_rows), lambda i, s: (0, i))] * 2
        + [ANYWHERE] * 2,
        [shape_of((MORE_ROWS, HALF))] * 2 + [shape_of((WINDOW_HALF, 2 * WIDTH))],
        [full(MORE_ROWS, HALF)] * 2 + [full(WINDOW_HALF, 2 * WIDTH)],
        [
            pltpu.VMEM(window_shape, BF16),
            pltpu.VMEM(turned_shape, BF16),
            pltpu.VMEM((window_shape[0], WIDTH), F32),
            pltpu.VMEM((window_shape[0], WIDTH), F32),
            pltpu.SemaphoreType.DMA((PIECES + 1,)),
        ],
        blocks * PAIRS * 4 * 2 * SPAN * SPAN * LANES,
        58,
        after=[send_in, send_down, keep_in],
    )
    edge_grad = swapped_cores(edge_grad)
    (normed,) = held_until((normed,), second_in, second_down)

    send_a = weight_grad(normed, grad_other[:, :FIRST_CUT])
    send_b = weight_grad(normed, grad_other[:, FIRST_CUT:])
    keep_a = weight_grad(normed, grad_own[:, :FIRST_CUT])
    keep_b = weight_grad(normed, grad_own[:, FIRST_CUT:])
    late_a, late_b = swapped_cores(send_a), swapped_cores(send_b)

    (late_info,) = held_until(
        (info,), keep_a, keep_b, late_a, late_b, sum_in, sum_down
    )
    (grad_tokens,) = call(
        input_grad_kernel,
        late_info,
        (steps,),
        [tokens, grad_own, grad_other, edge_grad, hidden_grad, gain_rows, weight_qkv],
        [by_rows(rows, WIDTH), by_rows(rows, HALF), by_rows(rows, HALF)]
        + [full(WINDOW_HALF, 2 * WIDTH), by_rows(rows, WIDTH)]
        + [full(8, WIDTH), full(WIDTH, 2 * WIDE)],
        [shape_of((ROWS, WIDTH), F32)],
        [by_rows(rows, WIDTH)],
        [pltpu.VMEM((rows, HALF), BF16)],
        2 * ROWS * WIDTH * 2 * HALF,
        28,
    )
    rounds_a = scatter_rounds(keep_a, late_a, own_rows, False)
    rounds_b = scatter_rounds(keep_b, late_b, own_rows, True)
    sum_in, sum_down = held_until((sum_in, sum_down), next(rounds_a), next(rounds_b))
    second = rounds_a.send((grad_tokens,)), rounds_b.send((grad_tokens,))
    owned_early = scatter_finish(sum_in, sum_down, gates=second)
    sum_a, sum_b = rounds_a.send((owned_early,)), rounds_b.send((owned_early,))
    owned_in, owned_down = owned_early[:, :HALF], owned_early[:, HALF:]

    flat_grad = scatter_finish(sum_a, sum_b)
    gain_grads = jnp.stack(
        [
            gain_part(flat_qkv, flat_grad, norm_attn_gain),
            gain_part(shard_in, owned_in, norm_mlp_gain),
        ]
    )
    owned_qkv = flat_grad.reshape(own_rows, 3, THIRD)
    owned_in = jnp.stack(
        [
            jnp.concatenate([owned_in[:, :UNITS], owned_in[:, 2 * UNITS : -64]], axis=1),
            jnp.concatenate([owned_in[:, UNITS : 2 * UNITS], owned_in[:, -64:]], axis=1),
        ],
        axis=1,
    )
    owned_attn = owned_down[:, :THIRD].T
    owned_out = owned_down[:, THIRD : THIRD + UNITS + HEAD_DIM].T
    (gain_grads,) = held_until((gain_grads,), owned_in, owned_attn, owned_out)
    gain_grads = gain_grads + swapped_cores(gain_grads)
    owned_gain_one, owned_gain_two = gain_grads[0], gain_grads[1]
    return (
        layer_out,
        grad_tokens,
        owned_gain_one,
        owned_qkv,
        owned_attn,
        owned_gain_two,
        owned_in,
        owned_out,
    )


def solution(mesh):
    placed = (
        P(("dp", "tensor"), None),
        P("dp"),
        P("dp"),
        P("dp", None, "tensor"),
        P("tensor", "dp"),
        P("dp"),
        P("dp", None, "tensor"),
        P("tensor", "dp"),
        P(("dp", "tensor"), None),
    )
    return jax.shard_map(
        body,
        mesh=mesh,
        in_specs=placed,
        out_specs=(
            P(("dp", "tensor"), None),
            P(("dp", "tensor"), None),
            P("dp"),
            P("dp", None, "tensor"),
            P("tensor", "dp"),
            P("dp"),
            P("dp", None, "tensor"),
            P("tensor", "dp"),
        ),
        check_vma=False,
    )
```
